32 devices in a mesh: section: 2 (over core), dp: 16 (over z, y, x).
Axes of the slice: x: 2, y: 2, z: 4, core: 2. Of those that a mesh axis runs over, the one named last changes fastest.
Arguments:
- clips: bfloat16 [8, 16, 4, 8, 8, 128], P(None, 'dp'), may hold values from -6 to 6
- cotangent: bfloat16 [8, 16, 4, 8, 8, 128], P(None, 'dp'), may hold values from -6 to 6
- weights: bfloat16 [2, 3456, 128], P('section', 'dp'), may hold values from -0.078125 to 0.078125
Outputs:
- section_outs: bfloat16 [2, 8, 16, 4, 8, 8, 128], P('section', None, 'dp')
- weight_grads: float32 [2, 3456, 128], P('section', 'dp')
The draws below stay inside these ranges and needn't reach their ends.
All inputs are finite; a program needn't handle non-finite values.
Results may differ from the reference program's by a relative error of at most 0.027.
Values may be sent and summed in bfloat16 or wider, within the bound.
No kernel may reach another device: no remote copies, remote signals or barrier semaphores. Data moves between devices by JAX's collectives and lax.ppermute only.
A program may use at most 64 MiB of HBM per device.

```python
import jax
import jax.numpy as jnp
from jax import lax

C = 128
TF = 4
HT = 8
WT = 8
MB = 8
CLIPS = 16
KROWS = 3456
N_SECTION = 2


def levels(key, shape, shards, low, top_value):
    def one(position, shards_of):
        draws = jax.random.uniform(jax.random.fold_in(jax.random.fold_in(key, 6), position), (shards_of,), jnp.float32, low / len(shards), top_value / len(shards))
        return jnp.repeat(jnp.exp(draws), shape[position] // shards_of).reshape((-1,) + (1,) * (len(shape) - position - 1))

    factor_of = one(*shards[0])
    for cut in shards[1:]:
        factor_of = factor_of * one(*cut)
    return factor_of


def noise(rng, extent, scale, reach, cuts=(), held_as=jnp.bfloat16):
    level = levels(rng, extent, cuts, -0.22, 0.18) if cuts else 1.0
    entries = jax.random.normal(rng, extent, jnp.float32) * scale * level
    return jnp.minimum(jnp.maximum(entries, -reach), reach).astype(held_as)


def setup_inputs(seed: int = 0) -> dict:
    arg_keys = jax.random.split(jax.random.key(seed), 4)
    clips = noise(arg_keys[0], (MB, CLIPS, TF, HT, WT, C), 1.0, 6.0, ((1, 16),))
    cotangent = noise(arg_keys[1], (MB, CLIPS, TF, HT, WT, C), 1.0, 6.0, ((1, 16),))
    weights = noise(arg_keys[2], (N_SECTION, KROWS, C), (2 * KROWS) ** -0.5, 0.078125, ((0, 2), (1, 16)))
    return {"clips": clips, "cotangent": cotangent, "weights": weights}


def gather_patches(field):
    frames, height, width, channels = field.shape
    first_frame = field[:1]
    padded = jnp.concatenate([first_frame, first_frame, field], axis=0)
    padded = jnp.pad(padded, ((0, 0), (1, 1), (1, 1), (0, 0)))
    pieces = [padded[offset_time:offset_time + frames, offset_row:offset_row + height, offset_col:offset_col + width] for offset_time in range(3) for offset_row in range(3) for offset_col in range(3)]
    return jnp.stack(pieces, axis=3).reshape(frames * height * width, 27 * channels)

def squash_columns(activation):
    squashed = jax.nn.silu(activation.astype(jnp.float32)).astype(jnp.bfloat16)
    return gather_patches(squashed)

def layer_forward(activation, weight):
    branch = jnp.dot(squash_columns(activation), weight, preferred_element_type=jnp.float32)
    return (activation.astype(jnp.float32) + branch.reshape(activation.shape)).astype(jnp.bfloat16)

def input_gradient(activation, upstream, weight):
    flat_grad = upstream.reshape(-1, weight.shape[1])
    column_grad = lax.dot_general(flat_grad, weight, (((1,), (1,)), ((), ())), preferred_element_type=jnp.float32)
    base = activation.astype(jnp.float32)
    _, unfold = jax.vjp(gather_patches, base)
    field_grad = unfold(column_grad)[0]
    sigmoid_value = jax.nn.sigmoid(base)
    slope = sigmoid_value * (1.0 + base * (1.0 - sigmoid_value))
    return (upstream.astype(jnp.float32) + field_grad * slope).astype(jnp.bfloat16)

def weight_term(activation, upstream):
    flat_grad = upstream.reshape(-1, upstream.shape[-1])
    return lax.dot_general(squash_columns(activation), flat_grad, (((0,), (0,)), ((), ())), preferred_element_type=jnp.float32)

def reference(clips, cotangent, weights):
    section_count = weights.shape[0]
    lead_shape = clips.shape[:2]
    acts = clips.reshape((-1,) + clips.shape[2:])
    inputs_kept = []
    outputs_kept = []
    for section in range(section_count):
        inputs_kept.append(acts)
        layer_weight = weights[section]

        def run_one(activation, layer_weight=layer_weight):
            return layer_forward(activation, layer_weight)
        acts = lax.map(run_one, acts)
        outputs_kept.append(acts)
    grad = cotangent.reshape(acts.shape)
    grads_kept = [None] * section_count
    for section in reversed(range(section_count)):
        layer_weight = weights[section]

        def accumulate(running, pair, layer_weight=layer_weight):
            activation, upstream = pair
            return (running + weight_term(activation, upstream), input_gradient(activation, upstream, layer_weight))
        start_total = jnp.zeros(layer_weight.shape, jnp.float32)
        running, grad = lax.scan(accumulate, start_total, (inputs_kept[section], grad))
        grads_kept[section] = running
    section_outs = jnp.stack(outputs_kept).reshape((section_count,) + lead_shape + clips.shape[2:])
    return (section_outs, jnp.stack(grads_kept))
```

```python
import functools

import jax
import jax.numpy as jnp
from jax import lax
from jax.experimental import pallas as pl
from jax.experimental.pallas import tpu as pltpu
from jax.sharding import PartitionSpec as P


def passed_along(block, axis, distance):
    devices = range(lax.axis_size(axis))
    route = [(i - distance, i) for i in devices if i - distance in devices]
    return lax.ppermute(block, axis, route)


def gather_patches(field):
    frames, height, width, channels = field.shape
    first_frame = field[:1]
    padded = jnp.concatenate([first_frame, first_frame, field], axis=0)
    padded = jnp.pad(padded, ((0, 0), (1, 1), (1, 1), (0, 0)))
    pieces = [
        padded[
            offset_time : offset_time + frames,
            offset_row : offset_row + height,
            offset_col : offset_col + width,
        ]
        for offset_time in range(3)
        for offset_row in range(3)
        for offset_col in range(3)
    ]
    return jnp.stack(pieces, axis=3).reshape(frames * height * width, 27 * channels)


def squash_field(activation):
    return jax.nn.silu(activation.astype(jnp.float32)).astype(jnp.bfloat16)


def squash_columns(activation):
    return gather_patches(squash_field(activation))


def layer_forward(activation, weight):
    branch = jnp.dot(squash_columns(activation), weight, preferred_element_type=jnp.float32)
    return (activation.astype(jnp.float32) + branch.reshape(activation.shape)).astype(jnp.bfloat16)


def input_gradient(activation, upstream, weight):
    flat_grad = upstream.reshape(-1, weight.shape[1])
    column_grad = lax.dot_general(
        flat_grad, weight, (((1,), (1,)), ((), ())), preferred_element_type=jnp.float32
    )
    base = activation.astype(jnp.float32)
    _, unfold = jax.vjp(gather_patches, base)
    field_grad = unfold(column_grad)[0]
    sigmoid_value = jax.nn.sigmoid(base)
    slope = sigmoid_value * (1.0 + base * (1.0 - sigmoid_value))
    return (upstream.astype(jnp.float32) + field_grad * slope).astype(jnp.bfloat16)


def weight_term(activation, upstream):
    flat_grad = upstream.reshape(-1, upstream.shape[-1])
    return lax.dot_general(
        squash_columns(activation),
        flat_grad,
        (((0,), (0,)), ((), ())),
        preferred_element_type=jnp.float32,
    )


def many_sections(clips, cotangent, weights):
    section_total = lax.axis_size("section")
    section_index = lax.axis_index("section")
    weight = lax.all_gather(weights, "dp", axis=1, tiled=True)[0]
    local_clips = clips[:, 0]
    local_grads = cotangent[:, 0]
    micro_count = local_clips.shape[0]
    step_count = micro_count + section_total - 1
    empty_field = jnp.zeros(local_clips.shape[1:], jnp.bfloat16)

    def forward_step(step_index, carry):
        received, saved_inputs, produced = carry
        micro_index = step_index - section_index
        active = (micro_index >= 0) & (micro_index < micro_count)
        slot_index = jnp.clip(micro_index, 0, micro_count - 1)
        fresh = lax.dynamic_index_in_dim(local_clips, slot_index, 0, keepdims=False)
        layer_input = jnp.where(section_index == 0, fresh, received)
        layer_output = layer_forward(layer_input, weight)
        kept_input = jnp.where(
            active,
            layer_input,
            lax.dynamic_index_in_dim(saved_inputs, slot_index, 0, keepdims=False),
        )
        kept_output = jnp.where(
            active, layer_output, lax.dynamic_index_in_dim(produced, slot_index, 0, keepdims=False)
        )
        saved_inputs = lax.dynamic_update_index_in_dim(saved_inputs, kept_input, slot_index, 0)
        produced = lax.dynamic_update_index_in_dim(produced, kept_output, slot_index, 0)
        received = passed_along(layer_output, "section", 1)
        return (received, saved_inputs, produced)

    start_forward = (empty_field, jnp.zeros_like(local_clips), jnp.zeros_like(local_clips))
    _, saved_inputs, produced = lax.fori_loop(0, step_count, forward_step, start_forward)

    def backward_step(step_index, carry):
        received, grad_total, kept_grads = carry
        micro_index = step_index - (section_total - 1 - section_index)
        active = (micro_index >= 0) & (micro_index < micro_count)
        slot_index = jnp.clip(micro_index, 0, micro_count - 1)
        fresh = lax.dynamic_index_in_dim(local_grads, slot_index, 0, keepdims=False)
        upstream = jnp.where(section_index == section_total - 1, fresh, received)
        activation = lax.dynamic_index_in_dim(saved_inputs, slot_index, 0, keepdims=False)
        grad_total = grad_total + jnp.where(active, weight_term(activation, upstream), 0.0)
        layer_grad = input_gradient(activation, upstream, weight)
        received = passed_along(layer_grad, "section", -1)
        return (received, grad_total, kept_grads)

    start_backward = (
        empty_field,
        jnp.zeros(weight.shape, jnp.float32),
        jnp.zeros_like(local_grads),
    )
    _, grad_total, kept_grads = lax.fori_loop(0, step_count, backward_step, start_backward)
    grad_share = lax.psum_scatter(
        grad_total.astype(jnp.bfloat16), "dp", scatter_dimension=0, tiled=True
    ).astype(jnp.float32)
    return (produced[None, :, None], grad_share[None])


def silu_of(value):
    return value * jax.nn.sigmoid(value)


def slope_of(value):
    sigmoid_value = jax.nn.sigmoid(value)
    return sigmoid_value * (1.0 + value * (1.0 - sigmoid_value))


def column_shifts(rows, width):
    height, flat, channels = rows.shape
    cells = rows.reshape(height * flat // width, width, channels)
    column = lax.broadcasted_iota(jnp.int32, cells.shape, 1)
    before = jnp.where(column == 0, 0.0, pltpu.roll(cells, 1, 1))
    after = jnp.where(column == width - 1, 0.0, pltpu.roll(cells, width - 1, 1))
    return [piece.reshape(rows.shape).astype(jnp.bfloat16) for piece in (before, cells, after)]


def whole(count):
    return [pl.BlockSpec(memory_space=pltpu.VMEM)] * count


def call(body, inputs, outputs, scratch, flops, scalar):
    return pl.pallas_call(
        body,
        out_shape=[jax.ShapeDtypeStruct(shape, dtype) for shape, dtype in outputs],
        in_specs=[pl.BlockSpec(memory_space=pltpu.SMEM)] + whole(len(inputs)),
        out_specs=whole(len(outputs)),
        scratch_shapes=scratch,
        compiler_params=pltpu.CompilerParams(vmem_limit_bytes=48 * 1024 * 1024),
        cost_estimate=pl.CostEstimate(flops=flops, bytes_accessed=4_000_000, transcendentals=0),
    )(scalar, *inputs)


def prepare_body(place, clips, cotangent, shifted, base, upstream, held):
    micro, frames, height, width, channels = clips.shape
    section = place[0]

    def reorder(source, target):
        for m in range(micro):
            held[:, :, m * width : (m + 1) * width, :] = source[m].astype(jnp.float32)
        for t in range(frames):
            target[t] = held[t].astype(jnp.bfloat16)

    zero_row = jnp.zeros((3, frames, 1) + shifted.shape[3:], jnp.bfloat16)
    shifted[:, :, :1] = zero_row
    shifted[:, :, height + 1 :] = zero_row
    reorder(clips, base)
    reorder(cotangent, upstream)

    @pl.when(section == 0)
    def _():
        for t in range(frames):
            squashed = silu_of(base[t].astype(jnp.float32)).astype(jnp.bfloat16)
            for k, piece in enumerate(column_shifts(squashed.astype(jnp.float32), width)):
                shifted[k, t, 1 : height + 1] = piece

    @pl.when(section != 0)
    def _():
        for t in range(frames):
            for k, piece in enumerate(column_shifts(upstream[t].astype(jnp.float32), width)):
                shifted[k, t, 1 : height + 1] = piece


def unpack_weights(place, pieces, table):
    own, beside, below, diagonal_low, diagonal_high = pieces
    planes, rows, _ = own.shape
    half = diagonal_low.shape[0]
    z, y, x = place[1], place[2], place[3]

    def put(shard, plane_step, row, column):
        plane = lax.rem(z + planes - plane_step, planes)
        start = pl.multiple_of((plane * 4 + row * 2 + column) * rows, 8)
        table[pl.ds(start, rows), :] = shard.astype(jnp.float32)

    for d in range(planes):
        put(own[d], d, y, x)
        put(beside[d], d, y, 1 - x)
        put(below[d], d, 1 - y, x)
        put(diagonal_low[d] if d < half else diagonal_high[d - half], d, 1 - y, 1 - x)


def forward_weights(table, channels):
    rows = 9 * channels
    return jnp.concatenate(
        [table[t * rows : (t + 1) * rows, :].astype(jnp.bfloat16) for t in range(3)], axis=1
    )


def backward_weights(table, channels):
    return jnp.concatenate(
        [
            jnp.concatenate(
                [
                    table[(t * 9 + k) * channels : (t * 9 + k + 1) * channels, :].astype(jnp.bfloat16)
                    for k in reversed(range(9))
                ],
                axis=1,
            )
            for t in range(3)
        ],
        axis=0,
    )


def row_patches(shifted, t, height):
    flat, channels = shifted.shape[3:]
    return jnp.concatenate(
        [
            shifted[k, t, e : e + height].reshape(height * flat, channels)
            for e in range(3)
            for k in range(3)
        ],
        axis=1,
    )


def forward_product(shifted, weights, branch, frames, height):
    channels = branch.shape[-1]
    for t in range(frames):
        part = jnp.dot(row_patches(shifted, t, height), weights, preferred_element_type=jnp.float32)
        for tap in range(3):
            piece = part[:, tap * channels : (tap + 1) * channels]
            for target in range(frames):
                if max(target + tap - 2, 0) != t:
                    continue
                branch[target] += piece


def backward_product(shifted, weights, branch, frames, height):
    channels = branch.shape[-1]
    for t in range(frames):
        part = lax.dot_general(
            row_patches(shifted, t, height),
            weights,
            (((1,), (1,)), ((), ())),
            preferred_element_type=jnp.float32,
        )
        for tap in range(3):
            branch[max(t + tap - 2, 0)] += part[:, tap * channels : (tap + 1) * channels]


def first_body(place, own, beside, below, low, high, shifted, base, result, table, branch):
    frames, height, flat, channels = base.shape
    section = place[0]
    unpack_weights(place, (own, beside, below, low, high), table)
    branch[...] = jnp.zeros_like(branch)

    @pl.when(section == 0)
    def _():
        forward_product(shifted, forward_weights(table, channels), branch, frames, height)
        for t in range(frames):
            total = base[t].astype(jnp.float32) + branch[t].reshape(height, flat, channels)
            result[t] = total.astype(jnp.bfloat16)

    @pl.when(section != 0)
    def _():
        backward_product(shifted, backward_weights(table, channels), branch, frames, height)
        for t in range(frames):
            result[t] = branch[t].reshape(height, flat, channels).astype(jnp.bfloat16)


def second_body(width, place, shifted, mine, other, upstream, own, beside, below, low, high, turned, grads, terms):
    frames, height, flat, channels = upstream.shape
    planes, rows, _ = own.shape
    section, z, y, x = place[0], place[1], place[2], place[3]
    cells = height * flat
    zero_row = jnp.zeros((3, frames, 1, flat, channels), jnp.bfloat16)
    grads[:, :, :1] = zero_row
    grads[:, :, height + 1 :] = zero_row

    def place_grads(fields):
        for t in range(frames):
            for tap in range(3):
                sources = [s for s in range(frames) if max(s + tap - 2, 0) == t]
                if sources:
                    total = functools.reduce(lambda p, q: p + q, [fields(s) for s in sources])
                    grads[tap, t, 1 : height + 1] = total.astype(jnp.bfloat16)
                else:
                    grads[tap, t, 1 : height + 1] = jnp.zeros((height, flat, channels), jnp.bfloat16)

    @pl.when(section == 0)
    def _():
        for t in range(frames):
            value = upstream[t].astype(jnp.float32) + slope_of(mine[t].astype(jnp.float32)) * other[
                t
            ].astype(jnp.float32)
            grads[2, t, 1 : height + 1] = value.astype(jnp.bfloat16)
            for k in range(3):
                piece = shifted[k, t, 1 : height + 1].reshape(cells, channels)
                turned[k * channels : (k + 1) * channels, t * cells : (t + 1) * cells] = piece.T
        place_grads(lambda s: grads[2, s, 1 : height + 1].astype(jnp.float32))

    @pl.when(section != 0)
    def _():
        for t in range(frames):
            squashed = silu_of(other[t].astype(jnp.float32)).astype(jnp.bfloat16)
            for k, piece in enumerate(column_shifts(squashed.astype(jnp.float32), width)):
                piece = piece.reshape(cells, channels)
                turned[k * channels : (k + 1) * channels, t * cells : (t + 1) * cells] = piece.T
        place_grads(lambda s: upstream[s].astype(jnp.float32))

    for tap in range(3):
        moved = jnp.concatenate(
            [
                grads[tap, :, 2 - e : 2 - e + height].reshape(frames * cells, channels)
                for e in range(3)
            ],
            axis=1,
        )
        part = jnp.dot(turned[...], moved, preferred_element_type=jnp.float32)
        for e in range(3):
            for k in range(3):
                start = (tap * 9 + e * 3 + k) * channels
                terms[start : start + channels, :] = part[
                    k * channels : (k + 1) * channels, e * channels : (e + 1) * channels
                ]

    half = low.shape[0]

    def take(plane_step, row, column):
        plane = lax.rem(z + plane_step, planes)
        start = pl.multiple_of((plane * 4 + row * 2 + column) * rows, 8)
        return terms[pl.ds(start, rows), :].astype(jnp.bfloat16)

    for d in range(planes):
        own[d] = take(d, y, x)
        beside[d] = take(d, y, 1 - x)
        below[d] = take(d, 1 - y, x)
        if d < half:
            low[d] = take(d, 1 - y, 1 - x)
        else:
            high[d - half] = take(d, 1 - y, 1 - x)


def third_body(place, own, beside, below, low, high, mine, other, produced, table, branch, shifted):
    micro, frames, height, width, channels = produced.shape
    flat = micro * width
    section = place[0]

    @pl.when(section == 0)
    def _():
        for t in range(frames):
            branch[t] = mine[t].astype(jnp.float32).reshape(height * flat, channels)

    @pl.when(section != 0)
    def _():
        unpack_weights(place, (own, beside, below, low, high), table)
        zero_row = jnp.zeros((3, frames, 1, flat, channels), jnp.bfloat16)
        shifted[:, :, :1] = zero_row
        shifted[:, :, height + 1 :] = zero_row
        for t in range(frames):
            value = other[t].astype(jnp.float32)
            branch[t] = value.reshape(height * flat, channels)
            squashed = silu_of(value).astype(jnp.bfloat16)
            for k, piece in enumerate(column_shifts(squashed.astype(jnp.float32), width)):
                shifted[k, t, 1 : height + 1] = piece
        forward_product(shifted, forward_weights(table, channels), branch, frames, height)

    for t in range(frames):
        cells = branch[t].reshape(height, flat, channels)
        for m in range(micro):
            produced[m, t] = cells[:, m * width : (m + 1) * width, :].astype(jnp.bfloat16)


def paired_sections(clips, cotangent, weights):
    dp_total = lax.axis_size("dp")
    planes = dp_total // 4
    half = planes // 2
    local_clips, local_grads, shard = clips[:, 0], cotangent[:, 0], weights[0]
    micro, frames, height, width, channels = local_clips.shape
    rows = shard.shape[0]
    flat = micro * width
    cells = height * flat
    section, index = lax.axis_index("section"), lax.axis_index("dp")
    place = jnp.stack([section, index // 4, index // 2 % 2, index % 2]).astype(jnp.int32)

    def to_plane(block, step):
        return lax.ppermute(block, "dp", [(i, (i + 4 * step) % dp_total) for i in range(dp_total)])

    def across(block, bit):
        return lax.ppermute(block, "dp", [(i, i ^ bit) for i in range(dp_total)])

    field = (frames, height, flat, channels)
    padded = (3, frames, height + 2, flat, channels)
    bf16, f32 = jnp.bfloat16, jnp.float32
    unit = 2 * micro * frames * height * width * channels * channels * 27

    own = jnp.stack([shard] + [to_plane(shard, d) for d in range(1, planes)])
    beside, below = across(own, 1), across(own, 2)
    low, high = across(beside[:half], 2), across(below[half:], 1)
    pieces = (own, beside, below, low, high)

    shifted, base, upstream = call(
        prepare_body,
        (local_clips, local_grads),
        [(padded, bf16), (field, bf16), (field, bf16)],
        [pltpu.VMEM(field, f32)],
        unit // 8,
        place,
    )
    table = pltpu.VMEM((dp_total * rows, channels), f32)
    branch = pltpu.VMEM((frames, cells, channels), f32)
    (mine,) = call(
        first_body, pieces + (shifted, base), [(field, bf16)], [table, branch], unit, place
    )
    other = lax.ppermute(mine, "section", [(0, 1), (1, 0)])
    own_t, beside_t, below_t, low_t, high_t = call(
        functools.partial(second_body, width),
        (shifted, mine, other, upstream),
        [((planes, rows, channels), bf16)] * 3
        + [((half, rows, channels), bf16), ((planes - half, rows, channels), bf16)],
        [
            pltpu.VMEM((3 * channels, frames * cells), bf16),
            pltpu.VMEM(padded, bf16),
            table,
        ],
        unit,
        place,
    )
    (produced,) = call(
        third_body,
        pieces + (mine, other),
        [(local_clips.shape, bf16)],
        [table, branch, pltpu.VMEM(padded, bf16)],
        unit,
        place,
    )

    def added(*terms):
        return functools.reduce(lambda p, q: p + q, [term.astype(f32) for term in terms])

    low_in, high_in = across(low_t, 2), across(high_t, 1)
    beside_in = across(
        jnp.concatenate([added(beside_t[:half], low_in).astype(bf16), beside_t[half:]]), 1
    )
    below_in = across(
        jnp.concatenate([below_t[:half], added(below_t[half:], high_in).astype(bf16)]), 2
    )
    line = added(own_t, beside_in, below_in)
    sent = line.astype(bf16)
    total = added(line[0], *[to_plane(sent[d], d) for d in range(1, planes)])
    return (produced[None, :, None], total[None])


def solution(mesh):
    dp_total = mesh.shape["dp"]
    paired = mesh.shape["section"] == 2 and dp_total % 8 == 0
    placed = (
        P(None, "dp", None, None, None, None),
        P(None, "dp", None, None, None, None),
        P("section", "dp", None),
    )
    return jax.shard_map(
        paired_sections if paired else many_sections,
        mesh=mesh,
        in_specs=placed,
        out_specs=(P("section", None, "dp", None, None, None, None), P("section", "dp", None)),
        check_vma=False,
    )
```

```python
import functools

import jax
import jax.numpy as jnp
from jax import lax
from jax.experimental import pallas as pl
from jax.experimental.pallas import tpu as pltpu
from jax.sharding import PartitionSpec as P


def passed_along(block, axis, distance):
    devices = range(lax.axis_size(axis))
    route = [(i - distance, i) for i in devices if i - distance in devices]
    return lax.ppermute(block, axis, route)


def gather_patches(field):
    frames, height, width, channels = field.shape
    first_frame = field[:1]
    padded = jnp.concatenate([first_frame, first_frame, field], axis=0)
    padded = jnp.pad(padded, ((0, 0), (1, 1), (1, 1), (0, 0)))
    pieces = [
        padded[
            offset_time : offset_time + frames,
            offset_row : offset_row + height,
            offset_col : offset_col + width,
        ]
        for offset_time in range(3)
        for offset_row in range(3)
        for offset_col in range(3)
    ]
    return jnp.stack(pieces, axis=3).reshape(frames * height * width, 27 * channels)


def squash_field(activation):
    return jax.nn.silu(activation.astype(jnp.float32)).astype(jnp.bfloat16)


def squash_columns(activation):
    return gather_patches(squash_field(activation))


def layer_forward(activation, weight):
    branch = jnp.dot(squash_columns(activation), weight, preferred_element_type=jnp.float32)
    return (activation.astype(jnp.float32) + branch.reshape(activation.shape)).astype(jnp.bfloat16)


def input_gradient(activation, upstream, weight):
    flat_grad = upstream.reshape(-1, weight.shape[1])
    column_grad = lax.dot_general(
        flat_grad, weight, (((1,), (1,)), ((), ())), preferred_element_type=jnp.float32
    )
    base = activation.astype(jnp.float32)
    _, unfold = jax.vjp(gather_patches, base)
    field_grad = unfold(column_grad)[0]
    sigmoid_value = jax.nn.sigmoid(base)
    slope = sigmoid_value * (1.0 + base * (1.0 - sigmoid_value))
    return (upstream.astype(jnp.float32) + field_grad * slope).astype(jnp.bfloat16)


def weight_term(activation, upstream):
    flat_grad = upstream.reshape(-1, upstream.shape[-1])
    return lax.dot_general(
        squash_columns(activation),
        flat_grad,
        (((0,), (0,)), ((), ())),
        preferred_element_type=jnp.float32,
    )


def many_sections(clips, cotangent, weights):
    section_total = lax.axis_size("section")
    section_index = lax.axis_index("section")
    weight = lax.all_gather(weights, "dp", axis=1, tiled=True)[0]
    local_clips = clips[:, 0]
    local_grads = cotangent[:, 0]
    micro_count = local_clips.shape[0]
    step_count = micro_count + section_total - 1
    empty_field = jnp.zeros(local_clips.shape[1:], jnp.bfloat16)

    def forward_step(step_index, carry):
        received, saved_inputs, produced = carry
        micro_index = step_index - section_index
        active = (micro_index >= 0) & (micro_index < micro_count)
        slot_index = jnp.clip(micro_index, 0, micro_count - 1)
        fresh = lax.dynamic_index_in_dim(local_clips, slot_index, 0, keepdims=False)
        layer_input = jnp.where(section_index == 0, fresh, received)
        layer_output = layer_forward(layer_input, weight)
        kept_input = jnp.where(
            active,
            layer_input,
            lax.dynamic_index_in_dim(saved_inputs, slot_index, 0, keepdims=False),
        )
        kept_output = jnp.where(
            active, layer_output, lax.dynamic_index_in_dim(produced, slot_index, 0, keepdims=False)
        )
        saved_inputs = lax.dynamic_update_index_in_dim(saved_inputs, kept_input, slot_index, 0)
        produced = lax.dynamic_update_index_in_dim(produced, kept_output, slot_index, 0)
        received = passed_along(layer_output, "section", 1)
        return (received, saved_inputs, produced)

    start_forward = (empty_field, jnp.zeros_like(local_clips), jnp.zeros_like(local_clips))
    _, saved_inputs, produced = lax.fori_loop(0, step_count, forward_step, start_forward)

    def backward_step(step_index, carry):
        received, grad_total, kept_grads = carry
        micro_index = step_index - (section_total - 1 - section_index)
        active = (micro_index >= 0) & (micro_index < micro_count)
        slot_index = jnp.clip(micro_index, 0, micro_count - 1)
        fresh = lax.dynamic_index_in_dim(local_grads, slot_index, 0, keepdims=False)
        upstream = jnp.where(section_index == section_total - 1, fresh, received)
        activation = lax.dynamic_index_in_dim(saved_inputs, slot_index, 0, keepdims=False)
        grad_total = grad_total + jnp.where(active, weight_term(activation, upstream), 0.0)
        layer_grad = input_gradient(activation, upstream, weight)
        received = passed_along(layer_grad, "section", -1)
        return (received, grad_total, kept_grads)

    start_backward = (
        empty_field,
        jnp.zeros(weight.shape, jnp.float32),
        jnp.zeros_like(local_grads),
    )
    _, grad_total, kept_grads = lax.fori_loop(0, step_count, backward_step, start_backward)
    grad_share = lax.psum_scatter(
        grad_total.astype(jnp.bfloat16), "dp", scatter_dimension=0, tiled=True
    ).astype(jnp.float32)
    return (produced[None, :, None], grad_share[None])


def silu_of(value):
    return value * jax.nn.sigmoid(value)


def slope_of(value):
    sigmoid_value = jax.nn.sigmoid(value)
    return sigmoid_value * (1.0 + value * (1.0 - sigmoid_value))


def column_shifts(rows, width):
    height, flat, channels = rows.shape
    cells = rows.reshape(height * flat // width, width, channels)
    column = lax.broadcasted_iota(jnp.int32, cells.shape, 1)
    before = jnp.where(column == 0, 0.0, pltpu.roll(cells, 1, 1))
    after = jnp.where(column == width - 1, 0.0, pltpu.roll(cells, width - 1, 1))
    return [piece.reshape(rows.shape).astype(jnp.bfloat16) for piece in (before, cells, after)]


def whole(count):
    return [pl.BlockSpec(memory_space=pltpu.VMEM)] * count


def call(body, inputs, outputs, scratch, flops, place):
    return pl.pallas_call(
        body,
        out_shape=[jax.ShapeDtypeStruct(shape, dtype) for shape, dtype in outputs],
        in_specs=[pl.BlockSpec(memory_space=pltpu.SMEM)] + whole(len(inputs)),
        out_specs=whole(len(outputs)),
        scratch_shapes=scratch,
        compiler_params=pltpu.CompilerParams(vmem_limit_bytes=48 * 1024 * 1024),
        cost_estimate=pl.CostEstimate(flops=flops, bytes_accessed=4_000_000, transcendentals=0),
    )(place, *inputs)


def prepare_body(place, clips, cotangent, shifted, base, upstream, held):
    micro, frames, height, width, channels = clips.shape
    section = place[0]

    def reorder(source, target):
        for m in range(micro):
            held[:, :, m * width : (m + 1) * width, :] = source[m].astype(jnp.float32)
        for t in range(frames):
            target[t] = held[t].astype(jnp.bfloat16)

    zero_row = jnp.zeros((3, frames, 1) + shifted.shape[3:], jnp.bfloat16)
    shifted[:, :, :1] = zero_row
    shifted[:, :, height + 1 :] = zero_row
    reorder(clips, base)
    reorder(cotangent, upstream)

    @pl.when(section == 0)
    def _():
        for t in range(frames):
            squashed = silu_of(base[t].astype(jnp.float32)).astype(jnp.bfloat16)
            for k, piece in enumerate(column_shifts(squashed.astype(jnp.float32), width)):
                shifted[k, t, 1 : height + 1] = piece

    @pl.when(section != 0)
    def _():
        for t in range(frames):
            for k, piece in enumerate(column_shifts(upstream[t].astype(jnp.float32), width)):
                shifted[k, t, 1 : height + 1] = piece


def unpack_weights(shards, table):
    beside, planes, rows, _ = shards.shape
    for c in range(beside):
        for z in range(planes):
            start = (z * beside + c) * rows
            table[start : start + rows, :] = shards[c, z].astype(jnp.float32)


def forward_weights(table, channels):
    rows = 9 * channels
    return jnp.concatenate(
        [table[t * rows : (t + 1) * rows, :].astype(jnp.bfloat16) for t in range(3)], axis=1
    )


def backward_weights(table, channels):
    return jnp.concatenate(
        [
            jnp.concatenate(
                [
                    table[(t * 9 + k) * channels : (t * 9 + k + 1) * channels, :].astype(jnp.bfloat16)
                    for k in reversed(range(9))
                ],
                axis=1,
            )
            for t in range(3)
        ],
        axis=0,
    )


def row_patches(shifted, t, height):
    flat, channels = shifted.shape[3:]
    return jnp.concatenate(
        [
            shifted[k, t, e : e + height].reshape(height * flat, channels)
            for e in range(3)
            for k in range(3)
        ],
        axis=1,
    )


def forward_product(shifted, weights, branch, frames, height):
    channels = branch.shape[-1]
    for t in range(frames):
        part = jnp.dot(row_patches(shifted, t, height), weights, preferred_element_type=jnp.float32)
        for tap in range(3):
            piece = part[:, tap * channels : (tap + 1) * channels]
            for target in range(frames):
                if max(target + tap - 2, 0) != t:
                    continue
                branch[target] += piece


def backward_product(shifted, weights, branch, frames, height):
    channels = branch.shape[-1]
    for t in range(frames):
        part = lax.dot_general(
            row_patches(shifted, t, height),
            weights,
            (((1,), (1,)), ((), ())),
            preferred_element_type=jnp.float32,
        )
        for tap in range(3):
            branch[max(t + tap - 2, 0)] += part[:, tap * channels : (tap + 1) * channels]


def first_body(place, shards, shifted, base, result, table, branch):
    frames, height, flat, channels = base.shape
    section = place[0]
    unpack_weights(shards, table)
    branch[...] = jnp.zeros_like(branch)

    @pl.when(section == 0)
    def _():
        forward_product(shifted, forward_weights(table, channels), branch, frames, height)
        for t in range(frames):
            total = base[t].astype(jnp.float32) + branch[t].reshape(height, flat, channels)
            result[t] = total.astype(jnp.bfloat16)

    @pl.when(section != 0)
    def _():
        backward_product(shifted, backward_weights(table, channels), branch, frames, height)
        for t in range(frames):
            result[t] = branch[t].reshape(height, flat, channels).astype(jnp.bfloat16)


def second_body(width, place, shifted, mine, other, upstream, shares, turned, grads, terms):
    frames, height, flat, channels = upstream.shape
    beside, planes, rows, _ = shares.shape
    section = place[0]
    cells = height * flat
    zero_row = jnp.zeros((3, frames, 1, flat, channels), jnp.bfloat16)
    grads[:, :, :1] = zero_row
    grads[:, :, height + 1 :] = zero_row

    def place_grads(fields):
        for t in range(frames):
            for tap in range(3):
                sources = [s for s in range(frames) if max(s + tap - 2, 0) == t]
                if sources:
                    total = functools.reduce(lambda p, q: p + q, [fields(s) for s in sources])
                    grads[tap, t, 1 : height + 1] = total.astype(jnp.bfloat16)
                else:
                    grads[tap, t, 1 : height + 1] = jnp.zeros((height, flat, channels), jnp.bfloat16)

    @pl.when(section == 0)
    def _():
        for t in range(frames):
            value = upstream[t].astype(jnp.float32) + slope_of(mine[t].astype(jnp.float32)) * other[
                t
            ].astype(jnp.float32)
            grads[2, t, 1 : height + 1] = value.astype(jnp.bfloat16)
            for k in range(3):
                piece = shifted[k, t, 1 : height + 1].reshape(cells, channels)
                turned[k * channels : (k + 1) * channels, t * cells : (t + 1) * cells] = piece.T
        place_grads(lambda s: grads[2, s, 1 : height + 1].astype(jnp.float32))

    @pl.when(section != 0)
    def _():
        for t in range(frames):
            squashed = silu_of(other[t].astype(jnp.float32)).astype(jnp.bfloat16)
            for k, piece in enumerate(column_shifts(squashed.astype(jnp.float32), width)):
                piece = piece.reshape(cells, channels)
                turned[k * channels : (k + 1) * channels, t * cells : (t + 1) * cells] = piece.T
        place_grads(lambda s: upstream[s].astype(jnp.float32))

    for tap in range(3):
        moved = jnp.concatenate(
            [
                grads[tap, :, 2 - e : 2 - e + height].reshape(frames * cells, channels)
                for e in range(3)
            ],
            axis=1,
        )
        part = jnp.dot(turned[...], moved, preferred_element_type=jnp.float32)
        for e in range(3):
            for k in range(3):
                start = (tap * 9 + e * 3 + k) * channels
                terms[start : start + channels, :] = part[
                    k * channels : (k + 1) * channels, e * channels : (e + 1) * channels
                ]

    for c in range(beside):
        for z in range(planes):
            start = (z * beside + c) * rows
            shares[c, z] = terms[start : start + rows, :].astype(jnp.bfloat16)


def third_body(place, shards, mine, other, produced, table, branch, shifted):
    micro, frames, height, width, channels = produced.shape
    flat = micro * width
    section = place[0]

    @pl.when(section == 0)
    def _():
        for t in range(frames):
            branch[t] = mine[t].astype(jnp.float32).reshape(height * flat, channels)

    @pl.when(section != 0)
    def _():
        unpack_weights(shards, table)
        zero_row = jnp.zeros((3, frames, 1, flat, channels), jnp.bfloat16)
        shifted[:, :, :1] = zero_row
        shifted[:, :, height + 1 :] = zero_row
        for t in range(frames):
            value = other[t].astype(jnp.float32)
            branch[t] = value.reshape(height * flat, channels)
            squashed = silu_of(value).astype(jnp.bfloat16)
            for k, piece in enumerate(column_shifts(squashed.astype(jnp.float32), width)):
                shifted[k, t, 1 : height + 1] = piece
        forward_product(shifted, forward_weights(table, channels), branch, frames, height)

    for t in range(frames):
        cells = branch[t].reshape(height, flat, channels)
        for m in range(micro):
            produced[m, t] = cells[:, m * width : (m + 1) * width, :].astype(jnp.bfloat16)


def paired_sections(clips, cotangent, weights):
    dp_total = lax.axis_size("dp")
    beside = 4
    planes = dp_total // beside
    local_clips, local_grads, shard = clips[:, 0], cotangent[:, 0], weights[0]
    micro, frames, height, width, channels = local_clips.shape
    rows = shard.shape[0]
    flat = micro * width
    cells = height * flat
    place = jnp.stack([lax.axis_index("section")]).astype(jnp.int32)
    columns_of = [[c + beside * z for z in range(planes)] for c in range(beside)]
    planes_of = [[c + beside * z for c in range(beside)] for z in range(planes)]

    def swapped(blocks, groups):
        return lax.all_to_all(blocks, "dp", 0, 0, axis_index_groups=groups, tiled=True)

    field = (frames, height, flat, channels)
    padded = (3, frames, height + 2, flat, channels)
    bf16, f32 = jnp.bfloat16, jnp.float32
    unit = 2 * micro * frames * height * width * channels * channels * 27

    line = swapped(jnp.broadcast_to(shard, (planes,) + shard.shape), columns_of)
    shards = swapped(jnp.broadcast_to(line, (beside,) + line.shape), planes_of)

    shifted, base, upstream = call(
        prepare_body,
        (local_clips, local_grads),
        [(padded, bf16), (field, bf16), (field, bf16)],
        [pltpu.VMEM(field, f32)],
        unit // 8,
        place,
    )
    table = pltpu.VMEM((dp_total * rows, channels), f32)
    branch = pltpu.VMEM((frames, cells, channels), f32)
    (mine,) = call(
        first_body, (shards, shifted, base), [(field, bf16)], [table, branch], unit, place
    )
    other = lax.ppermute(mine, "section", [(0, 1), (1, 0)])
    (shares,) = call(
        functools.partial(second_body, width),
        (shifted, mine, other, upstream),
        [((beside, planes, rows, channels), bf16)],
        [
            pltpu.VMEM((3 * channels, frames * cells), bf16),
            pltpu.VMEM(padded, bf16),
            table,
        ],
        unit,
        place,
    )
    (produced,) = call(
        third_body,
        (shards, mine, other),
        [(local_clips.shape, bf16)],
        [table, branch, pltpu.VMEM(padded, bf16)],
        unit,
        place,
    )
    line_sum = swapped(shares, planes_of).astype(f32).sum(0).astype(bf16)
    total = swapped(line_sum, columns_of).astype(f32).sum(0)
    return (produced[None, :, None], total[None])


def solution(mesh):
    dp_total = mesh.shape["dp"]
    paired = mesh.shape["section"] == 2 and dp_total % 8 == 0
    placed = (
        P(None, "dp", None, None, None, None),
        P(None, "dp", None, None, None, None),
        P("section", "dp", None),
    )
    return jax.shard_map(
        paired_sections if paired else many_sections,
        mesh=mesh,
        in_specs=placed,
        out_specs=(P("section", None, "dp", None, None, None, None), P("section", "dp", None)),
        check_vma=False,
    )
```

```python
import functools

import jax
import jax.numpy as jnp
from jax import lax
from jax.experimental import pallas as pl
from jax.experimental.pallas import tpu as pltpu
from jax.sharding import PartitionSpec as P


def passed_along(block, axis, distance):
    devices = range(lax.axis_size(axis))
    route = [(i - distance, i) for i in devices if i - distance in devices]
    return lax.ppermute(block, axis, route)


def gather_patches(field):
    frames, height, width, channels = field.shape
    first_frame = field[:1]
    padded = jnp.concatenate([first_frame, first_frame, field], axis=0)
    padded = jnp.pad(padded, ((0, 0), (1, 1), (1, 1), (0, 0)))
    pieces = [
        padded[
            offset_time : offset_time + frames,
            offset_row : offset_row + height,
            offset_col : offset_col + width,
        ]
        for offset_time in range(3)
        for offset_row in range(3)
        for offset_col in range(3)
    ]
    return jnp.stack(pieces, axis=3).reshape(frames * height * width, 27 * channels)


def squash_field(activation):
    return jax.nn.silu(activation.astype(jnp.float32)).astype(jnp.bfloat16)


def squash_columns(activation):
    return gather_patches(squash_field(activation))


def layer_forward(activation, weight):
    branch = jnp.dot(squash_columns(activation), weight, preferred_element_type=jnp.float32)
    return (activation.astype(jnp.float32) + branch.reshape(activation.shape)).astype(jnp.bfloat16)


def input_gradient(activation, upstream, weight):
    flat_grad = upstream.reshape(-1, weight.shape[1])
    column_grad = lax.dot_general(
        flat_grad, weight, (((1,), (1,)), ((), ())), preferred_element_type=jnp.float32
    )
    base = activation.astype(jnp.float32)
    _, unfold = jax.vjp(gather_patches, base)
    field_grad = unfold(column_grad)[0]
    sigmoid_value = jax.nn.sigmoid(base)
    slope = sigmoid_value * (1.0 + base * (1.0 - sigmoid_value))
    return (upstream.astype(jnp.float32) + field_grad * slope).astype(jnp.bfloat16)


def weight_term(activation, upstream):
    flat_grad = upstream.reshape(-1, upstream.shape[-1])
    return lax.dot_general(
        squash_columns(activation),
        flat_grad,
        (((0,), (0,)), ((), ())),
        preferred_element_type=jnp.float32,
    )


def many_sections(clips, cotangent, weights):
    section_total = lax.axis_size("section")
    section_index = lax.axis_index("section")
    weight = lax.all_gather(weights, "dp", axis=1, tiled=True)[0]
    local_clips = clips[:, 0]
    local_grads = cotangent[:, 0]
    micro_count = local_clips.shape[0]
    step_count = micro_count + section_total - 1
    empty_field = jnp.zeros(local_clips.shape[1:], jnp.bfloat16)

    def forward_step(step_index, carry):
        received, saved_inputs, produced = carry
        micro_index = step_index - section_index
        active = (micro_index >= 0) & (micro_index < micro_count)
        slot_index = jnp.clip(micro_index, 0, micro_count - 1)
        fresh = lax.dynamic_index_in_dim(local_clips, slot_index, 0, keepdims=False)
        layer_input = jnp.where(section_index == 0, fresh, received)
        layer_output = layer_forward(layer_input, weight)
        kept_input = jnp.where(
            active,
            layer_input,
            lax.dynamic_index_in_dim(saved_inputs, slot_index, 0, keepdims=False),
        )
        kept_output = jnp.where(
            active, layer_output, lax.dynamic_index_in_dim(produced, slot_index, 0, keepdims=False)
        )
        saved_inputs = lax.dynamic_update_index_in_dim(saved_inputs, kept_input, slot_index, 0)
        produced = lax.dynamic_update_index_in_dim(produced, kept_output, slot_index, 0)
        received = passed_along(layer_output, "section", 1)
        return (received, saved_inputs, produced)

    start_forward = (empty_field, jnp.zeros_like(local_clips), jnp.zeros_like(local_clips))
    _, saved_inputs, produced = lax.fori_loop(0, step_count, forward_step, start_forward)

    def backward_step(step_index, carry):
        received, grad_total, kept_grads = carry
        micro_index = step_index - (section_total - 1 - section_index)
        active = (micro_index >= 0) & (micro_index < micro_count)
        slot_index = jnp.clip(micro_index, 0, micro_count - 1)
        fresh = lax.dynamic_index_in_dim(local_grads, slot_index, 0, keepdims=False)
        upstream = jnp.where(section_index == section_total - 1, fresh, received)
        activation = lax.dynamic_index_in_dim(saved_inputs, slot_index, 0, keepdims=False)
        grad_total = grad_total + jnp.where(active, weight_term(activation, upstream), 0.0)
        layer_grad = input_gradient(activation, upstream, weight)
        received = passed_along(layer_grad, "section", -1)
        return (received, grad_total, kept_grads)

    start_backward = (
        empty_field,
        jnp.zeros(weight.shape, jnp.float32),
        jnp.zeros_like(local_grads),
    )
    _, grad_total, kept_grads = lax.fori_loop(0, step_count, backward_step, start_backward)
    grad_share = lax.psum_scatter(
        grad_total.astype(jnp.bfloat16), "dp", scatter_dimension=0, tiled=True
    ).astype(jnp.float32)
    return (produced[None, :, None], grad_share[None])


def silu_of(value):
    return value * jax.nn.sigmoid(value)


def slope_of(value):
    sigmoid_value = jax.nn.sigmoid(value)
    return sigmoid_value * (1.0 + value * (1.0 - sigmoid_value))


def column_shifts(rows, width):
    height, flat, channels = rows.shape
    cells = rows.reshape(height * flat // width, width, channels)
    column = lax.broadcasted_iota(jnp.int32, cells.shape, 1)
    before = jnp.where(column == 0, 0.0, pltpu.roll(cells, 1, 1))
    after = jnp.where(column == width - 1, 0.0, pltpu.roll(cells, width - 1, 1))
    return [piece.reshape(rows.shape).astype(jnp.bfloat16) for piece in (before, cells, after)]


def whole(count):
    return [pl.BlockSpec(memory_space=pltpu.VMEM)] * count


def call(body, inputs, outputs, scratch, flops, place):
    return pl.pallas_call(
        body,
        out_shape=[jax.ShapeDtypeStruct(shape, dtype) for shape, dtype in outputs],
        in_specs=[pl.BlockSpec(memory_space=pltpu.SMEM)] + whole(len(inputs)),
        out_specs=whole(len(outputs)),
        scratch_shapes=scratch,
        compiler_params=pltpu.CompilerParams(vmem_limit_bytes=48 * 1024 * 1024),
        cost_estimate=pl.CostEstimate(flops=flops, bytes_accessed=4_000_000, transcendentals=0),
    )(place, *inputs)


def prepare_body(place, clips, cotangent, shard, shifted, base, upstream, shard_copy, held):
    micro, frames, height, width, channels = clips.shape
    section = place[0]
    shard_copy[...] = shard[...]

    def reorder(source, target):
        for m in range(micro):
            held[:, :, m * width : (m + 1) * width, :] = source[m].astype(jnp.float32)
        for t in range(frames):
            target[t] = held[t].astype(jnp.bfloat16)

    zero_row = jnp.zeros((3, frames, 1) + shifted.shape[3:], jnp.bfloat16)
    shifted[:, :, :1] = zero_row
    shifted[:, :, height + 1 :] = zero_row
    reorder(clips, base)
    reorder(cotangent, upstream)

    @pl.when(section == 0)
    def _():
        for t in range(frames):
            squashed = silu_of(base[t].astype(jnp.float32)).astype(jnp.bfloat16)
            for k, piece in enumerate(column_shifts(squashed.astype(jnp.float32), width)):
                shifted[k, t, 1 : height + 1] = piece

    @pl.when(section != 0)
    def _():
        for t in range(frames):
            for k, piece in enumerate(column_shifts(upstream[t].astype(jnp.float32), width)):
                shifted[k, t, 1 : height + 1] = piece


def chips_beside(y, x):
    return ((y, x), (y, 1 - x), (1 - y, x), (1 - y, 1 - x))


def shard_rows(place, planes, rows, plane_step, chip):
    plane = lax.rem(place[1] + plane_step, planes)
    row, column = chips_beside(place[2], place[3])[chip]
    return pl.ds(pl.multiple_of((plane * 4 + row * 2 + column) * rows, 8), rows)


def unpack_weights(place, near, far, table):
    planes, rows = far[0].shape[0] + 1, near[0].shape[0]
    for chip in range(4):
        table[shard_rows(place, planes, rows, 0, chip), :] = near[chip][...].astype(jnp.float32)
        for d in range(1, planes):
            table[shard_rows(place, planes, rows, planes - d, chip), :] = far[chip][d - 1].astype(
                jnp.float32
            )


def forward_weights(table, channels):
    rows = 9 * channels
    return jnp.concatenate(
        [table[t * rows : (t + 1) * rows, :].astype(jnp.bfloat16) for t in range(3)], axis=1
    )


def backward_weights(table, channels):
    return jnp.concatenate(
        [
            jnp.concatenate(
                [
                    table[(t * 9 + k) * channels : (t * 9 + k + 1) * channels, :].astype(jnp.bfloat16)
                    for k in reversed(range(9))
                ],
                axis=1,
            )
            for t in range(3)
        ],
        axis=0,
    )


def row_patches(shifted, t, height):
    flat, channels = shifted.shape[3:]
    return jnp.concatenate(
        [
            shifted[k, t, e : e + height].reshape(height * flat, channels)
            for e in range(3)
            for k in range(3)
        ],
        axis=1,
    )


def forward_product(shifted, weights, branch, frames, height):
    channels = branch.shape[-1]
    for t in range(frames):
        part = jnp.dot(row_patches(shifted, t, height), weights, preferred_element_type=jnp.float32)
        for tap in range(3):
            piece = part[:, tap * channels : (tap + 1) * channels]
            for target in range(frames):
                if max(target + tap - 2, 0) != t:
                    continue
                branch[target] += piece


def backward_product(shifted, weights, branch, frames, height):
    channels = branch.shape[-1]
    for t in range(frames):
        part = lax.dot_general(
            row_patches(shifted, t, height),
            weights,
            (((1,), (1,)), ((), ())),
            preferred_element_type=jnp.float32,
        )
        for tap in range(3):
            branch[max(t + tap - 2, 0)] += part[:, tap * channels : (tap + 1) * channels]


def first_body(place, *refs):
    near, far = refs[:4], refs[4:8]
    shifted, base, result, table, branch = refs[8:]
    frames, height, flat, channels = base.shape
    section = place[0]
    unpack_weights(place, near, far, table)
    branch[...] = jnp.zeros_like(branch)

    @pl.when(section == 0)
    def _():
        forward_product(shifted, forward_weights(table, channels), branch, frames, height)
        for t in range(frames):
            total = base[t].astype(jnp.float32) + branch[t].reshape(height, flat, channels)
            result[t] = total.astype(jnp.bfloat16)

    @pl.when(section != 0)
    def _():
        backward_product(shifted, backward_weights(table, channels), branch, frames, height)
        for t in range(frames):
            result[t] = branch[t].reshape(height, flat, channels).astype(jnp.bfloat16)


def second_body(width, place, shifted, mine, other, upstream, *refs):
    near, far = refs[:4], refs[4:8]
    turned, grads, terms = refs[8:]
    frames, height, flat, channels = upstream.shape
    planes, rows = far[0].shape[0] + 1, near[0].shape[0]
    section = place[0]
    cells = height * flat
    zero_row = jnp.zeros((3, frames, 1, flat, channels), jnp.bfloat16)
    grads[:, :, :1] = zero_row
    grads[:, :, height + 1 :] = zero_row

    def place_grads(fields):
        for t in range(frames):
            for tap in range(3):
                sources = [s for s in range(frames) if max(s + tap - 2, 0) == t]
                if sources:
                    total = functools.reduce(lambda p, q: p + q, [fields(s) for s in sources])
                    grads[tap, t, 1 : height + 1] = total.astype(jnp.bfloat16)
                else:
                    grads[tap, t, 1 : height + 1] = jnp.zeros((height, flat, channels), jnp.bfloat16)

    @pl.when(section == 0)
    def _():
        for t in range(frames):
            value = upstream[t].astype(jnp.float32) + slope_of(mine[t].astype(jnp.float32)) * other[
                t
            ].astype(jnp.float32)
            grads[2, t, 1 : height + 1] = value.astype(jnp.bfloat16)
            for k in range(3):
                piece = shifted[k, t, 1 : height + 1].reshape(cells, channels)
                turned[k * channels : (k + 1) * channels, t * cells : (t + 1) * cells] = piece.T
        place_grads(lambda s: grads[2, s, 1 : height + 1].astype(jnp.float32))

    @pl.when(section != 0)
    def _():
        for t in range(frames):
            squashed = silu_of(other[t].astype(jnp.float32)).astype(jnp.bfloat16)
            for k, piece in enumerate(column_shifts(squashed.astype(jnp.float32), width)):
                piece = piece.reshape(cells, channels)
                turned[k * channels : (k + 1) * channels, t * cells : (t + 1) * cells] = piece.T
        place_grads(lambda s: upstream[s].astype(jnp.float32))

    for tap in range(3):
        moved = jnp.concatenate(
            [
                grads[tap, :, 2 - e : 2 - e + height].reshape(frames * cells, channels)
                for e in range(3)
            ],
            axis=1,
        )
        part = jnp.dot(turned[...], moved, preferred_element_type=jnp.float32)
        for e in range(3):
            for k in range(3):
                start = (tap * 9 + e * 3 + k) * channels
                terms[start : start + channels, :] = part[
                    k * channels : (k + 1) * channels, e * channels : (e + 1) * channels
                ]

    for chip in range(4):
        near[chip][...] = terms[shard_rows(place, planes, rows, 0, chip), :].astype(near[chip].dtype)
        for d in range(1, planes):
            share = terms[shard_rows(place, planes, rows, d, chip), :]
            far[chip][d - 1] = share.astype(jnp.bfloat16)


def third_body(place, *refs):
    near, far = refs[:4], refs[4:8]
    mine, other, produced, table, branch, shifted = refs[8:]
    micro, frames, height, width, channels = produced.shape
    flat = micro * width
    section = place[0]

    @pl.when(section == 0)
    def _():
        for t in range(frames):
            branch[t] = mine[t].astype(jnp.float32).reshape(height * flat, channels)

    @pl.when(section != 0)
    def _():
        unpack_weights(place, near, far, table)
        zero_row = jnp.zeros((3, frames, 1, flat, channels), jnp.bfloat16)
        shifted[:, :, :1] = zero_row
        shifted[:, :, height + 1 :] = zero_row
        for t in range(frames):
            value = other[t].astype(jnp.float32)
            branch[t] = value.reshape(height * flat, channels)
            squashed = silu_of(value).astype(jnp.bfloat16)
            for k, piece in enumerate(column_shifts(squashed.astype(jnp.float32), width)):
                shifted[k, t, 1 : height + 1] = piece
        forward_product(shifted, forward_weights(table, channels), branch, frames, height)

    for t in range(frames):
        cells = branch[t].reshape(height, flat, channels)
        for m in range(micro):
            produced[m, t] = cells[:, m * width : (m + 1) * width, :].astype(jnp.bfloat16)


def paired_sections(clips, cotangent, weights):
    dp_total = lax.axis_size("dp")
    planes = dp_total // 4
    local_clips, local_grads, shard = clips[:, 0], cotangent[:, 0], weights[0]
    micro, frames, height, width, channels = local_clips.shape
    rows = shard.shape[0]
    flat = micro * width
    cells = height * flat
    section, index = lax.axis_index("section"), lax.axis_index("dp")
    place = jnp.stack([section, index // 4, index // 2 % 2, index % 2]).astype(jnp.int32)

    def to_plane(block, step):
        return lax.ppermute(block, "dp", [(i, (i + 4 * step) % dp_total) for i in range(dp_total)])

    def across(block, bits):
        return lax.ppermute(block, "dp", [(i, i ^ bits) for i in range(dp_total)])

    field = (frames, height, flat, channels)
    padded = (3, frames, height + 2, flat, channels)
    bf16, f32 = jnp.bfloat16, jnp.float32
    unit = 2 * micro * frames * height * width * channels * channels * 27

    from_planes = [to_plane(shard, d) for d in range(1, planes)]
    near = [across(shard, bits) for bits in range(1, 4)]
    shifted, base, upstream, shard_copy = call(
        prepare_body,
        (local_clips, local_grads, shard),
        [(padded, bf16), (field, bf16), (field, bf16), (shard.shape, bf16)],
        [pltpu.VMEM(field, f32)],
        unit // 8,
        place,
    )
    from_planes, near, shifted, base, upstream, shard_copy = lax.optimization_barrier(
        (from_planes, near, shifted, base, upstream, shard_copy)
    )
    line = jnp.stack(from_planes)
    far = [line] + [across(line, bits) for bits in range(1, 4)]
    shards = (shard_copy, *near, *far)

    table = pltpu.VMEM((dp_total * rows, channels), f32)
    branch = pltpu.VMEM((frames, cells, channels), f32)
    (mine,) = call(
        first_body, shards + (shifted, base), [(field, bf16)], [table, branch], unit, place
    )
    other = lax.ppermute(mine, "section", [(0, 1), (1, 0)])
    shares = call(
        functools.partial(second_body, width),
        (shifted, mine, other, upstream),
        [((rows, channels), f32)]
        + [((rows, channels), bf16)] * 3
        + [((planes - 1, rows, channels), bf16)] * 4,
        [
            pltpu.VMEM((3 * channels, frames * cells), bf16),
            pltpu.VMEM(padded, bf16),
            table,
        ],
        unit,
        place,
    )
    near_terms, far_terms = shares[:4], shares[4:]
    (produced,) = call(
        third_body,
        shards + (mine, other),
        [(local_clips.shape, bf16)],
        [table, branch, pltpu.VMEM(padded, bf16)],
        unit,
        place,
    )

    def added(*terms):
        return functools.reduce(lambda p, q: p + q, [term.astype(f32) for term in terms])

    line_sum = added(far_terms[0], *[across(far_terms[bits], bits) for bits in range(1, 4)])
    line_sum = line_sum.astype(bf16)
    total = added(
        near_terms[0],
        *[across(near_terms[bits], bits) for bits in range(1, 4)],
        *[to_plane(line_sum[d - 1], d) for d in range(1, planes)],
    )
    return (produced[None, :, None], total[None])


def solution(mesh):
    dp_total = mesh.shape["dp"]
    paired = mesh.shape["section"] == 2 and dp_total % 8 == 0
    placed = (
        P(None, "dp", None, None, None, None),
        P(None, "dp", None, None, None, None),
        P("section", "dp", None),
    )
    return jax.shard_map(
        paired_sections if paired else many_sections,
        mesh=mesh,
        in_specs=placed,
        out_specs=(P("section", None, "dp", None, None, None, None), P("section", "dp", None)),
        check_vma=False,
    )
```

```python
import functools

import jax
import jax.numpy as jnp
from jax import lax
from jax.experimental import pallas as pl
from jax.experimental.pallas import tpu as pltpu
from jax.sharding import PartitionSpec as P


def passed_along(block, axis, distance):
    devices = range(lax.axis_size(axis))
    route = [(i - distance, i) for i in devices if i - distance in devices]
    return lax.ppermute(block, axis, route)


def gather_patches(field):
    frames, height, width, channels = field.shape
    first_frame = field[:1]
    padded = jnp.concatenate([first_frame, first_frame, field], axis=0)
    padded = jnp.pad(padded, ((0, 0), (1, 1), (1, 1), (0, 0)))
    pieces = [
        padded[
            offset_time : offset_time + frames,
            offset_row : offset_row + height,
            offset_col : offset_col + width,
        ]
        for offset_time in range(3)
        for offset_row in range(3)
        for offset_col in range(3)
    ]
    return jnp.stack(pieces, axis=3).reshape(frames * height * width, 27 * channels)


def squash_field(activation):
    return jax.nn.silu(activation.astype(jnp.float32)).astype(jnp.bfloat16)


def squash_columns(activation):
    return gather_patches(squash_field(activation))


def layer_forward(activation, weight):
    branch = jnp.dot(squash_columns(activation), weight, preferred_element_type=jnp.float32)
    return (activation.astype(jnp.float32) + branch.reshape(activation.shape)).astype(jnp.bfloat16)


def input_gradient(activation, upstream, weight):
    flat_grad = upstream.reshape(-1, weight.shape[1])
    column_grad = lax.dot_general(
        flat_grad, weight, (((1,), (1,)), ((), ())), preferred_element_type=jnp.float32
    )
    base = activation.astype(jnp.float32)
    _, unfold = jax.vjp(gather_patches, base)
    field_grad = unfold(column_grad)[0]
    sigmoid_value = jax.nn.sigmoid(base)
    slope = sigmoid_value * (1.0 + base * (1.0 - sigmoid_value))
    return (upstream.astype(jnp.float32) + field_grad * slope).astype(jnp.bfloat16)


def weight_term(activation, upstream):
    flat_grad = upstream.reshape(-1, upstream.shape[-1])
    return lax.dot_general(
        squash_columns(activation),
        flat_grad,
        (((0,), (0,)), ((), ())),
        preferred_element_type=jnp.float32,
    )


def many_sections(clips, cotangent, weights):
    section_total = lax.axis_size("section")
    section_index = lax.axis_index("section")
    weight = lax.all_gather(weights, "dp", axis=1, tiled=True)[0]
    local_clips = clips[:, 0]
    local_grads = cotangent[:, 0]
    micro_count = local_clips.shape[0]
    step_count = micro_count + section_total - 1
    empty_field = jnp.zeros(local_clips.shape[1:], jnp.bfloat16)

    def forward_step(step_index, carry):
        received, saved_inputs, produced = carry
        micro_index = step_index - section_index
        active = (micro_index >= 0) & (micro_index < micro_count)
        slot_index = jnp.clip(micro_index, 0, micro_count - 1)
        fresh = lax.dynamic_index_in_dim(local_clips, slot_index, 0, keepdims=False)
        layer_input = jnp.where(section_index == 0, fresh, received)
        layer_output = layer_forward(layer_input, weight)
        kept_input = jnp.where(
            active,
            layer_input,
            lax.dynamic_index_in_dim(saved_inputs, slot_index, 0, keepdims=False),
        )
        kept_output = jnp.where(
            active, layer_output, lax.dynamic_index_in_dim(produced, slot_index, 0, keepdims=False)
        )
        saved_inputs = lax.dynamic_update_index_in_dim(saved_inputs, kept_input, slot_index, 0)
        produced = lax.dynamic_update_index_in_dim(produced, kept_output, slot_index, 0)
        received = passed_along(layer_output, "section", 1)
        return (received, saved_inputs, produced)

    start_forward = (empty_field, jnp.zeros_like(local_clips), jnp.zeros_like(local_clips))
    _, saved_inputs, produced = lax.fori_loop(0, step_count, forward_step, start_forward)

    def backward_step(step_index, carry):
        received, grad_total, kept_grads = carry
        micro_index = step_index - (section_total - 1 - section_index)
        active = (micro_index >= 0) & (micro_index < micro_count)
        slot_index = jnp.clip(micro_index, 0, micro_count - 1)
        fresh = lax.dynamic_index_in_dim(local_grads, slot_index, 0, keepdims=False)
        upstream = jnp.where(section_index == section_total - 1, fresh, received)
        activation = lax.dynamic_index_in_dim(saved_inputs, slot_index, 0, keepdims=False)
        grad_total = grad_total + jnp.where(active, weight_term(activation, upstream), 0.0)
        layer_grad = input_gradient(activation, upstream, weight)
        received = passed_along(layer_grad, "section", -1)
        return (received, grad_total, kept_grads)

    start_backward = (
        empty_field,
        jnp.zeros(weight.shape, jnp.float32),
        jnp.zeros_like(local_grads),
    )
    _, grad_total, kept_grads = lax.fori_loop(0, step_count, backward_step, start_backward)
    grad_share = lax.psum_scatter(
        grad_total.astype(jnp.bfloat16), "dp", scatter_dimension=0, tiled=True
    ).astype(jnp.float32)
    return (produced[None, :, None], grad_share[None])


def silu_of(value):
    return value * jax.nn.sigmoid(value)


def slope_of(value):
    sigmoid_value = jax.nn.sigmoid(value)
    return sigmoid_value * (1.0 + value * (1.0 - sigmoid_value))


def column_shifts(rows, width):
    height, flat, channels = rows.shape
    cells = rows.reshape(height * flat // width, width, channels)
    column = lax.broadcasted_iota(jnp.int32, cells.shape, 1)
    before = jnp.where(column == 0, 0.0, pltpu.roll(cells, 1, 1))
    after = jnp.where(column == width - 1, 0.0, pltpu.roll(cells, width - 1, 1))
    return [piece.reshape(rows.shape).astype(jnp.bfloat16) for piece in (before, cells, after)]


def whole(count):
    return [pl.BlockSpec(memory_space=pltpu.VMEM)] * count


def call(body, inputs, outputs, scratch, flops, place, far=False):
    return pl.pallas_call(
        body,
        out_shape=[jax.ShapeDtypeStruct(shape, dtype) for shape, dtype in outputs],
        in_specs=[pl.BlockSpec(memory_space=pltpu.SMEM)]
        + ([pl.BlockSpec(memory_space=pl.ANY)] * len(inputs) if far else whole(len(inputs))),
        out_specs=whole(len(outputs)),
        scratch_shapes=scratch,
        compiler_params=pltpu.CompilerParams(vmem_limit_bytes=48 * 1024 * 1024),
        cost_estimate=pl.CostEstimate(flops=flops, bytes_accessed=4_000_000, transcendentals=0),
    )(place, *inputs)


def turn_into(turned, k, t, piece):
    channels = piece.shape[-1]
    flat = piece.reshape(-1, channels)
    cells = flat.shape[0]
    turned[k * channels : (k + 1) * channels, t * cells : (t + 1) * cells] = flat.T


def move_grads(grads, field):
    _, frames, padded_height, flat, channels = grads.shape
    height = padded_height - 2
    zero_row = jnp.zeros((3, frames, 1, flat, channels), jnp.bfloat16)
    grads[:, :, :1] = zero_row
    grads[:, :, height + 1 :] = zero_row
    for t in range(frames):
        for tap in range(3):
            sources = [s for s in range(frames) if max(s + tap - 2, 0) == t]
            if sources:
                total = functools.reduce(lambda p, q: p + q, [field(s) for s in sources])
                grads[tap, t, 1 : height + 1] = total.astype(jnp.bfloat16)
            else:
                grads[tap, t, 1 : height + 1] = jnp.zeros((height, flat, channels), jnp.bfloat16)


def prepare_body(place, clips_far, cotangent_far, shard_far, *refs):
    shifted, base, upstream, shard, ready, held, clips, cotangent, sems = refs
    micro, frames, height, width, channels = clips.shape
    section = place[0]
    copies = [
        pltpu.make_async_copy(source, target, sems.at[k])
        for k, (source, target) in enumerate(
            ((clips_far, clips), (cotangent_far, cotangent), (shard_far, shard))
        )
    ]
    for copy in copies:
        copy.start()

    def reorder(source, target):
        for m in range(micro):
            held[:, :, m * width : (m + 1) * width, :] = source[m].astype(jnp.float32)
        for t in range(frames):
            target[t] = held[t].astype(jnp.bfloat16)

    zero_row = jnp.zeros((3, frames, 1) + shifted.shape[3:], jnp.bfloat16)
    shifted[:, :, :1] = zero_row
    shifted[:, :, height + 1 :] = zero_row
    copies[0].wait()
    reorder(clips, base)
    copies[1].wait()
    reorder(cotangent, upstream)
    copies[2].wait()

    @pl.when(section == 0)
    def _():
        for t in range(frames):
            squashed = silu_of(base[t].astype(jnp.float32)).astype(jnp.bfloat16)
            for k, piece in enumerate(column_shifts(squashed.astype(jnp.float32), width)):
                shifted[k, t, 1 : height + 1] = piece
                turn_into(ready, k, t, piece)

    @pl.when(section != 0)
    def _():
        for t in range(frames):
            for k, piece in enumerate(column_shifts(upstream[t].astype(jnp.float32), width)):
                shifted[k, t, 1 : height + 1] = piece


def chips_beside(y, x):
    return ((y, x), (y, 1 - x), (1 - y, x), (1 - y, 1 - x))


def shard_rows(place, planes, rows, plane_step, chip):
    plane = lax.rem(place[1] + plane_step, planes)
    row, column = chips_beside(place[2], place[3])[chip]
    return pl.ds(pl.multiple_of((plane * 4 + row * 2 + column) * rows, 8), rows)


def unpack_weights(place, near, far, table):
    planes, rows = far[0].shape[0] + 1, near[0].shape[0]
    for chip in range(4):
        table[shard_rows(place, planes, rows, 0, chip), :] = near[chip][...].astype(jnp.float32)
        for d in range(1, planes):
            table[shard_rows(place, planes, rows, planes - d, chip), :] = far[chip][d - 1].astype(
                jnp.float32
            )


def forward_weights(table, channels):
    rows = 9 * channels
    return jnp.concatenate(
        [table[t * rows : (t + 1) * rows, :].astype(jnp.bfloat16) for t in range(3)], axis=1
    )


def backward_weights(table, channels):
    return jnp.concatenate(
        [
            jnp.concatenate(
                [
                    table[(t * 9 + k) * channels : (t * 9 + k + 1) * channels, :].astype(jnp.bfloat16)
                    for k in reversed(range(9))
                ],
                axis=1,
            )
            for t in range(3)
        ],
        axis=0,
    )


def row_patches(shifted, t, height):
    flat, channels = shifted.shape[3:]
    return jnp.concatenate(
        [
            shifted[k, t, e : e + height].reshape(height * flat, channels)
            for e in range(3)
            for k in range(3)
        ],
        axis=1,
    )


def forward_product(shifted, weights, branch, frames, height):
    channels = branch.shape[-1]
    for t in range(frames):
        part = jnp.dot(row_patches(shifted, t, height), weights, preferred_element_type=jnp.float32)
        for tap in range(3):
            piece = part[:, tap * channels : (tap + 1) * channels]
            for target in range(frames):
                if max(target + tap - 2, 0) != t:
                    continue
                branch[target] += piece


def backward_product(shifted, weights, branch, frames, height):
    channels = branch.shape[-1]
    for t in range(frames):
        part = lax.dot_general(
            row_patches(shifted, t, height),
            weights,
            (((1,), (1,)), ((), ())),
            preferred_element_type=jnp.float32,
        )
        for tap in range(3):
            branch[max(t + tap - 2, 0)] += part[:, tap * channels : (tap + 1) * channels]


def first_body(place, *refs):
    near, far = refs[:4], refs[4:8]
    shifted, base, result, table, branch = refs[8:]
    frames, height, flat, channels = base.shape
    section = place[0]
    unpack_weights(place, near, far, table)
    branch[...] = jnp.zeros_like(branch)

    @pl.when(section == 0)
    def _():
        forward_product(shifted, forward_weights(table, channels), branch, frames, height)
        for t in range(frames):
            total = base[t].astype(jnp.float32) + branch[t].reshape(height, flat, channels)
            result[t] = total.astype(jnp.bfloat16)

    @pl.when(section != 0)
    def _():
        backward_product(shifted, backward_weights(table, channels), branch, frames, height)
        for t in range(frames):
            result[t] = branch[t].reshape(height, flat, channels).astype(jnp.bfloat16)


def second_body(width, place, ready, mine, other, upstream, *refs):
    near, far = refs[:4], refs[4:8]
    turned, grads, terms = refs[8:]
    frames, height, flat, channels = upstream.shape
    planes, rows = far[0].shape[0] + 1, near[0].shape[0]
    section = place[0]
    cells = height * flat

    def product(left):
        for tap in range(3):
            moved = jnp.concatenate(
                [
                    grads[tap, :, 2 - e : 2 - e + height].reshape(frames * cells, channels)
                    for e in range(3)
                ],
                axis=1,
            )
            part = jnp.dot(left[...], moved, preferred_element_type=jnp.float32)
            for e in range(3):
                for k in range(3):
                    start = (tap * 9 + e * 3 + k) * channels
                    terms[start : start + channels, :] = part[
                        k * channels : (k + 1) * channels, e * channels : (e + 1) * channels
                    ]

    @pl.when(section == 0)
    def _():
        for t in range(frames):
            value = upstream[t].astype(jnp.float32) + slope_of(mine[t].astype(jnp.float32)) * other[
                t
            ].astype(jnp.float32)
            grads[2, t, 1 : height + 1] = value.astype(jnp.bfloat16)
        move_grads(grads, lambda s: grads[2, s, 1 : height + 1].astype(jnp.float32))
        product(ready)

    @pl.when(section != 0)
    def _():
        move_grads(grads, lambda s: upstream[s].astype(jnp.float32))
        for t in range(frames):
            squashed = silu_of(other[t].astype(jnp.float32)).astype(jnp.bfloat16)
            for k, piece in enumerate(column_shifts(squashed.astype(jnp.float32), width)):
                turn_into(turned, k, t, piece)
        product(turned)

    for chip in range(4):
        near[chip][...] = terms[shard_rows(place, planes, rows, 0, chip), :].astype(near[chip].dtype)
        for d in range(1, planes):
            share = terms[shard_rows(place, planes, rows, d, chip), :]
            far[chip][d - 1] = share.astype(jnp.bfloat16)


def third_body(place, *refs):
    near, far = refs[:4], refs[4:8]
    mine, other, produced, table, branch, shifted = refs[8:]
    micro, frames, height, width, channels = produced.shape
    flat = micro * width
    section = place[0]

    @pl.when(section == 0)
    def _():
        for t in range(frames):
            branch[t] = mine[t].astype(jnp.float32).reshape(height * flat, channels)

    @pl.when(section != 0)
    def _():
        unpack_weights(place, near, far, table)
        zero_row = jnp.zeros((3, frames, 1, flat, channels), jnp.bfloat16)
        shifted[:, :, :1] = zero_row
        shifted[:, :, height + 1 :] = zero_row
        for t in range(frames):
            value = other[t].astype(jnp.float32)
            branch[t] = value.reshape(height * flat, channels)
            squashed = silu_of(value).astype(jnp.bfloat16)
            for k, piece in enumerate(column_shifts(squashed.astype(jnp.float32), width)):
                shifted[k, t, 1 : height + 1] = piece
        forward_product(shifted, forward_weights(table, channels), branch, frames, height)

    for t in range(frames):
        cells = branch[t].reshape(height, flat, channels)
        for m in range(micro):
            produced[m, t] = cells[:, m * width : (m + 1) * width, :].astype(jnp.bfloat16)


def paired_sections(clips, cotangent, weights):
    dp_total = lax.axis_size("dp")
    planes = dp_total // 4
    local_clips, local_grads, shard = clips[:, 0], cotangent[:, 0], weights[0]
    micro, frames, height, width, channels = local_clips.shape
    rows = shard.shape[0]
    flat = micro * width
    cells = height * flat
    section, index = lax.axis_index("section"), lax.axis_index("dp")
    place = jnp.stack([section, index // 4, index // 2 % 2, index % 2]).astype(jnp.int32)

    def to_plane(block, step):
        return lax.ppermute(block, "dp", [(i, (i + 4 * step) % dp_total) for i in range(dp_total)])

    def across(block, bits):
        return lax.ppermute(block, "dp", [(i, i ^ bits) for i in range(dp_total)])

    field = (frames, height, flat, channels)
    padded = (3, frames, height + 2, flat, channels)
    bf16, f32 = jnp.bfloat16, jnp.float32
    unit = 2 * micro * frames * height * width * channels * channels * 27

    near = [across(shard, bits) for bits in range(1, 4)]
    from_planes = [to_plane(shard, d) for d in range(1, planes)]
    near, from_planes = lax.optimization_barrier((near, from_planes))
    line = jnp.stack(from_planes)
    far = [line] + [across(line, bits) for bits in range(1, 4)]
    turned = (3 * channels, frames * cells)
    shifted, base, upstream, shard_copy, ready = call(
        prepare_body,
        (local_clips, local_grads, shard),
        [(padded, bf16), (field, bf16), (field, bf16), (shard.shape, bf16), (turned, bf16)],
        [
            pltpu.VMEM(field, f32),
            pltpu.VMEM(local_clips.shape, bf16),
            pltpu.VMEM(local_clips.shape, bf16),
            pltpu.SemaphoreType.DMA((3,)),
        ],
        unit // 8,
        place,
        far=True,
    )
    shards = (shard_copy, *near, *far)

    table = pltpu.VMEM((dp_total * rows, channels), f32)
    branch = pltpu.VMEM((frames, cells, channels), f32)
    (mine,) = call(
        first_body, shards + (shifted, base), [(field, bf16)], [table, branch], unit, place
    )
    other = lax.ppermute(mine, "section", [(0, 1), (1, 0)])
    shares = call(
        functools.partial(second_body, width),
        (ready, mine, other, upstream),
        [((rows, channels), f32)]
        + [((rows, channels), bf16)] * 3
        + [((planes - 1, rows, channels), bf16)] * 4,
        [
            pltpu.VMEM(turned, bf16),
            pltpu.VMEM(padded, bf16),
            table,
        ],
        unit,
        place,
    )
    near_terms, far_terms = shares[:4], shares[4:]
    (produced,) = call(
        third_body,
        shards + (mine, other),
        [(local_clips.shape, bf16)],
        [table, branch, pltpu.VMEM(padded, bf16)],
        unit,
        place,
    )

    def added(*terms):
        return functools.reduce(lambda p, q: p + q, [term.astype(f32) for term in terms])

    far_in = [across(far_terms[bits], bits) for bits in range(1, 4)]
    far_in, produced, near_terms = lax.optimization_barrier((far_in, produced, near_terms))
    line_sum = added(far_terms[0], *far_in).astype(bf16)
    from_line = [to_plane(line_sum[d - 1], d) for d in range(1, planes)]
    near_in = [across(near_terms[bits], bits) for bits in range(1, 4)]
    total = added(near_terms[0], *near_in, *from_line)
    return (produced[None, :, None], total[None])


def solution(mesh):
    dp_total = mesh.shape["dp"]
    paired = mesh.shape["section"] == 2 and dp_total % 8 == 0
    placed = (
        P(None, "dp", None, None, None, None),
        P(None, "dp", None, None, None, None),
        P("section", "dp", None),
    )
    return jax.shard_map(
        paired_sections if paired else many_sections,
        mesh=mesh,
        in_specs=placed,
        out_specs=(P("section", None, "dp", None, None, None, None), P("section", "dp", None)),
        check_vma=False,
    )
```

```python
import functools

import jax
import jax.numpy as jnp
from jax import lax
from jax.experimental import pallas as pl
from jax.experimental.pallas import tpu as pltpu
from jax.sharding import PartitionSpec as P


def passed_along(block, axis, distance):
    devices = range(lax.axis_size(axis))
    route = [(i - distance, i) for i in devices if i - distance in devices]
    return lax.ppermute(block, axis, route)


def gather_patches(field):
    frames, height, width, channels = field.shape
    first_frame = field[:1]
    padded = jnp.concatenate([first_frame, first_frame, field], axis=0)
    padded = jnp.pad(padded, ((0, 0), (1, 1), (1, 1), (0, 0)))
    pieces = [
        padded[
            offset_time : offset_time + frames,
            offset_row : offset_row + height,
            offset_col : offset_col + width,
        ]
        for offset_time in range(3)
        for offset_row in range(3)
        for offset_col in range(3)
    ]
    return jnp.stack(pieces, axis=3).reshape(frames * height * width, 27 * channels)


def squash_field(activation):
    return jax.nn.silu(activation.astype(jnp.float32)).astype(jnp.bfloat16)


def squash_columns(activation):
    return gather_patches(squash_field(activation))


def layer_forward(activation, weight):
    branch = jnp.dot(squash_columns(activation), weight, preferred_element_type=jnp.float32)
    return (activation.astype(jnp.float32) + branch.reshape(activation.shape)).astype(jnp.bfloat16)


def input_gradient(activation, upstream, weight):
    flat_grad = upstream.reshape(-1, weight.shape[1])
    column_grad = lax.dot_general(
        flat_grad, weight, (((1,), (1,)), ((), ())), preferred_element_type=jnp.float32
    )
    base = activation.astype(jnp.float32)
    _, unfold = jax.vjp(gather_patches, base)
    field_grad = unfold(column_grad)[0]
    sigmoid_value = jax.nn.sigmoid(base)
    slope = sigmoid_value * (1.0 + base * (1.0 - sigmoid_value))
    return (upstream.astype(jnp.float32) + field_grad * slope).astype(jnp.bfloat16)


def weight_term(activation, upstream):
    flat_grad = upstream.reshape(-1, upstream.shape[-1])
    return lax.dot_general(
        squash_columns(activation),
        flat_grad,
        (((0,), (0,)), ((), ())),
        preferred_element_type=jnp.float32,
    )


def many_sections(clips, cotangent, weights):
    section_total = lax.axis_size("section")
    section_index = lax.axis_index("section")
    weight = lax.all_gather(weights, "dp", axis=1, tiled=True)[0]
    local_clips = clips[:, 0]
    local_grads = cotangent[:, 0]
    micro_count = local_clips.shape[0]
    step_count = micro_count + section_total - 1
    empty_field = jnp.zeros(local_clips.shape[1:], jnp.bfloat16)

    def forward_step(step_index, carry):
        received, saved_inputs, produced = carry
        micro_index = step_index - section_index
        active = (micro_index >= 0) & (micro_index < micro_count)
        slot_index = jnp.clip(micro_index, 0, micro_count - 1)
        fresh = lax.dynamic_index_in_dim(local_clips, slot_index, 0, keepdims=False)
        layer_input = jnp.where(section_index == 0, fresh, received)
        layer_output = layer_forward(layer_input, weight)
        kept_input = jnp.where(
            active,
            layer_input,
            lax.dynamic_index_in_dim(saved_inputs, slot_index, 0, keepdims=False),
        )
        kept_output = jnp.where(
            active, layer_output, lax.dynamic_index_in_dim(produced, slot_index, 0, keepdims=False)
        )
        saved_inputs = lax.dynamic_update_index_in_dim(saved_inputs, kept_input, slot_index, 0)
        produced = lax.dynamic_update_index_in_dim(produced, kept_output, slot_index, 0)
        received = passed_along(layer_output, "section", 1)
        return (received, saved_inputs, produced)

    start_forward = (empty_field, jnp.zeros_like(local_clips), jnp.zeros_like(local_clips))
    _, saved_inputs, produced = lax.fori_loop(0, step_count, forward_step, start_forward)

    def backward_step(step_index, carry):
        received, grad_total, kept_grads = carry
        micro_index = step_index - (section_total - 1 - section_index)
        active = (micro_index >= 0) & (micro_index < micro_count)
        slot_index = jnp.clip(micro_index, 0, micro_count - 1)
        fresh = lax.dynamic_index_in_dim(local_grads, slot_index, 0, keepdims=False)
        upstream = jnp.where(section_index == section_total - 1, fresh, received)
        activation = lax.dynamic_index_in_dim(saved_inputs, slot_index, 0, keepdims=False)
        grad_total = grad_total + jnp.where(active, weight_term(activation, upstream), 0.0)
        layer_grad = input_gradient(activation, upstream, weight)
        received = passed_along(layer_grad, "section", -1)
        return (received, grad_total, kept_grads)

    start_backward = (
        empty_field,
        jnp.zeros(weight.shape, jnp.float32),
        jnp.zeros_like(local_grads),
    )
    _, grad_total, kept_grads = lax.fori_loop(0, step_count, backward_step, start_backward)
    grad_share = lax.psum_scatter(
        grad_total.astype(jnp.bfloat16), "dp", scatter_dimension=0, tiled=True
    ).astype(jnp.float32)
    return (produced[None, :, None], grad_share[None])


def silu_of(value):
    return value * jax.nn.sigmoid(value)


def slope_of(value):
    sigmoid_value = jax.nn.sigmoid(value)
    return sigmoid_value * (1.0 + value * (1.0 - sigmoid_value))


def column_shifts(rows, width):
    height, flat, channels = rows.shape
    cells = rows.reshape(height * flat // width, width, channels)
    column = lax.broadcasted_iota(jnp.int32, cells.shape, 1)
    before = jnp.where(column == 0, 0.0, pltpu.roll(cells, 1, 1))
    after = jnp.where(column == width - 1, 0.0, pltpu.roll(cells, width - 1, 1))
    return [piece.reshape(rows.shape).astype(jnp.bfloat16) for piece in (before, cells, after)]


def whole(count):
    return [pl.BlockSpec(memory_space=pltpu.VMEM)] * count


def call(body, inputs, outputs, scratch, flops, place, far=False):
    return pl.pallas_call(
        body,
        out_shape=[jax.ShapeDtypeStruct(shape, dtype) for shape, dtype in outputs],
        in_specs=[pl.BlockSpec(memory_space=pltpu.SMEM)]
        + ([pl.BlockSpec(memory_space=pl.ANY)] * len(inputs) if far else whole(len(inputs))),
        out_specs=whole(len(outputs)),
        scratch_shapes=scratch,
        compiler_params=pltpu.CompilerParams(vmem_limit_bytes=48 * 1024 * 1024),
        cost_estimate=pl.CostEstimate(flops=flops, bytes_accessed=4_000_000, transcendentals=0),
    )(place, *inputs)


def turn_into(turned, k, t, piece):
    channels = piece.shape[-1]
    flat = piece.reshape(-1, channels)
    cells = flat.shape[0]
    turned[k * channels : (k + 1) * channels, t * cells : (t + 1) * cells] = flat.T


def move_grads(grads, field):
    _, frames, padded_height, flat, channels = grads.shape
    height = padded_height - 2
    zero_row = jnp.zeros((3, frames, 1, flat, channels), jnp.bfloat16)
    grads[:, :, :1] = zero_row
    grads[:, :, height + 1 :] = zero_row
    for t in range(frames):
        for tap in range(3):
            sources = [s for s in range(frames) if max(s + tap - 2, 0) == t]
            if sources:
                total = functools.reduce(lambda p, q: p + q, [field(s) for s in sources])
                grads[tap, t, 1 : height + 1] = total.astype(jnp.bfloat16)
            else:
                grads[tap, t, 1 : height + 1] = jnp.zeros((height, flat, channels), jnp.bfloat16)


def prepare_body(place, clips_far, cotangent_far, shard_far, *refs):
    shifted, base, upstream, shard, ready, held, clips, cotangent, sems = refs
    micro, frames, height, width, channels = clips.shape
    section = place[0]
    copies = [
        pltpu.make_async_copy(source, target, sems.at[k])
        for k, (source, target) in enumerate(
            ((clips_far, clips), (cotangent_far, cotangent), (shard_far, shard))
        )
    ]
    for copy in copies:
        copy.start()

    def reorder(source, target):
        for m in range(micro):
            held[:, :, m * width : (m + 1) * width, :] = source[m].astype(jnp.float32)
        for t in range(frames):
            target[t] = held[t].astype(jnp.bfloat16)

    zero_row = jnp.zeros((3, frames, 1) + shifted.shape[3:], jnp.bfloat16)
    shifted[:, :, :1] = zero_row
    shifted[:, :, height + 1 :] = zero_row
    copies[0].wait()
    reorder(clips, base)
    copies[1].wait()
    reorder(cotangent, upstream)
    copies[2].wait()

    @pl.when(section == 0)
    def _():
        for t in range(frames):
            squashed = silu_of(base[t].astype(jnp.float32)).astype(jnp.bfloat16)
            for k, piece in enumerate(column_shifts(squashed.astype(jnp.float32), width)):
                shifted[k, t, 1 : height + 1] = piece
                turn_into(ready, k, t, piece)

    @pl.when(section != 0)
    def _():
        for t in range(frames):
            for k, piece in enumerate(column_shifts(upstream[t].astype(jnp.float32), width)):
                shifted[k, t, 1 : height + 1] = piece


def chips_beside(y, x):
    return ((y, x), (y, 1 - x), (1 - y, x), (1 - y, 1 - x))


def shard_rows(place, rows, plane_bits, chip):
    plane = place[1] ^ plane_bits
    row, column = chips_beside(place[2], place[3])[chip]
    return pl.ds(pl.multiple_of((plane * 4 + row * 2 + column) * rows, 8), rows)


def unpack_weights(place, near, far, table):
    planes, rows = far[0].shape[0] + 1, near[0].shape[0]
    for chip in range(4):
        table[shard_rows(place, rows, 0, chip), :] = near[chip][...].astype(jnp.float32)
        for d in range(1, planes):
            table[shard_rows(place, rows, d, chip), :] = far[chip][d - 1].astype(jnp.float32)


def forward_weights(table, channels):
    rows = 9 * channels
    return jnp.concatenate(
        [table[t * rows : (t + 1) * rows, :].astype(jnp.bfloat16) for t in range(3)], axis=1
    )


def backward_weights(table, channels):
    return jnp.concatenate(
        [
            jnp.concatenate(
                [
                    table[(t * 9 + k) * channels : (t * 9 + k + 1) * channels, :].astype(jnp.bfloat16)
                    for k in reversed(range(9))
                ],
                axis=1,
            )
            for t in range(3)
        ],
        axis=0,
    )


def row_patches(shifted, t, height):
    flat, channels = shifted.shape[3:]
    return jnp.concatenate(
        [
            shifted[k, t, e : e + height].reshape(height * flat, channels)
            for e in range(3)
            for k in range(3)
        ],
        axis=1,
    )


def forward_product(shifted, weights, branch, frames, height):
    channels = branch.shape[-1]
    for t in range(frames):
        part = jnp.dot(row_patches(shifted, t, height), weights, preferred_element_type=jnp.float32)
        for tap in range(3):
            piece = part[:, tap * channels : (tap + 1) * channels]
            for target in range(frames):
                if max(target + tap - 2, 0) != t:
                    continue
                branch[target] += piece


def backward_product(shifted, weights, branch, frames, height):
    channels = branch.shape[-1]
    for t in range(frames):
        part = lax.dot_general(
            row_patches(shifted, t, height),
            weights,
            (((1,), (1,)), ((), ())),
            preferred_element_type=jnp.float32,
        )
        for tap in range(3):
            branch[max(t + tap - 2, 0)] += part[:, tap * channels : (tap + 1) * channels]


def first_body(place, *refs):
    near, far = refs[:4], refs[4:8]
    shifted, base, result, table, branch = refs[8:]
    frames, height, flat, channels = base.shape
    section = place[0]
    unpack_weights(place, near, far, table)
    branch[...] = jnp.zeros_like(branch)

    @pl.when(section == 0)
    def _():
        forward_product(shifted, forward_weights(table, channels), branch, frames, height)
        for t in range(frames):
            total = base[t].astype(jnp.float32) + branch[t].reshape(height, flat, channels)
            result[t] = total.astype(jnp.bfloat16)

    @pl.when(section != 0)
    def _():
        backward_product(shifted, backward_weights(table, channels), branch, frames, height)
        for t in range(frames):
            result[t] = branch[t].reshape(height, flat, channels).astype(jnp.bfloat16)


def second_body(width, place, ready, mine, other, upstream, *refs):
    near, far = refs[:3], refs[3:7]
    turned, grads, terms = refs[7:]
    frames, height, flat, channels = upstream.shape
    planes, rows = far[0].shape[0] + 1, near[0].shape[0]
    section = place[0]
    cells = height * flat

    def product(left):
        for tap in range(3):
            moved = jnp.concatenate(
                [
                    grads[tap, :, 2 - e : 2 - e + height].reshape(frames * cells, channels)
                    for e in range(3)
                ],
                axis=1,
            )
            part = jnp.dot(left[...], moved, preferred_element_type=jnp.float32)
            for e in range(3):
                for k in range(3):
                    start = (tap * 9 + e * 3 + k) * channels
                    terms[start : start + channels, :] = part[
                        k * channels : (k + 1) * channels, e * channels : (e + 1) * channels
                    ]

    @pl.when(section == 0)
    def _():
        for t in range(frames):
            value = upstream[t].astype(jnp.float32) + slope_of(mine[t].astype(jnp.float32)) * other[
                t
            ].astype(jnp.float32)
            grads[2, t, 1 : height + 1] = value.astype(jnp.bfloat16)
        move_grads(grads, lambda s: grads[2, s, 1 : height + 1].astype(jnp.float32))
        product(ready)

    @pl.when(section != 0)
    def _():
        move_grads(grads, lambda s: upstream[s].astype(jnp.float32))
        for t in range(frames):
            squashed = silu_of(other[t].astype(jnp.float32)).astype(jnp.bfloat16)
            for k, piece in enumerate(column_shifts(squashed.astype(jnp.float32), width)):
                turn_into(turned, k, t, piece)
        product(turned)

    for chip in range(4):
        for d in range(planes):
            share = terms[shard_rows(place, rows, d, chip), :]
            if chip == 3:
                far[3][d] = share.astype(jnp.bfloat16)
            elif d:
                far[chip][d - 1] = share.astype(jnp.bfloat16)
            else:
                near[chip][...] = share.astype(near[chip].dtype)


def third_body(place, *refs):
    near, far = refs[:4], refs[4:8]
    mine, other, produced, table, branch, shifted = refs[8:]
    micro, frames, height, width, channels = produced.shape
    flat = micro * width
    section = place[0]

    @pl.when(section == 0)
    def _():
        for t in range(frames):
            branch[t] = mine[t].astype(jnp.float32).reshape(height * flat, channels)

    @pl.when(section != 0)
    def _():
        unpack_weights(place, near, far, table)
        zero_row = jnp.zeros((3, frames, 1, flat, channels), jnp.bfloat16)
        shifted[:, :, :1] = zero_row
        shifted[:, :, height + 1 :] = zero_row
        for t in range(frames):
            value = other[t].astype(jnp.float32)
            branch[t] = value.reshape(height * flat, channels)
            squashed = silu_of(value).astype(jnp.bfloat16)
            for k, piece in enumerate(column_shifts(squashed.astype(jnp.float32), width)):
                shifted[k, t, 1 : height + 1] = piece
        forward_product(shifted, forward_weights(table, channels), branch, frames, height)

    for t in range(frames):
        cells = branch[t].reshape(height, flat, channels)
        for m in range(micro):
            produced[m, t] = cells[:, m * width : (m + 1) * width, :].astype(jnp.bfloat16)


def paired_sections(clips, cotangent, weights):
    dp_total = lax.axis_size("dp")
    planes = dp_total // 4
    local_clips, local_grads, shard = clips[:, 0], cotangent[:, 0], weights[0]
    micro, frames, height, width, channels = local_clips.shape
    rows = shard.shape[0]
    flat = micro * width
    cells = height * flat
    section, index = lax.axis_index("section"), lax.axis_index("dp")
    place = jnp.stack([section, index // 4, index // 2 % 2, index % 2]).astype(jnp.int32)

    def across(block, bits):
        return lax.ppermute(block, "dp", [(i, i ^ bits) for i in range(dp_total)])

    field = (frames, height, flat, channels)
    padded = (3, frames, height + 2, flat, channels)
    bf16, f32 = jnp.bfloat16, jnp.float32
    unit = 2 * micro * frames * height * width * channels * channels * 27

    near = [across(shard, bits) for bits in range(1, 3)]
    from_planes = [across(shard, 4 * d) for d in range(1, planes)]
    near, from_planes, late_shard = lax.optimization_barrier((near, from_planes, shard))
    line = jnp.stack(from_planes)
    line, late_shard = lax.optimization_barrier((line, late_shard))
    near.append(across(late_shard, 3))
    far = [line] + [across(line, bits) for bits in range(1, 4)]
    turned = (3 * channels, frames * cells)
    shifted, base, upstream, shard_copy, ready = call(
        prepare_body,
        (local_clips, local_grads, shard),
        [(padded, bf16), (field, bf16), (field, bf16), (shard.shape, bf16), (turned, bf16)],
        [
            pltpu.VMEM(field, f32),
            pltpu.VMEM(local_clips.shape, bf16),
            pltpu.VMEM(local_clips.shape, bf16),
            pltpu.SemaphoreType.DMA((3,)),
        ],
        unit // 8,
        place,
        far=True,
    )
    shards = (shard_copy, *near, *far)

    table = pltpu.VMEM((dp_total * rows, channels), f32)
    branch = pltpu.VMEM((frames, cells, channels), f32)
    (mine,) = call(
        first_body, shards + (shifted, base), [(field, bf16)], [table, branch], unit, place
    )
    other = lax.ppermute(mine, "section", [(0, 1), (1, 0)])
    shares = call(
        functools.partial(second_body, width),
        (ready, mine, other, upstream),
        [((rows, channels), f32)]
        + [((rows, channels), bf16)] * 2
        + [((planes - 1, rows, channels), bf16)] * 3
        + [((planes, rows, channels), bf16)],
        [
            pltpu.VMEM(turned, bf16),
            pltpu.VMEM(padded, bf16),
            table,
        ],
        unit,
        place,
    )
    near_terms, far_terms = shares[:3], shares[3:]
    (produced,) = call(
        third_body,
        shards + (mine, other),
        [(local_clips.shape, bf16)],
        [table, branch, pltpu.VMEM(padded, bf16)],
        unit,
        place,
    )

    def added(*terms):
        return functools.reduce(lambda p, q: p + q, [term.astype(f32) for term in terms])

    far_in = [across(far_terms[bits], bits) for bits in (3, 2, 1)]
    far_in, produced, near_terms = lax.optimization_barrier((far_in, produced, near_terms))
    diagonal, below, beside = far_in
    line_sum = added(far_terms[0], diagonal[1:], below, beside).astype(bf16)
    from_line = [across(line_sum[d - 1], 4 * d) for d in range(1, planes)]
    near_in = [across(near_terms[bits], bits) for bits in range(1, 3)]
    total = added(near_terms[0], diagonal[0], *near_in, *from_line)
    return (produced[None, :, None], total[None])


def solution(mesh):
    dp_total = mesh.shape["dp"]
    paired = mesh.shape["section"] == 2 and dp_total in (8, 16, 32)
    placed = (
        P(None, "dp", None, None, None, None),
        P(None, "dp", None, None, None, None),
        P("section", "dp", None),
    )
    return jax.shard_map(
        paired_sections if paired else many_sections,
        mesh=mesh,
        in_specs=placed,
        out_specs=(P("section", None, "dp", None, None, None, None), P("section", "dp", None)),
        check_vma=False,
    )
```

```python
import functools

import jax
import jax.numpy as jnp
from jax import lax
from jax.experimental import pallas as pl
from jax.experimental.pallas import tpu as pltpu
from jax.sharding import PartitionSpec as P


def passed_along(block, axis, distance):
    devices = range(lax.axis_size(axis))
    route = [(i - distance, i) for i in devices if i - distance in devices]
    return lax.ppermute(block, axis, route)


def gather_patches(field):
    frames, height, width, channels = field.shape
    first_frame = field[:1]
    padded = jnp.concatenate([first_frame, first_frame, field], axis=0)
    padded = jnp.pad(padded, ((0, 0), (1, 1), (1, 1), (0, 0)))
    pieces = [
        padded[
            offset_time : offset_time + frames,
            offset_row : offset_row + height,
            offset_col : offset_col + width,
        ]
        for offset_time in range(3)
        for offset_row in range(3)
        for offset_col in range(3)
    ]
    return jnp.stack(pieces, axis=3).reshape(frames * height * width, 27 * channels)


def squash_field(activation):
    return jax.nn.silu(activation.astype(jnp.float32)).astype(jnp.bfloat16)


def squash_columns(activation):
    return gather_patches(squash_field(activation))


def layer_forward(activation, weight):
    branch = jnp.dot(squash_columns(activation), weight, preferred_element_type=jnp.float32)
    return (activation.astype(jnp.float32) + branch.reshape(activation.shape)).astype(jnp.bfloat16)


def input_gradient(activation, upstream, weight):
    flat_grad = upstream.reshape(-1, weight.shape[1])
    column_grad = lax.dot_general(
        flat_grad, weight, (((1,), (1,)), ((), ())), preferred_element_type=jnp.float32
    )
    base = activation.astype(jnp.float32)
    _, unfold = jax.vjp(gather_patches, base)
    field_grad = unfold(column_grad)[0]
    sigmoid_value = jax.nn.sigmoid(base)
    slope = sigmoid_value * (1.0 + base * (1.0 - sigmoid_value))
    return (upstream.astype(jnp.float32) + field_grad * slope).astype(jnp.bfloat16)


def weight_term(activation, upstream):
    flat_grad = upstream.reshape(-1, upstream.shape[-1])
    return lax.dot_general(
        squash_columns(activation),
        flat_grad,
        (((0,), (0,)), ((), ())),
        preferred_element_type=jnp.float32,
    )


def many_sections(clips, cotangent, weights):
    section_total = lax.axis_size("section")
    section_index = lax.axis_index("section")
    weight = lax.all_gather(weights, "dp", axis=1, tiled=True)[0]
    local_clips = clips[:, 0]
    local_grads = cotangent[:, 0]
    micro_count = local_clips.shape[0]
    step_count = micro_count + section_total - 1
    empty_field = jnp.zeros(local_clips.shape[1:], jnp.bfloat16)

    def forward_step(step_index, carry):
        received, saved_inputs, produced = carry
        micro_index = step_index - section_index
        active = (micro_index >= 0) & (micro_index < micro_count)
        slot_index = jnp.clip(micro_index, 0, micro_count - 1)
        fresh = lax.dynamic_index_in_dim(local_clips, slot_index, 0, keepdims=False)
        layer_input = jnp.where(section_index == 0, fresh, received)
        layer_output = layer_forward(layer_input, weight)
        kept_input = jnp.where(
            active,
            layer_input,
            lax.dynamic_index_in_dim(saved_inputs, slot_index, 0, keepdims=False),
        )
        kept_output = jnp.where(
            active, layer_output, lax.dynamic_index_in_dim(produced, slot_index, 0, keepdims=False)
        )
        saved_inputs = lax.dynamic_update_index_in_dim(saved_inputs, kept_input, slot_index, 0)
        produced = lax.dynamic_update_index_in_dim(produced, kept_output, slot_index, 0)
        received = passed_along(layer_output, "section", 1)
        return (received, saved_inputs, produced)

    start_forward = (empty_field, jnp.zeros_like(local_clips), jnp.zeros_like(local_clips))
    _, saved_inputs, produced = lax.fori_loop(0, step_count, forward_step, start_forward)

    def backward_step(step_index, carry):
        received, grad_total, kept_grads = carry
        micro_index = step_index - (section_total - 1 - section_index)
        active = (micro_index >= 0) & (micro_index < micro_count)
        slot_index = jnp.clip(micro_index, 0, micro_count - 1)
        fresh = lax.dynamic_index_in_dim(local_grads, slot_index, 0, keepdims=False)
        upstream = jnp.where(section_index == section_total - 1, fresh, received)
        activation = lax.dynamic_index_in_dim(saved_inputs, slot_index, 0, keepdims=False)
        grad_total = grad_total + jnp.where(active, weight_term(activation, upstream), 0.0)
        layer_grad = input_gradient(activation, upstream, weight)
        received = passed_along(layer_grad, "section", -1)
        return (received, grad_total, kept_grads)

    start_backward = (
        empty_field,
        jnp.zeros(weight.shape, jnp.float32),
        jnp.zeros_like(local_grads),
    )
    _, grad_total, kept_grads = lax.fori_loop(0, step_count, backward_step, start_backward)
    grad_share = lax.psum_scatter(
        grad_total.astype(jnp.bfloat16), "dp", scatter_dimension=0, tiled=True
    ).astype(jnp.float32)
    return (produced[None, :, None], grad_share[None])


def silu_of(value):
    return value * jax.nn.sigmoid(value)


def slope_of(value):
    sigmoid_value = jax.nn.sigmoid(value)
    return sigmoid_value * (1.0 + value * (1.0 - sigmoid_value))


def column_shifts(rows, width):
    height, flat, channels = rows.shape
    cells = rows.reshape(height * flat // width, width, channels)
    column = lax.broadcasted_iota(jnp.int32, cells.shape, 1)
    before = jnp.where(column == 0, 0.0, pltpu.roll(cells, 1, 1))
    after = jnp.where(column == width - 1, 0.0, pltpu.roll(cells, width - 1, 1))
    return [piece.reshape(rows.shape).astype(jnp.bfloat16) for piece in (before, cells, after)]


def whole(count):
    return [pl.BlockSpec(memory_space=pltpu.VMEM)] * count


def call(body, inputs, outputs, scratch, flops, place, far=False):
    return pl.pallas_call(
        body,
        out_shape=[jax.ShapeDtypeStruct(shape, dtype) for shape, dtype in outputs],
        in_specs=[pl.BlockSpec(memory_space=pltpu.SMEM)]
        + ([pl.BlockSpec(memory_space=pl.ANY)] * len(inputs) if far else whole(len(inputs))),
        out_specs=whole(len(outputs)),
        scratch_shapes=scratch,
        compiler_params=pltpu.CompilerParams(vmem_limit_bytes=48 * 1024 * 1024),
        cost_estimate=pl.CostEstimate(flops=flops, bytes_accessed=4_000_000, transcendentals=0),
    )(place, *inputs)


def turn_into(turned, k, t, piece):
    channels = piece.shape[-1]
    flat = piece.reshape(-1, channels)
    cells = flat.shape[0]
    turned[k * channels : (k + 1) * channels, t * cells : (t + 1) * cells] = flat.T


def move_grads(grads, field):
    _, frames, padded_height, flat, channels = grads.shape
    height = padded_height - 2
    zero_row = jnp.zeros((3, frames, 1, flat, channels), jnp.bfloat16)
    grads[:, :, :1] = zero_row
    grads[:, :, height + 1 :] = zero_row
    for t in range(frames):
        for tap in range(3):
            sources = [s for s in range(frames) if max(s + tap - 2, 0) == t]
            if sources:
                total = functools.reduce(lambda p, q: p + q, [field(s) for s in sources])
                grads[tap, t, 1 : height + 1] = total.astype(jnp.bfloat16)
            else:
                grads[tap, t, 1 : height + 1] = jnp.zeros((height, flat, channels), jnp.bfloat16)


def copy_body(place, source, target):
    target[...] = source[...]


def prepare_body(place, clips_far, cotangent_far, *refs):
    shifted, base, upstream, ready, held, clips, cotangent, sems = refs
    micro, frames, height, width, channels = clips.shape
    section = place[0]
    copies = [
        pltpu.make_async_copy(source, target, sems.at[k])
        for k, (source, target) in enumerate(
            ((clips_far, clips), (cotangent_far, cotangent))
        )
    ]
    for copy in copies:
        copy.start()

    def reorder(source, target):
        for m in range(micro):
            held[:, :, m * width : (m + 1) * width, :] = source[m].astype(jnp.float32)
        for t in range(frames):
            target[t] = held[t].astype(jnp.bfloat16)

    zero_row = jnp.zeros((3, frames, 1) + shifted.shape[3:], jnp.bfloat16)
    shifted[:, :, :1] = zero_row
    shifted[:, :, height + 1 :] = zero_row
    copies[0].wait()
    reorder(clips, base)
    copies[1].wait()
    reorder(cotangent, upstream)

    @pl.when(section == 0)
    def _():
        for t in range(frames):
            squashed = silu_of(base[t].astype(jnp.float32)).astype(jnp.bfloat16)
            for k, piece in enumerate(column_shifts(squashed.astype(jnp.float32), width)):
                shifted[k, t, 1 : height + 1] = piece
                turn_into(ready, k, t, piece)

    @pl.when(section != 0)
    def _():
        for t in range(frames):
            for k, piece in enumerate(column_shifts(upstream[t].astype(jnp.float32), width)):
                shifted[k, t, 1 : height + 1] = piece


def shard_rows(place, rows, first, second):
    far, near = jnp.where(place[0] == 0, first, second), jnp.where(place[0] == 0, second, first)
    return pl.ds(pl.multiple_of((place[1] ^ (4 * far + near)) * rows, 8), rows)


def unpack_weights(place, blocks, table):
    rows = blocks[0].shape[1]
    for second in range(4):
        for first in range(4):
            shard = blocks[second][first]
            table[shard_rows(place, rows, first, second), :] = shard.astype(jnp.float32)


def forward_weights(table, channels):
    rows = 9 * channels
    return jnp.concatenate(
        [table[t * rows : (t + 1) * rows, :].astype(jnp.bfloat16) for t in range(3)], axis=1
    )


def backward_weights(table, channels):
    return jnp.concatenate(
        [
            jnp.concatenate(
                [
                    table[(t * 9 + k) * channels : (t * 9 + k + 1) * channels, :].astype(jnp.bfloat16)
                    for k in reversed(range(9))
                ],
                axis=1,
            )
            for t in range(3)
        ],
        axis=0,
    )


def row_patches(shifted, t, height):
    flat, channels = shifted.shape[3:]
    return jnp.concatenate(
        [
            shifted[k, t, e : e + height].reshape(height * flat, channels)
            for e in range(3)
            for k in range(3)
        ],
        axis=1,
    )


def forward_product(shifted, weights, branch, frames, height):
    channels = branch.shape[-1]
    for t in range(frames):
        part = jnp.dot(row_patches(shifted, t, height), weights, preferred_element_type=jnp.float32)
        for tap in range(3):
            piece = part[:, tap * channels : (tap + 1) * channels]
            for target in range(frames):
                if max(target + tap - 2, 0) != t:
                    continue
                branch[target] += piece


def backward_product(shifted, weights, branch, frames, height):
    channels = branch.shape[-1]
    for t in range(frames):
        part = lax.dot_general(
            row_patches(shifted, t, height),
            weights,
            (((1,), (1,)), ((), ())),
            preferred_element_type=jnp.float32,
        )
        for tap in range(3):
            branch[max(t + tap - 2, 0)] += part[:, tap * channels : (tap + 1) * channels]


def first_body(place, *refs):
    blocks = refs[:4]
    shifted, base, result, table, branch = refs[4:]
    frames, height, flat, channels = base.shape
    section = place[0]
    unpack_weights(place, blocks, table)
    branch[...] = jnp.zeros_like(branch)

    @pl.when(section == 0)
    def _():
        forward_product(shifted, forward_weights(table, channels), branch, frames, height)
        for t in range(frames):
            total = base[t].astype(jnp.float32) + branch[t].reshape(height, flat, channels)
            result[t] = total.astype(jnp.bfloat16)

    @pl.when(section != 0)
    def _():
        backward_product(shifted, backward_weights(table, channels), branch, frames, height)
        for t in range(frames):
            result[t] = branch[t].reshape(height, flat, channels).astype(jnp.bfloat16)


def second_body(width, place, ready, mine, other, upstream, *refs):
    own, blocks = refs[0], refs[1:5]
    turned, grads, terms = refs[5:]
    frames, height, flat, channels = upstream.shape
    rows = own.shape[0]
    section = place[0]
    cells = height * flat

    def product(left):
        for tap in range(3):
            moved = jnp.concatenate(
                [
                    grads[tap, :, 2 - e : 2 - e + height].reshape(frames * cells, channels)
                    for e in range(3)
                ],
                axis=1,
            )
            part = jnp.dot(left[...], moved, preferred_element_type=jnp.float32)
            for e in range(3):
                for k in range(3):
                    start = (tap * 9 + e * 3 + k) * channels
                    terms[start : start + channels, :] = part[
                        k * channels : (k + 1) * channels, e * channels : (e + 1) * channels
                    ]

    @pl.when(section == 0)
    def _():
        for t in range(frames):
            value = upstream[t].astype(jnp.float32) + slope_of(mine[t].astype(jnp.float32)) * other[
                t
            ].astype(jnp.float32)
            grads[2, t, 1 : height + 1] = value.astype(jnp.bfloat16)
        move_grads(grads, lambda s: grads[2, s, 1 : height + 1].astype(jnp.float32))
        product(ready)

    @pl.when(section != 0)
    def _():
        move_grads(grads, lambda s: upstream[s].astype(jnp.float32))
        for t in range(frames):
            squashed = silu_of(other[t].astype(jnp.float32)).astype(jnp.bfloat16)
            for k, piece in enumerate(column_shifts(squashed.astype(jnp.float32), width)):
                turn_into(turned, k, t, piece)
        product(turned)

    for second in range(4):
        for first in range(4):
            share = terms[shard_rows(place, rows, first, second), :]
            if first == 0 and second == 0:
                own[...] = share
            elif second == 0:
                blocks[0][first - 1] = share.astype(jnp.bfloat16)
            else:
                blocks[second][first] = share.astype(jnp.bfloat16)


def third_body(place, *refs):
    blocks = refs[:4]
    mine, other, produced, table, branch, shifted = refs[4:]
    micro, frames, height, width, channels = produced.shape
    flat = micro * width
    section = place[0]

    @pl.when(section == 0)
    def _():
        for t in range(frames):
            branch[t] = mine[t].astype(jnp.float32).reshape(height * flat, channels)

    @pl.when(section != 0)
    def _():
        unpack_weights(place, blocks, table)
        zero_row = jnp.zeros((3, frames, 1, flat, channels), jnp.bfloat16)
        shifted[:, :, :1] = zero_row
        shifted[:, :, height + 1 :] = zero_row
        for t in range(frames):
            value = other[t].astype(jnp.float32)
            branch[t] = value.reshape(height * flat, channels)
            squashed = silu_of(value).astype(jnp.bfloat16)
            for k, piece in enumerate(column_shifts(squashed.astype(jnp.float32), width)):
                shifted[k, t, 1 : height + 1] = piece
        forward_product(shifted, forward_weights(table, channels), branch, frames, height)

    for t in range(frames):
        cells = branch[t].reshape(height, flat, channels)
        for m in range(micro):
            produced[m, t] = cells[:, m * width : (m + 1) * width, :].astype(jnp.bfloat16)


def paired_sections(clips, cotangent, weights):
    dp_total = lax.axis_size("dp")
    local_clips, local_grads, shard = clips[:, 0], cotangent[:, 0], weights[0]
    micro, frames, height, width, channels = local_clips.shape
    rows = shard.shape[0]
    flat = micro * width
    cells = height * flat
    place = jnp.stack([lax.axis_index("section"), lax.axis_index("dp")]).astype(jnp.int32)

    def traded(block, plane_first, step):
        bits = (4 * step, step) if plane_first else (step, 4 * step)
        route = [
            (s * dp_total + i, s * dp_total + (i ^ bits[s])) for s in range(2) for i in range(dp_total)
        ]
        return lax.ppermute(block, ("section", "dp"), route)

    field = (frames, height, flat, channels)
    padded = (3, frames, height + 2, flat, channels)
    bf16, f32 = jnp.bfloat16, jnp.float32
    unit = 2 * micro * frames * height * width * channels * channels * 27

    first = [traded(shard, True, step) for step in range(1, 4)]
    (shard_copy,) = call(copy_body, (shard,), [(shard.shape, bf16)], [], unit // 16, place)
    shard_copy, first = lax.optimization_barrier((shard_copy, first))
    line = jnp.stack([shard_copy] + first)
    blocks = (line, *[traded(line, False, step) for step in range(1, 4)])

    turned = (3 * channels, frames * cells)
    shifted, base, upstream, ready = call(
        prepare_body,
        (local_clips, local_grads),
        [(padded, bf16), (field, bf16), (field, bf16), (turned, bf16)],
        [
            pltpu.VMEM(field, f32),
            pltpu.VMEM(local_clips.shape, bf16),
            pltpu.VMEM(local_clips.shape, bf16),
            pltpu.SemaphoreType.DMA((2,)),
        ],
        unit // 8,
        place,
        far=True,
    )
    table = pltpu.VMEM((dp_total * rows, channels), f32)
    branch = pltpu.VMEM((frames, cells, channels), f32)
    (mine,) = call(
        first_body, blocks + (shifted, base), [(field, bf16)], [table, branch], unit, place
    )
    other = lax.ppermute(mine, "section", [(0, 1), (1, 0)])
    own, *terms = call(
        functools.partial(second_body, width),
        (ready, mine, other, upstream),
        [((rows, channels), f32), ((3, rows, channels), bf16)] + [((4, rows, channels), bf16)] * 3,
        [
            pltpu.VMEM(turned, bf16),
            pltpu.VMEM(padded, bf16),
            table,
        ],
        unit,
        place,
    )
    (produced,) = call(
        third_body,
        blocks + (mine, other),
        [(local_clips.shape, bf16)],
        [table, branch, pltpu.VMEM(padded, bf16)],
        unit,
        place,
    )

    def added(*terms):
        return functools.reduce(lambda p, q: p + q, [term.astype(f32) for term in terms])

    received = [traded(terms[step], False, step) for step in (3, 2, 1)]
    received, produced = lax.optimization_barrier((received, produced))
    line_sum = added(terms[0], *[block[1:] for block in received]).astype(bf16)
    own_sum = added(own, *[block[0] for block in received])
    total = added(own_sum, *[traded(line_sum[step - 1], True, step) for step in range(1, 4)])
    return (produced[None, :, None], total[None])


def solution(mesh):
    dp_total = mesh.shape["dp"]
    paired = mesh.shape["section"] == 2 and dp_total == 16
    placed = (
        P(None, "dp", None, None, None, None),
        P(None, "dp", None, None, None, None),
        P("section", "dp", None),
    )
    return jax.shard_map(
        paired_sections if paired else many_sections,
        mesh=mesh,
        in_specs=placed,
        out_specs=(P("section", None, "dp", None, None, None, None), P("section", "dp", None)),
        check_vma=False,
    )
```

```python
import functools

import jax
import jax.numpy as jnp
from jax import lax
from jax.experimental import pallas as pl
from jax.experimental.pallas import tpu as pltpu
from jax.sharding import PartitionSpec as P


def passed_along(block, axis, distance):
    devices = range(lax.axis_size(axis))
    route = [(i - distance, i) for i in devices if i - distance in devices]
    return lax.ppermute(block, axis, route)


def gather_patches(field):
    frames, height, width, channels = field.shape
    first_frame = field[:1]
    padded = jnp.concatenate([first_frame, first_frame, field], axis=0)
    padded = jnp.pad(padded, ((0, 0), (1, 1), (1, 1), (0, 0)))
    pieces = [
        padded[
            offset_time : offset_time + frames,
            offset_row : offset_row + height,
            offset_col : offset_col + width,
        ]
        for offset_time in range(3)
        for offset_row in range(3)
        for offset_col in range(3)
    ]
    return jnp.stack(pieces, axis=3).reshape(frames * height * width, 27 * channels)


def squash_field(activation):
    return jax.nn.silu(activation.astype(jnp.float32)).astype(jnp.bfloat16)


def squash_columns(activation):
    return gather_patches(squash_field(activation))


def layer_forward(activation, weight):
    branch = jnp.dot(squash_columns(activation), weight, preferred_element_type=jnp.float32)
    return (activation.astype(jnp.float32) + branch.reshape(activation.shape)).astype(jnp.bfloat16)


def input_gradient(activation, upstream, weight):
    flat_grad = upstream.reshape(-1, weight.shape[1])
    column_grad = lax.dot_general(
        flat_grad, weight, (((1,), (1,)), ((), ())), preferred_element_type=jnp.float32
    )
    base = activation.astype(jnp.float32)
    _, unfold = jax.vjp(gather_patches, base)
    field_grad = unfold(column_grad)[0]
    sigmoid_value = jax.nn.sigmoid(base)
    slope = sigmoid_value * (1.0 + base * (1.0 - sigmoid_value))
    return (upstream.astype(jnp.float32) + field_grad * slope).astype(jnp.bfloat16)


def weight_term(activation, upstream):
    flat_grad = upstream.reshape(-1, upstream.shape[-1])
    return lax.dot_general(
        squash_columns(activation),
        flat_grad,
        (((0,), (0,)), ((), ())),
        preferred_element_type=jnp.float32,
    )


def many_sections(clips, cotangent, weights):
    section_total = lax.axis_size("section")
    section_index = lax.axis_index("section")
    weight = lax.all_gather(weights, "dp", axis=1, tiled=True)[0]
    local_clips = clips[:, 0]
    local_grads = cotangent[:, 0]
    micro_count = local_clips.shape[0]
    step_count = micro_count + section_total - 1
    empty_field = jnp.zeros(local_clips.shape[1:], jnp.bfloat16)

    def forward_step(step_index, carry):
        received, saved_inputs, produced = carry
        micro_index = step_index - section_index
        active = (micro_index >= 0) & (micro_index < micro_count)
        slot_index = jnp.clip(micro_index, 0, micro_count - 1)
        fresh = lax.dynamic_index_in_dim(local_clips, slot_index, 0, keepdims=False)
        layer_input = jnp.where(section_index == 0, fresh, received)
        layer_output = layer_forward(layer_input, weight)
        kept_input = jnp.where(
            active,
            layer_input,
            lax.dynamic_index_in_dim(saved_inputs, slot_index, 0, keepdims=False),
        )
        kept_output = jnp.where(
            active, layer_output, lax.dynamic_index_in_dim(produced, slot_index, 0, keepdims=False)
        )
        saved_inputs = lax.dynamic_update_index_in_dim(saved_inputs, kept_input, slot_index, 0)
        produced = lax.dynamic_update_index_in_dim(produced, kept_output, slot_index, 0)
        received = passed_along(layer_output, "section", 1)
        return (received, saved_inputs, produced)

    start_forward = (empty_field, jnp.zeros_like(local_clips), jnp.zeros_like(local_clips))
    _, saved_inputs, produced = lax.fori_loop(0, step_count, forward_step, start_forward)

    def backward_step(step_index, carry):
        received, grad_total, kept_grads = carry
        micro_index = step_index - (section_total - 1 - section_index)
        active = (micro_index >= 0) & (micro_index < micro_count)
        slot_index = jnp.clip(micro_index, 0, micro_count - 1)
        fresh = lax.dynamic_index_in_dim(local_grads, slot_index, 0, keepdims=False)
        upstream = jnp.where(section_index == section_total - 1, fresh, received)
        activation = lax.dynamic_index_in_dim(saved_inputs, slot_index, 0, keepdims=False)
        grad_total = grad_total + jnp.where(active, weight_term(activation, upstream), 0.0)
        layer_grad = input_gradient(activation, upstream, weight)
        received = passed_along(layer_grad, "section", -1)
        return (received, grad_total, kept_grads)

    start_backward = (
        empty_field,
        jnp.zeros(weight.shape, jnp.float32),
        jnp.zeros_like(local_grads),
    )
    _, grad_total, kept_grads = lax.fori_loop(0, step_count, backward_step, start_backward)
    grad_share = lax.psum_scatter(
        grad_total.astype(jnp.bfloat16), "dp", scatter_dimension=0, tiled=True
    ).astype(jnp.float32)
    return (produced[None, :, None], grad_share[None])


def silu_of(value):
    return value * jax.nn.sigmoid(value)


def slope_of(value):
    sigmoid_value = jax.nn.sigmoid(value)
    return sigmoid_value * (1.0 + value * (1.0 - sigmoid_value))


def column_shifts(rows, width):
    height, flat, channels = rows.shape
    cells = rows.reshape(height * flat // width, width, channels)
    column = lax.broadcasted_iota(jnp.int32, cells.shape, 1)
    before = jnp.where(column == 0, 0.0, pltpu.roll(cells, 1, 1))
    after = jnp.where(column == width - 1, 0.0, pltpu.roll(cells, width - 1, 1))
    return [piece.reshape(rows.shape).astype(jnp.bfloat16) for piece in (before, cells, after)]


def whole(count):
    return [pl.BlockSpec(memory_space=pltpu.VMEM)] * count


def call(body, inputs, outputs, scratch, flops, place, far=False):
    return pl.pallas_call(
        body,
        out_shape=[jax.ShapeDtypeStruct(shape, dtype) for shape, dtype in outputs],
        in_specs=[pl.BlockSpec(memory_space=pltpu.SMEM)]
        + ([pl.BlockSpec(memory_space=pl.ANY)] * len(inputs) if far else whole(len(inputs))),
        out_specs=whole(len(outputs)),
        scratch_shapes=scratch,
        compiler_params=pltpu.CompilerParams(vmem_limit_bytes=32 * 1024 * 1024),
        cost_estimate=pl.CostEstimate(flops=flops, bytes_accessed=4_000_000, transcendentals=0),
    )(place, *inputs)


def turn_into(turned, k, t, piece):
    channels = piece.shape[-1]
    flat = piece.reshape(-1, channels)
    cells = flat.shape[0]
    turned[k * channels : (k + 1) * channels, t * cells : (t + 1) * cells] = flat.T


def move_grads(grads, field):
    _, frames, padded_height, flat, channels = grads.shape
    height = padded_height - 2
    zero_row = jnp.zeros((3, frames, 1, flat, channels), jnp.bfloat16)
    grads[:, :, :1] = zero_row
    grads[:, :, height + 1 :] = zero_row
    for t in range(frames):
        for tap in range(3):
            sources = [s for s in range(frames) if max(s + tap - 2, 0) == t]
            if sources:
                total = functools.reduce(lambda p, q: p + q, [field(s) for s in sources])
                grads[tap, t, 1 : height + 1] = total.astype(jnp.bfloat16)


def copy_body(place, source, target):
    target[...] = source[...]


def prepare_body(place, clips_far, cotangent_far, *refs):
    shifted, base, upstream, ready, held, clips, cotangent, sems = refs
    micro, frames, height, width, channels = clips.shape
    section = place[0]
    copies = [
        pltpu.make_async_copy(source, target, sems.at[k])
        for k, (source, target) in enumerate(
            ((clips_far, clips), (cotangent_far, cotangent))
        )
    ]
    for copy in copies:
        copy.start()

    def reorder(source, target):
        for m in range(micro):
            held[:, :, m * width : (m + 1) * width, :] = source[m].astype(jnp.float32)
        for t in range(frames):
            target[t] = held[t].astype(jnp.bfloat16)

    zero_row = jnp.zeros((3, frames, 1) + shifted.shape[3:], jnp.bfloat16)
    shifted[:, :, :1] = zero_row
    shifted[:, :, height + 1 :] = zero_row
    copies[0].wait()
    reorder(clips, base)
    copies[1].wait()
    reorder(cotangent, upstream)

    @pl.when(section == 0)
    def _():
        for t in range(frames):
            squashed = silu_of(base[t].astype(jnp.float32)).astype(jnp.bfloat16)
            for k, piece in enumerate(column_shifts(squashed.astype(jnp.float32), width)):
                shifted[k, t, 1 : height + 1] = piece
                turn_into(ready, k, t, piece)

    @pl.when(section != 0)
    def _():
        for t in range(frames):
            for k, piece in enumerate(column_shifts(upstream[t].astype(jnp.float32), width)):
                shifted[k, t, 1 : height + 1] = piece


def shard_rows(place, rows, first, second):
    far, near = jnp.where(place[0] == 0, second, first), jnp.where(place[0] == 0, first, second)
    return pl.ds(pl.multiple_of((place[1] ^ (4 * far + near)) * rows, 8), rows)


def unpack_weights(place, blocks, table):
    rows = blocks[0].shape[1]
    for second in range(4):
        for first in range(4):
            shard = blocks[second][first]
            table[shard_rows(place, rows, first, second), :] = shard.astype(jnp.float32)


def forward_weights(table, channels):
    rows = 9 * channels
    return jnp.concatenate(
        [table[t * rows : (t + 1) * rows, :].astype(jnp.bfloat16) for t in range(3)], axis=1
    )


def backward_weights(table, channels):
    def turned_taps(times):
        blocks = []
        for k in reversed(range(9)):
            rows = [table[(t * 9 + k) * channels : (t * 9 + k + 1) * channels, :] for t in times]
            blocks.append(functools.reduce(lambda p, q: p + q, rows).astype(jnp.bfloat16))
        return jnp.concatenate(blocks, axis=1)

    return [turned_taps(times) for times in ((0,), (1,), (2,), (0, 1), (0, 1, 2))]


def row_patches(shifted, start, count, height):
    flat, channels = shifted.shape[3:]
    return jnp.concatenate(
        [
            shifted[k, start : start + count, e : e + height].reshape(count * height * flat, channels)
            for e in range(3)
            for k in range(3)
        ],
        axis=1,
    )


def forward_product(shifted, weights, branch, frames, height):
    cells, channels = branch.shape[1:]
    for start, count, first_tap in ((0, frames - 2, 0), (frames - 2, 1, 1), (frames - 1, 1, 2)):
        part = jnp.dot(
            row_patches(shifted, start, count, height),
            weights[:, first_tap * channels :],
            preferred_element_type=jnp.float32,
        )
        for t in range(start, start + count):
            rows = slice((t - start) * cells, (t - start + 1) * cells)
            for tap in range(first_tap, 3):
                piece = part[rows, (tap - first_tap) * channels : (tap - first_tap + 1) * channels]
                for target in range(frames):
                    if max(target + tap - 2, 0) == t:
                        branch[target] += piece


def backward_product(shifted, weights, branch, frames, height):
    cells, channels = branch.shape[1:]
    first, second, third, first_two, all_three = weights
    plan = (
        (2, frames - 2, ((first, -2), (second, -1), (third, 0))),
        (1, 1, ((third, 0), (first_two, -1))),
        (0, 1, ((all_three, 0),)),
    )
    for start, count, terms in plan:
        part = lax.dot_general(
            row_patches(shifted, start, count, height),
            jnp.concatenate([weight for weight, _ in terms], axis=0),
            (((1,), (1,)), ((), ())),
            preferred_element_type=jnp.float32,
        )
        for t in range(start, start + count):
            rows = slice((t - start) * cells, (t - start + 1) * cells)
            for column, (_, step) in enumerate(terms):
                branch[t + step] += part[rows, column * channels : (column + 1) * channels]


def first_body(place, *refs):
    blocks = refs[:4]
    shifted, base, result, table, branch = refs[4:]
    frames, height, flat, channels = base.shape
    section = place[0]
    unpack_weights(place, blocks, table)
    branch[...] = jnp.zeros_like(branch)

    @pl.when(section == 0)
    def _():
        forward_product(shifted, forward_weights(table, channels), branch, frames, height)
        for t in range(frames):
            total = base[t].astype(jnp.float32) + branch[t].reshape(height, flat, channels)
            result[t] = total.astype(jnp.bfloat16)

    @pl.when(section != 0)
    def _():
        backward_product(shifted, backward_weights(table, channels), branch, frames, height)
        for t in range(frames):
            result[t] = branch[t].reshape(height, flat, channels).astype(jnp.bfloat16)


def between_body(place, mine, upstream, slope, grads):
    frames = upstream.shape[0]

    @pl.when(place[0] == 0)
    def _():
        for t in range(frames):
            slope[t] = slope_of(mine[t].astype(jnp.float32))

    @pl.when(place[0] != 0)
    def _():
        move_grads(grads, lambda s: upstream[s].astype(jnp.float32))


def second_body(width, place, ready, slope, moved, other, upstream, *refs):
    own, blocks = refs[0], refs[1:5]
    turned, grads, terms = refs[5:]
    frames, height, flat, channels = upstream.shape
    rows = own.shape[0]
    section = place[0]
    cells = height * flat

    def product(left, right):
        for tap in range(3):
            count = frames - 2 + tap
            columns = jnp.concatenate(
                [
                    right[tap, :count, 2 - e : 2 - e + height].reshape(count * cells, channels)
                    for e in range(3)
                ],
                axis=1,
            )
            part = jnp.dot(left[:, : count * cells], columns, preferred_element_type=jnp.float32)
            for e in range(3):
                for k in range(3):
                    start = (tap * 9 + e * 3 + k) * channels
                    terms[start : start + channels, :] = part[
                        k * channels : (k + 1) * channels, e * channels : (e + 1) * channels
                    ]

    @pl.when(section == 0)
    def _():
        for t in range(frames):
            value = upstream[t].astype(jnp.float32) + slope[t] * other[t].astype(jnp.float32)
            grads[2, t, 1 : height + 1] = value.astype(jnp.bfloat16)
        move_grads(grads, lambda s: grads[2, s, 1 : height + 1].astype(jnp.float32))
        product(ready, grads)

    @pl.when(section != 0)
    def _():
        for t in range(frames):
            squashed = silu_of(other[t].astype(jnp.float32)).astype(jnp.bfloat16)
            for k, piece in enumerate(column_shifts(squashed.astype(jnp.float32), width)):
                turn_into(turned, k, t, piece)
        product(turned, moved)

    for second in range(4):
        for first in range(4):
            share = terms[shard_rows(place, rows, first, second), :]
            if first == 0 and second == 0:
                own[...] = share
            elif second == 0:
                blocks[0][first - 1] = share.astype(jnp.bfloat16)
            else:
                blocks[second][first] = share.astype(jnp.bfloat16)


def third_body(place, *refs):
    blocks = refs[:4]
    mine, other, produced, table, branch, shifted = refs[4:]
    micro, frames, height, width, channels = produced.shape
    flat = micro * width
    section = place[0]

    @pl.when(section == 0)
    def _():
        for t in range(frames):
            branch[t] = mine[t].astype(jnp.float32).reshape(height * flat, channels)

    @pl.when(section != 0)
    def _():
        unpack_weights(place, blocks, table)
        zero_row = jnp.zeros((3, frames, 1, flat, channels), jnp.bfloat16)
        shifted[:, :, :1] = zero_row
        shifted[:, :, height + 1 :] = zero_row
        for t in range(frames):
            value = other[t].astype(jnp.float32)
            branch[t] = value.reshape(height * flat, channels)
            squashed = silu_of(value).astype(jnp.bfloat16)
            for k, piece in enumerate(column_shifts(squashed.astype(jnp.float32), width)):
                shifted[k, t, 1 : height + 1] = piece
        forward_product(shifted, forward_weights(table, channels), branch, frames, height)

    for t in range(frames):
        cells = branch[t].reshape(height, flat, channels)
        for m in range(micro):
            produced[m, t] = cells[:, m * width : (m + 1) * width, :].astype(jnp.bfloat16)


def paired_sections(clips, cotangent, weights):
    dp_total = lax.axis_size("dp")
    local_clips, local_grads, shard = clips[:, 0], cotangent[:, 0], weights[0]
    micro, frames, height, width, channels = local_clips.shape
    rows = shard.shape[0]
    flat = micro * width
    cells = height * flat
    place = jnp.stack([lax.axis_index("section"), lax.axis_index("dp")]).astype(jnp.int32)

    def traded(block, along_z, step):
        bits = (step, 4 * step) if along_z else (4 * step, step)
        route = [
            (s * dp_total + i, s * dp_total + (i ^ bits[s])) for s in range(2) for i in range(dp_total)
        ]
        return lax.ppermute(block, ("section", "dp"), route)

    field = (frames, height, flat, channels)
    padded = (3, frames, height + 2, flat, channels)
    bf16, f32 = jnp.bfloat16, jnp.float32
    unit = 2 * micro * frames * height * width * channels * channels * 27

    first = [traded(shard, True, step) for step in range(1, 4)]
    (shard_copy,) = call(copy_body, (shard,), [(shard.shape, bf16)], [], unit // 16, place)
    shard_copy, first = lax.optimization_barrier((shard_copy, first))
    line = jnp.stack([shard_copy] + first)
    blocks = (line, *[traded(line, False, step) for step in range(1, 4)])

    turned = (3 * channels, frames * cells)
    shifted, base, upstream, ready = call(
        prepare_body,
        (local_clips, local_grads),
        [(padded, bf16), (field, bf16), (field, bf16), (turned, bf16)],
        [
            pltpu.VMEM(field, f32),
            pltpu.VMEM(local_clips.shape, bf16),
            pltpu.VMEM(local_clips.shape, bf16),
            pltpu.SemaphoreType.DMA((2,)),
        ],
        unit // 8,
        place,
        far=True,
    )
    table = pltpu.VMEM((dp_total * rows, channels), f32)
    branch = pltpu.VMEM((frames, cells, channels), f32)
    (mine,) = call(
        first_body, blocks + (shifted, base), [(field, bf16)], [table, branch], unit, place
    )
    other = lax.ppermute(mine, "section", [(0, 1), (1, 0)])
    slope, moved = call(
        between_body, (mine, upstream), [(field, f32), (padded, bf16)], [], unit // 8, place
    )
    slope, moved, other = lax.optimization_barrier((slope, moved, other))
    own, *terms = call(
        functools.partial(second_body, width),
        (ready, slope, moved, other, upstream),
        [((rows, channels), f32), ((3, rows, channels), bf16)] + [((4, rows, channels), bf16)] * 3,
        [
            pltpu.VMEM(turned, bf16),
            pltpu.VMEM(padded, bf16),
            table,
        ],
        unit,
        place,
    )
    (produced,) = call(
        third_body,
        blocks + (mine, other),
        [(local_clips.shape, bf16)],
        [table, branch, pltpu.VMEM(padded, bf16)],
        unit,
        place,
    )

    def added(*terms):
        return functools.reduce(lambda p, q: p + q, [term.astype(f32) for term in terms])

    received = [traded(terms[step], False, step) for step in (3, 2, 1)]
    received, produced = lax.optimization_barrier((received, produced))
    line_sum = added(terms[0], *[block[1:] for block in received]).astype(bf16)
    own_sum = added(own, *[block[0] for block in received])
    total = added(own_sum, *[traded(line_sum[step - 1], True, step) for step in range(1, 4)])
    return (produced[None, :, None], total[None])


def solution(mesh):
    dp_total = mesh.shape["dp"]
    paired = mesh.shape["section"] == 2 and dp_total == 16
    placed = (
        P(None, "dp", None, None, None, None),
        P(None, "dp", None, None, None, None),
        P("section", "dp", None),
    )
    return jax.shard_map(
        paired_sections if paired else many_sections,
        mesh=mesh,
        in_specs=placed,
        out_specs=(P("section", None, "dp", None, None, None, None), P("section", "dp", None)),
        check_vma=False,
    )
```

```python
import functools

import jax
import jax.numpy as jnp
from jax import lax
from jax.experimental import pallas as pl
from jax.experimental.pallas import tpu as pltpu
from jax.sharding import PartitionSpec as P


def passed_along(block, axis, distance):
    devices = range(lax.axis_size(axis))
    route = [(i - distance, i) for i in devices if i - distance in devices]
    return lax.ppermute(block, axis, route)


def gather_patches(field):
    frames, height, width, channels = field.shape
    first_frame = field[:1]
    padded = jnp.concatenate([first_frame, first_frame, field], axis=0)
    padded = jnp.pad(padded, ((0, 0), (1, 1), (1, 1), (0, 0)))
    pieces = [
        padded[
            offset_time : offset_time + frames,
            offset_row : offset_row + height,
            offset_col : offset_col + width,
        ]
        for offset_time in range(3)
        for offset_row in range(3)
        for offset_col in range(3)
    ]
    return jnp.stack(pieces, axis=3).reshape(frames * height * width, 27 * channels)


def squash_field(activation):
    return jax.nn.silu(activation.astype(jnp.float32)).astype(jnp.bfloat16)


def squash_columns(activation):
    return gather_patches(squash_field(activation))


def layer_forward(activation, weight):
    branch = jnp.dot(squash_columns(activation), weight, preferred_element_type=jnp.float32)
    return (activation.astype(jnp.float32) + branch.reshape(activation.shape)).astype(jnp.bfloat16)


def input_gradient(activation, upstream, weight):
    flat_grad = upstream.reshape(-1, weight.shape[1])
    column_grad = lax.dot_general(
        flat_grad, weight, (((1,), (1,)), ((), ())), preferred_element_type=jnp.float32
    )
    base = activation.astype(jnp.float32)
    _, unfold = jax.vjp(gather_patches, base)
    field_grad = unfold(column_grad)[0]
    sigmoid_value = jax.nn.sigmoid(base)
    slope = sigmoid_value * (1.0 + base * (1.0 - sigmoid_value))
    return (upstream.astype(jnp.float32) + field_grad * slope).astype(jnp.bfloat16)


def weight_term(activation, upstream):
    flat_grad = upstream.reshape(-1, upstream.shape[-1])
    return lax.dot_general(
        squash_columns(activation),
        flat_grad,
        (((0,), (0,)), ((), ())),
        preferred_element_type=jnp.float32,
    )


def many_sections(clips, cotangent, weights):
    section_total = lax.axis_size("section")
    section_index = lax.axis_index("section")
    weight = lax.all_gather(weights, "dp", axis=1, tiled=True)[0]
    local_clips = clips[:, 0]
    local_grads = cotangent[:, 0]
    micro_count = local_clips.shape[0]
    step_count = micro_count + section_total - 1
    empty_field = jnp.zeros(local_clips.shape[1:], jnp.bfloat16)

    def forward_step(step_index, carry):
        received, saved_inputs, produced = carry
        micro_index = step_index - section_index
        active = (micro_index >= 0) & (micro_index < micro_count)
        slot_index = jnp.clip(micro_index, 0, micro_count - 1)
        fresh = lax.dynamic_index_in_dim(local_clips, slot_index, 0, keepdims=False)
        layer_input = jnp.where(section_index == 0, fresh, received)
        layer_output = layer_forward(layer_input, weight)
        kept_input = jnp.where(
            active,
            layer_input,
            lax.dynamic_index_in_dim(saved_inputs, slot_index, 0, keepdims=False),
        )
        kept_output = jnp.where(
            active, layer_output, lax.dynamic_index_in_dim(produced, slot_index, 0, keepdims=False)
        )
        saved_inputs = lax.dynamic_update_index_in_dim(saved_inputs, kept_input, slot_index, 0)
        produced = lax.dynamic_update_index_in_dim(produced, kept_output, slot_index, 0)
        received = passed_along(layer_output, "section", 1)
        return (received, saved_inputs, produced)

    start_forward = (empty_field, jnp.zeros_like(local_clips), jnp.zeros_like(local_clips))
    _, saved_inputs, produced = lax.fori_loop(0, step_count, forward_step, start_forward)

    def backward_step(step_index, carry):
        received, grad_total, kept_grads = carry
        micro_index = step_index - (section_total - 1 - section_index)
        active = (micro_index >= 0) & (micro_index < micro_count)
        slot_index = jnp.clip(micro_index, 0, micro_count - 1)
        fresh = lax.dynamic_index_in_dim(local_grads, slot_index, 0, keepdims=False)
        upstream = jnp.where(section_index == section_total - 1, fresh, received)
        activation = lax.dynamic_index_in_dim(saved_inputs, slot_index, 0, keepdims=False)
        grad_total = grad_total + jnp.where(active, weight_term(activation, upstream), 0.0)
        layer_grad = input_gradient(activation, upstream, weight)
        received = passed_along(layer_grad, "section", -1)
        return (received, grad_total, kept_grads)

    start_backward = (
        empty_field,
        jnp.zeros(weight.shape, jnp.float32),
        jnp.zeros_like(local_grads),
    )
    _, grad_total, kept_grads = lax.fori_loop(0, step_count, backward_step, start_backward)
    grad_share = lax.psum_scatter(
        grad_total.astype(jnp.bfloat16), "dp", scatter_dimension=0, tiled=True
    ).astype(jnp.float32)
    return (produced[None, :, None], grad_share[None])


def silu_of(value):
    return value * jax.nn.sigmoid(value)


def slope_of(value):
    sigmoid_value = jax.nn.sigmoid(value)
    return sigmoid_value * (1.0 + value * (1.0 - sigmoid_value))


def column_shifts(rows, width):
    height, flat, channels = rows.shape
    cells = rows.reshape(height * flat // width, width, channels)
    column = lax.broadcasted_iota(jnp.int32, cells.shape, 1)
    before = jnp.where(column == 0, 0.0, pltpu.roll(cells, 1, 1))
    after = jnp.where(column == width - 1, 0.0, pltpu.roll(cells, width - 1, 1))
    return [piece.reshape(rows.shape).astype(jnp.bfloat16) for piece in (before, cells, after)]


def whole(count):
    return [pl.BlockSpec(memory_space=pltpu.VMEM)] * count


def call(body, inputs, outputs, scratch, flops, place, far=False):
    return pl.pallas_call(
        body,
        out_shape=[jax.ShapeDtypeStruct(shape, dtype) for shape, dtype in outputs],
        in_specs=[pl.BlockSpec(memory_space=pltpu.SMEM)]
        + ([pl.BlockSpec(memory_space=pl.ANY)] * len(inputs) if far else whole(len(inputs))),
        out_specs=whole(len(outputs)),
        scratch_shapes=scratch,
        compiler_params=pltpu.CompilerParams(vmem_limit_bytes=32 * 1024 * 1024),
        cost_estimate=pl.CostEstimate(flops=flops, bytes_accessed=4_000_000, transcendentals=0),
    )(place, *inputs)


def turn_into(turned, k, t, piece):
    channels = piece.shape[-1]
    flat = piece.reshape(-1, channels)
    cells = flat.shape[0]
    turned[k * channels : (k + 1) * channels, t * cells : (t + 1) * cells] = flat.T


def move_grads(grads, field):
    _, frames, padded_height, flat, channels = grads.shape
    height = padded_height - 2
    zero_row = jnp.zeros((3, frames, 1, flat, channels), jnp.bfloat16)
    grads[:, :, :1] = zero_row
    grads[:, :, height + 1 :] = zero_row
    for t in range(frames):
        for tap in range(3):
            sources = [s for s in range(frames) if max(s + tap - 2, 0) == t]
            if sources:
                total = functools.reduce(lambda p, q: p + q, [field(s) for s in sources])
                grads[tap, t, 1 : height + 1] = total.astype(jnp.bfloat16)


def copy_body(place, source, target):
    target[...] = source[...]


def prepare_body(place, clips_far, cotangent_far, *refs):
    shifted, base, upstream, ready, held, clips, cotangent, sems = refs
    micro, frames, height, width, channels = clips.shape
    section = place[0]
    copies = [
        pltpu.make_async_copy(source, target, sems.at[k])
        for k, (source, target) in enumerate(
            ((clips_far, clips), (cotangent_far, cotangent))
        )
    ]
    for copy in copies:
        copy.start()

    def reorder(source, target):
        for m in range(micro):
            held[:, :, m * width : (m + 1) * width, :] = source[m].astype(jnp.float32)
        for t in range(frames):
            target[t] = held[t].astype(jnp.bfloat16)

    zero_row = jnp.zeros((3, frames, 1) + shifted.shape[3:], jnp.bfloat16)
    shifted[:, :, :1] = zero_row
    shifted[:, :, height + 1 :] = zero_row
    copies[0].wait()
    reorder(clips, base)
    copies[1].wait()
    reorder(cotangent, upstream)

    @pl.when(section == 0)
    def _():
        for t in range(frames):
            squashed = silu_of(base[t].astype(jnp.float32)).astype(jnp.bfloat16)
            for k, piece in enumerate(column_shifts(squashed.astype(jnp.float32), width)):
                shifted[k, t, 1 : height + 1] = piece
                turn_into(ready, k, t, piece)

    @pl.when(section != 0)
    def _():
        for t in range(frames):
            for k, piece in enumerate(column_shifts(upstream[t].astype(jnp.float32), width)):
                shifted[k, t, 1 : height + 1] = piece


def shard_rows(place, rows, first, second):
    far, near = jnp.where(place[0] == 0, first, second), jnp.where(place[0] == 0, second, first)
    return pl.ds(pl.multiple_of((place[1] ^ (4 * far + near)) * rows, 8), rows)


def unpack_weights(place, blocks, table):
    rows = blocks[0].shape[1]
    for second in range(4):
        for first in range(4):
            shard = blocks[second][first]
            table[shard_rows(place, rows, first, second), :] = shard.astype(jnp.float32)


def forward_weights(table, channels):
    rows = 9 * channels
    return jnp.concatenate(
        [table[t * rows : (t + 1) * rows, :].astype(jnp.bfloat16) for t in range(3)], axis=1
    )


def backward_weights(table, channels):
    def turned_taps(times):
        blocks = []
        for k in reversed(range(9)):
            rows = [table[(t * 9 + k) * channels : (t * 9 + k + 1) * channels, :] for t in times]
            blocks.append(functools.reduce(lambda p, q: p + q, rows).astype(jnp.bfloat16))
        return jnp.concatenate(blocks, axis=1)

    return [turned_taps(times) for times in ((0,), (1,), (2,), (0, 1), (0, 1, 2))]


def row_patches(shifted, start, count, height):
    flat, channels = shifted.shape[3:]
    return jnp.concatenate(
        [
            shifted[k, start : start + count, e : e + height].reshape(count * height * flat, channels)
            for e in range(3)
            for k in range(3)
        ],
        axis=1,
    )


def forward_product(shifted, weights, branch, frames, height):
    cells, channels = branch.shape[1:]
    for start, count, first_tap in ((0, frames - 2, 0), (frames - 2, 1, 1), (frames - 1, 1, 2)):
        part = jnp.dot(
            row_patches(shifted, start, count, height),
            weights[:, first_tap * channels :],
            preferred_element_type=jnp.float32,
        )
        for t in range(start, start + count):
            rows = slice((t - start) * cells, (t - start + 1) * cells)
            for tap in range(first_tap, 3):
                piece = part[rows, (tap - first_tap) * channels : (tap - first_tap + 1) * channels]
                for target in range(frames):
                    if max(target + tap - 2, 0) == t:
                        branch[target] += piece


def backward_product(shifted, weights, branch, frames, height):
    cells, channels = branch.shape[1:]
    first, second, third, first_two, all_three = weights
    plan = (
        (2, frames - 2, ((first, -2), (second, -1), (third, 0))),
        (1, 1, ((third, 0), (first_two, -1))),
        (0, 1, ((all_three, 0),)),
    )
    for start, count, terms in plan:
        part = lax.dot_general(
            row_patches(shifted, start, count, height),
            jnp.concatenate([weight for weight, _ in terms], axis=0),
            (((1,), (1,)), ((), ())),
            preferred_element_type=jnp.float32,
        )
        for t in range(start, start + count):
            rows = slice((t - start) * cells, (t - start + 1) * cells)
            for column, (_, step) in enumerate(terms):
                branch[t + step] += part[rows, column * channels : (column + 1) * channels]


def first_body(place, *refs):
    blocks = refs[:4]
    shifted, base, result, table, branch = refs[4:]
    frames, height, flat, channels = base.shape
    section = place[0]
    unpack_weights(place, blocks, table)
    branch[...] = jnp.zeros_like(branch)

    @pl.when(section == 0)
    def _():
        forward_product(shifted, forward_weights(table, channels), branch, frames, height)
        for t in range(frames):
            total = base[t].astype(jnp.float32) + branch[t].reshape(height, flat, channels)
            result[t] = total.astype(jnp.bfloat16)

    @pl.when(section != 0)
    def _():
        backward_product(shifted, backward_weights(table, channels), branch, frames, height)
        for t in range(frames):
            result[t] = branch[t].reshape(height, flat, channels).astype(jnp.bfloat16)


def between_body(place, mine, upstream, slope, grads):
    frames = upstream.shape[0]

    @pl.when(place[0] == 0)
    def _():
        for t in range(frames):
            slope[t] = slope_of(mine[t].astype(jnp.float32))

    @pl.when(place[0] != 0)
    def _():
        move_grads(grads, lambda s: upstream[s].astype(jnp.float32))


def second_body(width, place, ready, slope, moved, other, upstream, *refs):
    own, blocks = refs[0], refs[1:5]
    turned, grads, terms = refs[5:]
    frames, height, flat, channels = upstream.shape
    rows = own.shape[0]
    section = place[0]
    cells = height * flat

    def product(left, right):
        for tap in range(3):
            count = frames - 2 + tap
            columns = jnp.concatenate(
                [
                    right[tap, :count, 2 - e : 2 - e + height].reshape(count * cells, channels)
                    for e in range(3)
                ],
                axis=1,
            )
            part = jnp.dot(left[:, : count * cells], columns, preferred_element_type=jnp.float32)
            for e in range(3):
                for k in range(3):
                    start = (tap * 9 + e * 3 + k) * channels
                    terms[start : start + channels, :] = part[
                        k * channels : (k + 1) * channels, e * channels : (e + 1) * channels
                    ]

    @pl.when(section == 0)
    def _():
        for t in range(frames):
            value = upstream[t].astype(jnp.float32) + slope[t] * other[t].astype(jnp.float32)
            grads[2, t, 1 : height + 1] = value.astype(jnp.bfloat16)
        move_grads(grads, lambda s: grads[2, s, 1 : height + 1].astype(jnp.float32))
        product(ready, grads)

    @pl.when(section != 0)
    def _():
        for t in range(frames):
            squashed = silu_of(other[t].astype(jnp.float32)).astype(jnp.bfloat16)
            for k, piece in enumerate(column_shifts(squashed.astype(jnp.float32), width)):
                turn_into(turned, k, t, piece)
        product(turned, moved)

    for second in range(4):
        for first in range(4):
            share = terms[shard_rows(place, rows, first, second), :]
            if first == 0 and second == 0:
                own[...] = share
            elif second == 0:
                blocks[0][first - 1] = share.astype(jnp.bfloat16)
            else:
                blocks[second][first] = share.astype(jnp.bfloat16)


def third_body(place, *refs):
    blocks = refs[:4]
    mine, other, produced, table, branch, shifted = refs[4:]
    micro, frames, height, width, channels = produced.shape
    flat = micro * width
    section = place[0]

    @pl.when(section == 0)
    def _():
        for t in range(frames):
            branch[t] = mine[t].astype(jnp.float32).reshape(height * flat, channels)

    @pl.when(section != 0)
    def _():
        unpack_weights(place, blocks, table)
        zero_row = jnp.zeros((3, frames, 1, flat, channels), jnp.bfloat16)
        shifted[:, :, :1] = zero_row
        shifted[:, :, height + 1 :] = zero_row
        for t in range(frames):
            value = other[t].astype(jnp.float32)
            branch[t] = value.reshape(height * flat, channels)
            squashed = silu_of(value).astype(jnp.bfloat16)
            for k, piece in enumerate(column_shifts(squashed.astype(jnp.float32), width)):
                shifted[k, t, 1 : height + 1] = piece
        forward_product(shifted, forward_weights(table, channels), branch, frames, height)

    for t in range(frames):
        cells = branch[t].reshape(height, flat, channels)
        for m in range(micro):
            produced[m, t] = cells[:, m * width : (m + 1) * width, :].astype(jnp.bfloat16)


def paired_sections(clips, cotangent, weights):
    dp_total = lax.axis_size("dp")
    local_clips, local_grads, shard = clips[:, 0], cotangent[:, 0], weights[0]
    micro, frames, height, width, channels = local_clips.shape
    rows = shard.shape[0]
    flat = micro * width
    cells = height * flat
    place = jnp.stack([lax.axis_index("section"), lax.axis_index("dp")]).astype(jnp.int32)

    def traded(block, along_z, step):
        bits = (4 * step, step) if along_z else (step, 4 * step)
        route = [
            (s * dp_total + i, s * dp_total + (i ^ bits[s])) for s in range(2) for i in range(dp_total)
        ]
        return lax.ppermute(block, ("section", "dp"), route)

    field = (frames, height, flat, channels)
    padded = (3, frames, height + 2, flat, channels)
    bf16, f32 = jnp.bfloat16, jnp.float32
    unit = 2 * micro * frames * height * width * channels * channels * 27

    first = [traded(shard, True, step) for step in range(1, 4)]
    (shard_copy,) = call(copy_body, (shard,), [(shard.shape, bf16)], [], unit // 16, place)
    shard_copy, first = lax.optimization_barrier((shard_copy, first))
    line = jnp.stack([shard_copy] + first)
    blocks = (line, *[traded(line, False, step) for step in range(1, 4)])

    turned = (3 * channels, frames * cells)
    shifted, base, upstream, ready = call(
        prepare_body,
        (local_clips, local_grads),
        [(padded, bf16), (field, bf16), (field, bf16), (turned, bf16)],
        [
            pltpu.VMEM(field, f32),
            pltpu.VMEM(local_clips.shape, bf16),
            pltpu.VMEM(local_clips.shape, bf16),
            pltpu.SemaphoreType.DMA((2,)),
        ],
        unit // 8,
        place,
        far=True,
    )
    table = pltpu.VMEM((dp_total * rows, channels), f32)
    branch = pltpu.VMEM((frames, cells, channels), f32)
    (mine,) = call(
        first_body, blocks + (shifted, base), [(field, bf16)], [table, branch], unit, place
    )
    other = lax.ppermute(mine, "section", [(0, 1), (1, 0)])
    slope, moved = call(
        between_body, (mine, upstream), [(field, f32), (padded, bf16)], [], unit // 8, place
    )
    slope, moved, other = lax.optimization_barrier((slope, moved, other))
    own, *terms = call(
        functools.partial(second_body, width),
        (ready, slope, moved, other, upstream),
        [((rows, channels), f32), ((3, rows, channels), bf16)] + [((4, rows, channels), bf16)] * 3,
        [
            pltpu.VMEM(turned, bf16),
            pltpu.VMEM(padded, bf16),
            table,
        ],
        unit,
        place,
    )
    (produced,) = call(
        third_body,
        blocks + (mine, other),
        [(local_clips.shape, bf16)],
        [table, branch, pltpu.VMEM(padded, bf16)],
        unit,
        place,
    )

    def added(*terms):
        return functools.reduce(lambda p, q: p + q, [term.astype(f32) for term in terms])

    received = [traded(terms[step], False, step) for step in (3, 2, 1)]
    received, produced = lax.optimization_barrier((received, produced))
    line_sum = added(terms[0], *[block[1:] for block in received]).astype(bf16)
    own_sum = added(own, *[block[0] for block in received])
    total = added(own_sum, *[traded(line_sum[step - 1], True, step) for step in range(1, 4)])
    return (produced[None, :, None], total[None])


def solution(mesh):
    dp_total = mesh.shape["dp"]
    paired = mesh.shape["section"] == 2 and dp_total == 16
    placed = (
        P(None, "dp", None, None, None, None),
        P(None, "dp", None, None, None, None),
        P("section", "dp", None),
    )
    return jax.shard_map(
        paired_sections if paired else many_sections,
        mesh=mesh,
        in_specs=placed,
        out_specs=(P("section", None, "dp", None, None, None, None), P("section", "dp", None)),
        check_vma=False,
    )
```

```python
import functools

import jax
import jax.numpy as jnp
from jax import lax
from jax.experimental import pallas as pl
from jax.experimental.pallas import tpu as pltpu
from jax.sharding import PartitionSpec as P


def passed_along(block, axis, distance):
    devices = range(lax.axis_size(axis))
    route = [(i - distance, i) for i in devices if i - distance in devices]
    return lax.ppermute(block, axis, route)


def gather_patches(field):
    frames, height, width, channels = field.shape
    first_frame = field[:1]
    padded = jnp.concatenate([first_frame, first_frame, field], axis=0)
    padded = jnp.pad(padded, ((0, 0), (1, 1), (1, 1), (0, 0)))
    pieces = [
        padded[
            offset_time : offset_time + frames,
            offset_row : offset_row + height,
            offset_col : offset_col + width,
        ]
        for offset_time in range(3)
        for offset_row in range(3)
        for offset_col in range(3)
    ]
    return jnp.stack(pieces, axis=3).reshape(frames * height * width, 27 * channels)


def squash_field(activation):
    return jax.nn.silu(activation.astype(jnp.float32)).astype(jnp.bfloat16)


def squash_columns(activation):
    return gather_patches(squash_field(activation))


def layer_forward(activation, weight):
    branch = jnp.dot(squash_columns(activation), weight, preferred_element_type=jnp.float32)
    return (activation.astype(jnp.float32) + branch.reshape(activation.shape)).astype(jnp.bfloat16)


def input_gradient(activation, upstream, weight):
    flat_grad = upstream.reshape(-1, weight.shape[1])
    column_grad = lax.dot_general(
        flat_grad, weight, (((1,), (1,)), ((), ())), preferred_element_type=jnp.float32
    )
    base = activation.astype(jnp.float32)
    _, unfold = jax.vjp(gather_patches, base)
    field_grad = unfold(column_grad)[0]
    sigmoid_value = jax.nn.sigmoid(base)
    slope = sigmoid_value * (1.0 + base * (1.0 - sigmoid_value))
    return (upstream.astype(jnp.float32) + field_grad * slope).astype(jnp.bfloat16)


def weight_term(activation, upstream):
    flat_grad = upstream.reshape(-1, upstream.shape[-1])
    return lax.dot_general(
        squash_columns(activation),
        flat_grad,
        (((0,), (0,)), ((), ())),
        preferred_element_type=jnp.float32,
    )


def many_sections(clips, cotangent, weights):
    section_total = lax.axis_size("section")
    section_index = lax.axis_index("section")
    weight = lax.all_gather(weights, "dp", axis=1, tiled=True)[0]
    local_clips = clips[:, 0]
    local_grads = cotangent[:, 0]
    micro_count = local_clips.shape[0]
    step_count = micro_count + section_total - 1
    empty_field = jnp.zeros(local_clips.shape[1:], jnp.bfloat16)

    def forward_step(step_index, carry):
        received, saved_inputs, produced = carry
        micro_index = step_index - section_index
        active = (micro_index >= 0) & (micro_index < micro_count)
        slot_index = jnp.clip(micro_index, 0, micro_count - 1)
        fresh = lax.dynamic_index_in_dim(local_clips, slot_index, 0, keepdims=False)
        layer_input = jnp.where(section_index == 0, fresh, received)
        layer_output = layer_forward(layer_input, weight)
        kept_input = jnp.where(
            active,
            layer_input,
            lax.dynamic_index_in_dim(saved_inputs, slot_index, 0, keepdims=False),
        )
        kept_output = jnp.where(
            active, layer_output, lax.dynamic_index_in_dim(produced, slot_index, 0, keepdims=False)
        )
        saved_inputs = lax.dynamic_update_index_in_dim(saved_inputs, kept_input, slot_index, 0)
        produced = lax.dynamic_update_index_in_dim(produced, kept_output, slot_index, 0)
        received = passed_along(layer_output, "section", 1)
        return (received, saved_inputs, produced)

    start_forward = (empty_field, jnp.zeros_like(local_clips), jnp.zeros_like(local_clips))
    _, saved_inputs, produced = lax.fori_loop(0, step_count, forward_step, start_forward)

    def backward_step(step_index, carry):
        received, grad_total, kept_grads = carry
        micro_index = step_index - (section_total - 1 - section_index)
        active = (micro_index >= 0) & (micro_index < micro_count)
        slot_index = jnp.clip(micro_index, 0, micro_count - 1)
        fresh = lax.dynamic_index_in_dim(local_grads, slot_index, 0, keepdims=False)
        upstream = jnp.where(section_index == section_total - 1, fresh, received)
        activation = lax.dynamic_index_in_dim(saved_inputs, slot_index, 0, keepdims=False)
        grad_total = grad_total + jnp.where(active, weight_term(activation, upstream), 0.0)
        layer_grad = input_gradient(activation, upstream, weight)
        received = passed_along(layer_grad, "section", -1)
        return (received, grad_total, kept_grads)

    start_backward = (
        empty_field,
        jnp.zeros(weight.shape, jnp.float32),
        jnp.zeros_like(local_grads),
    )
    _, grad_total, kept_grads = lax.fori_loop(0, step_count, backward_step, start_backward)
    grad_share = lax.psum_scatter(
        grad_total.astype(jnp.bfloat16), "dp", scatter_dimension=0, tiled=True
    ).astype(jnp.float32)
    return (produced[None, :, None], grad_share[None])


def silu_of(value):
    return value * jax.nn.sigmoid(value)


def slope_of(value):
    sigmoid_value = jax.nn.sigmoid(value)
    return sigmoid_value * (1.0 + value * (1.0 - sigmoid_value))


def column_shifts(rows, width):
    height, flat, channels = rows.shape
    cells = rows.reshape(height * flat // width, width, channels)
    column = lax.broadcasted_iota(jnp.int32, cells.shape, 1)
    before = jnp.where(column == 0, 0.0, pltpu.roll(cells, 1, 1))
    after = jnp.where(column == width - 1, 0.0, pltpu.roll(cells, width - 1, 1))
    return [piece.reshape(rows.shape).astype(jnp.bfloat16) for piece in (before, cells, after)]


def whole(count):
    return [pl.BlockSpec(memory_space=pltpu.VMEM)] * count


def call(body, inputs, outputs, scratch, flops, place, far=False):
    return pl.pallas_call(
        body,
        out_shape=[jax.ShapeDtypeStruct(shape, dtype) for shape, dtype in outputs],
        in_specs=[pl.BlockSpec(memory_space=pltpu.SMEM)]
        + ([pl.BlockSpec(memory_space=pl.ANY)] * len(inputs) if far else whole(len(inputs))),
        out_specs=whole(len(outputs)),
        scratch_shapes=scratch,
        compiler_params=pltpu.CompilerParams(vmem_limit_bytes=32 * 1024 * 1024),
        cost_estimate=pl.CostEstimate(flops=flops, bytes_accessed=4_000_000, transcendentals=0),
    )(place, *inputs)


def turn_into(turned, k, t, piece):
    channels = piece.shape[-1]
    flat = piece.reshape(-1, channels)
    cells = flat.shape[0]
    turned[k * channels : (k + 1) * channels, t * cells : (t + 1) * cells] = flat.T


def move_grads(grads, field):
    _, frames, padded_height, flat, channels = grads.shape
    height = padded_height - 2
    zero_row = jnp.zeros((3, frames, 1, flat, channels), jnp.bfloat16)
    grads[:, :, :1] = zero_row
    grads[:, :, height + 1 :] = zero_row
    for t in range(frames):
        for tap in range(3):
            sources = [s for s in range(frames) if max(s + tap - 2, 0) == t]
            if sources:
                total = functools.reduce(lambda p, q: p + q, [field(s) for s in sources])
                grads[tap, t, 1 : height + 1] = total.astype(jnp.bfloat16)


def copy_body(place, source, target):
    target[...] = source[...]


def prepare_body(place, clips_far, cotangent_far, *refs):
    shifted, base, upstream, ready, held, clips, cotangent, sems = refs
    micro, frames, height, width, channels = clips.shape
    section = place[0]
    copies = [
        pltpu.make_async_copy(source, target, sems.at[k])
        for k, (source, target) in enumerate(
            ((clips_far, clips), (cotangent_far, cotangent))
        )
    ]
    for copy in copies:
        copy.start()

    def reorder(source, target):
        for m in range(micro):
            held[:, :, m * width : (m + 1) * width, :] = source[m].astype(jnp.float32)
        for t in range(frames):
            target[t] = held[t].astype(jnp.bfloat16)

    zero_row = jnp.zeros((3, frames, 1) + shifted.shape[3:], jnp.bfloat16)
    shifted[:, :, :1] = zero_row
    shifted[:, :, height + 1 :] = zero_row
    copies[0].wait()
    reorder(clips, base)
    copies[1].wait()
    reorder(cotangent, upstream)

    @pl.when(section == 0)
    def _():
        for t in range(frames):
            squashed = silu_of(base[t].astype(jnp.float32)).astype(jnp.bfloat16)
            for k, piece in enumerate(column_shifts(squashed.astype(jnp.float32), width)):
                shifted[k, t, 1 : height + 1] = piece
                turn_into(ready, k, t, piece)

    @pl.when(section != 0)
    def _():
        for t in range(frames):
            for k, piece in enumerate(column_shifts(upstream[t].astype(jnp.float32), width)):
                shifted[k, t, 1 : height + 1] = piece


GATHERED = ((0, 3, 2, 1), (0, 2, 1, 3))
SUMMED = ((0, 3, 2, 1), (0, 3, 1, 2))


def shard_rows(place, rows, first, seconds):
    far, near = jnp.where(place[0] == 0, first, seconds[1]), jnp.where(place[0] == 0, seconds[0], first)
    return pl.ds(pl.multiple_of((place[1] ^ (4 * far + near)) * rows, 8), rows)


def unpack_weights(place, blocks, table):
    rows = blocks[0].shape[1]
    for block, *seconds in zip(blocks, *GATHERED):
        for first in range(4):
            table[shard_rows(place, rows, first, seconds), :] = block[first].astype(jnp.float32)


def forward_weights(table, channels):
    rows = 9 * channels
    return jnp.concatenate(
        [table[t * rows : (t + 1) * rows, :].astype(jnp.bfloat16) for t in range(3)], axis=1
    )


def backward_weights(table, channels):
    def turned_taps(times):
        blocks = []
        for k in reversed(range(9)):
            rows = [table[(t * 9 + k) * channels : (t * 9 + k + 1) * channels, :] for t in times]
            blocks.append(functools.reduce(lambda p, q: p + q, rows).astype(jnp.bfloat16))
        return jnp.concatenate(blocks, axis=1)

    return [turned_taps(times) for times in ((0,), (1,), (2,), (0, 1), (0, 1, 2))]


def row_patches(shifted, start, count, height):
    flat, channels = shifted.shape[3:]
    return jnp.concatenate(
        [
            shifted[k, start : start + count, e : e + height].reshape(count * height * flat, channels)
            for e in range(3)
            for k in range(3)
        ],
        axis=1,
    )


def forward_product(shifted, weights, branch, frames, height):
    cells, channels = branch.shape[1:]
    for start, count, first_tap in ((0, frames - 2, 0), (frames - 2, 1, 1), (frames - 1, 1, 2)):
        part = jnp.dot(
            row_patches(shifted, start, count, height),
            weights[:, first_tap * channels :],
            preferred_element_type=jnp.float32,
        )
        for t in range(start, start + count):
            rows = slice((t - start) * cells, (t - start + 1) * cells)
            for tap in range(first_tap, 3):
                piece = part[rows, (tap - first_tap) * channels : (tap - first_tap + 1) * channels]
                for target in range(frames):
                    if max(target + tap - 2, 0) == t:
                        branch[target] += piece


def backward_product(shifted, weights, branch, frames, height):
    cells, channels = branch.shape[1:]
    first, second, third, first_two, all_three = weights
    plan = (
        (2, frames - 2, ((first, -2), (second, -1), (third, 0))),
        (1, 1, ((third, 0), (first_two, -1))),
        (0, 1, ((all_three, 0),)),
    )
    for start, count, terms in plan:
        part = lax.dot_general(
            row_patches(shifted, start, count, height),
            jnp.concatenate([weight for weight, _ in terms], axis=0),
            (((1,), (1,)), ((), ())),
            preferred_element_type=jnp.float32,
        )
        for t in range(start, start + count):
            rows = slice((t - start) * cells, (t - start + 1) * cells)
            for column, (_, step) in enumerate(terms):
                branch[t + step] += part[rows, column * channels : (column + 1) * channels]


def first_body(place, *refs):
    blocks = refs[:4]
    shifted, base, result, table, branch = refs[4:]
    frames, height, flat, channels = base.shape
    section = place[0]
    unpack_weights(place, blocks, table)
    branch[...] = jnp.zeros_like(branch)

    @pl.when(section == 0)
    def _():
        forward_product(shifted, forward_weights(table, channels), branch, frames, height)
        for t in range(frames):
            total = base[t].astype(jnp.float32) + branch[t].reshape(height, flat, channels)
            result[t] = total.astype(jnp.bfloat16)

    @pl.when(section != 0)
    def _():
        backward_product(shifted, backward_weights(table, channels), branch, frames, height)
        for t in range(frames):
            result[t] = branch[t].reshape(height, flat, channels).astype(jnp.bfloat16)


def between_body(place, mine, upstream, slope, grads):
    frames = upstream.shape[0]

    @pl.when(place[0] == 0)
    def _():
        for t in range(frames):
            slope[t] = slope_of(mine[t].astype(jnp.float32))

    @pl.when(place[0] != 0)
    def _():
        move_grads(grads, lambda s: upstream[s].astype(jnp.float32))


def second_body(width, place, ready, slope, moved, other, upstream, *refs):
    own, blocks = refs[0], refs[1:5]
    turned, grads, terms = refs[5:]
    frames, height, flat, channels = upstream.shape
    rows = own.shape[0]
    section = place[0]
    cells = height * flat

    def product(left, right):
        for tap in range(3):
            count = frames - 2 + tap
            columns = jnp.concatenate(
                [
                    right[tap, :count, 2 - e : 2 - e + height].reshape(count * cells, channels)
                    for e in range(3)
                ],
                axis=1,
            )
            part = jnp.dot(left[:, : count * cells], columns, preferred_element_type=jnp.float32)
            for e in range(3):
                for k in range(3):
                    start = (tap * 9 + e * 3 + k) * channels
                    terms[start : start + channels, :] = part[
                        k * channels : (k + 1) * channels, e * channels : (e + 1) * channels
                    ]

    @pl.when(section == 0)
    def _():
        for t in range(frames):
            value = upstream[t].astype(jnp.float32) + slope[t] * other[t].astype(jnp.float32)
            grads[2, t, 1 : height + 1] = value.astype(jnp.bfloat16)
        move_grads(grads, lambda s: grads[2, s, 1 : height + 1].astype(jnp.float32))
        product(ready, grads)

    @pl.when(section != 0)
    def _():
        for t in range(frames):
            squashed = silu_of(other[t].astype(jnp.float32)).astype(jnp.bfloat16)
            for k, piece in enumerate(column_shifts(squashed.astype(jnp.float32), width)):
                turn_into(turned, k, t, piece)
        product(turned, moved)

    for block, *seconds in zip(blocks, *SUMMED):
        for first in range(4):
            share = terms[shard_rows(place, rows, first, seconds), :]
            if seconds[0]:
                block[first] = share.astype(jnp.bfloat16)
            elif first:
                block[first - 1] = share.astype(jnp.bfloat16)
            else:
                own[...] = share


def third_body(place, *refs):
    blocks = refs[:4]
    mine, other, produced, table, branch, shifted = refs[4:]
    micro, frames, height, width, channels = produced.shape
    flat = micro * width
    section = place[0]

    @pl.when(section == 0)
    def _():
        for t in range(frames):
            branch[t] = mine[t].astype(jnp.float32).reshape(height * flat, channels)

    @pl.when(section != 0)
    def _():
        unpack_weights(place, blocks, table)
        zero_row = jnp.zeros((3, frames, 1, flat, channels), jnp.bfloat16)
        shifted[:, :, :1] = zero_row
        shifted[:, :, height + 1 :] = zero_row
        for t in range(frames):
            value = other[t].astype(jnp.float32)
            branch[t] = value.reshape(height * flat, channels)
            squashed = silu_of(value).astype(jnp.bfloat16)
            for k, piece in enumerate(column_shifts(squashed.astype(jnp.float32), width)):
                shifted[k, t, 1 : height + 1] = piece
        forward_product(shifted, forward_weights(table, channels), branch, frames, height)

    for t in range(frames):
        cells = branch[t].reshape(height, flat, channels)
        for m in range(micro):
            produced[m, t] = cells[:, m * width : (m + 1) * width, :].astype(jnp.bfloat16)


def paired_sections(clips, cotangent, weights):
    dp_total = lax.axis_size("dp")
    local_clips, local_grads, shard = clips[:, 0], cotangent[:, 0], weights[0]
    micro, frames, height, width, channels = local_clips.shape
    rows = shard.shape[0]
    flat = micro * width
    cells = height * flat
    place = jnp.stack([lax.axis_index("section"), lax.axis_index("dp")]).astype(jnp.int32)

    in_plane_first = place[0] != 0

    def traded(block, bits):
        route = [
            (s * dp_total + i, s * dp_total + (i ^ bits[s])) for s in range(2) for i in range(dp_total)
        ]
        return lax.ppermute(block, ("section", "dp"), route)

    field = (frames, height, flat, channels)
    padded = (3, frames, height + 2, flat, channels)
    bf16, f32 = jnp.bfloat16, jnp.float32
    unit = 2 * micro * frames * height * width * channels * channels * 27

    first = [traded(shard, (4 * step, step)) for step in range(1, 4)]
    (shard_copy,) = call(copy_body, (shard,), [(shard.shape, bf16)], [], unit // 16, place)
    shard_copy, first = lax.optimization_barrier((shard_copy, first))
    line = jnp.stack([shard_copy] + first)
    second = traded(line, (3, 8))
    third = traded(line, (2, 4))
    second, third_line, local_clips, local_grads = lax.optimization_barrier(
        (second, line, local_clips, local_grads)
    )
    fourth = traded(jnp.where(in_plane_first, second, third_line), (1, 4))
    blocks = (line, second, third, fourth)

    turned = (3 * channels, frames * cells)
    shifted, base, upstream, ready = call(
        prepare_body,
        (local_clips, local_grads),
        [(padded, bf16), (field, bf16), (field, bf16), (turned, bf16)],
        [
            pltpu.VMEM(field, f32),
            pltpu.VMEM(local_clips.shape, bf16),
            pltpu.VMEM(local_clips.shape, bf16),
            pltpu.SemaphoreType.DMA((2,)),
        ],
        unit // 8,
        place,
        far=True,
    )
    table = pltpu.VMEM((dp_total * rows, channels), f32)
    branch = pltpu.VMEM((frames, cells, channels), f32)
    (mine,) = call(
        first_body, blocks + (shifted, base), [(field, bf16)], [table, branch], unit, place
    )
    other = lax.ppermute(mine, "section", [(0, 1), (1, 0)])
    slope, moved = call(
        between_body, (mine, upstream), [(field, f32), (padded, bf16)], [], unit // 8, place
    )
    slope, moved, other = lax.optimization_barrier((slope, moved, other))
    own, *terms = call(
        functools.partial(second_body, width),
        (ready, slope, moved, other, upstream),
        [((rows, channels), f32), ((3, rows, channels), bf16)] + [((4, rows, channels), bf16)] * 3,
        [
            pltpu.VMEM(turned, bf16),
            pltpu.VMEM(padded, bf16),
            table,
        ],
        unit,
        place,
    )
    def added(*terms):
        return functools.reduce(lambda p, q: p + q, [term.astype(f32) for term in terms])

    across = traded(terms[1], (3, 4))
    beside = traded(terms[2], (2, 4))
    handed_on = jnp.where(in_plane_first, added(terms[3], across).astype(bf16), terms[3])
    handed_on, late_other = lax.optimization_barrier((handed_on, other))
    (produced,) = call(
        third_body,
        blocks + (mine, late_other),
        [(local_clips.shape, bf16)],
        [table, branch, pltpu.VMEM(padded, bf16)],
        unit,
        place,
    )
    last = traded(handed_on, (1, 8))
    last, produced = lax.optimization_barrier((last, produced))
    across = jnp.where(in_plane_first, 0.0, across.astype(f32))
    line_sum = added(terms[0], across[1:], beside[1:], last[1:]).astype(bf16)
    own_sum = added(own, across[0], beside[0], last[0])
    total = added(own_sum, *[traded(line_sum[step - 1], (4 * step, step)) for step in (3, 2, 1)])
    return (produced[None, :, None], total[None])


def solution(mesh):
    dp_total = mesh.shape["dp"]
    paired = mesh.shape["section"] == 2 and dp_total == 16
    placed = (
        P(None, "dp", None, None, None, None),
        P(None, "dp", None, None, None, None),
        P("section", "dp", None),
    )
    return jax.shard_map(
        paired_sections if paired else many_sections,
        mesh=mesh,
        in_specs=placed,
        out_specs=(P("section", None, "dp", None, None, None, None), P("section", "dp", None)),
        check_vma=False,
    )
```

```python
import functools

import jax
import jax.numpy as jnp
from jax import lax
from jax.experimental import pallas as pl
from jax.experimental.pallas import tpu as pltpu
from jax.sharding import PartitionSpec as P


def passed_along(block, axis, distance):
    devices = range(lax.axis_size(axis))
    route = [(i - distance, i) for i in devices if i - distance in devices]
    return lax.ppermute(block, axis, route)


def gather_patches(field):
    frames, height, width, channels = field.shape
    first_frame = field[:1]
    padded = jnp.concatenate([first_frame, first_frame, field], axis=0)
    padded = jnp.pad(padded, ((0, 0), (1, 1), (1, 1), (0, 0)))
    pieces = [
        padded[
            offset_time : offset_time + frames,
            offset_row : offset_row + height,
            offset_col : offset_col + width,
        ]
        for offset_time in range(3)
        for offset_row in range(3)
        for offset_col in range(3)
    ]
    return jnp.stack(pieces, axis=3).reshape(frames * height * width, 27 * channels)


def squash_field(activation):
    return jax.nn.silu(activation.astype(jnp.float32)).astype(jnp.bfloat16)


def squash_columns(activation):
    return gather_patches(squash_field(activation))


def layer_forward(activation, weight):
    branch = jnp.dot(squash_columns(activation), weight, preferred_element_type=jnp.float32)
    return (activation.astype(jnp.float32) + branch.reshape(activation.shape)).astype(jnp.bfloat16)


def input_gradient(activation, upstream, weight):
    flat_grad = upstream.reshape(-1, weight.shape[1])
    column_grad = lax.dot_general(
        flat_grad, weight, (((1,), (1,)), ((), ())), preferred_element_type=jnp.float32
    )
    base = activation.astype(jnp.float32)
    _, unfold = jax.vjp(gather_patches, base)
    field_grad = unfold(column_grad)[0]
    sigmoid_value = jax.nn.sigmoid(base)
    slope = sigmoid_value * (1.0 + base * (1.0 - sigmoid_value))
    return (upstream.astype(jnp.float32) + field_grad * slope).astype(jnp.bfloat16)


def weight_term(activation, upstream):
    flat_grad = upstream.reshape(-1, upstream.shape[-1])
    return lax.dot_general(
        squash_columns(activation),
        flat_grad,
        (((0,), (0,)), ((), ())),
        preferred_element_type=jnp.float32,
    )


def many_sections(clips, cotangent, weights):
    section_total = lax.axis_size("section")
    section_index = lax.axis_index("section")
    weight = lax.all_gather(weights, "dp", axis=1, tiled=True)[0]
    local_clips = clips[:, 0]
    local_grads = cotangent[:, 0]
    micro_count = local_clips.shape[0]
    step_count = micro_count + section_total - 1
    empty_field = jnp.zeros(local_clips.shape[1:], jnp.bfloat16)

    def forward_step(step_index, carry):
        received, saved_inputs, produced = carry
        micro_index = step_index - section_index
        active = (micro_index >= 0) & (micro_index < micro_count)
        slot_index = jnp.clip(micro_index, 0, micro_count - 1)
        fresh = lax.dynamic_index_in_dim(local_clips, slot_index, 0, keepdims=False)
        layer_input = jnp.where(section_index == 0, fresh, received)
        layer_output = layer_forward(layer_input, weight)
        kept_input = jnp.where(
            active,
            layer_input,
            lax.dynamic_index_in_dim(saved_inputs, slot_index, 0, keepdims=False),
        )
        kept_output = jnp.where(
            active, layer_output, lax.dynamic_index_in_dim(produced, slot_index, 0, keepdims=False)
        )
        saved_inputs = lax.dynamic_update_index_in_dim(saved_inputs, kept_input, slot_index, 0)
        produced = lax.dynamic_update_index_in_dim(produced, kept_output, slot_index, 0)
        received = passed_along(layer_output, "section", 1)
        return (received, saved_inputs, produced)

    start_forward = (empty_field, jnp.zeros_like(local_clips), jnp.zeros_like(local_clips))
    _, saved_inputs, produced = lax.fori_loop(0, step_count, forward_step, start_forward)

    def backward_step(step_index, carry):
        received, grad_total, kept_grads = carry
        micro_index = step_index - (section_total - 1 - section_index)
        active = (micro_index >= 0) & (micro_index < micro_count)
        slot_index = jnp.clip(micro_index, 0, micro_count - 1)
        fresh = lax.dynamic_index_in_dim(local_grads, slot_index, 0, keepdims=False)
        upstream = jnp.where(section_index == section_total - 1, fresh, received)
        activation = lax.dynamic_index_in_dim(saved_inputs, slot_index, 0, keepdims=False)
        grad_total = grad_total + jnp.where(active, weight_term(activation, upstream), 0.0)
        layer_grad = input_gradient(activation, upstream, weight)
        received = passed_along(layer_grad, "section", -1)
        return (received, grad_total, kept_grads)

    start_backward = (
        empty_field,
        jnp.zeros(weight.shape, jnp.float32),
        jnp.zeros_like(local_grads),
    )
    _, grad_total, kept_grads = lax.fori_loop(0, step_count, backward_step, start_backward)
    grad_share = lax.psum_scatter(
        grad_total.astype(jnp.bfloat16), "dp", scatter_dimension=0, tiled=True
    ).astype(jnp.float32)
    return (produced[None, :, None], grad_share[None])


def summed(terms):
    return functools.reduce(lambda p, q: p + q, terms)


def silu_of(value):
    return value * jax.nn.sigmoid(value)


def slope_of(value):
    sigmoid_value = jax.nn.sigmoid(value)
    return sigmoid_value * (1.0 + value * (1.0 - sigmoid_value))


def column_shifts(rows, width):
    height, flat, channels = rows.shape
    cells = rows.reshape(height * flat // width, width, channels)
    column = lax.broadcasted_iota(jnp.int32, cells.shape, 1)
    before = jnp.where(column == 0, 0.0, pltpu.roll(cells, 1, 1))
    after = jnp.where(column == width - 1, 0.0, pltpu.roll(cells, width - 1, 1))
    return [piece.reshape(rows.shape).astype(jnp.bfloat16) for piece in (before, cells, after)]


def whole(count):
    return [pl.BlockSpec(memory_space=pltpu.VMEM)] * count


def call(body, inputs, outputs, scratch, flops, place, far=False):
    return pl.pallas_call(
        body,
        out_shape=[jax.ShapeDtypeStruct(shape, dtype) for shape, dtype in outputs],
        in_specs=[pl.BlockSpec(memory_space=pltpu.SMEM)]
        + ([pl.BlockSpec(memory_space=pl.ANY)] * len(inputs) if far else whole(len(inputs))),
        out_specs=whole(len(outputs)),
        scratch_shapes=scratch,
        compiler_params=pltpu.CompilerParams(vmem_limit_bytes=32 * 1024 * 1024),
        cost_estimate=pl.CostEstimate(flops=flops, bytes_accessed=4_000_000, transcendentals=0),
    )(place, *inputs)


def turn_into(turned, k, t, piece):
    channels = piece.shape[-1]
    flat = piece.reshape(-1, channels)
    cells = flat.shape[0]
    turned[k * channels : (k + 1) * channels, t * cells : (t + 1) * cells] = flat.T


def pad_rows(grads):
    count, padded_height, flat, channels = grads.shape
    zero_row = jnp.zeros((count, 1, flat, channels), jnp.bfloat16)
    grads[:, :1] = zero_row
    grads[:, padded_height - 1 :] = zero_row


def place_grads(grads, fields):
    height = fields[0].shape[0]
    first_two = fields[0] + fields[1]
    for t, field in enumerate((*fields, first_two, first_two + fields[2])):
        grads[t, 1 : height + 1] = field.astype(jnp.bfloat16)


def copy_body(place, source, target):
    target[...] = source[...]


def prepare_body(place, clips_far, cotangent_far, *refs):
    shifted, base, upstream, ready, held, clips, cotangent, sems = refs
    micro, frames, height, width, channels = clips.shape
    section = place[0]
    copies = [
        pltpu.make_async_copy(source, target, sems.at[k])
        for k, (source, target) in enumerate(
            ((clips_far, clips), (cotangent_far, cotangent))
        )
    ]
    for copy in copies:
        copy.start()

    def reorder(source, target):
        for m in range(micro):
            held[:, :, m * width : (m + 1) * width, :] = source[m].astype(jnp.float32)
        for t in range(frames):
            target[t] = held[t].astype(jnp.bfloat16)

    zero_row = jnp.zeros((3, frames, 1) + shifted.shape[3:], jnp.bfloat16)
    shifted[:, :, :1] = zero_row
    shifted[:, :, height + 1 :] = zero_row
    copies[0].wait()
    reorder(clips, base)
    copies[1].wait()
    reorder(cotangent, upstream)

    @pl.when(section == 0)
    def _():
        for t in range(frames):
            squashed = silu_of(base[t].astype(jnp.float32)).astype(jnp.bfloat16)
            for k, piece in enumerate(column_shifts(squashed.astype(jnp.float32), width)):
                shifted[k, t, 1 : height + 1] = piece
                turn_into(ready, k, t, piece)

    @pl.when(section != 0)
    def _():
        for t in range(frames):
            for k, piece in enumerate(column_shifts(upstream[t].astype(jnp.float32), width)):
                shifted[k, t, 1 : height + 1] = piece


def shard_rows(place, rows, first, second):
    far, near = jnp.where(place[0] == 0, first, second), jnp.where(place[0] == 0, second, first)
    return pl.ds(pl.multiple_of((place[1] ^ (4 * far + near)) * rows, 8), rows)


def unpack_weights(place, blocks, table):
    rows = blocks[0].shape[1]
    for second in range(4):
        for first in range(4):
            shard = blocks[second][first]
            table[shard_rows(place, rows, first, second), :] = shard.astype(jnp.float32)


def forward_weights(table, channels):
    rows = 9 * channels
    return jnp.concatenate(
        [table[t * rows : (t + 1) * rows, :].astype(jnp.bfloat16) for t in range(3)], axis=1
    )


def backward_weights(table, channels):
    def turned_taps(times):
        blocks = []
        for k in reversed(range(9)):
            rows = [table[(t * 9 + k) * channels : (t * 9 + k + 1) * channels, :] for t in times]
            blocks.append(summed(rows).astype(jnp.bfloat16))
        return jnp.concatenate(blocks, axis=1)

    return [turned_taps(times) for times in ((0,), (1,), (2,), (0, 1), (0, 1, 2))]


def row_patches(shifted, start, count, height):
    flat, channels = shifted.shape[3:]
    return jnp.concatenate(
        [
            shifted[k, start : start + count, e : e + height].reshape(count * height * flat, channels)
            for e in range(3)
            for k in range(3)
        ],
        axis=1,
    )


def forward_product(shifted, weights, frames, height):
    channels = shifted.shape[-1]
    cells = height * shifted.shape[-2]
    pieces = {}
    for start, count, first_tap in ((0, frames - 2, 0), (frames - 2, 1, 1), (frames - 1, 1, 2)):
        part = jnp.dot(
            row_patches(shifted, start, count, height),
            weights[:, first_tap * channels :],
            preferred_element_type=jnp.float32,
        )
        for t in range(start, start + count):
            rows = slice((t - start) * cells, (t - start + 1) * cells)
            for tap in range(first_tap, 3):
                columns = slice((tap - first_tap) * channels, (tap - first_tap + 1) * channels)
                pieces[t, tap] = part[rows, columns]
    return [
        summed([pieces[max(t + tap - 2, 0), tap] for tap in range(3)]) for t in range(frames)
    ]


def backward_product(shifted, weights, frames, height):
    channels = shifted.shape[-1]
    cells = height * shifted.shape[-2]
    first, second, third, first_two, all_three = weights
    plan = (
        (2, frames - 2, ((first, -2), (second, -1), (third, 0))),
        (1, 1, ((third, 0), (first_two, -1))),
        (0, 1, ((all_three, 0),)),
    )
    reaching = [[] for _ in range(frames)]
    for start, count, terms in plan:
        part = lax.dot_general(
            row_patches(shifted, start, count, height),
            jnp.concatenate([weight for weight, _ in terms], axis=0),
            (((1,), (1,)), ((), ())),
            preferred_element_type=jnp.float32,
        )
        for t in range(start, start + count):
            rows = slice((t - start) * cells, (t - start + 1) * cells)
            for column, (_, step) in enumerate(terms):
                reaching[t + step].append(part[rows, column * channels : (column + 1) * channels])
    return [summed(terms) for terms in reaching]


def first_body(place, *refs):
    blocks = refs[:4]
    shifted, base, result, table = refs[4:]
    frames, height, flat, channels = base.shape
    section = place[0]
    unpack_weights(place, blocks, table)

    @pl.when(section == 0)
    def _():
        branch = forward_product(shifted, forward_weights(table, channels), frames, height)
        for t in range(frames):
            total = base[t].astype(jnp.float32) + branch[t].reshape(height, flat, channels)
            result[t] = total.astype(jnp.bfloat16)

    @pl.when(section != 0)
    def _():
        branch = backward_product(shifted, backward_weights(table, channels), frames, height)
        for t in range(frames):
            result[t] = branch[t].reshape(height, flat, channels).astype(jnp.bfloat16)


def between_body(place, mine, upstream, slope, grads):
    frames = upstream.shape[0]

    @pl.when(place[0] == 0)
    def _():
        for t in range(frames):
            slope[t] = slope_of(mine[t].astype(jnp.float32))

    @pl.when(place[0] != 0)
    def _():
        pad_rows(grads)
        place_grads(grads, [upstream[t].astype(jnp.float32) for t in range(frames)])


def second_body(width, place, ready, slope, moved, other, upstream, *refs):
    own, blocks = refs[0], refs[1:5]
    turned, grads, terms = refs[5:]
    frames, height, flat, channels = upstream.shape
    rows = own.shape[0]
    section = place[0]
    cells = height * flat

    def product(left, right):
        for tap, met in enumerate(((frames + 1, 3), (frames, 2, 3), (0, 1, 2, 3))):
            columns = jnp.concatenate(
                [
                    jnp.concatenate(
                        [
                            right[f, 2 - e : 2 - e + height].reshape(cells, channels)
                            for e in range(3)
                        ],
                        axis=1,
                    )
                    for f in met
                ],
                axis=0,
            )
            part = jnp.dot(
                left[:, : len(met) * cells], columns, preferred_element_type=jnp.float32
            )
            for e in range(3):
                for k in range(3):
                    start = (tap * 9 + e * 3 + k) * channels
                    terms[start : start + channels, :] = part[
                        k * channels : (k + 1) * channels, e * channels : (e + 1) * channels
                    ]

    @pl.when(section == 0)
    def _():
        pad_rows(grads)
        values = [
            upstream[t].astype(jnp.float32) + slope[t] * other[t].astype(jnp.float32)
            for t in range(frames)
        ]
        place_grads(grads, [value.astype(jnp.bfloat16).astype(jnp.float32) for value in values])
        product(ready, grads)

    @pl.when(section != 0)
    def _():
        for t in range(frames):
            squashed = silu_of(other[t].astype(jnp.float32)).astype(jnp.bfloat16)
            for k, piece in enumerate(column_shifts(squashed.astype(jnp.float32), width)):
                turn_into(turned, k, t, piece)
        product(turned, moved)

    for second in range(4):
        for first in range(4):
            share = terms[shard_rows(place, rows, first, second), :]
            if first == 0 and second == 0:
                own[...] = share
            elif second == 0:
                blocks[0][first - 1] = share.astype(jnp.bfloat16)
            else:
                blocks[second][first] = share.astype(jnp.bfloat16)


def third_body(place, *refs):
    blocks = refs[:4]
    mine, other, produced, table, shifted = refs[4:]
    micro, frames, height, width, channels = produced.shape
    flat = micro * width
    section = place[0]

    def hand_out(t, cells):
        for m in range(micro):
            produced[m, t] = cells[:, m * width : (m + 1) * width, :].astype(jnp.bfloat16)

    @pl.when(section == 0)
    def _():
        for t in range(frames):
            hand_out(t, mine[t].astype(jnp.float32))

    @pl.when(section != 0)
    def _():
        unpack_weights(place, blocks, table)
        zero_row = jnp.zeros((3, frames, 1, flat, channels), jnp.bfloat16)
        shifted[:, :, :1] = zero_row
        shifted[:, :, height + 1 :] = zero_row
        for t in range(frames):
            squashed = silu_of(other[t].astype(jnp.float32)).astype(jnp.bfloat16)
            for k, piece in enumerate(column_shifts(squashed.astype(jnp.float32), width)):
                shifted[k, t, 1 : height + 1] = piece
        branch = forward_product(shifted, forward_weights(table, channels), frames, height)
        for t in range(frames):
            hand_out(t, other[t].astype(jnp.float32) + branch[t].reshape(height, flat, channels))


def paired_sections(clips, cotangent, weights):
    dp_total = lax.axis_size("dp")
    local_clips, local_grads, shard = clips[:, 0], cotangent[:, 0], weights[0]
    micro, frames, height, width, channels = local_clips.shape
    rows = shard.shape[0]
    flat = micro * width
    cells = height * flat
    place = jnp.stack([lax.axis_index("section"), lax.axis_index("dp")]).astype(jnp.int32)

    def traded(block, along_z, step):
        bits = (4 * step, step) if along_z else (step, 4 * step)
        route = [
            (s * dp_total + i, s * dp_total + (i ^ bits[s])) for s in range(2) for i in range(dp_total)
        ]
        return lax.ppermute(block, ("section", "dp"), route)

    field = (frames, height, flat, channels)
    padded = (3, frames, height + 2, flat, channels)
    met = (frames + 2, height + 2, flat, channels)
    bf16, f32 = jnp.bfloat16, jnp.float32
    unit = 2 * micro * frames * height * width * channels * channels * 27

    first = [traded(shard, True, step) for step in range(1, 4)]
    (shard_copy,) = call(copy_body, (shard,), [(shard.shape, bf16)], [], unit // 16, place)
    shard_copy, first = lax.optimization_barrier((shard_copy, first))
    line = jnp.stack([shard_copy] + first)
    blocks = (line, *[traded(line, False, step) for step in range(1, 4)])

    turned = (3 * channels, frames * cells)
    shifted, base, upstream, ready = call(
        prepare_body,
        (local_clips, local_grads),
        [(padded, bf16), (field, bf16), (field, bf16), (turned, bf16)],
        [
            pltpu.VMEM(field, f32),
            pltpu.VMEM(local_clips.shape, bf16),
            pltpu.VMEM(local_clips.shape, bf16),
            pltpu.SemaphoreType.DMA((2,)),
        ],
        unit // 8,
        place,
        far=True,
    )
    table = pltpu.VMEM((dp_total * rows, channels), f32)
    (mine,) = call(
        first_body, blocks + (shifted, base), [(field, bf16)], [table], unit, place
    )
    other = lax.ppermute(mine, "section", [(0, 1), (1, 0)])
    slope, moved = call(
        between_body, (mine, upstream), [(field, f32), (met, bf16)], [], unit // 8, place
    )
    slope, moved, other = lax.optimization_barrier((slope, moved, other))
    own, *terms = call(
        functools.partial(second_body, width),
        (ready, slope, moved, other, upstream),
        [((rows, channels), f32), ((3, rows, channels), bf16)] + [((4, rows, channels), bf16)] * 3,
        [
            pltpu.VMEM(turned, bf16),
            pltpu.VMEM(met, bf16),
            table,
        ],
        unit,
        place,
    )
    (produced,) = call(
        third_body,
        blocks + (mine, other),
        [(local_clips.shape, bf16)],
        [table, pltpu.VMEM(padded, bf16)],
        unit,
        place,
    )

    def added(*terms):
        return summed([term.astype(f32) for term in terms])

    received = [traded(terms[step], False, step) for step in (3, 2, 1)]
    received, produced = lax.optimization_barrier((received, produced))
    line_sum = added(terms[0], *[block[1:] for block in received]).astype(bf16)
    own_sum = added(own, *[block[0] for block in received])
    total = added(own_sum, *[traded(line_sum[step - 1], True, step) for step in (3, 2, 1)])
    return (produced[None, :, None], total[None])


def solution(mesh):
    dp_total = mesh.shape["dp"]
    paired = mesh.shape["section"] == 2 and dp_total == 16
    placed = (
        P(None, "dp", None, None, None, None),
        P(None, "dp", None, None, None, None),
        P("section", "dp", None),
    )
    return jax.shard_map(
        paired_sections if paired else many_sections,
        mesh=mesh,
        in_specs=placed,
        out_specs=(P("section", None, "dp", None, None, None, None), P("section", "dp", None)),
        check_vma=False,
    )
```

```python
import functools

import jax
import jax.numpy as jnp
from jax import lax
from jax.experimental import pallas as pl
from jax.experimental.pallas import tpu as pltpu
from jax.sharding import PartitionSpec as P


def passed_along(block, axis, distance):
    devices = range(lax.axis_size(axis))
    route = [(i - distance, i) for i in devices if i - distance in devices]
    return lax.ppermute(block, axis, route)


def gather_patches(field):
    frames, height, width, channels = field.shape
    first_frame = field[:1]
    padded = jnp.concatenate([first_frame, first_frame, field], axis=0)
    padded = jnp.pad(padded, ((0, 0), (1, 1), (1, 1), (0, 0)))
    pieces = [
        padded[
            offset_time : offset_time + frames,
            offset_row : offset_row + height,
            offset_col : offset_col + width,
        ]
        for offset_time in range(3)
        for offset_row in range(3)
        for offset_col in range(3)
    ]
    return jnp.stack(pieces, axis=3).reshape(frames * height * width, 27 * channels)


def squash_field(activation):
    return jax.nn.silu(activation.astype(jnp.float32)).astype(jnp.bfloat16)


def squash_columns(activation):
    return gather_patches(squash_field(activation))


def layer_forward(activation, weight):
    branch = jnp.dot(squash_columns(activation), weight, preferred_element_type=jnp.float32)
    return (activation.astype(jnp.float32) + branch.reshape(activation.shape)).astype(jnp.bfloat16)


def input_gradient(activation, upstream, weight):
    flat_grad = upstream.reshape(-1, weight.shape[1])
    column_grad = lax.dot_general(
        flat_grad, weight, (((1,), (1,)), ((), ())), preferred_element_type=jnp.float32
    )
    base = activation.astype(jnp.float32)
    _, unfold = jax.vjp(gather_patches, base)
    field_grad = unfold(column_grad)[0]
    sigmoid_value = jax.nn.sigmoid(base)
    slope = sigmoid_value * (1.0 + base * (1.0 - sigmoid_value))
    return (upstream.astype(jnp.float32) + field_grad * slope).astype(jnp.bfloat16)


def weight_term(activation, upstream):
    flat_grad = upstream.reshape(-1, upstream.shape[-1])
    return lax.dot_general(
        squash_columns(activation),
        flat_grad,
        (((0,), (0,)), ((), ())),
        preferred_element_type=jnp.float32,
    )


def many_sections(clips, cotangent, weights):
    section_total = lax.axis_size("section")
    section_index = lax.axis_index("section")
    weight = lax.all_gather(weights, "dp", axis=1, tiled=True)[0]
    local_clips = clips[:, 0]
    local_grads = cotangent[:, 0]
    micro_count = local_clips.shape[0]
    step_count = micro_count + section_total - 1
    empty_field = jnp.zeros(local_clips.shape[1:], jnp.bfloat16)

    def forward_step(step_index, carry):
        received, saved_inputs, produced = carry
        micro_index = step_index - section_index
        active = (micro_index >= 0) & (micro_index < micro_count)
        slot_index = jnp.clip(micro_index, 0, micro_count - 1)
        fresh = lax.dynamic_index_in_dim(local_clips, slot_index, 0, keepdims=False)
        layer_input = jnp.where(section_index == 0, fresh, received)
        layer_output = layer_forward(layer_input, weight)
        kept_input = jnp.where(
            active,
            layer_input,
            lax.dynamic_index_in_dim(saved_inputs, slot_index, 0, keepdims=False),
        )
        kept_output = jnp.where(
            active, layer_output, lax.dynamic_index_in_dim(produced, slot_index, 0, keepdims=False)
        )
        saved_inputs = lax.dynamic_update_index_in_dim(saved_inputs, kept_input, slot_index, 0)
        produced = lax.dynamic_update_index_in_dim(produced, kept_output, slot_index, 0)
        received = passed_along(layer_output, "section", 1)
        return (received, saved_inputs, produced)

    start_forward = (empty_field, jnp.zeros_like(local_clips), jnp.zeros_like(local_clips))
    _, saved_inputs, produced = lax.fori_loop(0, step_count, forward_step, start_forward)

    def backward_step(step_index, carry):
        received, grad_total, kept_grads = carry
        micro_index = step_index - (section_total - 1 - section_index)
        active = (micro_index >= 0) & (micro_index < micro_count)
        slot_index = jnp.clip(micro_index, 0, micro_count - 1)
        fresh = lax.dynamic_index_in_dim(local_grads, slot_index, 0, keepdims=False)
        upstream = jnp.where(section_index == section_total - 1, fresh, received)
        activation = lax.dynamic_index_in_dim(saved_inputs, slot_index, 0, keepdims=False)
        grad_total = grad_total + jnp.where(active, weight_term(activation, upstream), 0.0)
        layer_grad = input_gradient(activation, upstream, weight)
        received = passed_along(layer_grad, "section", -1)
        return (received, grad_total, kept_grads)

    start_backward = (
        empty_field,
        jnp.zeros(weight.shape, jnp.float32),
        jnp.zeros_like(local_grads),
    )
    _, grad_total, kept_grads = lax.fori_loop(0, step_count, backward_step, start_backward)
    grad_share = lax.psum_scatter(
        grad_total.astype(jnp.bfloat16), "dp", scatter_dimension=0, tiled=True
    ).astype(jnp.float32)
    return (produced[None, :, None], grad_share[None])


def summed(terms):
    return functools.reduce(lambda p, q: p + q, terms)


def silu_of(value):
    return value * jax.nn.sigmoid(value)


def slope_of(value):
    sigmoid_value = jax.nn.sigmoid(value)
    return sigmoid_value * (1.0 + value * (1.0 - sigmoid_value))


def column_shifts(rows, width):
    height, flat, channels = rows.shape
    cells = rows.reshape(height * flat // width, width, channels)
    column = lax.broadcasted_iota(jnp.int32, cells.shape, 1)
    before = jnp.where(column == 0, 0.0, pltpu.roll(cells, 1, 1))
    after = jnp.where(column == width - 1, 0.0, pltpu.roll(cells, width - 1, 1))
    return [piece.reshape(rows.shape).astype(jnp.bfloat16) for piece in (before, cells, after)]


def whole(count):
    return [pl.BlockSpec(memory_space=pltpu.VMEM)] * count


def call(body, inputs, outputs, scratch, flops, place, far=False):
    return pl.pallas_call(
        body,
        out_shape=[jax.ShapeDtypeStruct(shape, dtype) for shape, dtype in outputs],
        in_specs=[pl.BlockSpec(memory_space=pltpu.SMEM)]
        + ([pl.BlockSpec(memory_space=pl.ANY)] * len(inputs) if far else whole(len(inputs))),
        out_specs=whole(len(outputs)),
        scratch_shapes=scratch,
        compiler_params=pltpu.CompilerParams(vmem_limit_bytes=32 * 1024 * 1024),
        cost_estimate=pl.CostEstimate(flops=flops, bytes_accessed=4_000_000, transcendentals=0),
    )(place, *inputs)


def turn_into(turned, k, t, piece):
    channels = piece.shape[-1]
    flat = piece.reshape(-1, channels)
    cells = flat.shape[0]
    turned[k * channels : (k + 1) * channels, t * cells : (t + 1) * cells] = flat.T


def pad_rows(grads):
    count, padded_height, flat, channels = grads.shape
    zero_row = jnp.zeros((count, 1, flat, channels), jnp.bfloat16)
    grads[:, :1] = zero_row
    grads[:, padded_height - 1 :] = zero_row


def place_grads(grads, fields):
    height = fields[0].shape[0]
    first_two = fields[0] + fields[1]
    for t, field in enumerate((*fields, first_two, first_two + fields[2])):
        grads[t, 1 : height + 1] = field.astype(jnp.bfloat16)


def copy_body(place, source, target):
    target[...] = source[...]


def prepare_body(place, clips_far, cotangent_far, *refs):
    shifted, base, upstream, ready, held, clips, cotangent, sems = refs
    micro, frames, height, width, channels = clips.shape
    section = place[0]
    copies = [
        pltpu.make_async_copy(source, target, sems.at[k])
        for k, (source, target) in enumerate(
            ((clips_far, clips), (cotangent_far, cotangent))
        )
    ]
    for copy in copies:
        copy.start()

    def reorder(source, target):
        for m in range(micro):
            held[:, :, m * width : (m + 1) * width, :] = source[m].astype(jnp.float32)
        for t in range(frames):
            target[t] = held[t].astype(jnp.bfloat16)

    zero_row = jnp.zeros((3, frames, 1) + shifted.shape[3:], jnp.bfloat16)
    shifted[:, :, :1] = zero_row
    shifted[:, :, height + 1 :] = zero_row
    copies[0].wait()
    reorder(clips, base)
    copies[1].wait()
    reorder(cotangent, upstream)

    @pl.when(section == 0)
    def _():
        for t in range(frames):
            squashed = silu_of(base[t].astype(jnp.float32)).astype(jnp.bfloat16)
            for k, piece in enumerate(column_shifts(squashed.astype(jnp.float32), width)):
                shifted[k, t, 1 : height + 1] = piece
                turn_into(ready, k, t, piece)

    @pl.when(section != 0)
    def _():
        for t in range(frames):
            for k, piece in enumerate(column_shifts(upstream[t].astype(jnp.float32), width)):
                shifted[k, t, 1 : height + 1] = piece


GATHERED = ((0, 3, 2, 1), (0, 1, 2, 3))
SUMMED = ((0, 3, 2, 1), (0, 3, 2, 1))


def shard_rows(place, rows, first, seconds):
    far, near = jnp.where(place[0] == 0, first, seconds[1]), jnp.where(place[0] == 0, seconds[0], first)
    return pl.ds(pl.multiple_of((place[1] ^ (4 * far + near)) * rows, 8), rows)


def unpack_weights(place, blocks, table):
    line, *others = blocks
    rows = line.shape[1]
    early, others = others[:2], others[2:]
    firsts = (None, None, *early)
    for first_of, block, *seconds in zip(firsts, (line, *others), *GATHERED):
        for first in range(4):
            if first_of is None:
                shard = block[first]
            else:
                shard = block[first - 1] if first else first_of[...]
            table[shard_rows(place, rows, first, seconds), :] = shard.astype(jnp.float32)


def forward_weights(table, channels):
    rows = 9 * channels
    return jnp.concatenate(
        [table[t * rows : (t + 1) * rows, :].astype(jnp.bfloat16) for t in range(3)], axis=1
    )


def backward_weights(table, channels):
    def turned_taps(times):
        blocks = []
        for k in reversed(range(9)):
            rows = [table[(t * 9 + k) * channels : (t * 9 + k + 1) * channels, :] for t in times]
            blocks.append(summed(rows).astype(jnp.bfloat16))
        return jnp.concatenate(blocks, axis=1)

    return [turned_taps(times) for times in ((0,), (1,), (2,), (0, 1), (0, 1, 2))]


def row_patches(shifted, start, count, height):
    flat, channels = shifted.shape[3:]
    return jnp.concatenate(
        [
            shifted[k, start : start + count, e : e + height].reshape(count * height * flat, channels)
            for e in range(3)
            for k in range(3)
        ],
        axis=1,
    )


def forward_product(shifted, weights, frames, height):
    channels = shifted.shape[-1]
    cells = height * shifted.shape[-2]
    pieces = {}
    for start, count, first_tap in ((0, frames - 2, 0), (frames - 2, 1, 1), (frames - 1, 1, 2)):
        part = jnp.dot(
            row_patches(shifted, start, count, height),
            weights[:, first_tap * channels :],
            preferred_element_type=jnp.float32,
        )
        for t in range(start, start + count):
            rows = slice((t - start) * cells, (t - start + 1) * cells)
            for tap in range(first_tap, 3):
                columns = slice((tap - first_tap) * channels, (tap - first_tap + 1) * channels)
                pieces[t, tap] = part[rows, columns]
    return [
        summed([pieces[max(t + tap - 2, 0), tap] for tap in range(3)]) for t in range(frames)
    ]


def backward_product(shifted, weights, frames, height):
    channels = shifted.shape[-1]
    cells = height * shifted.shape[-2]
    first, second, third, first_two, all_three = weights
    plan = (
        (2, frames - 2, ((first, -2), (second, -1), (third, 0))),
        (1, 1, ((third, 0), (first_two, -1))),
        (0, 1, ((all_three, 0),)),
    )
    reaching = [[] for _ in range(frames)]
    for start, count, terms in plan:
        part = lax.dot_general(
            row_patches(shifted, start, count, height),
            jnp.concatenate([weight for weight, _ in terms], axis=0),
            (((1,), (1,)), ((), ())),
            preferred_element_type=jnp.float32,
        )
        for t in range(start, start + count):
            rows = slice((t - start) * cells, (t - start + 1) * cells)
            for column, (_, step) in enumerate(terms):
                reaching[t + step].append(part[rows, column * channels : (column + 1) * channels])
    return [summed(terms) for terms in reaching]


def first_body(place, *refs):
    blocks = refs[:6]
    shifted, base, result, table = refs[6:]
    frames, height, flat, channels = base.shape
    section = place[0]
    unpack_weights(place, blocks, table)

    @pl.when(section == 0)
    def _():
        branch = forward_product(shifted, forward_weights(table, channels), frames, height)
        for t in range(frames):
            total = base[t].astype(jnp.float32) + branch[t].reshape(height, flat, channels)
            result[t] = total.astype(jnp.bfloat16)

    @pl.when(section != 0)
    def _():
        branch = backward_product(shifted, backward_weights(table, channels), frames, height)
        for t in range(frames):
            result[t] = branch[t].reshape(height, flat, channels).astype(jnp.bfloat16)


def between_body(place, mine, upstream, slope, grads):
    frames = upstream.shape[0]

    @pl.when(place[0] == 0)
    def _():
        for t in range(frames):
            slope[t] = slope_of(mine[t].astype(jnp.float32))

    @pl.when(place[0] != 0)
    def _():
        pad_rows(grads)
        place_grads(grads, [upstream[t].astype(jnp.float32) for t in range(frames)])


def second_body(width, place, ready, slope, moved, other, upstream, *refs):
    own, blocks = refs[0], refs[1:5]
    turned, grads, terms = refs[5:]
    frames, height, flat, channels = upstream.shape
    rows = own.shape[0]
    section = place[0]
    cells = height * flat

    def product(left, right):
        for tap, met in enumerate(((frames + 1, 3), (frames, 2, 3), (0, 1, 2, 3))):
            columns = jnp.concatenate(
                [
                    jnp.concatenate(
                        [
                            right[f, 2 - e : 2 - e + height].reshape(cells, channels)
                            for e in range(3)
                        ],
                        axis=1,
                    )
                    for f in met
                ],
                axis=0,
            )
            part = jnp.dot(
                left[:, : len(met) * cells], columns, preferred_element_type=jnp.float32
            )
            for e in range(3):
                for k in range(3):
                    start = (tap * 9 + e * 3 + k) * channels
                    terms[start : start + channels, :] = part[
                        k * channels : (k + 1) * channels, e * channels : (e + 1) * channels
                    ]

    @pl.when(section == 0)
    def _():
        pad_rows(grads)
        values = [
            upstream[t].astype(jnp.float32) + slope[t] * other[t].astype(jnp.float32)
            for t in range(frames)
        ]
        place_grads(grads, [value.astype(jnp.bfloat16).astype(jnp.float32) for value in values])
        product(ready, grads)

    @pl.when(section != 0)
    def _():
        for t in range(frames):
            squashed = silu_of(other[t].astype(jnp.float32)).astype(jnp.bfloat16)
            for k, piece in enumerate(column_shifts(squashed.astype(jnp.float32), width)):
                turn_into(turned, k, t, piece)
        product(turned, moved)

    for block, *seconds in zip(blocks, *SUMMED):
        for first in range(4):
            share = terms[shard_rows(place, rows, first, seconds), :]
            if seconds[0]:
                block[first] = share.astype(jnp.bfloat16)
            elif first:
                block[first - 1] = share.astype(jnp.bfloat16)
            else:
                own[...] = share


def third_body(place, *refs):
    blocks = refs[:6]
    mine, other, produced, table, shifted = refs[6:]
    micro, frames, height, width, channels = produced.shape
    flat = micro * width
    section = place[0]

    def hand_out(t, cells):
        for m in range(micro):
            produced[m, t] = cells[:, m * width : (m + 1) * width, :].astype(jnp.bfloat16)

    @pl.when(section == 0)
    def _():
        for t in range(frames):
            hand_out(t, mine[t].astype(jnp.float32))

    @pl.when(section != 0)
    def _():
        unpack_weights(place, blocks, table)
        zero_row = jnp.zeros((3, frames, 1, flat, channels), jnp.bfloat16)
        shifted[:, :, :1] = zero_row
        shifted[:, :, height + 1 :] = zero_row
        for t in range(frames):
            squashed = silu_of(other[t].astype(jnp.float32)).astype(jnp.bfloat16)
            for k, piece in enumerate(column_shifts(squashed.astype(jnp.float32), width)):
                shifted[k, t, 1 : height + 1] = piece
        branch = forward_product(shifted, forward_weights(table, channels), frames, height)
        for t in range(frames):
            hand_out(t, other[t].astype(jnp.float32) + branch[t].reshape(height, flat, channels))


def paired_sections(clips, cotangent, weights):
    dp_total = lax.axis_size("dp")
    local_clips, local_grads, shard = clips[:, 0], cotangent[:, 0], weights[0]
    micro, frames, height, width, channels = local_clips.shape
    rows = shard.shape[0]
    flat = micro * width
    cells = height * flat
    place = jnp.stack([lax.axis_index("section"), lax.axis_index("dp")]).astype(jnp.int32)

    def traded(block, bits):
        route = [
            (s * dp_total + i, s * dp_total + (i ^ bits[s])) for s in range(2) for i in range(dp_total)
        ]
        return lax.ppermute(block, ("section", "dp"), route)

    field = (frames, height, flat, channels)
    padded = (3, frames, height + 2, flat, channels)
    met = (frames + 2, height + 2, flat, channels)
    bf16, f32 = jnp.bfloat16, jnp.float32
    unit = 2 * micro * frames * height * width * channels * channels * 27

    first = [traded(shard, (4 * step, step)) for step in range(1, 4)]
    early = [traded(shard, (2, 8)), traded(shard, (1, 12))]
    (shard_copy,) = call(copy_body, (shard,), [(shard.shape, bf16)], [], unit // 16, place)
    shard_copy, early, first = lax.optimization_barrier((shard_copy, early, first))
    line, late_line = jnp.stack([shard_copy] + first), jnp.stack(first)
    blocks = (
        line,
        *early,
        traded(line, (3, 4)),
        traded(late_line, (2, 8)),
        traded(late_line, (1, 12)),
    )
    turned = (3 * channels, frames * cells)
    shifted, base, upstream, ready = call(
        prepare_body,
        (local_clips, local_grads),
        [(padded, bf16), (field, bf16), (field, bf16), (turned, bf16)],
        [
            pltpu.VMEM(field, f32),
            pltpu.VMEM(local_clips.shape, bf16),
            pltpu.VMEM(local_clips.shape, bf16),
            pltpu.SemaphoreType.DMA((2,)),
        ],
        unit // 8,
        place,
        far=True,
    )
    table = pltpu.VMEM((dp_total * rows, channels), f32)
    (mine,) = call(
        first_body, blocks + (shifted, base), [(field, bf16)], [table], unit, place
    )
    other = lax.ppermute(mine, "section", [(0, 1), (1, 0)])
    slope, moved = call(
        between_body, (mine, upstream), [(field, f32), (met, bf16)], [], unit // 8, place
    )
    slope, moved, other = lax.optimization_barrier((slope, moved, other))
    own, *terms = call(
        functools.partial(second_body, width),
        (ready, slope, moved, other, upstream),
        [((rows, channels), f32), ((3, rows, channels), bf16)] + [((4, rows, channels), bf16)] * 3,
        [
            pltpu.VMEM(turned, bf16),
            pltpu.VMEM(met, bf16),
            table,
        ],
        unit,
        place,
    )
    (produced,) = call(
        third_body,
        blocks + (mine, other),
        [(local_clips.shape, bf16)],
        [table, pltpu.VMEM(padded, bf16)],
        unit,
        place,
    )

    def added(*terms):
        return summed([term.astype(f32) for term in terms])

    received = [traded(terms[1], (3, 12)), traded(terms[2], (2, 8)), traded(terms[3], (1, 4))]
    received, produced = lax.optimization_barrier((received, produced))
    line_sum = added(terms[0], *[block[1:] for block in received]).astype(bf16)
    own_sum = added(own, *[block[0] for block in received])
    total = added(own_sum, *[traded(line_sum[step - 1], (4 * step, step)) for step in (3, 2, 1)])
    return (produced[None, :, None], total[None])


def solution(mesh):
    dp_total = mesh.shape["dp"]
    paired = mesh.shape["section"] == 2 and dp_total == 16
    placed = (
        P(None, "dp", None, None, None, None),
        P(None, "dp", None, None, None, None),
        P("section", "dp", None),
    )
    return jax.shard_map(
        paired_sections if paired else many_sections,
        mesh=mesh,
        in_specs=placed,
        out_specs=(P("section", None, "dp", None, None, None, None), P("section", "dp", None)),
        check_vma=False,
    )
```

```python
import functools

import jax
import jax.numpy as jnp
from jax import lax
from jax.experimental import pallas as pl
from jax.experimental.pallas import tpu as pltpu
from jax.sharding import PartitionSpec as P


def passed_along(block, axis, distance):
    devices = range(lax.axis_size(axis))
    route = [(i - distance, i) for i in devices if i - distance in devices]
    return lax.ppermute(block, axis, route)


def gather_patches(field):
    frames, height, width, channels = field.shape
    first_frame = field[:1]
    padded = jnp.concatenate([first_frame, first_frame, field], axis=0)
    padded = jnp.pad(padded, ((0, 0), (1, 1), (1, 1), (0, 0)))
    pieces = [
        padded[
            offset_time : offset_time + frames,
            offset_row : offset_row + height,
            offset_col : offset_col + width,
        ]
        for offset_time in range(3)
        for offset_row in range(3)
        for offset_col in range(3)
    ]
    return jnp.stack(pieces, axis=3).reshape(frames * height * width, 27 * channels)


def squash_field(activation):
    return jax.nn.silu(activation.astype(jnp.float32)).astype(jnp.bfloat16)


def squash_columns(activation):
    return gather_patches(squash_field(activation))


def layer_forward(activation, weight):
    branch = jnp.dot(squash_columns(activation), weight, preferred_element_type=jnp.float32)
    return (activation.astype(jnp.float32) + branch.reshape(activation.shape)).astype(jnp.bfloat16)


def input_gradient(activation, upstream, weight):
    flat_grad = upstream.reshape(-1, weight.shape[1])
    column_grad = lax.dot_general(
        flat_grad, weight, (((1,), (1,)), ((), ())), preferred_element_type=jnp.float32
    )
    base = activation.astype(jnp.float32)
    _, unfold = jax.vjp(gather_patches, base)
    field_grad = unfold(column_grad)[0]
    sigmoid_value = jax.nn.sigmoid(base)
    slope = sigmoid_value * (1.0 + base * (1.0 - sigmoid_value))
    return (upstream.astype(jnp.float32) + field_grad * slope).astype(jnp.bfloat16)


def weight_term(activation, upstream):
    flat_grad = upstream.reshape(-1, upstream.shape[-1])
    return lax.dot_general(
        squash_columns(activation),
        flat_grad,
        (((0,), (0,)), ((), ())),
        preferred_element_type=jnp.float32,
    )


def many_sections(clips, cotangent, weights):
    section_total = lax.axis_size("section")
    section_index = lax.axis_index("section")
    weight = lax.all_gather(weights, "dp", axis=1, tiled=True)[0]
    local_clips = clips[:, 0]
    local_grads = cotangent[:, 0]
    micro_count = local_clips.shape[0]
    step_count = micro_count + section_total - 1
    empty_field = jnp.zeros(local_clips.shape[1:], jnp.bfloat16)

    def forward_step(step_index, carry):
        received, saved_inputs, produced = carry
        micro_index = step_index - section_index
        active = (micro_index >= 0) & (micro_index < micro_count)
        slot_index = jnp.clip(micro_index, 0, micro_count - 1)
        fresh = lax.dynamic_index_in_dim(local_clips, slot_index, 0, keepdims=False)
        layer_input = jnp.where(section_index == 0, fresh, received)
        layer_output = layer_forward(layer_input, weight)
        kept_input = jnp.where(
            active,
            layer_input,
            lax.dynamic_index_in_dim(saved_inputs, slot_index, 0, keepdims=False),
        )
        kept_output = jnp.where(
            active, layer_output, lax.dynamic_index_in_dim(produced, slot_index, 0, keepdims=False)
        )
        saved_inputs = lax.dynamic_update_index_in_dim(saved_inputs, kept_input, slot_index, 0)
        produced = lax.dynamic_update_index_in_dim(produced, kept_output, slot_index, 0)
        received = passed_along(layer_output, "section", 1)
        return (received, saved_inputs, produced)

    start_forward = (empty_field, jnp.zeros_like(local_clips), jnp.zeros_like(local_clips))
    _, saved_inputs, produced = lax.fori_loop(0, step_count, forward_step, start_forward)

    def backward_step(step_index, carry):
        received, grad_total, kept_grads = carry
        micro_index = step_index - (section_total - 1 - section_index)
        active = (micro_index >= 0) & (micro_index < micro_count)
        slot_index = jnp.clip(micro_index, 0, micro_count - 1)
        fresh = lax.dynamic_index_in_dim(local_grads, slot_index, 0, keepdims=False)
        upstream = jnp.where(section_index == section_total - 1, fresh, received)
        activation = lax.dynamic_index_in_dim(saved_inputs, slot_index, 0, keepdims=False)
        grad_total = grad_total + jnp.where(active, weight_term(activation, upstream), 0.0)
        layer_grad = input_gradient(activation, upstream, weight)
        received = passed_along(layer_grad, "section", -1)
        return (received, grad_total, kept_grads)

    start_backward = (
        empty_field,
        jnp.zeros(weight.shape, jnp.float32),
        jnp.zeros_like(local_grads),
    )
    _, grad_total, kept_grads = lax.fori_loop(0, step_count, backward_step, start_backward)
    grad_share = lax.psum_scatter(
        grad_total.astype(jnp.bfloat16), "dp", scatter_dimension=0, tiled=True
    ).astype(jnp.float32)
    return (produced[None, :, None], grad_share[None])


def summed(terms):
    return functools.reduce(lambda p, q: p + q, terms)


def frame_of(halves, t):
    return halves[t // halves[0].shape[0]].at[t % halves[0].shape[0]]


def silu_of(value):
    return value * jax.nn.sigmoid(value)


def slope_of(value):
    sigmoid_value = jax.nn.sigmoid(value)
    return sigmoid_value * (1.0 + value * (1.0 - sigmoid_value))


def column_shifts(rows, width):
    height, flat, channels = rows.shape
    cells = rows.reshape(height * flat // width, width, channels)
    column = lax.broadcasted_iota(jnp.int32, cells.shape, 1)
    before = jnp.where(column == 0, 0.0, pltpu.roll(cells, 1, 1))
    after = jnp.where(column == width - 1, 0.0, pltpu.roll(cells, width - 1, 1))
    return [piece.reshape(rows.shape).astype(jnp.bfloat16) for piece in (before, cells, after)]


def whole(count):
    return [pl.BlockSpec(memory_space=pltpu.VMEM)] * count


def call(body, inputs, outputs, scratch, flops, place, far=False):
    return pl.pallas_call(
        body,
        out_shape=[jax.ShapeDtypeStruct(shape, dtype) for shape, dtype in outputs],
        in_specs=[pl.BlockSpec(memory_space=pltpu.SMEM)]
        + ([pl.BlockSpec(memory_space=pl.ANY)] * len(inputs) if far else whole(len(inputs))),
        out_specs=whole(len(outputs)),
        scratch_shapes=scratch,
        compiler_params=pltpu.CompilerParams(vmem_limit_bytes=32 * 1024 * 1024),
        cost_estimate=pl.CostEstimate(flops=flops, bytes_accessed=4_000_000, transcendentals=0),
    )(place, *inputs)


def turn_into(turned, k, t, piece):
    channels = piece.shape[-1]
    flat = piece.reshape(-1, channels)
    cells = flat.shape[0]
    turned[k * channels : (k + 1) * channels, t * cells : (t + 1) * cells] = flat.T


def pad_rows(grads):
    count, padded_height, flat, channels = grads.shape
    zero_row = jnp.zeros((count, 1, flat, channels), jnp.bfloat16)
    grads[:, :1] = zero_row
    grads[:, padded_height - 1 :] = zero_row


def place_grads(grads, fields):
    height = fields[0].shape[0]
    first_two = fields[0] + fields[1]
    for t, field in enumerate((*fields, first_two, first_two + fields[2])):
        grads[t, 1 : height + 1] = field.astype(jnp.bfloat16)


def copy_body(place, source, target):
    target[...] = source[...]


def prepare_body(place, clips_far, cotangent_far, *refs):
    shifted, base, upstream, ready, held, clips, cotangent, sems = refs
    micro, frames, height, width, channels = clips.shape
    section = place[0]
    copies = [
        pltpu.make_async_copy(source, target, sems.at[k])
        for k, (source, target) in enumerate(
            ((clips_far, clips), (cotangent_far, cotangent))
        )
    ]
    for copy in copies:
        copy.start()

    def reorder(source, target):
        for m in range(micro):
            held[:, :, m * width : (m + 1) * width, :] = source[m].astype(jnp.float32)
        for t in range(frames):
            target[t] = held[t].astype(jnp.bfloat16)

    zero_row = jnp.zeros((3, frames, 1) + shifted.shape[3:], jnp.bfloat16)
    shifted[:, :, :1] = zero_row
    shifted[:, :, height + 1 :] = zero_row
    copies[0].wait()
    reorder(clips, base)
    copies[1].wait()
    reorder(cotangent, upstream)

    @pl.when(section == 0)
    def _():
        for t in range(frames):
            squashed = silu_of(base[t].astype(jnp.float32)).astype(jnp.bfloat16)
            for k, piece in enumerate(column_shifts(squashed.astype(jnp.float32), width)):
                shifted[k, t, 1 : height + 1] = piece
                turn_into(ready, k, t, piece)

    @pl.when(section != 0)
    def _():
        for t in range(frames):
            for k, piece in enumerate(column_shifts(upstream[t].astype(jnp.float32), width)):
                shifted[k, t, 1 : height + 1] = piece


def shard_rows(place, rows, first, second):
    far, near = jnp.where(place[0] == 0, first, second), jnp.where(place[0] == 0, second, first)
    return pl.ds(pl.multiple_of((place[1] ^ (4 * far + near)) * rows, 8), rows)


def unpack_weights(place, blocks, table):
    rows = blocks[0].shape[1]
    for second in range(4):
        for first in range(4):
            shard = blocks[second][first]
            table[shard_rows(place, rows, first, second), :] = shard.astype(jnp.float32)


def forward_weights(table, channels):
    rows = 9 * channels
    return jnp.concatenate(
        [table[t * rows : (t + 1) * rows, :].astype(jnp.bfloat16) for t in range(3)], axis=1
    )


def backward_weights(table, channels):
    def turned_taps(times):
        blocks = []
        for k in reversed(range(9)):
            rows = [table[(t * 9 + k) * channels : (t * 9 + k + 1) * channels, :] for t in times]
            blocks.append(summed(rows).astype(jnp.bfloat16))
        return jnp.concatenate(blocks, axis=1)

    return [turned_taps(times) for times in ((0,), (1,), (2,), (0, 1), (0, 1, 2))]


def row_patches(shifted, start, count, height):
    flat, channels = shifted.shape[3:]
    return jnp.concatenate(
        [
            shifted[k, start : start + count, e : e + height].reshape(count * height * flat, channels)
            for e in range(3)
            for k in range(3)
        ],
        axis=1,
    )


def forward_product(shifted, weights, frames, height):
    channels = shifted.shape[-1]
    cells = height * shifted.shape[-2]
    pieces = {}
    for start, count, first_tap in ((0, frames - 2, 0), (frames - 2, 1, 1), (frames - 1, 1, 2)):
        part = jnp.dot(
            row_patches(shifted, start, count, height),
            weights[:, first_tap * channels :],
            preferred_element_type=jnp.float32,
        )
        for t in range(start, start + count):
            rows = slice((t - start) * cells, (t - start + 1) * cells)
            for tap in range(first_tap, 3):
                columns = slice((tap - first_tap) * channels, (tap - first_tap + 1) * channels)
                pieces[t, tap] = part[rows, columns]
    return [
        summed([pieces[max(t + tap - 2, 0), tap] for tap in range(3)]) for t in range(frames)
    ]


def backward_product(shifted, weights, frames, height):
    channels = shifted.shape[-1]
    cells = height * shifted.shape[-2]
    first, second, third, first_two, all_three = weights
    plan = (
        (2, frames - 2, ((first, -2), (second, -1), (third, 0))),
        (1, 1, ((third, 0), (first_two, -1))),
        (0, 1, ((all_three, 0),)),
    )
    reaching = [[] for _ in range(frames)]
    for start, count, terms in plan:
        part = lax.dot_general(
            row_patches(shifted, start, count, height),
            jnp.concatenate([weight for weight, _ in terms], axis=0),
            (((1,), (1,)), ((), ())),
            preferred_element_type=jnp.float32,
        )
        for t in range(start, start + count):
            rows = slice((t - start) * cells, (t - start + 1) * cells)
            for column, (_, step) in enumerate(terms):
                reaching[t + step].append(part[rows, column * channels : (column + 1) * channels])
    return [summed(terms) for terms in reaching]


def first_body(place, *refs):
    blocks = refs[:4]
    shifted, base, *results, table = refs[4:]
    frames, height, flat, channels = base.shape
    section = place[0]
    unpack_weights(place, blocks, table)

    @pl.when(section == 0)
    def _():
        branch = forward_product(shifted, forward_weights(table, channels), frames, height)
        for t in range(frames):
            total = base[t].astype(jnp.float32) + branch[t].reshape(height, flat, channels)
            frame_of(results, t)[...] = total.astype(jnp.bfloat16)

    @pl.when(section != 0)
    def _():
        branch = backward_product(shifted, backward_weights(table, channels), frames, height)
        for t in range(frames):
            frame_of(results, t)[...] = branch[t].reshape(height, flat, channels).astype(jnp.bfloat16)


def between_body(place, mine_low, mine_high, upstream, slope, grads):
    frames = upstream.shape[0]

    @pl.when(place[0] == 0)
    def _():
        for t in range(frames):
            slope[t] = slope_of(frame_of((mine_low, mine_high), t)[...].astype(jnp.float32))

    @pl.when(place[0] != 0)
    def _():
        pad_rows(grads)
        place_grads(grads, [upstream[t].astype(jnp.float32) for t in range(frames)])


def second_body(width, place, ready, slope, moved, other_low, other_high, upstream, *refs):
    shares, turned, grads = refs
    frames, height, flat, channels = upstream.shape
    rows = shares.shape[2]
    section = place[0]
    cells = height * flat

    def product(left, right):
        taps, done = [], 0
        for met in ((frames + 1, 3), (frames, 2, 3), (0, 1, 2, 3)):
            columns = jnp.concatenate(
                [
                    jnp.concatenate(
                        [
                            right[f, 2 - e : 2 - e + height].reshape(cells, channels)
                            for e in range(3)
                        ],
                        axis=1,
                    )
                    for f in met
                ],
                axis=0,
            )
            part = jnp.dot(
                left[:, : len(met) * cells], columns, preferred_element_type=jnp.float32
            )
            for e in range(3):
                for k in range(3):
                    taps.append(
                        part[k * channels : (k + 1) * channels, e * channels : (e + 1) * channels]
                    )
            while (done + 1) * rows <= len(taps) * channels:
                pieces, row = [], done * rows
                while row < (done + 1) * rows:
                    tap_of, low = divmod(row, channels)
                    high = min(channels, low + (done + 1) * rows - row)
                    pieces.append(taps[tap_of][low:high])
                    row += high - low
                bits = place[1] ^ done
                far, near = bits // 4, bits % 4
                first = jnp.where(place[0] == 0, far, near)
                second = jnp.where(place[0] == 0, near, far)
                shares[second, first] = jnp.concatenate(pieces, axis=0).astype(jnp.bfloat16)
                done += 1

    @pl.when(section == 0)
    def _():
        pad_rows(grads)
        values = [
            upstream[t].astype(jnp.float32) + slope[t] * frame_of((other_low, other_high), t)[...].astype(jnp.float32)
            for t in range(frames)
        ]
        place_grads(grads, [value.astype(jnp.bfloat16).astype(jnp.float32) for value in values])
        product(ready, grads)

    @pl.when(section != 0)
    def _():
        for t in range(frames):
            squashed = silu_of(frame_of((other_low, other_high), t)[...].astype(jnp.float32)).astype(jnp.bfloat16)
            for k, piece in enumerate(column_shifts(squashed.astype(jnp.float32), width)):
                turn_into(turned, k, t, piece)
        product(turned, moved)


def third_body(place, *refs):
    blocks = refs[:4]
    mine, other, (produced, table, shifted) = refs[4:6], refs[6:8], refs[8:]
    micro, frames, height, width, channels = produced.shape
    flat = micro * width
    section = place[0]

    def hand_out(t, cells):
        for m in range(micro):
            produced[m, t] = cells[:, m * width : (m + 1) * width, :].astype(jnp.bfloat16)

    @pl.when(section == 0)
    def _():
        for t in range(frames):
            hand_out(t, frame_of(mine, t)[...].astype(jnp.float32))

    @pl.when(section != 0)
    def _():
        unpack_weights(place, blocks, table)
        zero_row = jnp.zeros((3, frames, 1, flat, channels), jnp.bfloat16)
        shifted[:, :, :1] = zero_row
        shifted[:, :, height + 1 :] = zero_row
        for t in range(frames):
            squashed = silu_of(frame_of(other, t)[...].astype(jnp.float32)).astype(jnp.bfloat16)
            for k, piece in enumerate(column_shifts(squashed.astype(jnp.float32), width)):
                shifted[k, t, 1 : height + 1] = piece
        branch = forward_product(shifted, forward_weights(table, channels), frames, height)
        for t in range(frames):
            hand_out(t, frame_of(other, t)[...].astype(jnp.float32) + branch[t].reshape(height, flat, channels))


def paired_sections(clips, cotangent, weights):
    dp_total = lax.axis_size("dp")
    local_clips, local_grads, shard = clips[:, 0], cotangent[:, 0], weights[0]
    micro, frames, height, width, channels = local_clips.shape
    rows = shard.shape[0]
    flat = micro * width
    cells = height * flat
    place = jnp.stack([lax.axis_index("section"), lax.axis_index("dp")]).astype(jnp.int32)

    def traded(block, along_z, step):
        bits = (4 * step, step) if along_z else (step, 4 * step)
        route = [
            (s * dp_total + i, s * dp_total + (i ^ bits[s])) for s in range(2) for i in range(dp_total)
        ]
        return lax.ppermute(block, ("section", "dp"), route)

    field = (frames, height, flat, channels)
    padded = (3, frames, height + 2, flat, channels)
    met = (frames + 2, height + 2, flat, channels)
    bf16, f32 = jnp.bfloat16, jnp.float32
    unit = 2 * micro * frames * height * width * channels * channels * 27

    first = [traded(shard, True, step) for step in range(1, 4)]
    (shard_copy,) = call(copy_body, (shard,), [(shard.shape, bf16)], [], unit // 16, place)
    shard_copy, first = lax.optimization_barrier((shard_copy, first))
    line = jnp.stack([shard_copy] + first)
    blocks = (line, *[traded(line, False, step) for step in range(1, 4)])

    turned = (3 * channels, frames * cells)
    shifted, base, upstream, ready = call(
        prepare_body,
        (local_clips, local_grads),
        [(padded, bf16), (field, bf16), (field, bf16), (turned, bf16)],
        [
            pltpu.VMEM(field, f32),
            pltpu.VMEM(local_clips.shape, bf16),
            pltpu.VMEM(local_clips.shape, bf16),
            pltpu.SemaphoreType.DMA((2,)),
        ],
        unit // 8,
        place,
        far=True,
    )
    table = pltpu.VMEM((dp_total * rows, channels), f32)
    half = (frames // 2, height, flat, channels)
    mine = call(first_body, blocks + (shifted, base), [(half, bf16)] * 2, [table], unit, place)
    other = [lax.ppermute(part, "section", [(0, 1), (1, 0)]) for part in mine]
    slope, moved = call(
        between_body, (*mine, upstream), [(field, f32), (met, bf16)], [], unit // 8, place
    )
    slope, moved, other = lax.optimization_barrier((slope, moved, other))
    (shares,) = call(
        functools.partial(second_body, width),
        (ready, slope, moved, *other, upstream),
        [((4, 4, rows, channels), bf16)],
        [pltpu.VMEM(turned, bf16), pltpu.VMEM(met, bf16)],
        unit,
        place,
    )
    (produced,) = call(
        third_body,
        blocks + (*mine, *other),
        [(local_clips.shape, bf16)],
        [table, pltpu.VMEM(padded, bf16)],
        unit,
        place,
    )

    def added(*terms):
        return summed([term.astype(f32) for term in terms])

    received = [traded(shares[step], False, step) for step in (1, 2, 3)]
    received, produced = lax.optimization_barrier((received, produced))
    line_sum = added(shares[0, 1:], *[block[1:] for block in received]).astype(bf16)
    own_sum = added(shares[0, 0], *[block[0] for block in received])
    total = added(own_sum, *[traded(line_sum[step - 1], True, step) for step in (3, 2, 1)])
    return (produced[None, :, None], total[None])


def solution(mesh):
    dp_total = mesh.shape["dp"]
    paired = mesh.shape["section"] == 2 and dp_total == 16
    placed = (
        P(None, "dp", None, None, None, None),
        P(None, "dp", None, None, None, None),
        P("section", "dp", None),
    )
    return jax.shard_map(
        paired_sections if paired else many_sections,
        mesh=mesh,
        in_specs=placed,
        out_specs=(P("section", None, "dp", None, None, None, None), P("section", "dp", None)),
        check_vma=False,
    )
```

```python
import functools

import jax
import jax.numpy as jnp
from jax import lax
from jax.experimental import pallas as pl
from jax.experimental.pallas import tpu as pltpu
from jax.sharding import PartitionSpec as P


def passed_along(block, axis, distance):
    devices = range(lax.axis_size(axis))
    route = [(i - distance, i) for i in devices if i - distance in devices]
    return lax.ppermute(block, axis, route)


def gather_patches(field):
    frames, height, width, channels = field.shape
    first_frame = field[:1]
    padded = jnp.concatenate([first_frame, first_frame, field], axis=0)
    padded = jnp.pad(padded, ((0, 0), (1, 1), (1, 1), (0, 0)))
    pieces = [
        padded[
            offset_time : offset_time + frames,
            offset_row : offset_row + height,
            offset_col : offset_col + width,
        ]
        for offset_time in range(3)
        for offset_row in range(3)
        for offset_col in range(3)
    ]
    return jnp.stack(pieces, axis=3).reshape(frames * height * width, 27 * channels)


def squash_field(activation):
    return jax.nn.silu(activation.astype(jnp.float32)).astype(jnp.bfloat16)


def squash_columns(activation):
    return gather_patches(squash_field(activation))


def layer_forward(activation, weight):
    branch = jnp.dot(squash_columns(activation), weight, preferred_element_type=jnp.float32)
    return (activation.astype(jnp.float32) + branch.reshape(activation.shape)).astype(jnp.bfloat16)


def input_gradient(activation, upstream, weight):
    flat_grad = upstream.reshape(-1, weight.shape[1])
    column_grad = lax.dot_general(
        flat_grad, weight, (((1,), (1,)), ((), ())), preferred_element_type=jnp.float32
    )
    base = activation.astype(jnp.float32)
    _, unfold = jax.vjp(gather_patches, base)
    field_grad = unfold(column_grad)[0]
    sigmoid_value = jax.nn.sigmoid(base)
    slope = sigmoid_value * (1.0 + base * (1.0 - sigmoid_value))
    return (upstream.astype(jnp.float32) + field_grad * slope).astype(jnp.bfloat16)


def weight_term(activation, upstream):
    flat_grad = upstream.reshape(-1, upstream.shape[-1])
    return lax.dot_general(
        squash_columns(activation),
        flat_grad,
        (((0,), (0,)), ((), ())),
        preferred_element_type=jnp.float32,
    )


def many_sections(clips, cotangent, weights):
    section_total = lax.axis_size("section")
    section_index = lax.axis_index("section")
    weight = lax.all_gather(weights, "dp", axis=1, tiled=True)[0]
    local_clips = clips[:, 0]
    local_grads = cotangent[:, 0]
    micro_count = local_clips.shape[0]
    step_count = micro_count + section_total - 1
    empty_field = jnp.zeros(local_clips.shape[1:], jnp.bfloat16)

    def forward_step(step_index, carry):
        received, saved_inputs, produced = carry
        micro_index = step_index - section_index
        active = (micro_index >= 0) & (micro_index < micro_count)
        slot_index = jnp.clip(micro_index, 0, micro_count - 1)
        fresh = lax.dynamic_index_in_dim(local_clips, slot_index, 0, keepdims=False)
        layer_input = jnp.where(section_index == 0, fresh, received)
        layer_output = layer_forward(layer_input, weight)
        kept_input = jnp.where(
            active,
            layer_input,
            lax.dynamic_index_in_dim(saved_inputs, slot_index, 0, keepdims=False),
        )
        kept_output = jnp.where(
            active, layer_output, lax.dynamic_index_in_dim(produced, slot_index, 0, keepdims=False)
        )
        saved_inputs = lax.dynamic_update_index_in_dim(saved_inputs, kept_input, slot_index, 0)
        produced = lax.dynamic_update_index_in_dim(produced, kept_output, slot_index, 0)
        received = passed_along(layer_output, "section", 1)
        return (received, saved_inputs, produced)

    start_forward = (empty_field, jnp.zeros_like(local_clips), jnp.zeros_like(local_clips))
    _, saved_inputs, produced = lax.fori_loop(0, step_count, forward_step, start_forward)

    def backward_step(step_index, carry):
        received, grad_total, kept_grads = carry
        micro_index = step_index - (section_total - 1 - section_index)
        active = (micro_index >= 0) & (micro_index < micro_count)
        slot_index = jnp.clip(micro_index, 0, micro_count - 1)
        fresh = lax.dynamic_index_in_dim(local_grads, slot_index, 0, keepdims=False)
        upstream = jnp.where(section_index == section_total - 1, fresh, received)
        activation = lax.dynamic_index_in_dim(saved_inputs, slot_index, 0, keepdims=False)
        grad_total = grad_total + jnp.where(active, weight_term(activation, upstream), 0.0)
        layer_grad = input_gradient(activation, upstream, weight)
        received = passed_along(layer_grad, "section", -1)
        return (received, grad_total, kept_grads)

    start_backward = (
        empty_field,
        jnp.zeros(weight.shape, jnp.float32),
        jnp.zeros_like(local_grads),
    )
    _, grad_total, kept_grads = lax.fori_loop(0, step_count, backward_step, start_backward)
    grad_share = lax.psum_scatter(
        grad_total.astype(jnp.bfloat16), "dp", scatter_dimension=0, tiled=True
    ).astype(jnp.float32)
    return (produced[None, :, None], grad_share[None])


def summed(terms):
    return functools.reduce(lambda p, q: p + q, terms)


def frame_of(halves, t):
    return halves[t // halves[0].shape[0]].at[t % halves[0].shape[0]]


def silu_of(value):
    return value * jax.nn.sigmoid(value)


def slope_of(value):
    sigmoid_value = jax.nn.sigmoid(value)
    return sigmoid_value * (1.0 + value * (1.0 - sigmoid_value))


def column_shifts(rows, width):
    height, flat, channels = rows.shape
    cells = rows.reshape(height * flat // width, width, channels)
    column = lax.broadcasted_iota(jnp.int32, cells.shape, 1)
    before = jnp.where(column == 0, 0.0, pltpu.roll(cells, 1, 1))
    after = jnp.where(column == width - 1, 0.0, pltpu.roll(cells, width - 1, 1))
    return [piece.reshape(rows.shape).astype(jnp.bfloat16) for piece in (before, cells, after)]


def whole(count):
    return [pl.BlockSpec(memory_space=pltpu.VMEM)] * count


def call(body, inputs, outputs, scratch, flops, far=False):
    return pl.pallas_call(
        body,
        out_shape=[jax.ShapeDtypeStruct(shape, dtype) for shape, dtype in outputs],
        in_specs=[pl.BlockSpec(memory_space=pl.ANY)] * len(inputs) if far else whole(len(inputs)),
        out_specs=whole(len(outputs)),
        scratch_shapes=scratch,
        compiler_params=pltpu.CompilerParams(vmem_limit_bytes=32 * 1024 * 1024),
        cost_estimate=pl.CostEstimate(flops=flops, bytes_accessed=4_000_000, transcendentals=0),
    )(*inputs)


def turn_into(turned, k, t, piece):
    channels = piece.shape[-1]
    flat = piece.reshape(-1, channels)
    cells = flat.shape[0]
    turned[k * channels : (k + 1) * channels, t * cells : (t + 1) * cells] = flat.T


def pad_rows(grads):
    count, padded_height, flat, channels = grads.shape
    zero_row = jnp.zeros((count, 1, flat, channels), jnp.bfloat16)
    grads[:, :1] = zero_row
    grads[:, padded_height - 1 :] = zero_row


def place_grads(grads, fields):
    height = fields[0].shape[0]
    first_two = fields[0] + fields[1]
    for t, field in enumerate((*fields, first_two, first_two + fields[2])):
        grads[t, 1 : height + 1] = field.astype(jnp.bfloat16)


def copy_body(source, target):
    target[...] = source[...]


def prepare_body(clips_far, cotangent_far, *refs):
    shifted, base, upstream, ready, held, clips, cotangent, sems = refs
    micro, frames, height, width, channels = clips.shape
    section = lax.axis_index("section")
    copies = [
        pltpu.make_async_copy(source, target, sems.at[k])
        for k, (source, target) in enumerate(
            ((clips_far, clips), (cotangent_far, cotangent))
        )
    ]
    for copy in copies:
        copy.start()

    def reorder(source, target):
        for m in range(micro):
            held[:, :, m * width : (m + 1) * width, :] = source[m].astype(jnp.float32)
        for t in range(frames):
            target[t] = held[t].astype(jnp.bfloat16)

    zero_row = jnp.zeros((3, frames, 1) + shifted.shape[3:], jnp.bfloat16)
    shifted[:, :, :1] = zero_row
    shifted[:, :, height + 1 :] = zero_row
    copies[0].wait()
    reorder(clips, base)
    copies[1].wait()
    reorder(cotangent, upstream)

    @pl.when(section == 0)
    def _():
        for t in range(frames):
            squashed = silu_of(base[t].astype(jnp.float32)).astype(jnp.bfloat16)
            for k, piece in enumerate(column_shifts(squashed.astype(jnp.float32), width)):
                shifted[k, t, 1 : height + 1] = piece
                turn_into(ready, k, t, piece)

    @pl.when(section != 0)
    def _():
        for t in range(frames):
            for k, piece in enumerate(column_shifts(upstream[t].astype(jnp.float32), width)):
                shifted[k, t, 1 : height + 1] = piece


def shard_rows(rows, first, second):
    section, index = lax.axis_index("section"), lax.axis_index("dp")
    far, near = jnp.where(section == 0, first, second), jnp.where(section == 0, second, first)
    return pl.ds(pl.multiple_of((index ^ (4 * far + near)) * rows, 8), rows)


def unpack_weights(blocks, table):
    rows = blocks[0].shape[1]
    for second in range(4):
        for first in range(4):
            shard = blocks[second][first]
            table[shard_rows(rows, first, second), :] = shard.astype(jnp.float32)


def forward_weights(table, channels):
    rows = 9 * channels
    return jnp.concatenate(
        [table[t * rows : (t + 1) * rows, :].astype(jnp.bfloat16) for t in range(3)], axis=1
    )


def backward_weights(table, channels):
    def turned_taps(times):
        blocks = []
        for k in reversed(range(9)):
            rows = [table[(t * 9 + k) * channels : (t * 9 + k + 1) * channels, :] for t in times]
            blocks.append(summed(rows).astype(jnp.bfloat16))
        return jnp.concatenate(blocks, axis=1)

    return [turned_taps(times) for times in ((0,), (1,), (2,), (0, 1), (0, 1, 2))]


def row_patches(shifted, start, count, height):
    flat, channels = shifted.shape[3:]
    return jnp.concatenate(
        [
            shifted[k, start : start + count, e : e + height].reshape(count * height * flat, channels)
            for e in range(3)
            for k in range(3)
        ],
        axis=1,
    )


def forward_product(shifted, weights, frames, height):
    channels = shifted.shape[-1]
    cells = height * shifted.shape[-2]
    pieces = {}
    for start, count, first_tap in ((0, frames - 2, 0), (frames - 2, 1, 1), (frames - 1, 1, 2)):
        part = jnp.dot(
            row_patches(shifted, start, count, height),
            weights[:, first_tap * channels :],
            preferred_element_type=jnp.float32,
        )
        for t in range(start, start + count):
            rows = slice((t - start) * cells, (t - start + 1) * cells)
            for tap in range(first_tap, 3):
                columns = slice((tap - first_tap) * channels, (tap - first_tap + 1) * channels)
                pieces[t, tap] = part[rows, columns]
    return [
        summed([pieces[max(t + tap - 2, 0), tap] for tap in range(3)]) for t in range(frames)
    ]


def backward_product(shifted, weights, frames, height):
    channels = shifted.shape[-1]
    cells = height * shifted.shape[-2]
    first, second, third, first_two, all_three = weights
    plan = (
        (2, frames - 2, ((first, -2), (second, -1), (third, 0))),
        (1, 1, ((third, 0), (first_two, -1))),
        (0, 1, ((all_three, 0),)),
    )
    reaching = [[] for _ in range(frames)]
    for start, count, terms in plan:
        part = lax.dot_general(
            row_patches(shifted, start, count, height),
            jnp.concatenate([weight for weight, _ in terms], axis=0),
            (((1,), (1,)), ((), ())),
            preferred_element_type=jnp.float32,
        )
        for t in range(start, start + count):
            rows = slice((t - start) * cells, (t - start + 1) * cells)
            for column, (_, step) in enumerate(terms):
                reaching[t + step].append(part[rows, column * channels : (column + 1) * channels])
    return [summed(terms) for terms in reaching]


def first_body(*refs):
    blocks = refs[:4]
    shifted, base, *results, table = refs[4:]
    frames, height, flat, channels = base.shape
    section = lax.axis_index("section")
    unpack_weights(blocks, table)

    @pl.when(section == 0)
    def _():
        branch = forward_product(shifted, forward_weights(table, channels), frames, height)
        for t in range(frames):
            total = base[t].astype(jnp.float32) + branch[t].reshape(height, flat, channels)
            frame_of(results, t)[...] = total.astype(jnp.bfloat16)

    @pl.when(section != 0)
    def _():
        branch = backward_product(shifted, backward_weights(table, channels), frames, height)
        for t in range(frames):
            frame_of(results, t)[...] = branch[t].reshape(height, flat, channels).astype(jnp.bfloat16)


def between_body(mine_low, mine_high, upstream, slope, grads):
    frames = upstream.shape[0]

    @pl.when(lax.axis_index("section") == 0)
    def _():
        for t in range(frames):
            slope[t] = slope_of(frame_of((mine_low, mine_high), t)[...].astype(jnp.float32))

    @pl.when(lax.axis_index("section") != 0)
    def _():
        pad_rows(grads)
        place_grads(grads, [upstream[t].astype(jnp.float32) for t in range(frames)])


def second_body(width, ready, slope, moved, other_low, other_high, upstream, *refs):
    shares, turned, grads = refs
    frames, height, flat, channels = upstream.shape
    rows = shares.shape[2]
    section = lax.axis_index("section")
    cells = height * flat

    def product(left, right):
        taps, done = [], 0
        for met in ((frames + 1, 3), (frames, 2, 3), (0, 1, 2, 3)):
            columns = jnp.concatenate(
                [
                    jnp.concatenate(
                        [
                            right[f, 2 - e : 2 - e + height].reshape(cells, channels)
                            for e in range(3)
                        ],
                        axis=1,
                    )
                    for f in met
                ],
                axis=0,
            )
            part = jnp.dot(
                left[:, : len(met) * cells], columns, preferred_element_type=jnp.float32
            )
            for e in range(3):
                for k in range(3):
                    taps.append(
                        part[k * channels : (k + 1) * channels, e * channels : (e + 1) * channels]
                    )
            while (done + 1) * rows <= len(taps) * channels:
                pieces, row = [], done * rows
                while row < (done + 1) * rows:
                    tap_of, low = divmod(row, channels)
                    high = min(channels, low + (done + 1) * rows - row)
                    pieces.append(taps[tap_of][low:high])
                    row += high - low
                bits = lax.axis_index("dp") ^ done
                far, near = bits // 4, bits % 4
                first = jnp.where(section == 0, far, near)
                second = jnp.where(section == 0, near, far)
                shares[second, first] = jnp.concatenate(pieces, axis=0).astype(jnp.bfloat16)
                done += 1

    @pl.when(section == 0)
    def _():
        pad_rows(grads)
        values = [
            upstream[t].astype(jnp.float32) + slope[t] * frame_of((other_low, other_high), t)[...].astype(jnp.float32)
            for t in range(frames)
        ]
        place_grads(grads, [value.astype(jnp.bfloat16).astype(jnp.float32) for value in values])
        product(ready, grads)

    @pl.when(section != 0)
    def _():
        for t in range(frames):
            squashed = silu_of(frame_of((other_low, other_high), t)[...].astype(jnp.float32)).astype(jnp.bfloat16)
            for k, piece in enumerate(column_shifts(squashed.astype(jnp.float32), width)):
                turn_into(turned, k, t, piece)
        product(turned, moved)


def third_body(*refs):
    blocks = refs[:4]
    mine, other, (produced, table, shifted) = refs[4:6], refs[6:8], refs[8:]
    micro, frames, height, width, channels = produced.shape
    flat = micro * width
    section = lax.axis_index("section")

    def hand_out(t, cells):
        for m in range(micro):
            produced[m, t] = cells[:, m * width : (m + 1) * width, :].astype(jnp.bfloat16)

    @pl.when(section == 0)
    def _():
        for t in range(frames):
            hand_out(t, frame_of(mine, t)[...].astype(jnp.float32))

    @pl.when(section != 0)
    def _():
        unpack_weights(blocks, table)
        zero_row = jnp.zeros((3, frames, 1, flat, channels), jnp.bfloat16)
        shifted[:, :, :1] = zero_row
        shifted[:, :, height + 1 :] = zero_row
        for t in range(frames):
            squashed = silu_of(frame_of(other, t)[...].astype(jnp.float32)).astype(jnp.bfloat16)
            for k, piece in enumerate(column_shifts(squashed.astype(jnp.float32), width)):
                shifted[k, t, 1 : height + 1] = piece
        branch = forward_product(shifted, forward_weights(table, channels), frames, height)
        for t in range(frames):
            hand_out(t, frame_of(other, t)[...].astype(jnp.float32) + branch[t].reshape(height, flat, channels))


def paired_sections(clips, cotangent, weights):
    dp_total = lax.axis_size("dp")
    local_clips, local_grads, shard = clips[:, 0], cotangent[:, 0], weights[0]
    micro, frames, height, width, channels = local_clips.shape
    rows = shard.shape[0]
    flat = micro * width
    cells = height * flat

    def traded(block, along_z, step):
        bits = (4 * step, step) if along_z else (step, 4 * step)
        route = [
            (s * dp_total + i, s * dp_total + (i ^ bits[s])) for s in range(2) for i in range(dp_total)
        ]
        return lax.ppermute(block, ("section", "dp"), route)

    field = (frames, height, flat, channels)
    padded = (3, frames, height + 2, flat, channels)
    met = (frames + 2, height + 2, flat, channels)
    bf16, f32 = jnp.bfloat16, jnp.float32
    unit = 2 * micro * frames * height * width * channels * channels * 27

    first = [traded(shard, True, step) for step in range(1, 4)]
    (shard_copy,) = call(copy_body, (shard,), [(shard.shape, bf16)], [], unit // 16)
    shard_copy, first = lax.optimization_barrier((shard_copy, first))
    line = jnp.stack([shard_copy] + first)
    blocks = (line, *[traded(line, False, step) for step in range(1, 4)])

    turned = (3 * channels, frames * cells)
    shifted, base, upstream, ready = call(
        prepare_body,
        (local_clips, local_grads),
        [(padded, bf16), (field, bf16), (field, bf16), (turned, bf16)],
        [
            pltpu.VMEM(field, f32),
            pltpu.VMEM(local_clips.shape, bf16),
            pltpu.VMEM(local_clips.shape, bf16),
            pltpu.SemaphoreType.DMA((2,)),
        ],
        unit // 8,
        far=True,
    )
    table = pltpu.VMEM((dp_total * rows, channels), f32)
    half = (frames // 2, height, flat, channels)
    mine = call(first_body, blocks + (shifted, base), [(half, bf16)] * 2, [table], unit)
    other = [lax.ppermute(part, "section", [(0, 1), (1, 0)]) for part in mine]
    slope, moved = call(
        between_body, (*mine, upstream), [(field, f32), (met, bf16)], [], unit // 8
    )
    slope, moved, other = lax.optimization_barrier((slope, moved, other))
    (shares,) = call(
        functools.partial(second_body, width),
        (ready, slope, moved, *other, upstream),
        [((4, 4, rows, channels), bf16)],
        [pltpu.VMEM(turned, bf16), pltpu.VMEM(met, bf16)],
        unit,
    )
    (produced,) = call(
        third_body,
        blocks + (*mine, *other),
        [(local_clips.shape, bf16)],
        [table, pltpu.VMEM(padded, bf16)],
        unit,
    )

    def added(*terms):
        return summed([term.astype(f32) for term in terms])

    received = [traded(shares[step], False, step) for step in (1, 2, 3)]
    received, produced = lax.optimization_barrier((received, produced))
    line_sum = added(shares[0, 1:], *[block[1:] for block in received]).astype(bf16)
    own_sum = added(shares[0, 0], *[block[0] for block in received])
    total = added(own_sum, *[traded(line_sum[step - 1], True, step) for step in (3, 2, 1)])
    return (produced[None, :, None], total[None])


def solution(mesh):
    dp_total = mesh.shape["dp"]
    paired = mesh.shape["section"] == 2 and dp_total == 16
    placed = (
        P(None, "dp", None, None, None, None),
        P(None, "dp", None, None, None, None),
        P("section", "dp", None),
    )
    return jax.shard_map(
        paired_sections if paired else many_sections,
        mesh=mesh,
        in_specs=placed,
        out_specs=(P("section", None, "dp", None, None, None, None), P("section", "dp", None)),
        check_vma=False,
    )
```

```python
import functools

import jax
import jax.numpy as jnp
from jax import lax
from jax.experimental import pallas as pl
from jax.experimental.pallas import tpu as pltpu
from jax.sharding import PartitionSpec as P


def passed_along(block, axis, distance):
    devices = range(lax.axis_size(axis))
    route = [(i - distance, i) for i in devices if i - distance in devices]
    return lax.ppermute(block, axis, route)


def gather_patches(field):
    frames, height, width, channels = field.shape
    first_frame = field[:1]
    padded = jnp.concatenate([first_frame, first_frame, field], axis=0)
    padded = jnp.pad(padded, ((0, 0), (1, 1), (1, 1), (0, 0)))
    pieces = [
        padded[
            offset_time : offset_time + frames,
            offset_row : offset_row + height,
            offset_col : offset_col + width,
        ]
        for offset_time in range(3)
        for offset_row in range(3)
        for offset_col in range(3)
    ]
    return jnp.stack(pieces, axis=3).reshape(frames * height * width, 27 * channels)


def squash_field(activation):
    return jax.nn.silu(activation.astype(jnp.float32)).astype(jnp.bfloat16)


def squash_columns(activation):
    return gather_patches(squash_field(activation))


def layer_forward(activation, weight):
    branch = jnp.dot(squash_columns(activation), weight, preferred_element_type=jnp.float32)
    return (activation.astype(jnp.float32) + branch.reshape(activation.shape)).astype(jnp.bfloat16)


def input_gradient(activation, upstream, weight):
    flat_grad = upstream.reshape(-1, weight.shape[1])
    column_grad = lax.dot_general(
        flat_grad, weight, (((1,), (1,)), ((), ())), preferred_element_type=jnp.float32
    )
    base = activation.astype(jnp.float32)
    _, unfold = jax.vjp(gather_patches, base)
    field_grad = unfold(column_grad)[0]
    sigmoid_value = jax.nn.sigmoid(base)
    slope = sigmoid_value * (1.0 + base * (1.0 - sigmoid_value))
    return (upstream.astype(jnp.float32) + field_grad * slope).astype(jnp.bfloat16)


def weight_term(activation, upstream):
    flat_grad = upstream.reshape(-1, upstream.shape[-1])
    return lax.dot_general(
        squash_columns(activation),
        flat_grad,
        (((0,), (0,)), ((), ())),
        preferred_element_type=jnp.float32,
    )


def many_sections(clips, cotangent, weights):
    section_total = lax.axis_size("section")
    section_index = lax.axis_index("section")
    weight = lax.all_gather(weights, "dp", axis=1, tiled=True)[0]
    local_clips = clips[:, 0]
    local_grads = cotangent[:, 0]
    micro_count = local_clips.shape[0]
    step_count = micro_count + section_total - 1
    empty_field = jnp.zeros(local_clips.shape[1:], jnp.bfloat16)

    def forward_step(step_index, carry):
        received, saved_inputs, produced = carry
        micro_index = step_index - section_index
        active = (micro_index >= 0) & (micro_index < micro_count)
        slot_index = jnp.clip(micro_index, 0, micro_count - 1)
        fresh = lax.dynamic_index_in_dim(local_clips, slot_index, 0, keepdims=False)
        layer_input = jnp.where(section_index == 0, fresh, received)
        layer_output = layer_forward(layer_input, weight)
        kept_input = jnp.where(
            active,
            layer_input,
            lax.dynamic_index_in_dim(saved_inputs, slot_index, 0, keepdims=False),
        )
        kept_output = jnp.where(
            active, layer_output, lax.dynamic_index_in_dim(produced, slot_index, 0, keepdims=False)
        )
        saved_inputs = lax.dynamic_update_index_in_dim(saved_inputs, kept_input, slot_index, 0)
        produced = lax.dynamic_update_index_in_dim(produced, kept_output, slot_index, 0)
        received = passed_along(layer_output, "section", 1)
        return (received, saved_inputs, produced)

    start_forward = (empty_field, jnp.zeros_like(local_clips), jnp.zeros_like(local_clips))
    _, saved_inputs, produced = lax.fori_loop(0, step_count, forward_step, start_forward)

    def backward_step(step_index, carry):
        received, grad_total, kept_grads = carry
        micro_index = step_index - (section_total - 1 - section_index)
        active = (micro_index >= 0) & (micro_index < micro_count)
        slot_index = jnp.clip(micro_index, 0, micro_count - 1)
        fresh = lax.dynamic_index_in_dim(local_grads, slot_index, 0, keepdims=False)
        upstream = jnp.where(section_index == section_total - 1, fresh, received)
        activation = lax.dynamic_index_in_dim(saved_inputs, slot_index, 0, keepdims=False)
        grad_total = grad_total + jnp.where(active, weight_term(activation, upstream), 0.0)
        layer_grad = input_gradient(activation, upstream, weight)
        received = passed_along(layer_grad, "section", -1)
        return (received, grad_total, kept_grads)

    start_backward = (
        empty_field,
        jnp.zeros(weight.shape, jnp.float32),
        jnp.zeros_like(local_grads),
    )
    _, grad_total, kept_grads = lax.fori_loop(0, step_count, backward_step, start_backward)
    grad_share = lax.psum_scatter(
        grad_total.astype(jnp.bfloat16), "dp", scatter_dimension=0, tiled=True
    ).astype(jnp.float32)
    return (produced[None, :, None], grad_share[None])


def summed(terms):
    return functools.reduce(lambda p, q: p + q, terms)


def frame_of(halves, t):
    return halves[t // halves[0].shape[0]].at[t % halves[0].shape[0]]


def silu_of(value):
    return value * jax.nn.sigmoid(value)


def slope_of(value):
    sigmoid_value = jax.nn.sigmoid(value)
    return sigmoid_value * (1.0 + value * (1.0 - sigmoid_value))


def column_shifts(rows, width):
    height, flat, channels = rows.shape
    cells = rows.reshape(height * flat // width, width, channels)
    column = lax.broadcasted_iota(jnp.int32, cells.shape, 1)
    before = jnp.where(column == 0, 0.0, pltpu.roll(cells, 1, 1))
    after = jnp.where(column == width - 1, 0.0, pltpu.roll(cells, width - 1, 1))
    return [piece.reshape(rows.shape).astype(jnp.bfloat16) for piece in (before, cells, after)]


def whole(count):
    return [pl.BlockSpec(memory_space=pltpu.VMEM)] * count


def call(body, inputs, outputs, scratch, flops, far=False, aliases=None):
    return pl.pallas_call(
        body,
        out_shape=[jax.ShapeDtypeStruct(shape, dtype) for shape, dtype in outputs],
        in_specs=[pl.BlockSpec(memory_space=pl.ANY)] * len(inputs) if far else whole(len(inputs)),
        out_specs=whole(len(outputs)),
        scratch_shapes=scratch,
        input_output_aliases=aliases or {},
        compiler_params=pltpu.CompilerParams(vmem_limit_bytes=32 * 1024 * 1024),
        cost_estimate=pl.CostEstimate(flops=flops, bytes_accessed=4_000_000, transcendentals=0),
    )(*inputs)


def turn_into(turned, k, t, piece):
    channels = piece.shape[-1]
    flat = piece.reshape(-1, channels)
    cells = flat.shape[0]
    turned[k * channels : (k + 1) * channels, t * cells : (t + 1) * cells] = flat.T


def pad_rows(grads):
    count, padded_height, flat, channels = grads.shape
    zero_row = jnp.zeros((count, 1, flat, channels), jnp.bfloat16)
    grads[:, :1] = zero_row
    grads[:, padded_height - 1 :] = zero_row


def place_grads(grads, fields):
    height = fields[0].shape[0]
    first_two = fields[0] + fields[1]
    for t, field in enumerate((*fields, first_two, first_two + fields[2])):
        grads[t, 1 : height + 1] = field.astype(jnp.bfloat16)


def copy_body(source, target):
    target[...] = source[...]


def prepare_body(clips_far, cotangent_far, *refs):
    shifted, base, upstream, ready, held, clips, cotangent, sems = refs
    micro, frames, height, width, channels = clips.shape
    section = lax.axis_index("section")
    copies = [
        pltpu.make_async_copy(source, target, sems.at[k])
        for k, (source, target) in enumerate(
            ((clips_far, clips), (cotangent_far, cotangent))
        )
    ]
    for copy in copies:
        copy.start()

    def reorder(source, target):
        for m in range(micro):
            held[:, :, m * width : (m + 1) * width, :] = source[m].astype(jnp.float32)
        for t in range(frames):
            target[t] = held[t].astype(jnp.bfloat16)

    zero_row = jnp.zeros((3, frames, 1) + shifted.shape[3:], jnp.bfloat16)
    shifted[:, :, :1] = zero_row
    shifted[:, :, height + 1 :] = zero_row
    copies[0].wait()
    reorder(clips, base)
    copies[1].wait()
    reorder(cotangent, upstream)

    @pl.when(section == 0)
    def _():
        for t in range(frames):
            squashed = silu_of(base[t].astype(jnp.float32)).astype(jnp.bfloat16)
            for k, piece in enumerate(column_shifts(squashed.astype(jnp.float32), width)):
                shifted[k, t, 1 : height + 1] = piece
                turn_into(ready, k, t, piece)

    @pl.when(section != 0)
    def _():
        for t in range(frames):
            for k, piece in enumerate(column_shifts(upstream[t].astype(jnp.float32), width)):
                shifted[k, t, 1 : height + 1] = piece


def shard_rows(rows, first, second):
    section, index = lax.axis_index("section"), lax.axis_index("dp")
    far, near = jnp.where(section == 0, first, second), jnp.where(section == 0, second, first)
    return pl.ds(pl.multiple_of((index ^ (4 * far + near)) * rows, 8), rows)


def put_block(block, second, table):
    for first in range(4):
        rows = shard_rows(block.shape[1], first, second)
        table[rows, :] = block[first].astype(jnp.float32)


def fill_body(second, block, table_before, table):
    put_block(block, second, table)


def start_table_body(block, table):
    put_block(block, 0, table)


def last_sum_body(own, *refs):
    *received, total = refs
    total[...] = summed([own[...]] + [block[...].astype(jnp.float32) for block in received])


def forward_weights(table, channels):
    rows = 9 * channels
    return jnp.concatenate(
        [table[t * rows : (t + 1) * rows, :].astype(jnp.bfloat16) for t in range(3)], axis=1
    )


def backward_weights(table, channels):
    def turned_taps(times):
        blocks = []
        for k in reversed(range(9)):
            rows = [table[(t * 9 + k) * channels : (t * 9 + k + 1) * channels, :] for t in times]
            blocks.append(summed(rows).astype(jnp.bfloat16))
        return jnp.concatenate(blocks, axis=1)

    return [turned_taps(times) for times in ((0,), (1,), (2,), (0, 1), (0, 1, 2))]


def row_patches(shifted, start, count, height):
    flat, channels = shifted.shape[3:]
    return jnp.concatenate(
        [
            shifted[k, start : start + count, e : e + height].reshape(count * height * flat, channels)
            for e in range(3)
            for k in range(3)
        ],
        axis=1,
    )


def forward_product(shifted, weights, frames, height):
    channels = shifted.shape[-1]
    cells = height * shifted.shape[-2]
    pieces = {}
    for start, count, first_tap in ((0, frames - 2, 0), (frames - 2, 1, 1), (frames - 1, 1, 2)):
        part = jnp.dot(
            row_patches(shifted, start, count, height),
            weights[:, first_tap * channels :],
            preferred_element_type=jnp.float32,
        )
        for t in range(start, start + count):
            rows = slice((t - start) * cells, (t - start + 1) * cells)
            for tap in range(first_tap, 3):
                columns = slice((tap - first_tap) * channels, (tap - first_tap + 1) * channels)
                pieces[t, tap] = part[rows, columns]
    return [
        summed([pieces[max(t + tap - 2, 0), tap] for tap in range(3)]) for t in range(frames)
    ]


def backward_product(shifted, weights, frames, height):
    channels = shifted.shape[-1]
    cells = height * shifted.shape[-2]
    first, second, third, first_two, all_three = weights
    plan = (
        (2, frames - 2, ((first, -2), (second, -1), (third, 0))),
        (1, 1, ((third, 0), (first_two, -1))),
        (0, 1, ((all_three, 0),)),
    )
    reaching = [[] for _ in range(frames)]
    for start, count, terms in plan:
        part = lax.dot_general(
            row_patches(shifted, start, count, height),
            jnp.concatenate([weight for weight, _ in terms], axis=0),
            (((1,), (1,)), ((), ())),
            preferred_element_type=jnp.float32,
        )
        for t in range(start, start + count):
            rows = slice((t - start) * cells, (t - start + 1) * cells)
            for column, (_, step) in enumerate(terms):
                reaching[t + step].append(part[rows, column * channels : (column + 1) * channels])
    return [summed(terms) for terms in reaching]


def first_body(*refs):
    last_block, table_before, shifted, base, *results, table = refs
    frames, height, flat, channels = base.shape
    section = lax.axis_index("section")
    put_block(last_block, 1, table)

    @pl.when(section == 0)
    def _():
        branch = forward_product(shifted, forward_weights(table, channels), frames, height)
        for t in range(frames):
            total = base[t].astype(jnp.float32) + branch[t].reshape(height, flat, channels)
            frame_of(results, t)[...] = total.astype(jnp.bfloat16)

    @pl.when(section != 0)
    def _():
        branch = backward_product(shifted, backward_weights(table, channels), frames, height)
        for t in range(frames):
            frame_of(results, t)[...] = branch[t].reshape(height, flat, channels).astype(jnp.bfloat16)


def between_body(mine_low, mine_high, upstream, slope, grads):
    frames = upstream.shape[0]

    @pl.when(lax.axis_index("section") == 0)
    def _():
        for t in range(frames):
            slope[t] = slope_of(frame_of((mine_low, mine_high), t)[...].astype(jnp.float32))

    @pl.when(lax.axis_index("section") != 0)
    def _():
        pad_rows(grads)
        place_grads(grads, [upstream[t].astype(jnp.float32) for t in range(frames)])


def second_body(width, ready, slope, moved, other_low, other_high, upstream, *refs):
    shares, turned, grads = refs
    frames, height, flat, channels = upstream.shape
    rows = shares.shape[2]
    section = lax.axis_index("section")
    cells = height * flat

    def product(left, right):
        taps, done = [], 0
        for met in ((frames + 1, 3), (frames, 2, 3), (0, 1, 2, 3)):
            columns = jnp.concatenate(
                [
                    jnp.concatenate(
                        [
                            right[f, 2 - e : 2 - e + height].reshape(cells, channels)
                            for e in range(3)
                        ],
                        axis=1,
                    )
                    for f in met
                ],
                axis=0,
            )
            part = jnp.dot(
                left[:, : len(met) * cells], columns, preferred_element_type=jnp.float32
            )
            for e in range(3):
                for k in range(3):
                    taps.append(
                        part[k * channels : (k + 1) * channels, e * channels : (e + 1) * channels]
                    )
            while (done + 1) * rows <= len(taps) * channels:
                pieces, row = [], done * rows
                while row < (done + 1) * rows:
                    tap_of, low = divmod(row, channels)
                    high = min(channels, low + (done + 1) * rows - row)
                    pieces.append(taps[tap_of][low:high])
                    row += high - low
                bits = lax.axis_index("dp") ^ done
                far, near = bits // 4, bits % 4
                first = jnp.where(section == 0, far, near)
                second = jnp.where(section == 0, near, far)
                shares[second, first] = jnp.concatenate(pieces, axis=0).astype(jnp.bfloat16)
                done += 1

    @pl.when(section == 0)
    def _():
        pad_rows(grads)
        values = [
            upstream[t].astype(jnp.float32) + slope[t] * frame_of((other_low, other_high), t)[...].astype(jnp.float32)
            for t in range(frames)
        ]
        place_grads(grads, [value.astype(jnp.bfloat16).astype(jnp.float32) for value in values])
        product(ready, grads)

    @pl.when(section != 0)
    def _():
        for t in range(frames):
            squashed = silu_of(frame_of((other_low, other_high), t)[...].astype(jnp.float32)).astype(jnp.bfloat16)
            for k, piece in enumerate(column_shifts(squashed.astype(jnp.float32), width)):
                turn_into(turned, k, t, piece)
        product(turned, moved)


def third_body(*refs):
    table, (produced, shifted) = refs[0], refs[5:]
    mine, other = refs[1:3], refs[3:5]
    micro, frames, height, width, channels = produced.shape
    flat = micro * width
    section = lax.axis_index("section")

    def hand_out(t, cells):
        for m in range(micro):
            produced[m, t] = cells[:, m * width : (m + 1) * width, :].astype(jnp.bfloat16)

    @pl.when(section == 0)
    def _():
        for t in range(frames):
            hand_out(t, frame_of(mine, t)[...].astype(jnp.float32))

    @pl.when(section != 0)
    def _():
        zero_row = jnp.zeros((3, frames, 1, flat, channels), jnp.bfloat16)
        shifted[:, :, :1] = zero_row
        shifted[:, :, height + 1 :] = zero_row
        for t in range(frames):
            squashed = silu_of(frame_of(other, t)[...].astype(jnp.float32)).astype(jnp.bfloat16)
            for k, piece in enumerate(column_shifts(squashed.astype(jnp.float32), width)):
                shifted[k, t, 1 : height + 1] = piece
        branch = forward_product(shifted, forward_weights(table, channels), frames, height)
        for t in range(frames):
            hand_out(t, frame_of(other, t)[...].astype(jnp.float32) + branch[t].reshape(height, flat, channels))


def paired_sections(clips, cotangent, weights):
    dp_total = lax.axis_size("dp")
    local_clips, local_grads, shard = clips[:, 0], cotangent[:, 0], weights[0]
    micro, frames, height, width, channels = local_clips.shape
    rows = shard.shape[0]
    flat = micro * width
    cells = height * flat

    def traded(block, along_z, step):
        bits = (4 * step, step) if along_z else (step, 4 * step)
        route = [
            (s * dp_total + i, s * dp_total + (i ^ bits[s])) for s in range(2) for i in range(dp_total)
        ]
        return lax.ppermute(block, ("section", "dp"), route)

    field = (frames, height, flat, channels)
    padded = (3, frames, height + 2, flat, channels)
    met = (frames + 2, height + 2, flat, channels)
    bf16, f32 = jnp.bfloat16, jnp.float32
    unit = 2 * micro * frames * height * width * channels * channels * 27

    first = [traded(shard, True, step) for step in range(1, 4)]
    (shard_copy,) = call(copy_body, (shard,), [(shard.shape, bf16)], [], unit // 16)
    shard_copy, first = lax.optimization_barrier((shard_copy, first))
    line = jnp.stack([shard_copy] + first)
    blocks = [traded(line, False, step) for step in range(1, 4)]

    turned = (3 * channels, frames * cells)
    shifted, base, upstream, ready = call(
        prepare_body,
        (local_clips, local_grads),
        [(padded, bf16), (field, bf16), (field, bf16), (turned, bf16)],
        [
            pltpu.VMEM(field, f32),
            pltpu.VMEM(local_clips.shape, bf16),
            pltpu.VMEM(local_clips.shape, bf16),
            pltpu.SemaphoreType.DMA((2,)),
        ],
        unit // 8,
        far=True,
    )
    full = ((dp_total * rows, channels), f32)
    (table,) = call(start_table_body, (line,), [full], [], unit // 100)
    for second in (3, 2):
        (table,) = call(
            functools.partial(fill_body, second),
            (blocks[second - 1], table),
            [full],
            [],
            unit // 100,
            aliases={1: 0},
        )
    half = (frames // 2, height, flat, channels)
    *mine, table = call(
        first_body,
        (blocks[0], table, shifted, base),
        [(half, bf16)] * 2 + [full],
        [],
        unit,
        aliases={1: 2},
    )
    other = [lax.ppermute(part, "section", [(0, 1), (1, 0)]) for part in mine]
    slope, moved = call(
        between_body, (*mine, upstream), [(field, f32), (met, bf16)], [], unit // 8
    )
    slope, moved, other = lax.optimization_barrier((slope, moved, other))
    (shares,) = call(
        functools.partial(second_body, width),
        (ready, slope, moved, *other, upstream),
        [((4, 4, rows, channels), bf16)],
        [pltpu.VMEM(turned, bf16), pltpu.VMEM(met, bf16)],
        unit,
    )
    (produced,) = call(
        third_body,
        (table, *mine, *other),
        [(local_clips.shape, bf16)],
        [pltpu.VMEM(padded, bf16)],
        unit,
    )

    def added(*terms):
        return summed([term.astype(f32) for term in terms])

    received = [traded(shares[step], False, step) for step in (1, 2, 3)]
    received, produced = lax.optimization_barrier((received, produced))
    line_sum = added(shares[0, 1:], *[block[1:] for block in received]).astype(bf16)
    own_sum = added(shares[0, 0], *[block[0] for block in received])
    arrived = [traded(line_sum[step - 1], True, step) for step in range(1, 4)]
    (total,) = call(last_sum_body, (own_sum, *arrived), [(own_sum.shape, f32)], [], unit // 100)
    return (produced[None, :, None], total[None])


def solution(mesh):
    dp_total = mesh.shape["dp"]
    paired = mesh.shape["section"] == 2 and dp_total == 16
    placed = (
        P(None, "dp", None, None, None, None),
        P(None, "dp", None, None, None, None),
        P("section", "dp", None),
    )
    return jax.shard_map(
        paired_sections if paired else many_sections,
        mesh=mesh,
        in_specs=placed,
        out_specs=(P("section", None, "dp", None, None, None, None), P("section", "dp", None)),
        check_vma=False,
    )
```

```python
import functools

import jax
import jax.numpy as jnp
from jax import lax
from jax.experimental import pallas as pl
from jax.experimental.pallas import tpu as pltpu
from jax.sharding import PartitionSpec as P


def passed_along(block, axis, distance):
    devices = range(lax.axis_size(axis))
    route = [(i - distance, i) for i in devices if i - distance in devices]
    return lax.ppermute(block, axis, route)


def gather_patches(field):
    frames, height, width, channels = field.shape
    first_frame = field[:1]
    padded = jnp.concatenate([first_frame, first_frame, field], axis=0)
    padded = jnp.pad(padded, ((0, 0), (1, 1), (1, 1), (0, 0)))
    pieces = [
        padded[
            offset_time : offset_time + frames,
            offset_row : offset_row + height,
            offset_col : offset_col + width,
        ]
        for offset_time in range(3)
        for offset_row in range(3)
        for offset_col in range(3)
    ]
    return jnp.stack(pieces, axis=3).reshape(frames * height * width, 27 * channels)


def squash_field(activation):
    return jax.nn.silu(activation.astype(jnp.float32)).astype(jnp.bfloat16)


def squash_columns(activation):
    return gather_patches(squash_field(activation))


def layer_forward(activation, weight):
    branch = jnp.dot(squash_columns(activation), weight, preferred_element_type=jnp.float32)
    return (activation.astype(jnp.float32) + branch.reshape(activation.shape)).astype(jnp.bfloat16)


def input_gradient(activation, upstream, weight):
    flat_grad = upstream.reshape(-1, weight.shape[1])
    column_grad = lax.dot_general(
        flat_grad, weight, (((1,), (1,)), ((), ())), preferred_element_type=jnp.float32
    )
    base = activation.astype(jnp.float32)
    _, unfold = jax.vjp(gather_patches, base)
    field_grad = unfold(column_grad)[0]
    sigmoid_value = jax.nn.sigmoid(base)
    slope = sigmoid_value * (1.0 + base * (1.0 - sigmoid_value))
    return (upstream.astype(jnp.float32) + field_grad * slope).astype(jnp.bfloat16)


def weight_term(activation, upstream):
    flat_grad = upstream.reshape(-1, upstream.shape[-1])
    return lax.dot_general(
        squash_columns(activation),
        flat_grad,
        (((0,), (0,)), ((), ())),
        preferred_element_type=jnp.float32,
    )


def many_sections(clips, cotangent, weights):
    section_total = lax.axis_size("section")
    section_index = lax.axis_index("section")
    weight = lax.all_gather(weights, "dp", axis=1, tiled=True)[0]
    local_clips = clips[:, 0]
    local_grads = cotangent[:, 0]
    micro_count = local_clips.shape[0]
    step_count = micro_count + section_total - 1
    empty_field = jnp.zeros(local_clips.shape[1:], jnp.bfloat16)

    def forward_step(step_index, carry):
        received, saved_inputs, produced = carry
        micro_index = step_index - section_index
        active = (micro_index >= 0) & (micro_index < micro_count)
        slot_index = jnp.clip(micro_index, 0, micro_count - 1)
        fresh = lax.dynamic_index_in_dim(local_clips, slot_index, 0, keepdims=False)
        layer_input = jnp.where(section_index == 0, fresh, received)
        layer_output = layer_forward(layer_input, weight)
        kept_input = jnp.where(
            active,
            layer_input,
            lax.dynamic_index_in_dim(saved_inputs, slot_index, 0, keepdims=False),
        )
        kept_output = jnp.where(
            active, layer_output, lax.dynamic_index_in_dim(produced, slot_index, 0, keepdims=False)
        )
        saved_inputs = lax.dynamic_update_index_in_dim(saved_inputs, kept_input, slot_index, 0)
        produced = lax.dynamic_update_index_in_dim(produced, kept_output, slot_index, 0)
        received = passed_along(layer_output, "section", 1)
        return (received, saved_inputs, produced)

    start_forward = (empty_field, jnp.zeros_like(local_clips), jnp.zeros_like(local_clips))
    _, saved_inputs, produced = lax.fori_loop(0, step_count, forward_step, start_forward)

    def backward_step(step_index, carry):
        received, grad_total, kept_grads = carry
        micro_index = step_index - (section_total - 1 - section_index)
        active = (micro_index >= 0) & (micro_index < micro_count)
        slot_index = jnp.clip(micro_index, 0, micro_count - 1)
        fresh = lax.dynamic_index_in_dim(local_grads, slot_index, 0, keepdims=False)
        upstream = jnp.where(section_index == section_total - 1, fresh, received)
        activation = lax.dynamic_index_in_dim(saved_inputs, slot_index, 0, keepdims=False)
        grad_total = grad_total + jnp.where(active, weight_term(activation, upstream), 0.0)
        layer_grad = input_gradient(activation, upstream, weight)
        received = passed_along(layer_grad, "section", -1)
        return (received, grad_total, kept_grads)

    start_backward = (
        empty_field,
        jnp.zeros(weight.shape, jnp.float32),
        jnp.zeros_like(local_grads),
    )
    _, grad_total, kept_grads = lax.fori_loop(0, step_count, backward_step, start_backward)
    grad_share = lax.psum_scatter(
        grad_total.astype(jnp.bfloat16), "dp", scatter_dimension=0, tiled=True
    ).astype(jnp.float32)
    return (produced[None, :, None], grad_share[None])


def summed(terms):
    return functools.reduce(lambda p, q: p + q, terms)


def frame_of(halves, t):
    return halves[t // halves[0].shape[0]].at[t % halves[0].shape[0]]


def silu_of(value):
    return value * jax.nn.sigmoid(value)


def slope_of(value):
    sigmoid_value = jax.nn.sigmoid(value)
    return sigmoid_value * (1.0 + value * (1.0 - sigmoid_value))


def column_shifts(rows, width):
    height, flat, channels = rows.shape
    cells = rows.reshape(height * flat // width, width, channels)
    column = lax.broadcasted_iota(jnp.int32, cells.shape, 1)
    before = jnp.where(column == 0, 0.0, pltpu.roll(cells, 1, 1))
    after = jnp.where(column == width - 1, 0.0, pltpu.roll(cells, width - 1, 1))
    return [piece.reshape(rows.shape).astype(jnp.bfloat16) for piece in (before, cells, after)]


def whole(count):
    return [pl.BlockSpec(memory_space=pltpu.VMEM)] * count


def call(body, inputs, outputs, scratch, flops, far=False):
    return pl.pallas_call(
        body,
        out_shape=[jax.ShapeDtypeStruct(shape, dtype) for shape, dtype in outputs],
        in_specs=[pl.BlockSpec(memory_space=pl.ANY)] * len(inputs) if far else whole(len(inputs)),
        out_specs=whole(len(outputs)),
        scratch_shapes=scratch,
        compiler_params=pltpu.CompilerParams(vmem_limit_bytes=32 * 1024 * 1024),
        cost_estimate=pl.CostEstimate(flops=flops, bytes_accessed=4_000_000, transcendentals=0),
    )(*inputs)


def turn_into(turned, k, t, piece):
    channels = piece.shape[-1]
    flat = piece.reshape(-1, channels)
    cells = flat.shape[0]
    turned[k * channels : (k + 1) * channels, t * cells : (t + 1) * cells] = flat.T


def pad_rows(grads):
    count, padded_height, flat, channels = grads.shape
    zero_row = jnp.zeros((count, 1, flat, channels), jnp.bfloat16)
    grads[:, :1] = zero_row
    grads[:, padded_height - 1 :] = zero_row


def place_grads(grads, fields):
    height = fields[0].shape[0]
    first_two = fields[0] + fields[1]
    for t, field in enumerate((*fields, first_two, first_two + fields[2])):
        grads[t, 1 : height + 1] = field.astype(jnp.bfloat16)


def copy_body(source, target):
    target[...] = source[...]


def prepare_body(clips_far, cotangent_far, *refs):
    shifted, base, upstream, ready, held, clips, cotangent, sems = refs
    micro, frames, height, width, channels = clips.shape
    section = lax.axis_index("section")
    copies = [
        pltpu.make_async_copy(source, target, sems.at[k])
        for k, (source, target) in enumerate(
            ((clips_far, clips), (cotangent_far, cotangent))
        )
    ]
    for copy in copies:
        copy.start()

    def reorder(source, target):
        for m in range(micro):
            held[:, :, m * width : (m + 1) * width, :] = source[m].astype(jnp.float32)
        for t in range(frames):
            target[t] = held[t].astype(jnp.bfloat16)

    zero_row = jnp.zeros((3, frames, 1) + shifted.shape[3:], jnp.bfloat16)
    shifted[:, :, :1] = zero_row
    shifted[:, :, height + 1 :] = zero_row
    copies[0].wait()
    reorder(clips, base)
    copies[1].wait()
    reorder(cotangent, upstream)

    @pl.when(section == 0)
    def _():
        for t in range(frames):
            squashed = silu_of(base[t].astype(jnp.float32)).astype(jnp.bfloat16)
            for k, piece in enumerate(column_shifts(squashed.astype(jnp.float32), width)):
                shifted[k, t, 1 : height + 1] = piece
                turn_into(ready, k, t, piece)

    @pl.when(section != 0)
    def _():
        for t in range(frames):
            for k, piece in enumerate(column_shifts(upstream[t].astype(jnp.float32), width)):
                shifted[k, t, 1 : height + 1] = piece


def shard_rows(rows, first, second):
    section, index = lax.axis_index("section"), lax.axis_index("dp")
    far, near = jnp.where(section == 0, first, second), jnp.where(section == 0, second, first)
    return pl.ds(pl.multiple_of((index ^ (4 * far + near)) * rows, 8), rows)


GATHERED = ((0, 1, 2, 3), (0, 2, 3, 1))


def unpack_weights(blocks, table):
    rows = blocks[0].shape[1]
    section = lax.axis_index("section")
    for block, chip, plane in zip(blocks, *GATHERED):
        second = jnp.where(section == 0, chip, plane)
        for first in range(4):
            table[shard_rows(rows, first, second), :] = block[first].astype(jnp.float32)


def forward_weights(table, channels):
    rows = 9 * channels
    return jnp.concatenate(
        [table[t * rows : (t + 1) * rows, :].astype(jnp.bfloat16) for t in range(3)], axis=1
    )


def backward_weights(table, channels):
    def turned_taps(times):
        blocks = []
        for k in reversed(range(9)):
            rows = [table[(t * 9 + k) * channels : (t * 9 + k + 1) * channels, :] for t in times]
            blocks.append(summed(rows).astype(jnp.bfloat16))
        return jnp.concatenate(blocks, axis=1)

    return [turned_taps(times) for times in ((0,), (1,), (2,), (0, 1), (0, 1, 2))]


def row_patches(shifted, start, count, height):
    flat, channels = shifted.shape[3:]
    return jnp.concatenate(
        [
            shifted[k, start : start + count, e : e + height].reshape(count * height * flat, channels)
            for e in range(3)
            for k in range(3)
        ],
        axis=1,
    )


def forward_product(shifted, weights, frames, height):
    channels = shifted.shape[-1]
    cells = height * shifted.shape[-2]
    pieces = {}
    for start, count, first_tap in ((0, frames - 2, 0), (frames - 2, 1, 1), (frames - 1, 1, 2)):
        part = jnp.dot(
            row_patches(shifted, start, count, height),
            weights[:, first_tap * channels :],
            preferred_element_type=jnp.float32,
        )
        for t in range(start, start + count):
            rows = slice((t - start) * cells, (t - start + 1) * cells)
            for tap in range(first_tap, 3):
                columns = slice((tap - first_tap) * channels, (tap - first_tap + 1) * channels)
                pieces[t, tap] = part[rows, columns]
    return [
        summed([pieces[max(t + tap - 2, 0), tap] for tap in range(3)]) for t in range(frames)
    ]


def backward_product(shifted, weights, frames, height):
    channels = shifted.shape[-1]
    cells = height * shifted.shape[-2]
    first, second, third, first_two, all_three = weights
    plan = (
        (2, frames - 2, ((first, -2), (second, -1), (third, 0))),
        (1, 1, ((third, 0), (first_two, -1))),
        (0, 1, ((all_three, 0),)),
    )
    reaching = [[] for _ in range(frames)]
    for start, count, terms in plan:
        part = lax.dot_general(
            row_patches(shifted, start, count, height),
            jnp.concatenate([weight for weight, _ in terms], axis=0),
            (((1,), (1,)), ((), ())),
            preferred_element_type=jnp.float32,
        )
        for t in range(start, start + count):
            rows = slice((t - start) * cells, (t - start + 1) * cells)
            for column, (_, step) in enumerate(terms):
                reaching[t + step].append(part[rows, column * channels : (column + 1) * channels])
    return [summed(terms) for terms in reaching]


def first_body(*refs):
    blocks = refs[:4]
    shifted, base, *results, table = refs[4:]
    frames, height, flat, channels = base.shape
    section = lax.axis_index("section")
    unpack_weights(blocks, table)

    @pl.when(section == 0)
    def _():
        branch = forward_product(shifted, forward_weights(table, channels), frames, height)
        for t in range(frames):
            total = base[t].astype(jnp.float32) + branch[t].reshape(height, flat, channels)
            frame_of(results, t)[...] = total.astype(jnp.bfloat16)

    @pl.when(section != 0)
    def _():
        branch = backward_product(shifted, backward_weights(table, channels), frames, height)
        for t in range(frames):
            frame_of(results, t)[...] = branch[t].reshape(height, flat, channels).astype(jnp.bfloat16)


def between_body(mine_low, mine_high, upstream, slope, grads):
    frames = upstream.shape[0]

    @pl.when(lax.axis_index("section") == 0)
    def _():
        for t in range(frames):
            slope[t] = slope_of(frame_of((mine_low, mine_high), t)[...].astype(jnp.float32))

    @pl.when(lax.axis_index("section") != 0)
    def _():
        pad_rows(grads)
        place_grads(grads, [upstream[t].astype(jnp.float32) for t in range(frames)])


def second_body(width, ready, slope, moved, other_low, other_high, upstream, *refs):
    shares, turned, grads = refs
    frames, height, flat, channels = upstream.shape
    rows = shares.shape[2]
    section = lax.axis_index("section")
    cells = height * flat

    def product(left, right):
        taps, done = [], 0
        for met in ((frames + 1, 3), (frames, 2, 3), (0, 1, 2, 3)):
            columns = jnp.concatenate(
                [
                    jnp.concatenate(
                        [
                            right[f, 2 - e : 2 - e + height].reshape(cells, channels)
                            for e in range(3)
                        ],
                        axis=1,
                    )
                    for f in met
                ],
                axis=0,
            )
            part = jnp.dot(
                left[:, : len(met) * cells], columns, preferred_element_type=jnp.float32
            )
            for e in range(3):
                for k in range(3):
                    taps.append(
                        part[k * channels : (k + 1) * channels, e * channels : (e + 1) * channels]
                    )
            while (done + 1) * rows <= len(taps) * channels:
                pieces, row = [], done * rows
                while row < (done + 1) * rows:
                    tap_of, low = divmod(row, channels)
                    high = min(channels, low + (done + 1) * rows - row)
                    pieces.append(taps[tap_of][low:high])
                    row += high - low
                bits = lax.axis_index("dp") ^ done
                far, near = bits // 4, bits % 4
                first = jnp.where(section == 0, far, near)
                second = jnp.where(section == 0, near, far)
                shares[second, first] = jnp.concatenate(pieces, axis=0).astype(jnp.bfloat16)
                done += 1

    @pl.when(section == 0)
    def _():
        pad_rows(grads)
        values = [
            upstream[t].astype(jnp.float32) + slope[t] * frame_of((other_low, other_high), t)[...].astype(jnp.float32)
            for t in range(frames)
        ]
        place_grads(grads, [value.astype(jnp.bfloat16).astype(jnp.float32) for value in values])
        product(ready, grads)

    @pl.when(section != 0)
    def _():
        for t in range(frames):
            squashed = silu_of(frame_of((other_low, other_high), t)[...].astype(jnp.float32)).astype(jnp.bfloat16)
            for k, piece in enumerate(column_shifts(squashed.astype(jnp.float32), width)):
                turn_into(turned, k, t, piece)
        product(turned, moved)


def third_body(*refs):
    blocks = refs[:4]
    mine, other, (produced, table, shifted) = refs[4:6], refs[6:8], refs[8:]
    micro, frames, height, width, channels = produced.shape
    flat = micro * width
    section = lax.axis_index("section")

    def hand_out(t, cells):
        for m in range(micro):
            produced[m, t] = cells[:, m * width : (m + 1) * width, :].astype(jnp.bfloat16)

    @pl.when(section == 0)
    def _():
        for t in range(frames):
            hand_out(t, frame_of(mine, t)[...].astype(jnp.float32))

    @pl.when(section != 0)
    def _():
        unpack_weights(blocks, table)
        zero_row = jnp.zeros((3, frames, 1, flat, channels), jnp.bfloat16)
        shifted[:, :, :1] = zero_row
        shifted[:, :, height + 1 :] = zero_row
        for t in range(frames):
            squashed = silu_of(frame_of(other, t)[...].astype(jnp.float32)).astype(jnp.bfloat16)
            for k, piece in enumerate(column_shifts(squashed.astype(jnp.float32), width)):
                shifted[k, t, 1 : height + 1] = piece
        branch = forward_product(shifted, forward_weights(table, channels), frames, height)
        for t in range(frames):
            hand_out(t, frame_of(other, t)[...].astype(jnp.float32) + branch[t].reshape(height, flat, channels))


def paired_sections(clips, cotangent, weights):
    dp_total = lax.axis_size("dp")
    local_clips, local_grads, shard = clips[:, 0], cotangent[:, 0], weights[0]
    micro, frames, height, width, channels = local_clips.shape
    rows = shard.shape[0]
    flat = micro * width
    cells = height * flat

    def traded(block, bits):
        route = [
            (s * dp_total + i, s * dp_total + (i ^ bits[s])) for s in range(2) for i in range(dp_total)
        ]
        return lax.ppermute(block, ("section", "dp"), route)

    field = (frames, height, flat, channels)
    padded = (3, frames, height + 2, flat, channels)
    met = (frames + 2, height + 2, flat, channels)
    bf16, f32 = jnp.bfloat16, jnp.float32
    unit = 2 * micro * frames * height * width * channels * channels * 27

    first = [traded(shard, (4 * step, step)) for step in range(1, 4)]
    (shard_copy,) = call(copy_body, (shard,), [(shard.shape, bf16)], [], unit // 16)
    shard_copy, first = lax.optimization_barrier((shard_copy, first))
    line = jnp.stack([shard_copy] + first)
    blocks = (line, *[traded(line, (c, 4 * z)) for c, z in list(zip(*GATHERED))[1:]])

    turned = (3 * channels, frames * cells)
    shifted, base, upstream, ready = call(
        prepare_body,
        (local_clips, local_grads),
        [(padded, bf16), (field, bf16), (field, bf16), (turned, bf16)],
        [
            pltpu.VMEM(field, f32),
            pltpu.VMEM(local_clips.shape, bf16),
            pltpu.VMEM(local_clips.shape, bf16),
            pltpu.SemaphoreType.DMA((2,)),
        ],
        unit // 8,
        far=True,
    )
    table = pltpu.VMEM((dp_total * rows, channels), f32)
    half = (frames // 2, height, flat, channels)
    mine = call(first_body, blocks + (shifted, base), [(half, bf16)] * 2, [table], unit)
    other = [lax.ppermute(part, "section", [(0, 1), (1, 0)]) for part in mine]
    slope, moved = call(
        between_body, (*mine, upstream), [(field, f32), (met, bf16)], [], unit // 8
    )
    slope, moved, other = lax.optimization_barrier((slope, moved, other))
    (shares,) = call(
        functools.partial(second_body, width),
        (ready, slope, moved, *other, upstream),
        [((4, 4, rows, channels), bf16)],
        [pltpu.VMEM(turned, bf16), pltpu.VMEM(met, bf16)],
        unit,
    )
    (produced,) = call(
        third_body,
        blocks + (*mine, *other),
        [(local_clips.shape, bf16)],
        [table, pltpu.VMEM(padded, bf16)],
        unit,
    )

    def added(*terms):
        return summed([term.astype(f32) for term in terms])

    received = [traded(shares[step], (step, 4 * step)) for step in (1, 2, 3)]
    received, produced = lax.optimization_barrier((received, produced))
    line_sum = added(shares[0, 1:], *[block[1:] for block in received]).astype(bf16)
    own_sum = added(shares[0, 0], *[block[0] for block in received])
    total = added(own_sum, *[traded(line_sum[step - 1], (4 * step, step)) for step in (3, 2, 1)])
    return (produced[None, :, None], total[None])


def solution(mesh):
    dp_total = mesh.shape["dp"]
    paired = mesh.shape["section"] == 2 and dp_total == 16
    placed = (
        P(None, "dp", None, None, None, None),
        P(None, "dp", None, None, None, None),
        P("section", "dp", None),
    )
    return jax.shard_map(
        paired_sections if paired else many_sections,
        mesh=mesh,
        in_specs=placed,
        out_specs=(P("section", None, "dp", None, None, None, None), P("section", "dp", None)),
        check_vma=False,
    )
```

```python
import functools

import jax
import jax.numpy as jnp
from jax import lax
from jax.experimental import pallas as pl
from jax.experimental.pallas import tpu as pltpu
from jax.sharding import PartitionSpec as P


def passed_along(block, axis, distance):
    devices = range(lax.axis_size(axis))
    route = [(i - distance, i) for i in devices if i - distance in devices]
    return lax.ppermute(block, axis, route)


def gather_patches(field):
    frames, height, width, channels = field.shape
    first_frame = field[:1]
    padded = jnp.concatenate([first_frame, first_frame, field], axis=0)
    padded = jnp.pad(padded, ((0, 0), (1, 1), (1, 1), (0, 0)))
    pieces = [
        padded[
            offset_time : offset_time + frames,
            offset_row : offset_row + height,
            offset_col : offset_col + width,
        ]
        for offset_time in range(3)
        for offset_row in range(3)
        for offset_col in range(3)
    ]
    return jnp.stack(pieces, axis=3).reshape(frames * height * width, 27 * channels)


def squash_field(activation):
    return jax.nn.silu(activation.astype(jnp.float32)).astype(jnp.bfloat16)


def squash_columns(activation):
    return gather_patches(squash_field(activation))


def layer_forward(activation, weight):
    branch = jnp.dot(squash_columns(activation), weight, preferred_element_type=jnp.float32)
    return (activation.astype(jnp.float32) + branch.reshape(activation.shape)).astype(jnp.bfloat16)


def input_gradient(activation, upstream, weight):
    flat_grad = upstream.reshape(-1, weight.shape[1])
    column_grad = lax.dot_general(
        flat_grad, weight, (((1,), (1,)), ((), ())), preferred_element_type=jnp.float32
    )
    base = activation.astype(jnp.float32)
    _, unfold = jax.vjp(gather_patches, base)
    field_grad = unfold(column_grad)[0]
    sigmoid_value = jax.nn.sigmoid(base)
    slope = sigmoid_value * (1.0 + base * (1.0 - sigmoid_value))
    return (upstream.astype(jnp.float32) + field_grad * slope).astype(jnp.bfloat16)


def weight_term(activation, upstream):
    flat_grad = upstream.reshape(-1, upstream.shape[-1])
    return lax.dot_general(
        squash_columns(activation),
        flat_grad,
        (((0,), (0,)), ((), ())),
        preferred_element_type=jnp.float32,
    )


def many_sections(clips, cotangent, weights):
    section_total = lax.axis_size("section")
    section_index = lax.axis_index("section")
    weight = lax.all_gather(weights, "dp", axis=1, tiled=True)[0]
    local_clips = clips[:, 0]
    local_grads = cotangent[:, 0]
    micro_count = local_clips.shape[0]
    step_count = micro_count + section_total - 1
    empty_field = jnp.zeros(local_clips.shape[1:], jnp.bfloat16)

    def forward_step(step_index, carry):
        received, saved_inputs, produced = carry
        micro_index = step_index - section_index
        active = (micro_index >= 0) & (micro_index < micro_count)
        slot_index = jnp.clip(micro_index, 0, micro_count - 1)
        fresh = lax.dynamic_index_in_dim(local_clips, slot_index, 0, keepdims=False)
        layer_input = jnp.where(section_index == 0, fresh, received)
        layer_output = layer_forward(layer_input, weight)
        kept_input = jnp.where(
            active,
            layer_input,
            lax.dynamic_index_in_dim(saved_inputs, slot_index, 0, keepdims=False),
        )
        kept_output = jnp.where(
            active, layer_output, lax.dynamic_index_in_dim(produced, slot_index, 0, keepdims=False)
        )
        saved_inputs = lax.dynamic_update_index_in_dim(saved_inputs, kept_input, slot_index, 0)
        produced = lax.dynamic_update_index_in_dim(produced, kept_output, slot_index, 0)
        received = passed_along(layer_output, "section", 1)
        return (received, saved_inputs, produced)

    start_forward = (empty_field, jnp.zeros_like(local_clips), jnp.zeros_like(local_clips))
    _, saved_inputs, produced = lax.fori_loop(0, step_count, forward_step, start_forward)

    def backward_step(step_index, carry):
        received, grad_total, kept_grads = carry
        micro_index = step_index - (section_total - 1 - section_index)
        active = (micro_index >= 0) & (micro_index < micro_count)
        slot_index = jnp.clip(micro_index, 0, micro_count - 1)
        fresh = lax.dynamic_index_in_dim(local_grads, slot_index, 0, keepdims=False)
        upstream = jnp.where(section_index == section_total - 1, fresh, received)
        activation = lax.dynamic_index_in_dim(saved_inputs, slot_index, 0, keepdims=False)
        grad_total = grad_total + jnp.where(active, weight_term(activation, upstream), 0.0)
        layer_grad = input_gradient(activation, upstream, weight)
        received = passed_along(layer_grad, "section", -1)
        return (received, grad_total, kept_grads)

    start_backward = (
        empty_field,
        jnp.zeros(weight.shape, jnp.float32),
        jnp.zeros_like(local_grads),
    )
    _, grad_total, kept_grads = lax.fori_loop(0, step_count, backward_step, start_backward)
    grad_share = lax.psum_scatter(
        grad_total.astype(jnp.bfloat16), "dp", scatter_dimension=0, tiled=True
    ).astype(jnp.float32)
    return (produced[None, :, None], grad_share[None])


def summed(terms):
    return functools.reduce(lambda p, q: p + q, terms)


def frame_of(halves, t):
    return halves[t // halves[0].shape[0]].at[t % halves[0].shape[0]]


def silu_of(value):
    return value * jax.nn.sigmoid(value)


def slope_of(value):
    sigmoid_value = jax.nn.sigmoid(value)
    return sigmoid_value * (1.0 + value * (1.0 - sigmoid_value))


def column_shifts(rows, width):
    height, flat, channels = rows.shape
    cells = rows.reshape(height * flat // width, width, channels)
    column = lax.broadcasted_iota(jnp.int32, cells.shape, 1)
    before = jnp.where(column == 0, 0.0, pltpu.roll(cells, 1, 1))
    after = jnp.where(column == width - 1, 0.0, pltpu.roll(cells, width - 1, 1))
    return [piece.reshape(rows.shape).astype(jnp.bfloat16) for piece in (before, cells, after)]


def whole(count):
    return [pl.BlockSpec(memory_space=pltpu.VMEM)] * count


def call(body, inputs, outputs, scratch, flops, far=False):
    return pl.pallas_call(
        body,
        out_shape=[jax.ShapeDtypeStruct(shape, dtype) for shape, dtype in outputs],
        in_specs=[pl.BlockSpec(memory_space=pl.ANY)] * len(inputs) if far else whole(len(inputs)),
        out_specs=whole(len(outputs)),
        scratch_shapes=scratch,
        compiler_params=pltpu.CompilerParams(vmem_limit_bytes=32 * 1024 * 1024),
        cost_estimate=pl.CostEstimate(flops=flops, bytes_accessed=flops // 450, transcendentals=0),
    )(*inputs)


def turn_into(turned, k, t, piece):
    channels = piece.shape[-1]
    flat = piece.reshape(-1, channels)
    cells = flat.shape[0]
    turned[k * channels : (k + 1) * channels, t * cells : (t + 1) * cells] = flat.T


def pad_rows(grads):
    count, padded_height, flat, channels = grads.shape
    zero_row = jnp.zeros((count, 1, flat, channels), jnp.bfloat16)
    grads[:, :1] = zero_row
    grads[:, padded_height - 1 :] = zero_row


def place_grads(grads, fields):
    height = fields[0].shape[0]
    first_two = fields[0] + fields[1]
    for t, field in enumerate((*fields, first_two, first_two + fields[2])):
        grads[t, 1 : height + 1] = field.astype(jnp.bfloat16)


def copy_body(source, target):
    target[...] = source[...]


def prepare_body(clips_far, cotangent_far, *refs):
    shifted, base, upstream, ready, held, clips, cotangent, sems = refs
    micro, frames, height, width, channels = clips.shape
    section = lax.axis_index("section")
    copies = [
        pltpu.make_async_copy(source, target, sems.at[k])
        for k, (source, target) in enumerate(
            ((clips_far, clips), (cotangent_far, cotangent))
        )
    ]
    for copy in copies:
        copy.start()

    def reorder(source, target):
        for m in range(micro):
            held[:, :, m * width : (m + 1) * width, :] = source[m].astype(jnp.float32)
        for t in range(frames):
            target[t] = held[t].astype(jnp.bfloat16)

    zero_row = jnp.zeros((3, frames, 1) + shifted.shape[3:], jnp.bfloat16)
    shifted[:, :, :1] = zero_row
    shifted[:, :, height + 1 :] = zero_row
    copies[0].wait()
    reorder(clips, base)
    copies[1].wait()
    reorder(cotangent, upstream)

    @pl.when(section == 0)
    def _():
        for t in range(frames):
            squashed = silu_of(base[t].astype(jnp.float32)).astype(jnp.bfloat16)
            for k, piece in enumerate(column_shifts(squashed.astype(jnp.float32), width)):
                shifted[k, t, 1 : height + 1] = piece
                turn_into(ready, k, t, piece)

    @pl.when(section != 0)
    def _():
        for t in range(frames):
            for k, piece in enumerate(column_shifts(upstream[t].astype(jnp.float32), width)):
                shifted[k, t, 1 : height + 1] = piece


def shard_rows(rows, first, second):
    section, index = lax.axis_index("section"), lax.axis_index("dp")
    far, near = jnp.where(section == 0, first, second), jnp.where(section == 0, second, first)
    return pl.ds(pl.multiple_of((index ^ (4 * far + near)) * rows, 8), rows)


def unpack_weights(blocks, table):
    rows = blocks[0].shape[1]
    for second in range(4):
        for first in range(4):
            shard = blocks[second][first]
            table[shard_rows(rows, first, second), :] = shard.astype(jnp.float32)


def forward_weights(table, channels):
    rows = 9 * channels
    return jnp.concatenate(
        [table[t * rows : (t + 1) * rows, :].astype(jnp.bfloat16) for t in range(3)], axis=1
    )


def backward_weights(table, channels):
    def turned_taps(times):
        blocks = []
        for k in reversed(range(9)):
            rows = [table[(t * 9 + k) * channels : (t * 9 + k + 1) * channels, :] for t in times]
            blocks.append(summed(rows).astype(jnp.bfloat16))
        return jnp.concatenate(blocks, axis=1)

    return [turned_taps(times) for times in ((0,), (1,), (2,), (0, 1), (0, 1, 2))]


def row_patches(shifted, start, count, height):
    flat, channels = shifted.shape[3:]
    return jnp.concatenate(
        [
            shifted[k, start : start + count, e : e + height].reshape(count * height * flat, channels)
            for e in range(3)
            for k in range(3)
        ],
        axis=1,
    )


def forward_product(shifted, weights, frames, height):
    channels = shifted.shape[-1]
    cells = height * shifted.shape[-2]
    pieces = {}
    for start, count, first_tap in ((0, frames - 2, 0), (frames - 2, 1, 1), (frames - 1, 1, 2)):
        part = jnp.dot(
            row_patches(shifted, start, count, height),
            weights[:, first_tap * channels :],
            preferred_element_type=jnp.float32,
        )
        for t in range(start, start + count):
            rows = slice((t - start) * cells, (t - start + 1) * cells)
            for tap in range(first_tap, 3):
                columns = slice((tap - first_tap) * channels, (tap - first_tap + 1) * channels)
                pieces[t, tap] = part[rows, columns]
    return [
        summed([pieces[max(t + tap - 2, 0), tap] for tap in range(3)]) for t in range(frames)
    ]


def column(part, k, channels):
    return part[:, k * channels : (k + 1) * channels]


def against(patches, weights):
    return lax.dot_general(
        patches,
        jnp.concatenate(weights, axis=0),
        (((1,), (1,)), ((), ())),
        preferred_element_type=jnp.float32,
    )


def first_half_body(*refs):
    blocks, (shifted, base, result, table, carried) = refs[:4], refs[4:]
    frames, height, flat, channels = base.shape
    section = lax.axis_index("section")
    unpack_weights(blocks, table)

    @pl.when(section == 0)
    def _():
        weights = forward_weights(table, channels)
        part = jnp.dot(
            row_patches(shifted, 0, 1, height), weights, preferred_element_type=jnp.float32
        )
        taps = [column(part, k, channels) for k in range(3)]
        last = jnp.dot(
            row_patches(shifted, 1, 1, height),
            weights[:, 2 * channels :],
            preferred_element_type=jnp.float32,
        )
        carried[...] = taps[0]
        for t, branch in enumerate((taps[0] + taps[1] + taps[2], taps[0] + taps[1] + last)):
            total = base[t].astype(jnp.float32) + branch.reshape(height, flat, channels)
            result[t] = total.astype(jnp.bfloat16)

    @pl.when(section != 0)
    def _():
        _, second, third, _, _ = backward_weights(table, channels)
        part = against(row_patches(shifted, 3, 1, height), [third, second])
        own = against(row_patches(shifted, 2, 1, height), [third])
        for t, branch in enumerate((own + column(part, 1, channels), column(part, 0, channels))):
            result[t] = branch.reshape(height, flat, channels).astype(jnp.bfloat16)


def second_half_body(table, carried, shifted, base, result):
    frames, height, flat, channels = base.shape
    section = lax.axis_index("section")

    @pl.when(section == 0)
    def _():
        weights = forward_weights(table, channels)
        parts = []
        for t, taps in ((1, slice(0, 2)), (2, slice(1, 3)), (3, slice(2, 3))):
            columns = weights[:, taps.start * channels : taps.stop * channels]
            patches = row_patches(shifted, t, 1, height)
            parts.append(jnp.dot(patches, columns, preferred_element_type=jnp.float32))
        third = carried[...] + column(parts[0], 1, channels) + column(parts[1], 1, channels)
        fourth = column(parts[0], 0, channels) + column(parts[1], 0, channels) + parts[2]
        for t, branch in enumerate((third, fourth)):
            total = base[2 + t].astype(jnp.float32) + branch.reshape(height, flat, channels)
            result[t] = total.astype(jnp.bfloat16)

    @pl.when(section != 0)
    def _():
        first, second, third, first_two, all_three = backward_weights(table, channels)
        parts = [
            against(row_patches(shifted, t, 1, height), weights)
            for t, weights in (
                (3, [first]),
                (2, [second, first]),
                (1, [third, first_two]),
                (0, [all_three]),
            )
        ]
        early = column(parts[1], 1, channels) + column(parts[2], 1, channels) + parts[3]
        later = parts[0] + column(parts[1], 0, channels) + column(parts[2], 0, channels)
        for t, branch in enumerate((early, later)):
            result[t] = branch.reshape(height, flat, channels).astype(jnp.bfloat16)


def between_body(width, mine_low, mine_high, other_first, upstream, slope, grads, turned):
    frames = upstream.shape[0]
    section = lax.axis_index("section")

    @pl.when(section == 0)
    def _():
        for t in range(frames):
            here = slope_of(frame_of((mine_low, mine_high), t)[...].astype(jnp.float32))
            if t >= frames - 2:
                column_grad = other_first[t - 2].astype(jnp.float32)
                here = upstream[t].astype(jnp.float32) + here * column_grad
            slope[t] = here

    @pl.when(section != 0)
    def _():
        pad_rows(grads)
        place_grads(grads, [upstream[t].astype(jnp.float32) for t in range(frames)])
        for t in range(2):
            turn_squashed(turned, t, other_first[t], width)


def turn_squashed(turned, t, field, width):
    squashed = silu_of(field.astype(jnp.float32)).astype(jnp.bfloat16)
    for k, piece in enumerate(column_shifts(squashed.astype(jnp.float32), width)):
        turn_into(turned, k, t, piece)


def second_body(width, ready, slope, moved, turned_first, other_later, upstream, *refs):
    shares, turned, grads = refs
    frames, height, flat, channels = upstream.shape
    rows = shares.shape[2]
    section = lax.axis_index("section")
    cells = height * flat

    def product(left, right):
        taps, done = [], 0
        for met in ((frames + 1, 3), (frames, 2, 3), (0, 1, 2, 3)):
            columns = jnp.concatenate(
                [
                    jnp.concatenate(
                        [
                            right[f, 2 - e : 2 - e + height].reshape(cells, channels)
                            for e in range(3)
                        ],
                        axis=1,
                    )
                    for f in met
                ],
                axis=0,
            )
            part = jnp.dot(
                left[:, : len(met) * cells], columns, preferred_element_type=jnp.float32
            )
            for e in range(3):
                for k in range(3):
                    taps.append(
                        part[k * channels : (k + 1) * channels, e * channels : (e + 1) * channels]
                    )
            while (done + 1) * rows <= len(taps) * channels:
                pieces, row = [], done * rows
                while row < (done + 1) * rows:
                    tap_of, low = divmod(row, channels)
                    high = min(channels, low + (done + 1) * rows - row)
                    pieces.append(taps[tap_of][low:high])
                    row += high - low
                bits = lax.axis_index("dp") ^ done
                far, near = bits // 4, bits % 4
                first = jnp.where(section == 0, far, near)
                second = jnp.where(section == 0, near, far)
                shares[second, first] = jnp.concatenate(pieces, axis=0).astype(jnp.bfloat16)
                done += 1

    @pl.when(section == 0)
    def _():
        pad_rows(grads)
        values = [
            upstream[t].astype(jnp.float32) + slope[t] * other_later[t].astype(jnp.float32)
            for t in range(2)
        ] + [slope[t] for t in range(2, frames)]
        place_grads(grads, [value.astype(jnp.bfloat16).astype(jnp.float32) for value in values])
        product(ready[...], grads)

    @pl.when(section != 0)
    def _():
        for t in range(2, frames):
            turn_squashed(turned, t - 2, other_later[t - 2], width)
        product(jnp.concatenate([turned_first[...], turned[...]], axis=1), moved)


def third_body(*refs):
    table, (produced, shifted) = refs[0], refs[5:]
    mine, other = refs[1:3], refs[3:5]
    micro, frames, height, width, channels = produced.shape
    flat = micro * width
    section = lax.axis_index("section")

    def hand_out(t, cells):
        for m in range(micro):
            produced[m, t] = cells[:, m * width : (m + 1) * width, :].astype(jnp.bfloat16)

    @pl.when(section == 0)
    def _():
        for t in range(frames):
            hand_out(t, frame_of(mine, t)[...].astype(jnp.float32))

    @pl.when(section != 0)
    def _():
        zero_row = jnp.zeros((3, frames, 1, flat, channels), jnp.bfloat16)
        shifted[:, :, :1] = zero_row
        shifted[:, :, height + 1 :] = zero_row
        for t in range(frames):
            squashed = silu_of(frame_of(other, t)[...].astype(jnp.float32)).astype(jnp.bfloat16)
            for k, piece in enumerate(column_shifts(squashed.astype(jnp.float32), width)):
                shifted[k, t, 1 : height + 1] = piece
        branch = forward_product(shifted, forward_weights(table, channels), frames, height)
        for t in range(frames):
            hand_out(t, frame_of(other, t)[...].astype(jnp.float32) + branch[t].reshape(height, flat, channels))


def paired_sections(clips, cotangent, weights):
    dp_total = lax.axis_size("dp")
    local_clips, local_grads, shard = clips[:, 0], cotangent[:, 0], weights[0]
    micro, frames, height, width, channels = local_clips.shape
    rows = shard.shape[0]
    flat = micro * width
    cells = height * flat

    def traded(block, along_z, step):
        bits = (4 * step, step) if along_z else (step, 4 * step)
        route = [
            (s * dp_total + i, s * dp_total + (i ^ bits[s])) for s in range(2) for i in range(dp_total)
        ]
        return lax.ppermute(block, ("section", "dp"), route)

    field = (frames, height, flat, channels)
    padded = (3, frames, height + 2, flat, channels)
    met = (frames + 2, height + 2, flat, channels)
    bf16, f32 = jnp.bfloat16, jnp.float32
    unit = 2 * micro * frames * height * width * channels * channels * 27

    first = [traded(shard, True, step) for step in range(1, 4)]
    (shard_copy,) = call(copy_body, (shard,), [(shard.shape, bf16)], [], unit // 16)
    shard_copy, first = lax.optimization_barrier((shard_copy, first))
    line = jnp.stack([shard_copy] + first)
    blocks = (line, *[traded(line, False, step) for step in range(1, 4)])

    turned = (3 * channels, frames * cells)
    shifted, base, upstream, ready = call(
        prepare_body,
        (local_clips, local_grads),
        [(padded, bf16), (field, bf16), (field, bf16), (turned, bf16)],
        [
            pltpu.VMEM(field, f32),
            pltpu.VMEM(local_clips.shape, bf16),
            pltpu.VMEM(local_clips.shape, bf16),
            pltpu.SemaphoreType.DMA((2,)),
        ],
        unit // 8,
        far=True,
    )
    half = ((frames // 2, height, flat, channels), bf16)
    mine_first, table, carried = call(
        first_half_body,
        blocks + (shifted, base),
        [half, ((dp_total * rows, channels), f32), ((cells, channels), f32)],
        [],
        unit // 2,
    )
    other_first = lax.ppermute(mine_first, "section", [(0, 1), (1, 0)])
    (mine_later,) = call(
        second_half_body, (table, carried, shifted, base), [half], [], unit // 2
    )
    other_later = lax.ppermute(mine_later, "section", [(0, 1), (1, 0)])
    mine = (mine_first, mine_later)
    half_turned = (3 * channels, 2 * cells)
    slope, moved, turned_first = call(
        functools.partial(between_body, width),
        (*mine, other_first, upstream),
        [(field, f32), (met, bf16), (half_turned, bf16)],
        [],
        unit // 1000,
    )
    slope, moved, turned_first, other_later = lax.optimization_barrier(
        (slope, moved, turned_first, other_later)
    )
    (shares,) = call(
        functools.partial(second_body, width),
        (ready, slope, moved, turned_first, other_later, upstream),
        [((4, 4, rows, channels), bf16)],
        [pltpu.VMEM(half_turned, bf16), pltpu.VMEM(met, bf16)],
        unit,
    )
    (produced,) = call(
        third_body,
        (table, *mine, other_first, other_later),
        [(local_clips.shape, bf16)],
        [pltpu.VMEM(padded, bf16)],
        unit,
    )

    def added(*terms):
        return summed([term.astype(f32) for term in terms])

    received = [traded(shares[step], False, step) for step in (1, 2, 3)]
    received, produced = lax.optimization_barrier((received, produced))
    line_sum = added(shares[0, 1:], *[block[1:] for block in received]).astype(bf16)
    own_sum = added(shares[0, 0], *[block[0] for block in received])
    total = added(own_sum, *[traded(line_sum[step - 1], True, step) for step in (3, 2, 1)])
    return (produced[None, :, None], total[None])


def solution(mesh):
    dp_total = mesh.shape["dp"]
    paired = mesh.shape["section"] == 2 and dp_total == 16
    placed = (
        P(None, "dp", None, None, None, None),
        P(None, "dp", None, None, None, None),
        P("section", "dp", None),
    )
    return jax.shard_map(
        paired_sections if paired else many_sections,
        mesh=mesh,
        in_specs=placed,
        out_specs=(P("section", None, "dp", None, None, None, None), P("section", "dp", None)),
        check_vma=False,
    )
```

```python
import functools

import jax
import jax.numpy as jnp
from jax import lax
from jax.experimental import pallas as pl
from jax.experimental.pallas import tpu as pltpu
from jax.sharding import PartitionSpec as P


def passed_along(block, axis, distance):
    devices = range(lax.axis_size(axis))
    route = [(i - distance, i) for i in devices if i - distance in devices]
    return lax.ppermute(block, axis, route)


def gather_patches(field):
    frames, height, width, channels = field.shape
    first_frame = field[:1]
    padded = jnp.concatenate([first_frame, first_frame, field], axis=0)
    padded = jnp.pad(padded, ((0, 0), (1, 1), (1, 1), (0, 0)))
    pieces = [
        padded[
            offset_time : offset_time + frames,
            offset_row : offset_row + height,
            offset_col : offset_col + width,
        ]
        for offset_time in range(3)
        for offset_row in range(3)
        for offset_col in range(3)
    ]
    return jnp.stack(pieces, axis=3).reshape(frames * height * width, 27 * channels)


def squash_field(activation):
    return jax.nn.silu(activation.astype(jnp.float32)).astype(jnp.bfloat16)


def squash_columns(activation):
    return gather_patches(squash_field(activation))


def layer_forward(activation, weight):
    branch = jnp.dot(squash_columns(activation), weight, preferred_element_type=jnp.float32)
    return (activation.astype(jnp.float32) + branch.reshape(activation.shape)).astype(jnp.bfloat16)


def input_gradient(activation, upstream, weight):
    flat_grad = upstream.reshape(-1, weight.shape[1])
    column_grad = lax.dot_general(
        flat_grad, weight, (((1,), (1,)), ((), ())), preferred_element_type=jnp.float32
    )
    base = activation.astype(jnp.float32)
    _, unfold = jax.vjp(gather_patches, base)
    field_grad = unfold(column_grad)[0]
    sigmoid_value = jax.nn.sigmoid(base)
    slope = sigmoid_value * (1.0 + base * (1.0 - sigmoid_value))
    return (upstream.astype(jnp.float32) + field_grad * slope).astype(jnp.bfloat16)


def weight_term(activation, upstream):
    flat_grad = upstream.reshape(-1, upstream.shape[-1])
    return lax.dot_general(
        squash_columns(activation),
        flat_grad,
        (((0,), (0,)), ((), ())),
        preferred_element_type=jnp.float32,
    )


def many_sections(clips, cotangent, weights):
    section_total = lax.axis_size("section")
    section_index = lax.axis_index("section")
    weight = lax.all_gather(weights, "dp", axis=1, tiled=True)[0]
    local_clips = clips[:, 0]
    local_grads = cotangent[:, 0]
    micro_count = local_clips.shape[0]
    step_count = micro_count + section_total - 1
    empty_field = jnp.zeros(local_clips.shape[1:], jnp.bfloat16)

    def forward_step(step_index, carry):
        received, saved_inputs, produced = carry
        micro_index = step_index - section_index
        active = (micro_index >= 0) & (micro_index < micro_count)
        slot_index = jnp.clip(micro_index, 0, micro_count - 1)
        fresh = lax.dynamic_index_in_dim(local_clips, slot_index, 0, keepdims=False)
        layer_input = jnp.where(section_index == 0, fresh, received)
        layer_output = layer_forward(layer_input, weight)
        kept_input = jnp.where(
            active,
            layer_input,
            lax.dynamic_index_in_dim(saved_inputs, slot_index, 0, keepdims=False),
        )
        kept_output = jnp.where(
            active, layer_output, lax.dynamic_index_in_dim(produced, slot_index, 0, keepdims=False)
        )
        saved_inputs = lax.dynamic_update_index_in_dim(saved_inputs, kept_input, slot_index, 0)
        produced = lax.dynamic_update_index_in_dim(produced, kept_output, slot_index, 0)
        received = passed_along(layer_output, "section", 1)
        return (received, saved_inputs, produced)

    start_forward = (empty_field, jnp.zeros_like(local_clips), jnp.zeros_like(local_clips))
    _, saved_inputs, produced = lax.fori_loop(0, step_count, forward_step, start_forward)

    def backward_step(step_index, carry):
        received, grad_total, kept_grads = carry
        micro_index = step_index - (section_total - 1 - section_index)
        active = (micro_index >= 0) & (micro_index < micro_count)
        slot_index = jnp.clip(micro_index, 0, micro_count - 1)
        fresh = lax.dynamic_index_in_dim(local_grads, slot_index, 0, keepdims=False)
        upstream = jnp.where(section_index == section_total - 1, fresh, received)
        activation = lax.dynamic_index_in_dim(saved_inputs, slot_index, 0, keepdims=False)
        grad_total = grad_total + jnp.where(active, weight_term(activation, upstream), 0.0)
        layer_grad = input_gradient(activation, upstream, weight)
        received = passed_along(layer_grad, "section", -1)
        return (received, grad_total, kept_grads)

    start_backward = (
        empty_field,
        jnp.zeros(weight.shape, jnp.float32),
        jnp.zeros_like(local_grads),
    )
    _, grad_total, kept_grads = lax.fori_loop(0, step_count, backward_step, start_backward)
    grad_share = lax.psum_scatter(
        grad_total.astype(jnp.bfloat16), "dp", scatter_dimension=0, tiled=True
    ).astype(jnp.float32)
    return (produced[None, :, None], grad_share[None])


def summed(terms):
    return functools.reduce(lambda p, q: p + q, terms)


def frame_of(halves, t):
    return halves[t // halves[0].shape[0]].at[t % halves[0].shape[0]]


def silu_of(value):
    return value * jax.nn.sigmoid(value)


def slope_of(value):
    sigmoid_value = jax.nn.sigmoid(value)
    return sigmoid_value * (1.0 + value * (1.0 - sigmoid_value))


def column_shifts(rows, width):
    height, flat, channels = rows.shape
    cells = rows.reshape(height * flat // width, width, channels)
    column = lax.broadcasted_iota(jnp.int32, cells.shape, 1)
    before = jnp.where(column == 0, 0.0, pltpu.roll(cells, 1, 1))
    after = jnp.where(column == width - 1, 0.0, pltpu.roll(cells, width - 1, 1))
    return [piece.reshape(rows.shape).astype(jnp.bfloat16) for piece in (before, cells, after)]


def whole(count):
    return [pl.BlockSpec(memory_space=pltpu.VMEM)] * count


def call(body, inputs, outputs, scratch, flops, far=False):
    return pl.pallas_call(
        body,
        out_shape=[jax.ShapeDtypeStruct(shape, dtype) for shape, dtype in outputs],
        in_specs=[pl.BlockSpec(memory_space=pl.ANY)] * len(inputs) if far else whole(len(inputs)),
        out_specs=whole(len(outputs)),
        scratch_shapes=scratch,
        compiler_params=pltpu.CompilerParams(vmem_limit_bytes=32 * 1024 * 1024),
        cost_estimate=pl.CostEstimate(flops=flops, bytes_accessed=flops // 450, transcendentals=0),
    )(*inputs)


def turn_into(turned, k, t, piece):
    channels = piece.shape[-1]
    flat = piece.reshape(-1, channels)
    cells = flat.shape[0]
    turned[k * channels : (k + 1) * channels, t * cells : (t + 1) * cells] = flat.T


def pad_rows(grads):
    count, padded_height, flat, channels = grads.shape
    zero_row = jnp.zeros((count, 1, flat, channels), jnp.bfloat16)
    grads[:, :1] = zero_row
    grads[:, padded_height - 1 :] = zero_row


def place_grads(grads, fields):
    height = fields[0].shape[0]
    first_two = fields[0] + fields[1]
    for t, field in enumerate((*fields, first_two, first_two + fields[2])):
        grads[t, 1 : height + 1] = field.astype(jnp.bfloat16)


def copy_body(source, target):
    target[...] = source[...]


def prepare_body(clips_far, cotangent_far, *refs):
    shifted, base, upstream, ready, held, clips, cotangent, sems = refs
    micro, frames, height, width, channels = clips.shape
    section = lax.axis_index("section")
    copies = [
        pltpu.make_async_copy(source, target, sems.at[k])
        for k, (source, target) in enumerate(
            ((clips_far, clips), (cotangent_far, cotangent))
        )
    ]
    for copy in copies:
        copy.start()

    def reorder(source, target):
        for m in range(micro):
            held[:, :, m * width : (m + 1) * width, :] = source[m].astype(jnp.float32)
        for t in range(frames):
            target[t] = held[t].astype(jnp.bfloat16)

    zero_row = jnp.zeros((3, frames, 1) + shifted.shape[3:], jnp.bfloat16)
    shifted[:, :, :1] = zero_row
    shifted[:, :, height + 1 :] = zero_row
    copies[0].wait()
    reorder(clips, base)
    copies[1].wait()
    reorder(cotangent, upstream)

    @pl.when(section == 0)
    def _():
        for t in range(frames):
            squashed = silu_of(base[t].astype(jnp.float32)).astype(jnp.bfloat16)
            for k, piece in enumerate(column_shifts(squashed.astype(jnp.float32), width)):
                shifted[k, t, 1 : height + 1] = piece
                turn_into(ready, k, t, piece)

    @pl.when(section != 0)
    def _():
        for t in range(frames):
            for k, piece in enumerate(column_shifts(upstream[t].astype(jnp.float32), width)):
                shifted[k, t, 1 : height + 1] = piece


def shard_rows(rows, first, second):
    section, index = lax.axis_index("section"), lax.axis_index("dp")
    far, near = jnp.where(section == 0, first, second), jnp.where(section == 0, second, first)
    return pl.ds(pl.multiple_of((index ^ (4 * far + near)) * rows, 8), rows)


def unpack_weights(blocks, table):
    rows = blocks[0].shape[1]
    for second in range(4):
        for first in range(4):
            shard = blocks[second][first]
            table[shard_rows(rows, first, second), :] = shard.astype(jnp.float32)


def forward_weights(table, channels):
    rows = 9 * channels
    return jnp.concatenate(
        [table[t * rows : (t + 1) * rows, :].astype(jnp.bfloat16) for t in range(3)], axis=1
    )


def backward_weights(table, channels):
    def turned_taps(times):
        blocks = []
        for k in reversed(range(9)):
            rows = [table[(t * 9 + k) * channels : (t * 9 + k + 1) * channels, :] for t in times]
            blocks.append(summed(rows).astype(jnp.bfloat16))
        return jnp.concatenate(blocks, axis=1)

    return [turned_taps(times) for times in ((0,), (1,), (2,), (0, 1), (0, 1, 2))]


def row_patches(shifted, start, count, height):
    flat, channels = shifted.shape[3:]
    return jnp.concatenate(
        [
            shifted[k, start : start + count, e : e + height].reshape(count * height * flat, channels)
            for e in range(3)
            for k in range(3)
        ],
        axis=1,
    )


def forward_product(shifted, weights, frames, height):
    channels = shifted.shape[-1]
    cells = height * shifted.shape[-2]
    pieces = {}
    for start, count, first_tap in ((0, frames - 2, 0), (frames - 2, 1, 1), (frames - 1, 1, 2)):
        part = jnp.dot(
            row_patches(shifted, start, count, height),
            weights[:, first_tap * channels :],
            preferred_element_type=jnp.float32,
        )
        for t in range(start, start + count):
            rows = slice((t - start) * cells, (t - start + 1) * cells)
            for tap in range(first_tap, 3):
                columns = slice((tap - first_tap) * channels, (tap - first_tap + 1) * channels)
                pieces[t, tap] = part[rows, columns]
    return [
        summed([pieces[max(t + tap - 2, 0), tap] for tap in range(3)]) for t in range(frames)
    ]


def column(part, k, channels):
    return part[:, k * channels : (k + 1) * channels]


def against(patches, weights):
    return lax.dot_general(
        patches,
        jnp.concatenate(weights, axis=0),
        (((1,), (1,)), ((), ())),
        preferred_element_type=jnp.float32,
    )


def first_half_body(*refs):
    blocks, (shifted, base, result, table, carried) = refs[:4], refs[4:]
    frames, height, flat, channels = base.shape
    section = lax.axis_index("section")
    unpack_weights(blocks, table)

    @pl.when(section == 0)
    def _():
        weights = forward_weights(table, channels)
        part = jnp.dot(
            row_patches(shifted, 0, 1, height), weights, preferred_element_type=jnp.float32
        )
        taps = [column(part, k, channels) for k in range(3)]
        last = jnp.dot(
            row_patches(shifted, 1, 1, height),
            weights[:, 2 * channels :],
            preferred_element_type=jnp.float32,
        )
        carried[...] = taps[0]
        for t, branch in enumerate((taps[0] + taps[1] + taps[2], taps[0] + taps[1] + last)):
            total = base[t].astype(jnp.float32) + branch.reshape(height, flat, channels)
            result[t] = total.astype(jnp.bfloat16)

    @pl.when(section != 0)
    def _():
        first, second, third, _, _ = backward_weights(table, channels)
        part = against(row_patches(shifted, 3, 1, height), [third, second, first])
        carried[...] = column(part, 2, channels)
        own = against(row_patches(shifted, 2, 1, height), [third])
        for t, branch in enumerate((own + column(part, 1, channels), column(part, 0, channels))):
            result[t] = branch.reshape(height, flat, channels).astype(jnp.bfloat16)


def second_half_body(table, carried, shifted, base, result):
    frames, height, flat, channels = base.shape
    section = lax.axis_index("section")

    @pl.when(section == 0)
    def _():
        weights = forward_weights(table, channels)
        parts = []
        for t, taps in ((1, slice(0, 2)), (2, slice(1, 3)), (3, slice(2, 3))):
            columns = weights[:, taps.start * channels : taps.stop * channels]
            patches = row_patches(shifted, t, 1, height)
            parts.append(jnp.dot(patches, columns, preferred_element_type=jnp.float32))
        third = carried[...] + column(parts[0], 1, channels) + column(parts[1], 1, channels)
        fourth = column(parts[0], 0, channels) + column(parts[1], 0, channels) + parts[2]
        for t, branch in enumerate((third, fourth)):
            total = base[2 + t].astype(jnp.float32) + branch.reshape(height, flat, channels)
            result[t] = total.astype(jnp.bfloat16)

    @pl.when(section != 0)
    def _():
        first, second, third, first_two, all_three = backward_weights(table, channels)
        parts = [
            against(row_patches(shifted, t, 1, height), weights)
            for t, weights in (
                (2, [second, first]),
                (1, [third, first_two]),
                (0, [all_three]),
            )
        ]
        early = column(parts[0], 1, channels) + column(parts[1], 1, channels) + parts[2]
        later = carried[...] + column(parts[0], 0, channels) + column(parts[1], 0, channels)
        for t, branch in enumerate((early, later)):
            result[t] = branch.reshape(height, flat, channels).astype(jnp.bfloat16)


def between_body(width, mine_low, mine_high, other_first, upstream, slope, grads, turned):
    frames = upstream.shape[0]
    section = lax.axis_index("section")

    @pl.when(section == 0)
    def _():
        for t in range(frames):
            here = slope_of(frame_of((mine_low, mine_high), t)[...].astype(jnp.float32))
            if t >= frames - 2:
                column_grad = other_first[t - 2].astype(jnp.float32)
                here = upstream[t].astype(jnp.float32) + here * column_grad
            slope[t] = here

    @pl.when(section != 0)
    def _():
        pad_rows(grads)
        place_grads(grads, [upstream[t].astype(jnp.float32) for t in range(frames)])
        for t in range(2):
            turn_squashed(turned, t, other_first[t], width)


def turn_squashed(turned, t, field, width):
    squashed = silu_of(field.astype(jnp.float32)).astype(jnp.bfloat16)
    for k, piece in enumerate(column_shifts(squashed.astype(jnp.float32), width)):
        turn_into(turned, k, t, piece)


def second_body(width, ready, slope, moved, turned_first, other_later, upstream, *refs):
    shares, turned, grads = refs
    frames, height, flat, channels = upstream.shape
    rows = shares.shape[2]
    section = lax.axis_index("section")
    cells = height * flat

    def product(left, right):
        taps, done = [], 0
        for met in ((frames + 1, 3), (frames, 2, 3), (0, 1, 2, 3)):
            columns = jnp.concatenate(
                [
                    jnp.concatenate(
                        [
                            right[f, 2 - e : 2 - e + height].reshape(cells, channels)
                            for e in range(3)
                        ],
                        axis=1,
                    )
                    for f in met
                ],
                axis=0,
            )
            part = jnp.dot(
                left[:, : len(met) * cells], columns, preferred_element_type=jnp.float32
            )
            for e in range(3):
                for k in range(3):
                    taps.append(
                        part[k * channels : (k + 1) * channels, e * channels : (e + 1) * channels]
                    )
            while (done + 1) * rows <= len(taps) * channels:
                pieces, row = [], done * rows
                while row < (done + 1) * rows:
                    tap_of, low = divmod(row, channels)
                    high = min(channels, low + (done + 1) * rows - row)
                    pieces.append(taps[tap_of][low:high])
                    row += high - low
                bits = lax.axis_index("dp") ^ done
                far, near = bits // 4, bits % 4
                first = jnp.where(section == 0, far, near)
                second = jnp.where(section == 0, near, far)
                shares[second, first] = jnp.concatenate(pieces, axis=0).astype(jnp.bfloat16)
                done += 1

    @pl.when(section == 0)
    def _():
        pad_rows(grads)
        values = [
            upstream[t].astype(jnp.float32) + slope[t] * other_later[t].astype(jnp.float32)
            for t in range(2)
        ] + [slope[t] for t in range(2, frames)]
        place_grads(grads, [value.astype(jnp.bfloat16).astype(jnp.float32) for value in values])
        product(ready[...], grads)

    @pl.when(section != 0)
    def _():
        for t in range(2, frames):
            turn_squashed(turned, t - 2, other_later[t - 2], width)
        product(jnp.concatenate([turned_first[...], turned[...]], axis=1), moved)


def third_body(*refs):
    table, (produced, shifted) = refs[0], refs[5:]
    mine, other = refs[1:3], refs[3:5]
    micro, frames, height, width, channels = produced.shape
    flat = micro * width
    section = lax.axis_index("section")

    def hand_out(t, cells):
        for m in range(micro):
            produced[m, t] = cells[:, m * width : (m + 1) * width, :].astype(jnp.bfloat16)

    @pl.when(section == 0)
    def _():
        for t in range(frames):
            hand_out(t, frame_of(mine, t)[...].astype(jnp.float32))

    @pl.when(section != 0)
    def _():
        zero_row = jnp.zeros((3, frames, 1, flat, channels), jnp.bfloat16)
        shifted[:, :, :1] = zero_row
        shifted[:, :, height + 1 :] = zero_row
        for t in range(frames):
            squashed = silu_of(frame_of(other, t)[...].astype(jnp.float32)).astype(jnp.bfloat16)
            for k, piece in enumerate(column_shifts(squashed.astype(jnp.float32), width)):
                shifted[k, t, 1 : height + 1] = piece
        branch = forward_product(shifted, forward_weights(table, channels), frames, height)
        for t in range(frames):
            hand_out(t, frame_of(other, t)[...].astype(jnp.float32) + branch[t].reshape(height, flat, channels))


def paired_sections(clips, cotangent, weights):
    dp_total = lax.axis_size("dp")
    local_clips, local_grads, shard = clips[:, 0], cotangent[:, 0], weights[0]
    micro, frames, height, width, channels = local_clips.shape
    rows = shard.shape[0]
    flat = micro * width
    cells = height * flat

    def traded(block, along_z, step):
        bits = (4 * step, step) if along_z else (step, 4 * step)
        route = [
            (s * dp_total + i, s * dp_total + (i ^ bits[s])) for s in range(2) for i in range(dp_total)
        ]
        return lax.ppermute(block, ("section", "dp"), route)

    field = (frames, height, flat, channels)
    padded = (3, frames, height + 2, flat, channels)
    met = (frames + 2, height + 2, flat, channels)
    bf16, f32 = jnp.bfloat16, jnp.float32
    unit = 2 * micro * frames * height * width * channels * channels * 27

    first = [traded(shard, True, step) for step in range(1, 4)]
    (shard_copy,) = call(copy_body, (shard,), [(shard.shape, bf16)], [], unit // 16)
    shard_copy, first = lax.optimization_barrier((shard_copy, first))
    line = jnp.stack([shard_copy] + first)
    blocks = (line, *[traded(line, False, step) for step in range(1, 4)])

    turned = (3 * channels, frames * cells)
    shifted, base, upstream, ready = call(
        prepare_body,
        (local_clips, local_grads),
        [(padded, bf16), (field, bf16), (field, bf16), (turned, bf16)],
        [
            pltpu.VMEM(field, f32),
            pltpu.VMEM(local_clips.shape, bf16),
            pltpu.VMEM(local_clips.shape, bf16),
            pltpu.SemaphoreType.DMA((2,)),
        ],
        unit // 8,
        far=True,
    )
    half = ((frames // 2, height, flat, channels), bf16)
    mine_first, table, carried = call(
        first_half_body,
        blocks + (shifted, base),
        [half, ((dp_total * rows, channels), f32), ((cells, channels), f32)],
        [],
        unit // 2,
    )
    other_first = lax.ppermute(mine_first, "section", [(0, 1), (1, 0)])
    (mine_later,) = call(
        second_half_body, (table, carried, shifted, base), [half], [], unit // 2
    )
    other_later = lax.ppermute(mine_later, "section", [(0, 1), (1, 0)])
    mine = (mine_first, mine_later)
    half_turned = (3 * channels, 2 * cells)
    slope, moved, turned_first = call(
        functools.partial(between_body, width),
        (*mine, other_first, upstream),
        [(field, f32), (met, bf16), (half_turned, bf16)],
        [],
        unit // 1000,
    )
    slope, moved, turned_first, other_later = lax.optimization_barrier(
        (slope, moved, turned_first, other_later)
    )
    (shares,) = call(
        functools.partial(second_body, width),
        (ready, slope, moved, turned_first, other_later, upstream),
        [((4, 4, rows, channels), bf16)],
        [pltpu.VMEM(half_turned, bf16), pltpu.VMEM(met, bf16)],
        unit,
    )
    (produced,) = call(
        third_body,
        (table, *mine, other_first, other_later),
        [(local_clips.shape, bf16)],
        [pltpu.VMEM(padded, bf16)],
        unit,
    )

    def added(*terms):
        return summed([term.astype(f32) for term in terms])

    received = [traded(shares[step], False, step) for step in (1, 2, 3)]
    received, produced = lax.optimization_barrier((received, produced))
    line_sum = added(shares[0, 1:], *[block[1:] for block in received]).astype(bf16)
    own_sum = added(shares[0, 0], *[block[0] for block in received])
    total = added(own_sum, *[traded(line_sum[step - 1], True, step) for step in (3, 2, 1)])
    return (produced[None, :, None], total[None])


def solution(mesh):
    dp_total = mesh.shape["dp"]
    paired = mesh.shape["section"] == 2 and dp_total == 16
    placed = (
        P(None, "dp", None, None, None, None),
        P(None, "dp", None, None, None, None),
        P("section", "dp", None),
    )
    return jax.shard_map(
        paired_sections if paired else many_sections,
        mesh=mesh,
        in_specs=placed,
        out_specs=(P("section", None, "dp", None, None, None, None), P("section", "dp", None)),
        check_vma=False,
    )
```

```python
import functools

import jax
import jax.numpy as jnp
from jax import lax
from jax.experimental import pallas as pl
from jax.experimental.pallas import tpu as pltpu
from jax.sharding import PartitionSpec as P


def passed_along(block, axis, distance):
    devices = range(lax.axis_size(axis))
    route = [(i - distance, i) for i in devices if i - distance in devices]
    return lax.ppermute(block, axis, route)


def gather_patches(field):
    frames, height, width, channels = field.shape
    first_frame = field[:1]
    padded = jnp.concatenate([first_frame, first_frame, field], axis=0)
    padded = jnp.pad(padded, ((0, 0), (1, 1), (1, 1), (0, 0)))
    pieces = [
        padded[
            offset_time : offset_time + frames,
            offset_row : offset_row + height,
            offset_col : offset_col + width,
        ]
        for offset_time in range(3)
        for offset_row in range(3)
        for offset_col in range(3)
    ]
    return jnp.stack(pieces, axis=3).reshape(frames * height * width, 27 * channels)


def squash_field(activation):
    return jax.nn.silu(activation.astype(jnp.float32)).astype(jnp.bfloat16)


def squash_columns(activation):
    return gather_patches(squash_field(activation))


def layer_forward(activation, weight):
    branch = jnp.dot(squash_columns(activation), weight, preferred_element_type=jnp.float32)
    return (activation.astype(jnp.float32) + branch.reshape(activation.shape)).astype(jnp.bfloat16)


def input_gradient(activation, upstream, weight):
    flat_grad = upstream.reshape(-1, weight.shape[1])
    column_grad = lax.dot_general(
        flat_grad, weight, (((1,), (1,)), ((), ())), preferred_element_type=jnp.float32
    )
    base = activation.astype(jnp.float32)
    _, unfold = jax.vjp(gather_patches, base)
    field_grad = unfold(column_grad)[0]
    sigmoid_value = jax.nn.sigmoid(base)
    slope = sigmoid_value * (1.0 + base * (1.0 - sigmoid_value))
    return (upstream.astype(jnp.float32) + field_grad * slope).astype(jnp.bfloat16)


def weight_term(activation, upstream):
    flat_grad = upstream.reshape(-1, upstream.shape[-1])
    return lax.dot_general(
        squash_columns(activation),
        flat_grad,
        (((0,), (0,)), ((), ())),
        preferred_element_type=jnp.float32,
    )


def many_sections(clips, cotangent, weights):
    section_total = lax.axis_size("section")
    section_index = lax.axis_index("section")
    weight = lax.all_gather(weights, "dp", axis=1, tiled=True)[0]
    local_clips = clips[:, 0]
    local_grads = cotangent[:, 0]
    micro_count = local_clips.shape[0]
    step_count = micro_count + section_total - 1
    empty_field = jnp.zeros(local_clips.shape[1:], jnp.bfloat16)

    def forward_step(step_index, carry):
        received, saved_inputs, produced = carry
        micro_index = step_index - section_index
        active = (micro_index >= 0) & (micro_index < micro_count)
        slot_index = jnp.clip(micro_index, 0, micro_count - 1)
        fresh = lax.dynamic_index_in_dim(local_clips, slot_index, 0, keepdims=False)
        layer_input = jnp.where(section_index == 0, fresh, received)
        layer_output = layer_forward(layer_input, weight)
        kept_input = jnp.where(
            active,
            layer_input,
            lax.dynamic_index_in_dim(saved_inputs, slot_index, 0, keepdims=False),
        )
        kept_output = jnp.where(
            active, layer_output, lax.dynamic_index_in_dim(produced, slot_index, 0, keepdims=False)
        )
        saved_inputs = lax.dynamic_update_index_in_dim(saved_inputs, kept_input, slot_index, 0)
        produced = lax.dynamic_update_index_in_dim(produced, kept_output, slot_index, 0)
        received = passed_along(layer_output, "section", 1)
        return (received, saved_inputs, produced)

    start_forward = (empty_field, jnp.zeros_like(local_clips), jnp.zeros_like(local_clips))
    _, saved_inputs, produced = lax.fori_loop(0, step_count, forward_step, start_forward)

    def backward_step(step_index, carry):
        received, grad_total, kept_grads = carry
        micro_index = step_index - (section_total - 1 - section_index)
        active = (micro_index >= 0) & (micro_index < micro_count)
        slot_index = jnp.clip(micro_index, 0, micro_count - 1)
        fresh = lax.dynamic_index_in_dim(local_grads, slot_index, 0, keepdims=False)
        upstream = jnp.where(section_index == section_total - 1, fresh, received)
        activation = lax.dynamic_index_in_dim(saved_inputs, slot_index, 0, keepdims=False)
        grad_total = grad_total + jnp.where(active, weight_term(activation, upstream), 0.0)
        layer_grad = input_gradient(activation, upstream, weight)
        received = passed_along(layer_grad, "section", -1)
        return (received, grad_total, kept_grads)

    start_backward = (
        empty_field,
        jnp.zeros(weight.shape, jnp.float32),
        jnp.zeros_like(local_grads),
    )
    _, grad_total, kept_grads = lax.fori_loop(0, step_count, backward_step, start_backward)
    grad_share = lax.psum_scatter(
        grad_total.astype(jnp.bfloat16), "dp", scatter_dimension=0, tiled=True
    ).astype(jnp.float32)
    return (produced[None, :, None], grad_share[None])


def summed(terms):
    return functools.reduce(lambda p, q: p + q, terms)


def frame_of(halves, t):
    return halves[t // halves[0].shape[0]].at[t % halves[0].shape[0]]


def silu_of(value):
    return value * jax.nn.sigmoid(value)


def slope_of(value):
    sigmoid_value = jax.nn.sigmoid(value)
    return sigmoid_value * (1.0 + value * (1.0 - sigmoid_value))


def column_shifts(rows, width):
    height, flat, channels = rows.shape
    cells = rows.reshape(height * flat // width, width, channels)
    column = lax.broadcasted_iota(jnp.int32, cells.shape, 1)
    before = jnp.where(column == 0, 0.0, pltpu.roll(cells, 1, 1))
    after = jnp.where(column == width - 1, 0.0, pltpu.roll(cells, width - 1, 1))
    return [piece.reshape(rows.shape).astype(jnp.bfloat16) for piece in (before, cells, after)]


def whole(count):
    return [pl.BlockSpec(memory_space=pltpu.VMEM)] * count


def call(body, inputs, outputs, scratch, flops, far=False):
    return pl.pallas_call(
        body,
        out_shape=[jax.ShapeDtypeStruct(shape, dtype) for shape, dtype in outputs],
        in_specs=[pl.BlockSpec(memory_space=pl.ANY)] * len(inputs) if far else whole(len(inputs)),
        out_specs=whole(len(outputs)),
        scratch_shapes=scratch,
        compiler_params=pltpu.CompilerParams(vmem_limit_bytes=32 * 1024 * 1024),
        cost_estimate=pl.CostEstimate(flops=flops, bytes_accessed=4_000_000, transcendentals=0),
    )(*inputs)


def turn_into(turned, k, t, piece):
    channels = piece.shape[-1]
    flat = piece.reshape(-1, channels)
    cells = flat.shape[0]
    turned[k * channels : (k + 1) * channels, t * cells : (t + 1) * cells] = flat.T


def pad_rows(grads):
    count, padded_height, flat, channels = grads.shape
    zero_row = jnp.zeros((count, 1, flat, channels), jnp.bfloat16)
    grads[:, :1] = zero_row
    grads[:, padded_height - 1 :] = zero_row


def place_grads(grads, fields):
    height = fields[0].shape[0]
    first_two = fields[0] + fields[1]
    for t, field in enumerate((*fields, first_two, first_two + fields[2])):
        grads[t, 1 : height + 1] = field.astype(jnp.bfloat16)


def copy_body(source, target):
    target[...] = source[...]


def prepare_body(clips_far, cotangent_far, *refs):
    shifted, base, upstream, ready, held, clips, cotangent, sems = refs
    micro, frames, height, width, channels = clips.shape
    section = lax.axis_index("section")
    copies = [
        pltpu.make_async_copy(source, target, sems.at[k])
        for k, (source, target) in enumerate(
            ((clips_far, clips), (cotangent_far, cotangent))
        )
    ]
    for copy in copies:
        copy.start()

    def reorder(source, target):
        for m in range(micro):
            held[:, :, m * width : (m + 1) * width, :] = source[m].astype(jnp.float32)
        for t in range(frames):
            target[t] = held[t].astype(jnp.bfloat16)

    zero_row = jnp.zeros((3, frames, 1) + shifted.shape[3:], jnp.bfloat16)
    shifted[:, :, :1] = zero_row
    shifted[:, :, height + 1 :] = zero_row
    copies[0].wait()
    reorder(clips, base)
    copies[1].wait()
    reorder(cotangent, upstream)

    @pl.when(section == 0)
    def _():
        for t in range(frames):
            squashed = silu_of(base[t].astype(jnp.float32)).astype(jnp.bfloat16)
            for k, piece in enumerate(column_shifts(squashed.astype(jnp.float32), width)):
                shifted[k, t, 1 : height + 1] = piece
                turn_into(ready, k, t, piece)

    @pl.when(section != 0)
    def _():
        for t in range(frames):
            for k, piece in enumerate(column_shifts(upstream[t].astype(jnp.float32), width)):
                shifted[k, t, 1 : height + 1] = piece


def shard_rows(rows, first, second):
    section, index = lax.axis_index("section"), lax.axis_index("dp")
    far, near = jnp.where(section == 0, first, second), jnp.where(section == 0, second, first)
    return pl.ds(pl.multiple_of((index ^ (4 * far + near)) * rows, 8), rows)


GATHERED = ((0, 1, 2, 3), (0, 2, 1, 3))


def unpack_weights(blocks, table):
    rows = blocks[0].shape[1]
    section = lax.axis_index("section")
    for block, chip, plane in zip(blocks, *GATHERED):
        second = jnp.where(section == 0, chip, plane)
        for first in range(4):
            table[shard_rows(rows, first, second), :] = block[first].astype(jnp.float32)


def forward_weights(table, channels):
    rows = 9 * channels
    return jnp.concatenate(
        [table[t * rows : (t + 1) * rows, :].astype(jnp.bfloat16) for t in range(3)], axis=1
    )


def backward_weights(table, channels):
    def turned_taps(times):
        blocks = []
        for k in reversed(range(9)):
            rows = [table[(t * 9 + k) * channels : (t * 9 + k + 1) * channels, :] for t in times]
            blocks.append(summed(rows).astype(jnp.bfloat16))
        return jnp.concatenate(blocks, axis=1)

    return [turned_taps(times) for times in ((0,), (1,), (2,), (0, 1), (0, 1, 2))]


def row_patches(shifted, start, count, height):
    flat, channels = shifted.shape[3:]
    return jnp.concatenate(
        [
            shifted[k, start : start + count, e : e + height].reshape(count * height * flat, channels)
            for e in range(3)
            for k in range(3)
        ],
        axis=1,
    )


def forward_product(shifted, weights, frames, height):
    channels = shifted.shape[-1]
    cells = height * shifted.shape[-2]
    pieces = {}
    for start, count, first_tap in ((0, frames - 2, 0), (frames - 2, 1, 1), (frames - 1, 1, 2)):
        part = jnp.dot(
            row_patches(shifted, start, count, height),
            weights[:, first_tap * channels :],
            preferred_element_type=jnp.float32,
        )
        for t in range(start, start + count):
            rows = slice((t - start) * cells, (t - start + 1) * cells)
            for tap in range(first_tap, 3):
                columns = slice((tap - first_tap) * channels, (tap - first_tap + 1) * channels)
                pieces[t, tap] = part[rows, columns]
    return [
        summed([pieces[max(t + tap - 2, 0), tap] for tap in range(3)]) for t in range(frames)
    ]


def backward_product(shifted, weights, frames, height):
    channels = shifted.shape[-1]
    cells = height * shifted.shape[-2]
    first, second, third, first_two, all_three = weights
    plan = (
        (2, frames - 2, ((first, -2), (second, -1), (third, 0))),
        (1, 1, ((third, 0), (first_two, -1))),
        (0, 1, ((all_three, 0),)),
    )
    reaching = [[] for _ in range(frames)]
    for start, count, terms in plan:
        part = lax.dot_general(
            row_patches(shifted, start, count, height),
            jnp.concatenate([weight for weight, _ in terms], axis=0),
            (((1,), (1,)), ((), ())),
            preferred_element_type=jnp.float32,
        )
        for t in range(start, start + count):
            rows = slice((t - start) * cells, (t - start + 1) * cells)
            for column, (_, step) in enumerate(terms):
                reaching[t + step].append(part[rows, column * channels : (column + 1) * channels])
    return [summed(terms) for terms in reaching]


def first_body(*refs):
    blocks = refs[:4]
    shifted, base, *results, table = refs[4:]
    frames, height, flat, channels = base.shape
    section = lax.axis_index("section")
    unpack_weights(blocks, table)

    @pl.when(section == 0)
    def _():
        branch = forward_product(shifted, forward_weights(table, channels), frames, height)
        for t in range(frames):
            total = base[t].astype(jnp.float32) + branch[t].reshape(height, flat, channels)
            frame_of(results, t)[...] = total.astype(jnp.bfloat16)

    @pl.when(section != 0)
    def _():
        branch = backward_product(shifted, backward_weights(table, channels), frames, height)
        for t in range(frames):
            frame_of(results, t)[...] = branch[t].reshape(height, flat, channels).astype(jnp.bfloat16)


def between_body(mine_low, mine_high, upstream, slope, grads):
    frames = upstream.shape[0]

    @pl.when(lax.axis_index("section") == 0)
    def _():
        for t in range(frames):
            slope[t] = slope_of(frame_of((mine_low, mine_high), t)[...].astype(jnp.float32))

    @pl.when(lax.axis_index("section") != 0)
    def _():
        pad_rows(grads)
        place_grads(grads, [upstream[t].astype(jnp.float32) for t in range(frames)])


def second_body(width, ready, slope, moved, other_low, other_high, upstream, *refs):
    shares, turned, grads = refs
    frames, height, flat, channels = upstream.shape
    rows = shares.shape[2]
    section = lax.axis_index("section")
    cells = height * flat

    def product(left, right):
        taps, done = [], 0
        for met in ((frames + 1, 3), (frames, 2, 3), (0, 1, 2, 3)):
            columns = jnp.concatenate(
                [
                    jnp.concatenate(
                        [
                            right[f, 2 - e : 2 - e + height].reshape(cells, channels)
                            for e in range(3)
                        ],
                        axis=1,
                    )
                    for f in met
                ],
                axis=0,
            )
            part = jnp.dot(
                left[:, : len(met) * cells], columns, preferred_element_type=jnp.float32
            )
            for e in range(3):
                for k in range(3):
                    taps.append(
                        part[k * channels : (k + 1) * channels, e * channels : (e + 1) * channels]
                    )
            while (done + 1) * rows <= len(taps) * channels:
                pieces, row = [], done * rows
                while row < (done + 1) * rows:
                    tap_of, low = divmod(row, channels)
                    high = min(channels, low + (done + 1) * rows - row)
                    pieces.append(taps[tap_of][low:high])
                    row += high - low
                bits = lax.axis_index("dp") ^ done
                far, near = bits // 4, bits % 4
                first = jnp.where(section == 0, far, near)
                second = jnp.where(section == 0, near, far)
                shares[second, first] = jnp.concatenate(pieces, axis=0).astype(jnp.bfloat16)
                done += 1

    @pl.when(section == 0)
    def _():
        pad_rows(grads)
        values = [
            upstream[t].astype(jnp.float32) + slope[t] * frame_of((other_low, other_high), t)[...].astype(jnp.float32)
            for t in range(frames)
        ]
        place_grads(grads, [value.astype(jnp.bfloat16).astype(jnp.float32) for value in values])
        product(ready, grads)

    @pl.when(section != 0)
    def _():
        for t in range(frames):
            squashed = silu_of(frame_of((other_low, other_high), t)[...].astype(jnp.float32)).astype(jnp.bfloat16)
            for k, piece in enumerate(column_shifts(squashed.astype(jnp.float32), width)):
                turn_into(turned, k, t, piece)
        product(turned, moved)


def third_body(*refs):
    blocks = refs[:4]
    mine, other, (produced, table, shifted) = refs[4:6], refs[6:8], refs[8:]
    micro, frames, height, width, channels = produced.shape
    flat = micro * width
    section = lax.axis_index("section")

    def hand_out(t, cells):
        for m in range(micro):
            produced[m, t] = cells[:, m * width : (m + 1) * width, :].astype(jnp.bfloat16)

    @pl.when(section == 0)
    def _():
        for t in range(frames):
            hand_out(t, frame_of(mine, t)[...].astype(jnp.float32))

    @pl.when(section != 0)
    def _():
        unpack_weights(blocks, table)
        zero_row = jnp.zeros((3, frames, 1, flat, channels), jnp.bfloat16)
        shifted[:, :, :1] = zero_row
        shifted[:, :, height + 1 :] = zero_row
        for t in range(frames):
            squashed = silu_of(frame_of(other, t)[...].astype(jnp.float32)).astype(jnp.bfloat16)
            for k, piece in enumerate(column_shifts(squashed.astype(jnp.float32), width)):
                shifted[k, t, 1 : height + 1] = piece
        branch = forward_product(shifted, forward_weights(table, channels), frames, height)
        for t in range(frames):
            hand_out(t, frame_of(other, t)[...].astype(jnp.float32) + branch[t].reshape(height, flat, channels))


def paired_sections(clips, cotangent, weights):
    dp_total = lax.axis_size("dp")
    local_clips, local_grads, shard = clips[:, 0], cotangent[:, 0], weights[0]
    micro, frames, height, width, channels = local_clips.shape
    rows = shard.shape[0]
    flat = micro * width
    cells = height * flat

    def traded(block, bits):
        route = [
            (s * dp_total + i, s * dp_total + (i ^ bits[s])) for s in range(2) for i in range(dp_total)
        ]
        return lax.ppermute(block, ("section", "dp"), route)

    field = (frames, height, flat, channels)
    padded = (3, frames, height + 2, flat, channels)
    met = (frames + 2, height + 2, flat, channels)
    bf16, f32 = jnp.bfloat16, jnp.float32
    unit = 2 * micro * frames * height * width * channels * channels * 27

    first = [traded(shard, (4 * step, step)) for step in range(1, 4)]
    (shard_copy,) = call(copy_body, (shard,), [(shard.shape, bf16)], [], unit // 16)
    shard_copy, first = lax.optimization_barrier((shard_copy, first))
    line = jnp.stack([shard_copy] + first)
    blocks = (line, *[traded(line, (c, 4 * z)) for c, z in list(zip(*GATHERED))[1:]])

    turned = (3 * channels, frames * cells)
    shifted, base, upstream, ready = call(
        prepare_body,
        (local_clips, local_grads),
        [(padded, bf16), (field, bf16), (field, bf16), (turned, bf16)],
        [
            pltpu.VMEM(field, f32),
            pltpu.VMEM(local_clips.shape, bf16),
            pltpu.VMEM(local_clips.shape, bf16),
            pltpu.SemaphoreType.DMA((2,)),
        ],
        unit // 8,
        far=True,
    )
    table = pltpu.VMEM((dp_total * rows, channels), f32)
    half = (frames // 2, height, flat, channels)
    mine = call(first_body, blocks + (shifted, base), [(half, bf16)] * 2, [table], unit)
    other = [lax.ppermute(part, "section", [(0, 1), (1, 0)]) for part in mine]
    slope, moved = call(
        between_body, (*mine, upstream), [(field, f32), (met, bf16)], [], unit // 8
    )
    slope, moved, other = lax.optimization_barrier((slope, moved, other))
    (shares,) = call(
        functools.partial(second_body, width),
        (ready, slope, moved, *other, upstream),
        [((4, 4, rows, channels), bf16)],
        [pltpu.VMEM(turned, bf16), pltpu.VMEM(met, bf16)],
        unit,
    )
    (produced,) = call(
        third_body,
        blocks + (*mine, *other),
        [(local_clips.shape, bf16)],
        [table, pltpu.VMEM(padded, bf16)],
        unit,
    )

    def added(*terms):
        return summed([term.astype(f32) for term in terms])

    received = [traded(shares[step], (step, 4 * step)) for step in (1, 2, 3)]
    received, produced = lax.optimization_barrier((received, produced))
    line_sum = added(shares[0, 1:], *[block[1:] for block in received]).astype(bf16)
    own_sum = added(shares[0, 0], *[block[0] for block in received])
    total = added(own_sum, *[traded(line_sum[step - 1], (4 * step, step)) for step in (3, 2, 1)])
    return (produced[None, :, None], total[None])


def solution(mesh):
    dp_total = mesh.shape["dp"]
    paired = mesh.shape["section"] == 2 and dp_total == 16
    placed = (
        P(None, "dp", None, None, None, None),
        P(None, "dp", None, None, None, None),
        P("section", "dp", None),
    )
    return jax.shard_map(
        paired_sections if paired else many_sections,
        mesh=mesh,
        in_specs=placed,
        out_specs=(P("section", None, "dp", None, None, None, None), P("section", "dp", None)),
        check_vma=False,
    )
```

```python
import functools

import jax
import jax.numpy as jnp
from jax import lax
from jax.experimental import pallas as pl
from jax.experimental.pallas import tpu as pltpu
from jax.sharding import PartitionSpec as P


def passed_along(block, axis, distance):
    devices = range(lax.axis_size(axis))
    route = [(i - distance, i) for i in devices if i - distance in devices]
    return lax.ppermute(block, axis, route)


def gather_patches(field):
    frames, height, width, channels = field.shape
    first_frame = field[:1]
    padded = jnp.concatenate([first_frame, first_frame, field], axis=0)
    padded = jnp.pad(padded, ((0, 0), (1, 1), (1, 1), (0, 0)))
    pieces = [
        padded[
            offset_time : offset_time + frames,
            offset_row : offset_row + height,
            offset_col : offset_col + width,
        ]
        for offset_time in range(3)
        for offset_row in range(3)
        for offset_col in range(3)
    ]
    return jnp.stack(pieces, axis=3).reshape(frames * height * width, 27 * channels)


def squash_field(activation):
    return jax.nn.silu(activation.astype(jnp.float32)).astype(jnp.bfloat16)


def squash_columns(activation):
    return gather_patches(squash_field(activation))


def layer_forward(activation, weight):
    branch = jnp.dot(squash_columns(activation), weight, preferred_element_type=jnp.float32)
    return (activation.astype(jnp.float32) + branch.reshape(activation.shape)).astype(jnp.bfloat16)


def input_gradient(activation, upstream, weight):
    flat_grad = upstream.reshape(-1, weight.shape[1])
    column_grad = lax.dot_general(
        flat_grad, weight, (((1,), (1,)), ((), ())), preferred_element_type=jnp.float32
    )
    base = activation.astype(jnp.float32)
    _, unfold = jax.vjp(gather_patches, base)
    field_grad = unfold(column_grad)[0]
    sigmoid_value = jax.nn.sigmoid(base)
    slope = sigmoid_value * (1.0 + base * (1.0 - sigmoid_value))
    return (upstream.astype(jnp.float32) + field_grad * slope).astype(jnp.bfloat16)


def weight_term(activation, upstream):
    flat_grad = upstream.reshape(-1, upstream.shape[-1])
    return lax.dot_general(
        squash_columns(activation),
        flat_grad,
        (((0,), (0,)), ((), ())),
        preferred_element_type=jnp.float32,
    )


def many_sections(clips, cotangent, weights):
    section_total = lax.axis_size("section")
    section_index = lax.axis_index("section")
    weight = lax.all_gather(weights, "dp", axis=1, tiled=True)[0]
    local_clips = clips[:, 0]
    local_grads = cotangent[:, 0]
    micro_count = local_clips.shape[0]
    step_count = micro_count + section_total - 1
    empty_field = jnp.zeros(local_clips.shape[1:], jnp.bfloat16)

    def forward_step(step_index, carry):
        received, saved_inputs, produced = carry
        micro_index = step_index - section_index
        active = (micro_index >= 0) & (micro_index < micro_count)
        slot_index = jnp.clip(micro_index, 0, micro_count - 1)
        fresh = lax.dynamic_index_in_dim(local_clips, slot_index, 0, keepdims=False)
        layer_input = jnp.where(section_index == 0, fresh, received)
        layer_output = layer_forward(layer_input, weight)
        kept_input = jnp.where(
            active,
            layer_input,
            lax.dynamic_index_in_dim(saved_inputs, slot_index, 0, keepdims=False),
        )
        kept_output = jnp.where(
            active, layer_output, lax.dynamic_index_in_dim(produced, slot_index, 0, keepdims=False)
        )
        saved_inputs = lax.dynamic_update_index_in_dim(saved_inputs, kept_input, slot_index, 0)
        produced = lax.dynamic_update_index_in_dim(produced, kept_output, slot_index, 0)
        received = passed_along(layer_output, "section", 1)
        return (received, saved_inputs, produced)

    start_forward = (empty_field, jnp.zeros_like(local_clips), jnp.zeros_like(local_clips))
    _, saved_inputs, produced = lax.fori_loop(0, step_count, forward_step, start_forward)

    def backward_step(step_index, carry):
        received, grad_total, kept_grads = carry
        micro_index = step_index - (section_total - 1 - section_index)
        active = (micro_index >= 0) & (micro_index < micro_count)
        slot_index = jnp.clip(micro_index, 0, micro_count - 1)
        fresh = lax.dynamic_index_in_dim(local_grads, slot_index, 0, keepdims=False)
        upstream = jnp.where(section_index == section_total - 1, fresh, received)
        activation = lax.dynamic_index_in_dim(saved_inputs, slot_index, 0, keepdims=False)
        grad_total = grad_total + jnp.where(active, weight_term(activation, upstream), 0.0)
        layer_grad = input_gradient(activation, upstream, weight)
        received = passed_along(layer_grad, "section", -1)
        return (received, grad_total, kept_grads)

    start_backward = (
        empty_field,
        jnp.zeros(weight.shape, jnp.float32),
        jnp.zeros_like(local_grads),
    )
    _, grad_total, kept_grads = lax.fori_loop(0, step_count, backward_step, start_backward)
    grad_share = lax.psum_scatter(
        grad_total.astype(jnp.bfloat16), "dp", scatter_dimension=0, tiled=True
    ).astype(jnp.float32)
    return (produced[None, :, None], grad_share[None])


def summed(terms):
    return functools.reduce(lambda p, q: p + q, terms)


def frame_of(halves, t):
    return halves[t // halves[0].shape[0]].at[t % halves[0].shape[0]]


def silu_of(value):
    return value * jax.nn.sigmoid(value)


def slope_of(value):
    sigmoid_value = jax.nn.sigmoid(value)
    return sigmoid_value * (1.0 + value * (1.0 - sigmoid_value))


def column_shifts(rows, width):
    height, flat, channels = rows.shape
    cells = rows.reshape(height * flat // width, width, channels)
    column = lax.broadcasted_iota(jnp.int32, cells.shape, 1)
    before = jnp.where(column == 0, 0.0, pltpu.roll(cells, 1, 1))
    after = jnp.where(column == width - 1, 0.0, pltpu.roll(cells, width - 1, 1))
    return [piece.reshape(rows.shape).astype(jnp.bfloat16) for piece in (before, cells, after)]


def whole(count):
    return [pl.BlockSpec(memory_space=pltpu.VMEM)] * count


def call(body, inputs, outputs, scratch, flops, far=False):
    return pl.pallas_call(
        body,
        out_shape=[jax.ShapeDtypeStruct(shape, dtype) for shape, dtype in outputs],
        in_specs=[pl.BlockSpec(memory_space=pl.ANY)] * len(inputs) if far else whole(len(inputs)),
        out_specs=whole(len(outputs)),
        scratch_shapes=scratch,
        compiler_params=pltpu.CompilerParams(vmem_limit_bytes=32 * 1024 * 1024),
        cost_estimate=pl.CostEstimate(flops=flops, bytes_accessed=4_000_000, transcendentals=0),
    )(*inputs)


def turn_into(turned, k, t, piece):
    channels = piece.shape[-1]
    flat = piece.reshape(-1, channels)
    cells = flat.shape[0]
    turned[k * channels : (k + 1) * channels, t * cells : (t + 1) * cells] = flat.T


def pad_rows(grads):
    count, padded_height, flat, channels = grads.shape
    zero_row = jnp.zeros((count, 1, flat, channels), jnp.bfloat16)
    grads[:, :1] = zero_row
    grads[:, padded_height - 1 :] = zero_row


def place_grads(grads, fields):
    height = fields[0].shape[0]
    first_two = fields[0] + fields[1]
    for t, field in enumerate((*fields, first_two, first_two + fields[2])):
        grads[t, 1 : height + 1] = field.astype(jnp.bfloat16)


def copy_body(source, target):
    target[...] = source[...]


def prepare_body(clips_far, cotangent_far, *refs):
    shifted, base, upstream, ready, held, clips, cotangent, sems = refs
    micro, frames, height, width, channels = clips.shape
    section = lax.axis_index("section")
    copies = [
        pltpu.make_async_copy(source, target, sems.at[k])
        for k, (source, target) in enumerate(
            ((clips_far, clips), (cotangent_far, cotangent))
        )
    ]
    for copy in copies:
        copy.start()

    def reorder(source, target):
        for m in range(micro):
            held[:, :, m * width : (m + 1) * width, :] = source[m].astype(jnp.float32)
        for t in range(frames):
            target[t] = held[t].astype(jnp.bfloat16)

    zero_row = jnp.zeros((3, frames, 1) + shifted.shape[3:], jnp.bfloat16)
    shifted[:, :, :1] = zero_row
    shifted[:, :, height + 1 :] = zero_row
    copies[0].wait()
    reorder(clips, base)
    copies[1].wait()
    reorder(cotangent, upstream)

    @pl.when(section == 0)
    def _():
        for t in range(frames):
            squashed = silu_of(base[t].astype(jnp.float32)).astype(jnp.bfloat16)
            for k, piece in enumerate(column_shifts(squashed.astype(jnp.float32), width)):
                shifted[k, t, 1 : height + 1] = piece
                turn_into(ready, k, t, piece)

    @pl.when(section != 0)
    def _():
        for t in range(frames):
            for k, piece in enumerate(column_shifts(upstream[t].astype(jnp.float32), width)):
                shifted[k, t, 1 : height + 1] = piece


def shard_rows(rows, first, second):
    section, index = lax.axis_index("section"), lax.axis_index("dp")
    far, near = jnp.where(section == 0, first, second), jnp.where(section == 0, second, first)
    return pl.ds(pl.multiple_of((index ^ (4 * far + near)) * rows, 8), rows)


GATHERED = ((0, 1, 2, 3), (0, 2, 1, 3))


def unpack_weights(blocks, table):
    rows = blocks[0].shape[1]
    section = lax.axis_index("section")
    for block, chip, plane in zip(blocks, *GATHERED):
        second = jnp.where(section == 0, chip, plane)
        for first in range(4):
            table[shard_rows(rows, first, second), :] = block[first].astype(jnp.float32)


def forward_weights(table, channels):
    rows = 9 * channels
    return jnp.concatenate(
        [table[t * rows : (t + 1) * rows, :].astype(jnp.bfloat16) for t in range(3)], axis=1
    )


def backward_weights(table, channels):
    def turned_taps(times):
        blocks = []
        for k in reversed(range(9)):
            rows = [table[(t * 9 + k) * channels : (t * 9 + k + 1) * channels, :] for t in times]
            blocks.append(summed(rows).astype(jnp.bfloat16))
        return jnp.concatenate(blocks, axis=1)

    return [turned_taps(times) for times in ((0,), (1,), (2,), (0, 1), (0, 1, 2))]


def row_patches(shifted, start, count, height):
    flat, channels = shifted.shape[3:]
    return jnp.concatenate(
        [
            shifted[k, start : start + count, e : e + height].reshape(count * height * flat, channels)
            for e in range(3)
            for k in range(3)
        ],
        axis=1,
    )


def forward_product(shifted, weights, frames, height):
    channels = shifted.shape[-1]
    cells = height * shifted.shape[-2]
    pieces = {}
    for start, count, first_tap in ((0, frames - 2, 0), (frames - 2, 1, 1), (frames - 1, 1, 2)):
        part = jnp.dot(
            row_patches(shifted, start, count, height),
            weights[:, first_tap * channels :],
            preferred_element_type=jnp.float32,
        )
        for t in range(start, start + count):
            rows = slice((t - start) * cells, (t - start + 1) * cells)
            for tap in range(first_tap, 3):
                columns = slice((tap - first_tap) * channels, (tap - first_tap + 1) * channels)
                pieces[t, tap] = part[rows, columns]
    return [
        summed([pieces[max(t + tap - 2, 0), tap] for tap in range(3)]) for t in range(frames)
    ]


def backward_product(shifted, weights, frames, height):
    channels = shifted.shape[-1]
    cells = height * shifted.shape[-2]
    first, second, third, first_two, all_three = weights
    plan = (
        (2, frames - 2, ((first, -2), (second, -1), (third, 0))),
        (1, 1, ((third, 0), (first_two, -1))),
        (0, 1, ((all_three, 0),)),
    )
    reaching = [[] for _ in range(frames)]
    for start, count, terms in plan:
        part = lax.dot_general(
            row_patches(shifted, start, count, height),
            jnp.concatenate([weight for weight, _ in terms], axis=0),
            (((1,), (1,)), ((), ())),
            preferred_element_type=jnp.float32,
        )
        for t in range(start, start + count):
            rows = slice((t - start) * cells, (t - start + 1) * cells)
            for column, (_, step) in enumerate(terms):
                reaching[t + step].append(part[rows, column * channels : (column + 1) * channels])
    return [summed(terms) for terms in reaching]


def first_body(*refs):
    blocks = refs[:4]
    shifted, base, *results, table = refs[4:]
    frames, height, flat, channels = base.shape
    section = lax.axis_index("section")
    unpack_weights(blocks, table)

    @pl.when(section == 0)
    def _():
        branch = forward_product(shifted, forward_weights(table, channels), frames, height)
        for t in range(frames):
            total = base[t].astype(jnp.float32) + branch[t].reshape(height, flat, channels)
            frame_of(results, t)[...] = total.astype(jnp.bfloat16)

    @pl.when(section != 0)
    def _():
        branch = backward_product(shifted, backward_weights(table, channels), frames, height)
        for t in range(frames):
            frame_of(results, t)[...] = branch[t].reshape(height, flat, channels).astype(jnp.bfloat16)


def between_body(mine_low, mine_high, upstream, slope, grads):
    frames = upstream.shape[0]

    @pl.when(lax.axis_index("section") == 0)
    def _():
        for t in range(frames):
            slope[t] = slope_of(frame_of((mine_low, mine_high), t)[...].astype(jnp.float32))

    @pl.when(lax.axis_index("section") != 0)
    def _():
        pad_rows(grads)
        place_grads(grads, [upstream[t].astype(jnp.float32) for t in range(frames)])


def second_body(width, ready, slope, moved, other_low, other_high, upstream, *refs):
    shares, turned, grads = refs
    frames, height, flat, channels = upstream.shape
    rows = shares.shape[2]
    section = lax.axis_index("section")
    cells = height * flat

    def product(left, right):
        taps, done = [], 0
        for met in ((frames + 1, 3), (frames, 2, 3), (0, 1, 2, 3)):
            columns = jnp.concatenate(
                [
                    jnp.concatenate(
                        [
                            right[f, 2 - e : 2 - e + height].reshape(cells, channels)
                            for e in range(3)
                        ],
                        axis=1,
                    )
                    for f in met
                ],
                axis=0,
            )
            part = jnp.dot(
                left[:, : len(met) * cells], columns, preferred_element_type=jnp.float32
            )
            for e in range(3):
                for k in range(3):
                    taps.append(
                        part[k * channels : (k + 1) * channels, e * channels : (e + 1) * channels]
                    )
            while (done + 1) * rows <= len(taps) * channels:
                pieces, row = [], done * rows
                while row < (done + 1) * rows:
                    tap_of, low = divmod(row, channels)
                    high = min(channels, low + (done + 1) * rows - row)
                    pieces.append(taps[tap_of][low:high])
                    row += high - low
                bits = lax.axis_index("dp") ^ done
                far, near = bits // 4, bits % 4
                first = jnp.where(section == 0, far, near)
                second = jnp.where(section == 0, near, (4 - far) % 4)
                shares[second, first] = jnp.concatenate(pieces, axis=0).astype(jnp.bfloat16)
                done += 1

    @pl.when(section == 0)
    def _():
        pad_rows(grads)
        values = [
            upstream[t].astype(jnp.float32) + slope[t] * frame_of((other_low, other_high), t)[...].astype(jnp.float32)
            for t in range(frames)
        ]
        place_grads(grads, [value.astype(jnp.bfloat16).astype(jnp.float32) for value in values])
        product(ready, grads)

    @pl.when(section != 0)
    def _():
        for t in range(frames):
            squashed = silu_of(frame_of((other_low, other_high), t)[...].astype(jnp.float32)).astype(jnp.bfloat16)
            for k, piece in enumerate(column_shifts(squashed.astype(jnp.float32), width)):
                turn_into(turned, k, t, piece)
        product(turned, moved)


def third_body(*refs):
    blocks = refs[:4]
    mine, other, (produced, table, shifted) = refs[4:6], refs[6:8], refs[8:]
    micro, frames, height, width, channels = produced.shape
    flat = micro * width
    section = lax.axis_index("section")

    def hand_out(t, cells):
        for m in range(micro):
            produced[m, t] = cells[:, m * width : (m + 1) * width, :].astype(jnp.bfloat16)

    @pl.when(section == 0)
    def _():
        for t in range(frames):
            hand_out(t, frame_of(mine, t)[...].astype(jnp.float32))

    @pl.when(section != 0)
    def _():
        unpack_weights(blocks, table)
        zero_row = jnp.zeros((3, frames, 1, flat, channels), jnp.bfloat16)
        shifted[:, :, :1] = zero_row
        shifted[:, :, height + 1 :] = zero_row
        for t in range(frames):
            squashed = silu_of(frame_of(other, t)[...].astype(jnp.float32)).astype(jnp.bfloat16)
            for k, piece in enumerate(column_shifts(squashed.astype(jnp.float32), width)):
                shifted[k, t, 1 : height + 1] = piece
        branch = forward_product(shifted, forward_weights(table, channels), frames, height)
        for t in range(frames):
            hand_out(t, frame_of(other, t)[...].astype(jnp.float32) + branch[t].reshape(height, flat, channels))


def paired_sections(clips, cotangent, weights):
    dp_total = lax.axis_size("dp")
    local_clips, local_grads, shard = clips[:, 0], cotangent[:, 0], weights[0]
    micro, frames, height, width, channels = local_clips.shape
    rows = shard.shape[0]
    flat = micro * width
    cells = height * flat

    def traded(block, bits):
        route = [
            (s * dp_total + i, s * dp_total + (i ^ bits[s])) for s in range(2) for i in range(dp_total)
        ]
        return lax.ppermute(block, ("section", "dp"), route)

    field = (frames, height, flat, channels)
    padded = (3, frames, height + 2, flat, channels)
    met = (frames + 2, height + 2, flat, channels)
    bf16, f32 = jnp.bfloat16, jnp.float32
    unit = 2 * micro * frames * height * width * channels * channels * 27

    first = [traded(shard, (4 * step, step)) for step in range(1, 4)]
    (shard_copy,) = call(copy_body, (shard,), [(shard.shape, bf16)], [], unit // 16)
    shard_copy, first = lax.optimization_barrier((shard_copy, first))
    line = jnp.stack([shard_copy] + first)
    blocks = (line, *[traded(line, (c, 4 * z)) for c, z in list(zip(*GATHERED))[1:]])

    turned = (3 * channels, frames * cells)
    shifted, base, upstream, ready = call(
        prepare_body,
        (local_clips, local_grads),
        [(padded, bf16), (field, bf16), (field, bf16), (turned, bf16)],
        [
            pltpu.VMEM(field, f32),
            pltpu.VMEM(local_clips.shape, bf16),
            pltpu.VMEM(local_clips.shape, bf16),
            pltpu.SemaphoreType.DMA((2,)),
        ],
        unit // 8,
        far=True,
    )
    table = pltpu.VMEM((dp_total * rows, channels), f32)
    half = (frames // 2, height, flat, channels)
    mine = call(first_body, blocks + (shifted, base), [(half, bf16)] * 2, [table], unit)
    other = [lax.ppermute(part, "section", [(0, 1), (1, 0)]) for part in mine]
    slope, moved = call(
        between_body, (*mine, upstream), [(field, f32), (met, bf16)], [], unit // 8
    )
    slope, moved, other = lax.optimization_barrier((slope, moved, other))
    (shares,) = call(
        functools.partial(second_body, width),
        (ready, slope, moved, *other, upstream),
        [((4, 4, rows, channels), bf16)],
        [pltpu.VMEM(turned, bf16), pltpu.VMEM(met, bf16)],
        unit,
    )
    (produced,) = call(
        third_body,
        blocks + (*mine, *other),
        [(local_clips.shape, bf16)],
        [table, pltpu.VMEM(padded, bf16)],
        unit,
    )

    def added(*terms):
        return summed([term.astype(f32) for term in terms])

    received = [traded(shares[step], (step, 16 - 4 * step)) for step in (3, 2, 1)]
    received, produced = lax.optimization_barrier((received, produced))
    line_sum = added(shares[0, 1:], *[block[1:] for block in received]).astype(bf16)
    own_sum = added(shares[0, 0], *[block[0] for block in received])
    total = added(own_sum, *[traded(line_sum[step - 1], (4 * step, step)) for step in (3, 2, 1)])
    return (produced[None, :, None], total[None])


def solution(mesh):
    dp_total = mesh.shape["dp"]
    paired = mesh.shape["section"] == 2 and dp_total == 16
    placed = (
        P(None, "dp", None, None, None, None),
        P(None, "dp", None, None, None, None),
        P("section", "dp", None),
    )
    return jax.shard_map(
        paired_sections if paired else many_sections,
        mesh=mesh,
        in_specs=placed,
        out_specs=(P("section", None, "dp", None, None, None, None), P("section", "dp", None)),
        check_vma=False,
    )
```

```python
import functools

import jax
import jax.numpy as jnp
from jax import lax
from jax.experimental import pallas as pl
from jax.experimental.pallas import tpu as pltpu
from jax.sharding import PartitionSpec as P


def passed_along(block, axis, distance):
    devices = range(lax.axis_size(axis))
    route = [(i - distance, i) for i in devices if i - distance in devices]
    return lax.ppermute(block, axis, route)


def gather_patches(field):
    frames, height, width, channels = field.shape
    first_frame = field[:1]
    padded = jnp.concatenate([first_frame, first_frame, field], axis=0)
    padded = jnp.pad(padded, ((0, 0), (1, 1), (1, 1), (0, 0)))
    pieces = [
        padded[
            offset_time : offset_time + frames,
            offset_row : offset_row + height,
            offset_col : offset_col + width,
        ]
        for offset_time in range(3)
        for offset_row in range(3)
        for offset_col in range(3)
    ]
    return jnp.stack(pieces, axis=3).reshape(frames * height * width, 27 * channels)


def squash_field(activation):
    return jax.nn.silu(activation.astype(jnp.float32)).astype(jnp.bfloat16)


def squash_columns(activation):
    return gather_patches(squash_field(activation))


def layer_forward(activation, weight):
    branch = jnp.dot(squash_columns(activation), weight, preferred_element_type=jnp.float32)
    return (activation.astype(jnp.float32) + branch.reshape(activation.shape)).astype(jnp.bfloat16)


def input_gradient(activation, upstream, weight):
    flat_grad = upstream.reshape(-1, weight.shape[1])
    column_grad = lax.dot_general(
        flat_grad, weight, (((1,), (1,)), ((), ())), preferred_element_type=jnp.float32
    )
    base = activation.astype(jnp.float32)
    _, unfold = jax.vjp(gather_patches, base)
    field_grad = unfold(column_grad)[0]
    sigmoid_value = jax.nn.sigmoid(base)
    slope = sigmoid_value * (1.0 + base * (1.0 - sigmoid_value))
    return (upstream.astype(jnp.float32) + field_grad * slope).astype(jnp.bfloat16)


def weight_term(activation, upstream):
    flat_grad = upstream.reshape(-1, upstream.shape[-1])
    return lax.dot_general(
        squash_columns(activation),
        flat_grad,
        (((0,), (0,)), ((), ())),
        preferred_element_type=jnp.float32,
    )


def many_sections(clips, cotangent, weights):
    section_total = lax.axis_size("section")
    section_index = lax.axis_index("section")
    weight = lax.all_gather(weights, "dp", axis=1, tiled=True)[0]
    local_clips = clips[:, 0]
    local_grads = cotangent[:, 0]
    micro_count = local_clips.shape[0]
    step_count = micro_count + section_total - 1
    empty_field = jnp.zeros(local_clips.shape[1:], jnp.bfloat16)

    def forward_step(step_index, carry):
        received, saved_inputs, produced = carry
        micro_index = step_index - section_index
        active = (micro_index >= 0) & (micro_index < micro_count)
        slot_index = jnp.clip(micro_index, 0, micro_count - 1)
        fresh = lax.dynamic_index_in_dim(local_clips, slot_index, 0, keepdims=False)
        layer_input = jnp.where(section_index == 0, fresh, received)
        layer_output = layer_forward(layer_input, weight)
        kept_input = jnp.where(
            active,
            layer_input,
            lax.dynamic_index_in_dim(saved_inputs, slot_index, 0, keepdims=False),
        )
        kept_output = jnp.where(
            active, layer_output, lax.dynamic_index_in_dim(produced, slot_index, 0, keepdims=False)
        )
        saved_inputs = lax.dynamic_update_index_in_dim(saved_inputs, kept_input, slot_index, 0)
        produced = lax.dynamic_update_index_in_dim(produced, kept_output, slot_index, 0)
        received = passed_along(layer_output, "section", 1)
        return (received, saved_inputs, produced)

    start_forward = (empty_field, jnp.zeros_like(local_clips), jnp.zeros_like(local_clips))
    _, saved_inputs, produced = lax.fori_loop(0, step_count, forward_step, start_forward)

    def backward_step(step_index, carry):
        received, grad_total, kept_grads = carry
        micro_index = step_index - (section_total - 1 - section_index)
        active = (micro_index >= 0) & (micro_index < micro_count)
        slot_index = jnp.clip(micro_index, 0, micro_count - 1)
        fresh = lax.dynamic_index_in_dim(local_grads, slot_index, 0, keepdims=False)
        upstream = jnp.where(section_index == section_total - 1, fresh, received)
        activation = lax.dynamic_index_in_dim(saved_inputs, slot_index, 0, keepdims=False)
        grad_total = grad_total + jnp.where(active, weight_term(activation, upstream), 0.0)
        layer_grad = input_gradient(activation, upstream, weight)
        received = passed_along(layer_grad, "section", -1)
        return (received, grad_total, kept_grads)

    start_backward = (
        empty_field,
        jnp.zeros(weight.shape, jnp.float32),
        jnp.zeros_like(local_grads),
    )
    _, grad_total, kept_grads = lax.fori_loop(0, step_count, backward_step, start_backward)
    grad_share = lax.psum_scatter(
        grad_total.astype(jnp.bfloat16), "dp", scatter_dimension=0, tiled=True
    ).astype(jnp.float32)
    return (produced[None, :, None], grad_share[None])


def summed(terms):
    return functools.reduce(lambda p, q: p + q, terms)


def frame_of(halves, t):
    return halves[t // halves[0].shape[0]].at[t % halves[0].shape[0]]


def silu_of(value):
    return value * jax.nn.sigmoid(value)


def slope_of(value):
    sigmoid_value = jax.nn.sigmoid(value)
    return sigmoid_value * (1.0 + value * (1.0 - sigmoid_value))


def column_shifts(rows, width):
    height, flat, channels = rows.shape
    cells = rows.reshape(height * flat // width, width, channels)
    column = lax.broadcasted_iota(jnp.int32, cells.shape, 1)
    before = jnp.where(column == 0, 0.0, pltpu.roll(cells, 1, 1))
    after = jnp.where(column == width - 1, 0.0, pltpu.roll(cells, width - 1, 1))
    return [piece.reshape(rows.shape).astype(jnp.bfloat16) for piece in (before, cells, after)]


def whole(count):
    return [pl.BlockSpec(memory_space=pltpu.VMEM)] * count


def call(body, inputs, outputs, scratch, flops, far=False):
    return pl.pallas_call(
        body,
        out_shape=[jax.ShapeDtypeStruct(shape, dtype) for shape, dtype in outputs],
        in_specs=[pl.BlockSpec(memory_space=pl.ANY)] * len(inputs) if far else whole(len(inputs)),
        out_specs=whole(len(outputs)),
        scratch_shapes=scratch,
        compiler_params=pltpu.CompilerParams(vmem_limit_bytes=32 * 1024 * 1024),
        cost_estimate=pl.CostEstimate(flops=flops, bytes_accessed=4_000_000, transcendentals=0),
    )(*inputs)


def turn_into(turned, k, t, piece):
    channels = piece.shape[-1]
    flat = piece.reshape(-1, channels)
    cells = flat.shape[0]
    turned[k * channels : (k + 1) * channels, t * cells : (t + 1) * cells] = flat.T


def pad_rows(grads):
    count, padded_height, flat, channels = grads.shape
    zero_row = jnp.zeros((count, 1, flat, channels), jnp.bfloat16)
    grads[:, :1] = zero_row
    grads[:, padded_height - 1 :] = zero_row


def place_grads(grads, fields):
    height = fields[0].shape[0]
    first_two = fields[0] + fields[1]
    for t, field in enumerate((*fields, first_two, first_two + fields[2])):
        grads[t, 1 : height + 1] = field.astype(jnp.bfloat16)


def copy_body(source, target):
    target[...] = source[...]


def prepare_body(clips_far, cotangent_far, *refs):
    shifted, base, upstream, ready, held, clips, cotangent, sems = refs
    micro, frames, height, width, channels = clips.shape
    section = lax.axis_index("section")
    copies = [
        pltpu.make_async_copy(source, target, sems.at[k])
        for k, (source, target) in enumerate(
            ((clips_far, clips), (cotangent_far, cotangent))
        )
    ]
    for copy in copies:
        copy.start()

    def reorder(source, target):
        for m in range(micro):
            held[:, :, m * width : (m + 1) * width, :] = source[m].astype(jnp.float32)
        for t in range(frames):
            target[t] = held[t].astype(jnp.bfloat16)

    zero_row = jnp.zeros((3, frames, 1) + shifted.shape[3:], jnp.bfloat16)
    shifted[:, :, :1] = zero_row
    shifted[:, :, height + 1 :] = zero_row
    copies[0].wait()
    reorder(clips, base)
    copies[1].wait()
    reorder(cotangent, upstream)

    @pl.when(section == 0)
    def _():
        for t in range(frames):
            squashed = silu_of(base[t].astype(jnp.float32)).astype(jnp.bfloat16)
            for k, piece in enumerate(column_shifts(squashed.astype(jnp.float32), width)):
                shifted[k, t, 1 : height + 1] = piece
                turn_into(ready, k, t, piece)

    @pl.when(section != 0)
    def _():
        for t in range(frames):
            for k, piece in enumerate(column_shifts(upstream[t].astype(jnp.float32), width)):
                shifted[k, t, 1 : height + 1] = piece


def shard_rows(rows, first, second):
    section, index = lax.axis_index("section"), lax.axis_index("dp")
    far, near = jnp.where(section == 0, first, second), jnp.where(section == 0, second, first)
    return pl.ds(pl.multiple_of((index ^ (4 * far + near)) * rows, 8), rows)


GATHERED = ((0, 1, 2, 3), (0, 2, 1, 3))


def unpack_weights(blocks, table):
    rows = blocks[0].shape[1]
    section = lax.axis_index("section")
    for block, chip, plane in zip(blocks, *GATHERED):
        second = jnp.where(section == 0, chip, plane)
        for first in range(4):
            table[shard_rows(rows, first, second), :] = block[first].astype(jnp.float32)


def forward_weights(table, channels):
    rows = 9 * channels
    return jnp.concatenate(
        [table[t * rows : (t + 1) * rows, :].astype(jnp.bfloat16) for t in range(3)], axis=1
    )


def backward_weights(table, channels):
    def turned_taps(times):
        blocks = []
        for k in reversed(range(9)):
            rows = [table[(t * 9 + k) * channels : (t * 9 + k + 1) * channels, :] for t in times]
            blocks.append(summed(rows).astype(jnp.bfloat16))
        return jnp.concatenate(blocks, axis=1)

    return [turned_taps(times) for times in ((0,), (1,), (2,), (0, 1), (0, 1, 2))]


def row_patches(shifted, start, count, height):
    flat, channels = shifted.shape[3:]
    return jnp.concatenate(
        [
            shifted[k, start : start + count, e : e + height].reshape(count * height * flat, channels)
            for e in range(3)
            for k in range(3)
        ],
        axis=1,
    )


def forward_product(shifted, weights, frames, height):
    channels = shifted.shape[-1]
    cells = height * shifted.shape[-2]
    pieces = {}
    for start, count, first_tap in ((0, frames - 2, 0), (frames - 2, 1, 1), (frames - 1, 1, 2)):
        part = jnp.dot(
            row_patches(shifted, start, count, height),
            weights[:, first_tap * channels :],
            preferred_element_type=jnp.float32,
        )
        for t in range(start, start + count):
            rows = slice((t - start) * cells, (t - start + 1) * cells)
            for tap in range(first_tap, 3):
                columns = slice((tap - first_tap) * channels, (tap - first_tap + 1) * channels)
                pieces[t, tap] = part[rows, columns]
    return [
        summed([pieces[max(t + tap - 2, 0), tap] for tap in range(3)]) for t in range(frames)
    ]


def backward_product(shifted, weights, frames, height):
    channels = shifted.shape[-1]
    cells = height * shifted.shape[-2]
    first, second, third, first_two, all_three = weights
    plan = (
        (2, frames - 2, ((first, -2), (second, -1), (third, 0))),
        (1, 1, ((third, 0), (first_two, -1))),
        (0, 1, ((all_three, 0),)),
    )
    reaching = [[] for _ in range(frames)]
    for start, count, terms in plan:
        part = lax.dot_general(
            row_patches(shifted, start, count, height),
            jnp.concatenate([weight for weight, _ in terms], axis=0),
            (((1,), (1,)), ((), ())),
            preferred_element_type=jnp.float32,
        )
        for t in range(start, start + count):
            rows = slice((t - start) * cells, (t - start + 1) * cells)
            for column, (_, step) in enumerate(terms):
                reaching[t + step].append(part[rows, column * channels : (column + 1) * channels])
    return [summed(terms) for terms in reaching]


def first_body(*refs):
    blocks = refs[:4]
    shifted, base, *results, table = refs[4:]
    frames, height, flat, channels = base.shape
    section = lax.axis_index("section")
    unpack_weights(blocks, table)

    @pl.when(section == 0)
    def _():
        branch = forward_product(shifted, forward_weights(table, channels), frames, height)
        for t in range(frames):
            total = base[t].astype(jnp.float32) + branch[t].reshape(height, flat, channels)
            frame_of(results, t)[...] = total.astype(jnp.bfloat16)

    @pl.when(section != 0)
    def _():
        branch = backward_product(shifted, backward_weights(table, channels), frames, height)
        for t in range(frames):
            frame_of(results, t)[...] = branch[t].reshape(height, flat, channels).astype(jnp.bfloat16)


def between_body(mine_low, mine_high, upstream, slope, grads):
    frames = upstream.shape[0]

    @pl.when(lax.axis_index("section") == 0)
    def _():
        for t in range(frames):
            slope[t] = slope_of(frame_of((mine_low, mine_high), t)[...].astype(jnp.float32))

    @pl.when(lax.axis_index("section") != 0)
    def _():
        pad_rows(grads)
        place_grads(grads, [upstream[t].astype(jnp.float32) for t in range(frames)])


def second_body(width, ready, slope, moved, other_low, other_high, upstream, *refs):
    shares, turned, grads = refs
    frames, height, flat, channels = upstream.shape
    rows = shares.shape[2]
    section = lax.axis_index("section")
    cells = height * flat

    def product(left, right):
        taps, done = [], 0
        for met in ((frames + 1, 3), (frames, 2, 3), (0, 1, 2, 3)):
            columns = jnp.concatenate(
                [
                    jnp.concatenate(
                        [
                            right[f, 2 - e : 2 - e + height].reshape(cells, channels)
                            for e in range(3)
                        ],
                        axis=1,
                    )
                    for f in met
                ],
                axis=0,
            )
            part = jnp.dot(
                left[:, : len(met) * cells], columns, preferred_element_type=jnp.float32
            )
            for e in range(3):
                for k in range(3):
                    taps.append(
                        part[k * channels : (k + 1) * channels, e * channels : (e + 1) * channels]
                    )
            while (done + 1) * rows <= len(taps) * channels:
                pieces, row = [], done * rows
                while row < (done + 1) * rows:
                    tap_of, low = divmod(row, channels)
                    high = min(channels, low + (done + 1) * rows - row)
                    pieces.append(taps[tap_of][low:high])
                    row += high - low
                bits = lax.axis_index("dp") ^ done
                far, near = bits // 4, bits % 4
                first = jnp.where(section == 0, far, near)
                second = jnp.where(section == 0, near, jnp.where(far % 3 == 0, far, 3 - far))
                shares[second, first] = jnp.concatenate(pieces, axis=0).astype(jnp.bfloat16)
                done += 1

    @pl.when(section == 0)
    def _():
        pad_rows(grads)
        values = [
            upstream[t].astype(jnp.float32) + slope[t] * frame_of((other_low, other_high), t)[...].astype(jnp.float32)
            for t in range(frames)
        ]
        place_grads(grads, [value.astype(jnp.bfloat16).astype(jnp.float32) for value in values])
        product(ready, grads)

    @pl.when(section != 0)
    def _():
        for t in range(frames):
            squashed = silu_of(frame_of((other_low, other_high), t)[...].astype(jnp.float32)).astype(jnp.bfloat16)
            for k, piece in enumerate(column_shifts(squashed.astype(jnp.float32), width)):
                turn_into(turned, k, t, piece)
        product(turned, moved)


def third_body(*refs):
    blocks = refs[:4]
    mine, other, (produced, table, shifted) = refs[4:6], refs[6:8], refs[8:]
    micro, frames, height, width, channels = produced.shape
    flat = micro * width
    section = lax.axis_index("section")

    def hand_out(t, cells):
        for m in range(micro):
            produced[m, t] = cells[:, m * width : (m + 1) * width, :].astype(jnp.bfloat16)

    @pl.when(section == 0)
    def _():
        for t in range(frames):
            hand_out(t, frame_of(mine, t)[...].astype(jnp.float32))

    @pl.when(section != 0)
    def _():
        unpack_weights(blocks, table)
        zero_row = jnp.zeros((3, frames, 1, flat, channels), jnp.bfloat16)
        shifted[:, :, :1] = zero_row
        shifted[:, :, height + 1 :] = zero_row
        for t in range(frames):
            squashed = silu_of(frame_of(other, t)[...].astype(jnp.float32)).astype(jnp.bfloat16)
            for k, piece in enumerate(column_shifts(squashed.astype(jnp.float32), width)):
                shifted[k, t, 1 : height + 1] = piece
        branch = forward_product(shifted, forward_weights(table, channels), frames, height)
        for t in range(frames):
            hand_out(t, frame_of(other, t)[...].astype(jnp.float32) + branch[t].reshape(height, flat, channels))


def paired_sections(clips, cotangent, weights):
    dp_total = lax.axis_size("dp")
    local_clips, local_grads, shard = clips[:, 0], cotangent[:, 0], weights[0]
    micro, frames, height, width, channels = local_clips.shape
    rows = shard.shape[0]
    flat = micro * width
    cells = height * flat

    def traded(block, bits):
        route = [
            (s * dp_total + i, s * dp_total + (i ^ bits[s])) for s in range(2) for i in range(dp_total)
        ]
        return lax.ppermute(block, ("section", "dp"), route)

    field = (frames, height, flat, channels)
    padded = (3, frames, height + 2, flat, channels)
    met = (frames + 2, height + 2, flat, channels)
    bf16, f32 = jnp.bfloat16, jnp.float32
    unit = 2 * micro * frames * height * width * channels * channels * 27

    first = [traded(shard, (4 * step, step)) for step in range(1, 4)]
    (shard_copy,) = call(copy_body, (shard,), [(shard.shape, bf16)], [], unit // 16)
    shard_copy, first = lax.optimization_barrier((shard_copy, first))
    line = jnp.stack([shard_copy] + first)
    blocks = (line, *[traded(line, (c, 4 * z)) for c, z in list(zip(*GATHERED))[1:]])

    turned = (3 * channels, frames * cells)
    shifted, base, upstream, ready = call(
        prepare_body,
        (local_clips, local_grads),
        [(padded, bf16), (field, bf16), (field, bf16), (turned, bf16)],
        [
            pltpu.VMEM(field, f32),
            pltpu.VMEM(local_clips.shape, bf16),
            pltpu.VMEM(local_clips.shape, bf16),
            pltpu.SemaphoreType.DMA((2,)),
        ],
        unit // 8,
        far=True,
    )
    table = pltpu.VMEM((dp_total * rows, channels), f32)
    half = (frames // 2, height, flat, channels)
    mine = call(first_body, blocks + (shifted, base), [(half, bf16)] * 2, [table], unit)
    other = [lax.ppermute(part, "section", [(0, 1), (1, 0)]) for part in mine]
    slope, moved = call(
        between_body, (*mine, upstream), [(field, f32), (met, bf16)], [], unit // 8
    )
    slope, moved, other = lax.optimization_barrier((slope, moved, other))
    (shares,) = call(
        functools.partial(second_body, width),
        (ready, slope, moved, *other, upstream),
        [((4, 4, rows, channels), bf16)],
        [pltpu.VMEM(turned, bf16), pltpu.VMEM(met, bf16)],
        unit,
    )
    (produced,) = call(
        third_body,
        blocks + (*mine, *other),
        [(local_clips.shape, bf16)],
        [table, pltpu.VMEM(padded, bf16)],
        unit,
    )

    def added(*terms):
        return summed([term.astype(f32) for term in terms])

    received = [traded(shares[c], (c, 4 * z)) for c, z in ((1, 2), (2, 1), (3, 3))]
    received, produced = lax.optimization_barrier((received, produced))
    line_sum = added(shares[0, 1:], *[block[1:] for block in received]).astype(bf16)
    own_sum = added(shares[0, 0], *[block[0] for block in received])
    total = added(own_sum, *[traded(line_sum[step - 1], (4 * step, step)) for step in (3, 2, 1)])
    return (produced[None, :, None], total[None])


def solution(mesh):
    dp_total = mesh.shape["dp"]
    paired = mesh.shape["section"] == 2 and dp_total == 16
    placed = (
        P(None, "dp", None, None, None, None),
        P(None, "dp", None, None, None, None),
        P("section", "dp", None),
    )
    return jax.shard_map(
        paired_sections if paired else many_sections,
        mesh=mesh,
        in_specs=placed,
        out_specs=(P("section", None, "dp", None, None, None, None), P("section", "dp", None)),
        check_vma=False,
    )
```
